32 devices in a mesh: req: 2 (over y), ctx: 8 (over z, x), tp: 2 (over core).
Axes of the slice: x: 2, y: 2, z: 4, core: 2. Of those that a mesh axis runs over, the one named last changes fastest.
Arguments:
- hidden: bfloat16 [2048, 8192], P(('req', 'ctx')), parts along dimension 0, may hold values from -6 to 6
- suffix_hidden: bfloat16 [32, 8192], P(('req', 'ctx')), parts along dimension 0, may hold values from -6 to 6
- norm_gain: float32 [8192], replicated, may hold values from 0.1 to 1.9
- key_matrix: bfloat16 [8192, 512], P('ctx', 'tp'), may hold values from -0.0625 to 0.0625
- value_matrix: bfloat16 [8192, 512], P('ctx', 'tp'), may hold values from -0.0625 to 0.0625
- key_offset_bias: float32 [512], P('tp'), may hold values from -4 to 4
- value_offset_bias: float32 [512], P('tp'), may hold values from -4 to 4
- suffix_query_rows: bfloat16 [32, 4096], P(('req', 'ctx'), 'tp'), parts along dimension 0, may hold values from -100 to 100
- slot_keys: bfloat16 [64, 128, 512], P(('req', 'ctx'), None, 'tp'), parts along dimension 0, may hold values from -4 to 4
- slot_values: bfloat16 [64, 128, 512], P(('req', 'ctx'), None, 'tp'), parts along dimension 0, may hold values from -4 to 4
- page_slot_table: int32 [32], P('req'), parts along dimension 0, may hold values from 0 to 31, as said below
- split_page: int32 [2], P('req'), parts along dimension 0, may hold values from 4 to 8
Outputs:
- front_keys: bfloat16 [2048, 512], P(('req', 'ctx'), 'tp'), parts along dimension 0
- front_values: bfloat16 [2048, 512], P(('req', 'ctx'), 'tp'), parts along dimension 0
- attended: bfloat16 [32, 4096], P(('req', 'ctx'), 'tp'), parts along dimension 0
The draws below stay inside these ranges and needn't reach their ends.
There are 2 independent parts, one for each index of `req`. The reference program is written for one: setup_inputs(seed, part) draws one part's arguments, and reference() takes and returns one part's arrays. A program takes and returns all parts, laid end to end along the dimension named above; an argument that names none is the same for every part. Nothing has to cross between parts.
Inputs may be any that keep to these rules, and one draw needn't show every extreme that they name: `page_slot_table`: distinct storage slots; slot s lies on ctx device s // 4; no device holds more than 4 pages of a group, and some device holds exactly 4.
All inputs are finite; a program needn't handle non-finite values.
Results may differ from the reference program's by a relative error of at most 0.0063.
Values may be sent and summed in bfloat16 or wider, within the bound.
No kernel may reach another device: no remote copies, remote signals or barrier semaphores. Data moves between devices by JAX's collectives and lax.ppermute only.
A program may use at most 64 MiB of HBM per device.

```python
import math
import jax
import jax.numpy as jnp
from jax import lax

MODEL_WIDTH = 8192
QUERY_HEADS = 32
KEY_VALUE_HEADS = 4
HEAD_SIZE = 128
PAGE_TOKENS = 128
DEVICE_SLOTS = 4
QUERY_PER_KEY = 8
PAGES = 16
PROMPT_TOKENS = 2048
FRONT_TOK = 1024
SUFFIX_TOKENS = 16
N_CTX = 8


def owner_device(key):
    return jax.random.randint(jax.random.fold_in(key, 11), (), 0, N_CTX).astype(jnp.int32)


def draw_page_slot_table(key, part):
    owner = owner_device(key)
    key = jax.random.fold_in(key, 3)
    slot_count = N_CTX * DEVICE_SLOTS
    ranks = jax.random.permutation(key, slot_count).astype(jnp.int32)
    index = jnp.arange(slot_count, dtype=jnp.int32)
    owned = index // DEVICE_SLOTS == owner
    score = jnp.where(owned, slot_count + index, ranks)
    order = jnp.argsort(score, stable=True).astype(jnp.int32)
    return jnp.concatenate([order[:PAGES - DEVICE_SLOTS], order[slot_count - DEVICE_SLOTS:]], 0)


def draw_slot_keys(key, part):
    key = jax.random.fold_in(key, 5)
    array_dims = (N_CTX * DEVICE_SLOTS, PAGE_TOKENS, KEY_VALUE_HEADS * HEAD_SIZE)
    values = jnp.clip(jax.random.normal(key, array_dims, jnp.float32), -4.0, 4.0)
    return values.astype(jnp.bfloat16)


def draw_suffix_query_rows(key, part):
    key = jax.random.fold_in(key, 7)
    array_dims = (SUFFIX_TOKENS, QUERY_HEADS * HEAD_SIZE)
    values = jnp.clip(3.0 * jax.random.normal(key, array_dims, jnp.float32), -15.0, 15.0)
    return values.astype(jnp.bfloat16)


def levels(stream_key, shape, split, least, top_value):
    def one(dim, parts):
        steps = jax.random.uniform(jax.random.fold_in(jax.random.fold_in(stream_key, 6), dim), (parts,), jnp.float32, least / len(split), top_value / len(split))
        return jnp.repeat(jnp.exp(steps), shape[dim] // parts).reshape((-1,) + (1,) * (len(shape) - dim - 1))

    level = one(*split[0])
    for cut in split[1:]:
        level = level * one(*cut)
    return level


def bell_draw(key, extent, width, limit, cuts=(), kind=jnp.bfloat16):
    entries = jax.random.normal(key, extent, jnp.float32) * width
    if len(cuts) > 0:
        entries = levels(key, extent, cuts, -0.22, 0.18) * entries
    return jnp.clip(entries, min=-limit, max=limit).astype(kind)


def setup_inputs(seed: int = 0, part: int = 0) -> dict:
    splits = jax.random.split(jax.random.key(seed), 13)
    part_keys = jax.random.split(jax.random.fold_in(splits[12], part), 13)
    return {
        "hidden": bell_draw(part_keys[0], (FRONT_TOK, MODEL_WIDTH), 1.0, 6.0, ((0, 8),)),
        "suffix_hidden": bell_draw(part_keys[1], (SUFFIX_TOKENS, MODEL_WIDTH), 1.0, 6.0, ((0, 8),)),
        "norm_gain": jnp.clip(1.0 + 0.18 * jax.random.normal(splits[2], (MODEL_WIDTH,), jnp.float32), 0.1, 1.9),
        "key_matrix": bell_draw(splits[3], (MODEL_WIDTH, KEY_VALUE_HEADS * HEAD_SIZE), MODEL_WIDTH ** -0.5, 0.0625, ((0, 8), (1, 2))),
        "value_matrix": bell_draw(splits[4], (MODEL_WIDTH, KEY_VALUE_HEADS * HEAD_SIZE), MODEL_WIDTH ** -0.5, 0.0625, ((0, 8), (1, 2))),
        "key_offset_bias": bell_draw(splits[5], (KEY_VALUE_HEADS * HEAD_SIZE,), 1.0, 4.0, ((0, 2),), jnp.float32),
        "value_offset_bias": bell_draw(splits[6], (KEY_VALUE_HEADS * HEAD_SIZE,), 1.0, 4.0, ((0, 2),), jnp.float32),
        "suffix_query_rows": draw_suffix_query_rows(jax.random.fold_in(jax.random.fold_in(splits[12], part), 71), part),
        "slot_keys": draw_slot_keys(jax.random.fold_in(jax.random.fold_in(splits[12], part), 71), part),
        "slot_values": bell_draw(part_keys[9], (N_CTX * DEVICE_SLOTS, PAGE_TOKENS, KEY_VALUE_HEADS * HEAD_SIZE), 1.0, 4.0, ((0, 8), (2, 2))),
        "page_slot_table": draw_page_slot_table(jax.random.fold_in(jax.random.fold_in(splits[12], part), 71), part),
        "split_page": jax.random.randint(part_keys[11], (1,), PAGES // 4, PAGES // 2 + 1).astype(jnp.int32),
    }


epsilon = 1e-06
rope_base = 1000000.0
masked_score = -1e+30

def rms_rows(matrix, norm_gain):
    widened = matrix.astype(jnp.float32)
    inverse = lax.rsqrt(lax.optimization_barrier(jnp.mean(widened * widened, axis=-1, keepdims=True)) + epsilon)
    return (widened * inverse * norm_gain).astype(jnp.bfloat16)

def rotate(key_rows, positions, head_dim):
    row_count = key_rows.shape[0]
    split_heads = key_rows.reshape(row_count, -1, head_dim)
    half_dim = head_dim // 2
    inverse_freq = rope_base ** (-(jnp.arange(half_dim, dtype=jnp.float32) * (2.0 / head_dim)))
    angles = positions.astype(jnp.float32)[:, None] * inverse_freq[None, :]
    cosine = jnp.concatenate([jnp.cos(angles), jnp.cos(angles)], -1)[:, None, :]
    sine = jnp.concatenate([jnp.sin(angles), jnp.sin(angles)], -1)[:, None, :]
    turned = jnp.concatenate([-split_heads[..., half_dim:], split_heads[..., :half_dim]], -1)
    return (split_heads * cosine + turned * sine).reshape(row_count, -1)

def project_rows(matrix, norm_gain, key_matrix, value_matrix, key_offset_bias, value_offset_bias, positions):
    normed = rms_rows(matrix, norm_gain)
    raw_keys = jnp.dot(normed, key_matrix, preferred_element_type=jnp.float32) + key_offset_bias
    new_values = (jnp.dot(normed, value_matrix, preferred_element_type=jnp.float32) + value_offset_bias).astype(jnp.bfloat16)
    new_keys = rotate(raw_keys, positions, HEAD_SIZE).astype(jnp.bfloat16)
    return (new_keys, new_values)

def reference(hidden, suffix_hidden, norm_gain, key_matrix, value_matrix, key_offset_bias, value_offset_bias, suffix_query_rows, slot_keys, slot_values, page_slot_table, split_page):
    front_pos = jnp.arange(FRONT_TOK, dtype=jnp.int32)
    suffix_pos = PROMPT_TOKENS + jnp.arange(SUFFIX_TOKENS, dtype=jnp.int32)
    front_keys, front_values = project_rows(hidden, norm_gain, key_matrix, value_matrix, key_offset_bias, value_offset_bias, front_pos)
    suffix_keys, suffix_values = project_rows(suffix_hidden, norm_gain, key_matrix, value_matrix, key_offset_bias, value_offset_bias, suffix_pos)
    fetched_keys = slot_keys[page_slot_table].reshape(PROMPT_TOKENS, KEY_VALUE_HEADS * HEAD_SIZE)
    fetched_values = slot_values[page_slot_table].reshape(PROMPT_TOKENS, KEY_VALUE_HEADS * HEAD_SIZE)
    every_key = jnp.concatenate([front_keys, fetched_keys, suffix_keys], 0)
    every_value = jnp.concatenate([front_values, fetched_values, suffix_values], 0)
    cut_pos = split_page[0] * PAGE_TOKENS
    loaded_pos = jnp.arange(PROMPT_TOKENS, dtype=jnp.int32)
    prefix_seen = jnp.concatenate([front_pos < cut_pos, loaded_pos >= cut_pos], 0)
    suffix_seen = suffix_pos[None, :] <= suffix_pos[:, None]
    visible = jnp.concatenate([jnp.broadcast_to(prefix_seen[None, :], (SUFFIX_TOKENS, FRONT_TOK + PROMPT_TOKENS)), suffix_seen], 1)
    visible_rows = jnp.repeat(visible, QUERY_PER_KEY, axis=0)
    grouped_heads = suffix_query_rows.reshape(SUFFIX_TOKENS, KEY_VALUE_HEADS, QUERY_PER_KEY, HEAD_SIZE)
    outputs = []
    for current_head in range(KEY_VALUE_HEADS):
        query_rows = grouped_heads[:, current_head].reshape(SUFFIX_TOKENS * QUERY_PER_KEY, HEAD_SIZE)
        head_keys = every_key[:, current_head * HEAD_SIZE:(current_head + 1) * HEAD_SIZE]
        head_values = every_value[:, current_head * HEAD_SIZE:(current_head + 1) * HEAD_SIZE]
        scores = jnp.dot(query_rows, head_keys.T, preferred_element_type=jnp.float32) * (1.0 / math.sqrt(HEAD_SIZE))
        scores = jnp.where(visible_rows, scores, masked_score)
        row_top = lax.optimization_barrier(jnp.max(scores, axis=-1, keepdims=True))
        expos = jnp.where(visible_rows, jnp.exp(scores - row_top), 0.0)
        denominator = lax.optimization_barrier(jnp.sum(expos, axis=-1, keepdims=True))
        weights = expos.astype(jnp.bfloat16)
        numer = jnp.dot(weights, head_values, preferred_element_type=jnp.float32)
        outputs.append((numer / denominator).reshape(SUFFIX_TOKENS, QUERY_PER_KEY, HEAD_SIZE))
    attended = jnp.stack(outputs, 1).reshape(SUFFIX_TOKENS, QUERY_HEADS * HEAD_SIZE).astype(jnp.bfloat16)
    return (front_keys, front_values, attended)
```

```python
import math

import jax
import jax.numpy as jnp
from jax import lax
from jax.experimental import pallas as pl
from jax.experimental.pallas import tpu as pltpu
from jax.sharding import PartitionSpec as P

QUERY_HEADS = 32
KEY_VALUE_HEADS = 4
HEAD_SIZE = 128


epsilon = 1e-06
rope_base = 1000000.0
masked_score = -1e30


def rms_rows(matrix, norm_gain):
    widened = matrix.astype(jnp.float32)
    inverse = lax.rsqrt(jnp.mean(widened * widened, axis=-1, keepdims=True) + epsilon)
    return (widened * inverse * norm_gain).astype(jnp.bfloat16)


def rotate(key_rows, positions, head_dim):
    row_count = key_rows.shape[0]
    split_heads = key_rows.reshape(row_count, -1, head_dim)
    half_dim = head_dim // 2
    inverse_freq = rope_base ** (-(jnp.arange(half_dim, dtype=jnp.float32) * (2.0 / head_dim)))
    angles = positions.astype(jnp.float32)[:, None] * inverse_freq[None, :]
    cosine = jnp.concatenate([jnp.cos(angles), jnp.cos(angles)], -1)[:, None, :]
    sine = jnp.concatenate([jnp.sin(angles), jnp.sin(angles)], -1)[:, None, :]
    turned = jnp.concatenate([-split_heads[..., half_dim:], split_heads[..., :half_dim]], -1)
    return (split_heads * cosine + turned * sine).reshape(row_count, -1)


def gathered_plan(
    hidden,
    suffix_hidden,
    norm_gain,
    key_matrix,
    value_matrix,
    key_offset_bias,
    value_offset_bias,
    suffix_query_rows,
    slot_keys,
    slot_values,
    page_slot_table,
    split_page,
):
    ctx_index = lax.axis_index("ctx")
    queries = lax.all_gather(suffix_query_rows, "ctx", axis=0, tiled=True)
    front_rows = hidden.shape[0]
    suffix_rows = suffix_hidden.shape[0]
    page_size = slot_keys.shape[1]
    slot_count = slot_keys.shape[0]
    total_pages = page_slot_table.shape[0]
    prefix_len = total_pages * page_size
    normed = rms_rows(jnp.concatenate([hidden, suffix_hidden], 0), norm_gain)
    col_width = key_matrix.shape[1]

    def accumulate(block_rows):
        return jnp.dot(normed, block_rows, preferred_element_type=jnp.float32)

    key_acc = accumulate(lax.all_gather(key_matrix, "ctx", axis=0, tiled=True))
    value_acc = accumulate(lax.all_gather(value_matrix, "ctx", axis=0, tiled=True))
    front_pos = ctx_index * front_rows + jnp.arange(front_rows, dtype=jnp.int32)
    suffix_pos = prefix_len + ctx_index * suffix_rows + jnp.arange(suffix_rows, dtype=jnp.int32)
    new_keys = rotate(
        key_acc + key_offset_bias, jnp.concatenate([front_pos, suffix_pos], 0), HEAD_SIZE
    ).astype(jnp.bfloat16)
    new_values = (value_acc + value_offset_bias).astype(jnp.bfloat16)
    cut_pos = split_page[0] * page_size
    global_slot = ctx_index * slot_count + jnp.arange(slot_count, dtype=jnp.int32)
    page_index = jnp.arange(total_pages, dtype=jnp.int32)
    slot_hits = (page_slot_table[None, :] == global_slot[:, None]) & (
        page_index[None, :] >= split_page[0]
    )
    slot_live = jnp.max(slot_hits.astype(jnp.int32), axis=1) > 0
    every_key = jnp.concatenate(
        [new_keys[:front_rows], slot_keys.reshape(-1, col_width), new_keys[front_rows:]], 0
    )
    every_value = jnp.concatenate(
        [new_values[:front_rows], slot_values.reshape(-1, col_width), new_values[front_rows:]], 0
    )
    query_count = queries.shape[0]
    query_pos = prefix_len + jnp.arange(query_count, dtype=jnp.int32)
    prefix_seen = jnp.concatenate([front_pos < cut_pos, jnp.repeat(slot_live, page_size)], 0)
    suffix_seen = suffix_pos[None, :] <= query_pos[:, None]
    visible = jnp.concatenate(
        [jnp.broadcast_to(prefix_seen[None, :], (query_count, prefix_seen.shape[0])), suffix_seen],
        1,
    )
    visible_wide = visible[:, None, :]
    sharing_count = QUERY_HEADS // KEY_VALUE_HEADS
    local_heads = col_width // HEAD_SIZE
    grouped_heads = queries.reshape(query_count, local_heads, sharing_count, HEAD_SIZE)
    top_list = []
    total_list = []
    numer_list = []
    for current_head in range(local_heads):
        head_keys = every_key[:, current_head * HEAD_SIZE : (current_head + 1) * HEAD_SIZE]
        head_values = every_value[:, current_head * HEAD_SIZE : (current_head + 1) * HEAD_SIZE]
        scores = jnp.einsum(
            "qgd,ld->qgl",
            grouped_heads[:, current_head],
            head_keys,
            preferred_element_type=jnp.float32,
        ) * (1.0 / math.sqrt(HEAD_SIZE))
        scores = jnp.where(visible_wide, scores, masked_score)
        row_top = jnp.max(scores, axis=-1)
        expos = jnp.where(visible_wide, jnp.exp(scores - row_top[..., None]), 0.0)
        total_list.append(jnp.sum(expos, axis=-1))
        top_list.append(row_top)
        numer_list.append(
            jnp.einsum(
                "qgl,ld->qgd",
                expos.astype(jnp.bfloat16),
                head_values,
                preferred_element_type=jnp.float32,
            )
        )
    row_top = jnp.stack(top_list, 1)
    weight_total = jnp.stack(total_list, 1)
    numer = jnp.stack(numer_list, 1)
    global_top = lax.pmax(row_top, "ctx")
    factor = jnp.exp(row_top - global_top)
    own_total, own_numer = (
        lax.psum_scatter(
            (weight_total * factor).reshape(query_count, -1), "ctx", scatter_dimension=0, tiled=True
        ),
        lax.psum_scatter(
            (numer * factor[..., None]).reshape(query_count, -1),
            "ctx",
            scatter_dimension=0,
            tiled=True,
        ),
    )
    own_total = own_total.reshape(suffix_rows, local_heads, sharing_count)
    own_numer = own_numer.reshape(suffix_rows, local_heads, sharing_count, HEAD_SIZE)
    attended = (own_numer / own_total[..., None]).reshape(suffix_rows, -1).astype(jnp.bfloat16)
    return (new_keys[:front_rows], new_values[:front_rows], attended)

GROUPS = 4
PAIR = 2
LANES = 128
SCALE = 1.0 / math.sqrt(HEAD_SIZE)


def row_scale(values):
    mean = jnp.sum(values * values, axis=-1, keepdims=True) * (1.0 / values.shape[-1])
    return lax.rsqrt(mean + epsilon)


def norm_kernel(place_ref, hidden_ref, suffix_ref, gain_ref, *rest):
    outs, tail_ref = rest[:GROUPS], rest[GROUPS]
    core, ctx = place_ref[0], place_ref[1]
    z, x = ctx // PAIR, ctx % PAIR
    step = pl.program_id(0)
    rows = hidden_ref.shape[0]
    half_rows = rows * pl.num_programs(0)
    block = hidden_ref.shape[1] // (GROUPS * PAIR)
    per_block = block // LANES
    inverse = row_scale(hidden_ref[...].astype(jnp.float32))

    def offset(shift, side, j):
        owner = lax.rem(z + shift, GROUPS) * PAIR + lax.rem(x + side, PAIR)
        return pl.multiple_of(owner * block + j * LANES, LANES)

    for shift in range(GROUPS):
        for side in range(PAIR):
            for j in range(per_block):
                columns = pl.ds(offset(shift, side, j), LANES)
                piece = hidden_ref[:, columns].astype(jnp.float32) * inverse * gain_ref[:, columns]
                start = pl.multiple_of((side * per_block + j) * half_rows + step * rows, rows)
                outs[shift][pl.ds(start, rows), :] = piece.astype(jnp.bfloat16)

    @pl.when(step == 0)
    def _():
        both = suffix_ref[...].astype(jnp.float32)
        normed = both * row_scale(both) * gain_ref[...]
        tail_ref[...] = jnp.where(core == 0, normed[0:1], normed[1:2])
        for shift in range(GROUPS):
            pieces = [
                tail_ref[:, pl.ds(offset(shift, side, j), LANES)]
                for side in range(PAIR)
                for j in range(per_block)
            ]
            start = PAIR * per_block * half_rows
            outs[shift][start : start + PAIR * per_block, :] = jnp.concatenate(pieces, 0).astype(
                jnp.bfloat16
            )


def project_kernel(*refs):
    blocks = refs[: 2 * GROUPS]
    near_key, near_value, far_key, far_value = refs[2 * GROUPS : 2 * GROUPS + 4]
    outs = refs[2 * GROUPS + 4 : 3 * GROUPS + 4]
    lhs_ref = refs[3 * GROUPS + 4]
    depth = near_key.shape[0]
    pieces = 2 * depth // LANES
    half_rows = (blocks[0].shape[0] - pieces) // pieces
    rows = 2 * half_rows
    tails = []
    for i, block in enumerate(blocks):
        for j in range(pieces):
            lhs_ref[i * half_rows : (i + 1) * half_rows, j * LANES : (j + 1) * LANES] = block[
                j * half_rows : (j + 1) * half_rows, :
            ]
        tail = block[pieces * half_rows :, :].astype(jnp.float32)
        tails.append(jnp.concatenate([tail[j : j + 1] for j in range(pieces)], 1))
    tails.append(jnp.zeros((16 - len(tails), 2 * depth), jnp.float32))
    total = GROUPS * rows
    lhs_ref[total : total + 16, :] = jnp.concatenate(tails, 0).astype(jnp.bfloat16)

    def product(near, far):
        return jnp.dot(
            lhs_ref[:, :depth], near[...], preferred_element_type=jnp.float32
        ) + jnp.dot(lhs_ref[:, depth:], far[...], preferred_element_type=jnp.float32)

    keys = product(near_key, far_key)
    values = product(near_value, far_value)
    high = keys.astype(jnp.bfloat16).astype(jnp.float32)
    low = keys - high
    columns = []
    for array in (high, low, values):
        for j in range(array.shape[1] // LANES):
            columns.append(array[:, j * LANES : (j + 1) * LANES])
    for group in range(GROUPS):
        for t, column in enumerate(columns):
            outs[group][t * rows : (t + 1) * rows, :] = column[
                group * rows : (group + 1) * rows
            ].astype(jnp.bfloat16)
        ends = [c[total + 2 * group : total + 2 * group + 2] for c in columns]
        ends.append(jnp.zeros((16 - 2 * len(columns), LANES), jnp.float32))
        outs[group][len(columns) * rows :, :] = jnp.concatenate(ends, 0).astype(jnp.bfloat16)


def head_queries(query_ref, head, sharing):
    start = head * sharing * HEAD_SIZE
    return jnp.concatenate(
        [query_ref[:, start + g * HEAD_SIZE : start + (g + 1) * HEAD_SIZE] for g in range(sharing)], 0
    )


def times_transposed(a, b):
    return lax.dot_general(a, b, (((1,), (1,)), ((), ())), preferred_element_type=jnp.float32)


def loaded_kernel(place_ref, table_ref, split_ref, query_ref, key_ref, value_ref, top_ref, total_ref, numer_ref):
    ctx = place_ref[1]
    slots, page, width = key_ref.shape
    heads = width // HEAD_SIZE
    sharing = query_ref.shape[1] // width
    split = split_ref[0]
    live = []
    for s in range(slots):
        hit = jnp.int32(0)
        for p in range(table_ref.shape[0]):
            hit = hit | ((table_ref[p] == ctx * slots + s) & (p >= split)).astype(jnp.int32)
        live.append(hit)
    for head in range(heads):
        columns = slice(head * HEAD_SIZE, (head + 1) * HEAD_SIZE)
        queries = head_queries(query_ref, head, sharing)
        count = queries.shape[0]
        scores = [
            jnp.where(live[s] > 0, times_transposed(queries, key_ref[s, :, columns]) * SCALE, masked_score)
            for s in range(slots)
        ]
        top = scores[0].max(-1, keepdims=True)
        for s in range(1, slots):
            top = jnp.maximum(top, scores[s].max(-1, keepdims=True))
        total = jnp.zeros((count, 1), jnp.float32)
        numer = jnp.zeros((count, HEAD_SIZE), jnp.float32)
        for s in range(slots):
            expos = jnp.where(live[s] > 0, jnp.exp(scores[s] - top), 0.0)
            total += expos.sum(-1, keepdims=True)
            numer += jnp.dot(
                expos.astype(jnp.bfloat16), value_ref[s, :, columns], preferred_element_type=jnp.float32
            )
        rows = slice(head * count, (head + 1) * count)
        top_ref[rows, :] = jnp.broadcast_to(top, (count, LANES))
        total_ref[rows, :] = jnp.broadcast_to(total, (count, LANES))
        numer_ref[rows, :] = numer


def front_kernel(
    place_ref, split_ref, own, *refs
):
    received = refs[: GROUPS - 1]
    (key_bias, value_bias, cosine_ref, sine_ref, query_ref, top_ref, total_ref, numer_ref) = refs[
        GROUPS - 1 : GROUPS + 7
    ]
    front_key, front_value = refs[GROUPS + 7 : GROUPS + 9]
    outs = refs[GROUPS + 9 : -2]
    state_ref, stat_ref = refs[-2:]
    core, ctx = place_ref[0], place_ref[1]
    rows, width = front_key.shape
    half_rows = rows // 2
    heads = width // HEAD_SIZE
    n_ctx = len(outs)
    query_count = query_ref.shape[0]
    own_queries = query_count // n_ctx
    sharing = query_ref.shape[1] // width
    count = sharing * query_count
    visible = ctx < split_ref[0]

    def summed(start, size):
        value = own[start : start + size, :].astype(jnp.float32)
        for ref in received:
            value += ref[start : start + size, :].astype(jnp.float32)
        return value

    ends = summed(3 * heads * rows, 16)
    row_slot = lax.broadcasted_iota(jnp.int32, (count, 16), 0) % query_count
    query_position = lax.rem(ctx - row_slot // own_queries + n_ctx, n_ctx) * own_queries + row_slot % own_queries
    end_column = lax.broadcasted_iota(jnp.int32, (count, 16), 1)
    end_position = ctx * 2 + jnp.where(end_column == 0, core, 1 - core)
    end_seen = (end_column < 2) & (end_position <= query_position)
    pad = jnp.zeros((14, HEAD_SIZE), jnp.float32)
    for head in range(heads):
        columns = slice(head * HEAD_SIZE, (head + 1) * HEAD_SIZE)
        raw = summed(head * rows, rows) + summed((heads + head) * rows, rows)
        value = (summed((2 * heads + head) * rows, rows) + value_bias[:, columns]).astype(jnp.bfloat16)
        end_raw = ends[2 * head : 2 * head + 2] + ends[2 * (heads + head) : 2 * (heads + head) + 2]
        end_value = ends[2 * (2 * heads + head) : 2 * (2 * heads + head) + 2] + value_bias[:, columns]
        end_raw = jnp.concatenate([end_raw + key_bias[:, columns], pad], 0)
        end_value = jnp.concatenate([end_value, pad], 0).astype(jnp.bfloat16)
        raw = raw + key_bias[:, columns]

        def rotated(k, part):
            turned = pltpu.roll(k, HEAD_SIZE // 2, 1)
            return (k * cosine_ref[part, :] + turned * sine_ref[part, :]).astype(jnp.bfloat16)

        key = rotated(raw, slice(0, rows))
        end_key = rotated(end_raw, slice(rows, rows + 16))
        for half in range(2):
            to = pl.ds(pl.multiple_of(lax.rem(core + half, 2) * half_rows, half_rows), half_rows)
            front_key[to, columns] = key[half * half_rows : (half + 1) * half_rows]
            front_value[to, columns] = value[half * half_rows : (half + 1) * half_rows]
        queries = head_queries(query_ref, head, sharing)
        scores = jnp.where(visible, times_transposed(queries, key) * SCALE, masked_score)
        end_scores = jnp.where(end_seen, times_transposed(queries, end_key) * SCALE, masked_score)
        part = slice(head * count, (head + 1) * count)
        old_top = top_ref[part, :]
        top = jnp.maximum(scores.max(-1, keepdims=True), end_scores.max(-1, keepdims=True))
        top = jnp.maximum(old_top, top)
        factor = jnp.exp(old_top - top)
        expos = jnp.where(visible, jnp.exp(scores - top), 0.0)
        end_expos = jnp.where(end_seen, jnp.exp(end_scores - top[:, :16]), 0.0)
        total = total_ref[part, :] * factor + (
            expos.sum(-1, keepdims=True) + end_expos.sum(-1, keepdims=True)
        )
        numer = (
            numer_ref[part, :] * factor
            + jnp.dot(expos.astype(jnp.bfloat16), value, preferred_element_type=jnp.float32)
            + jnp.dot(end_expos.astype(jnp.bfloat16), end_value, preferred_element_type=jnp.float32)
        )
        state_ref[part, :] = numer
        lane = lax.broadcasted_iota(jnp.int32, (count, LANES), 1)
        stat_ref[part, :] = jnp.where(lane < LANES // 2, top, total)
    query_heads = heads * sharing
    for slot, out in enumerate(outs):
        for i in range(own_queries):
            pick = pl.ds(slot * own_queries + i, query_heads, stride=query_count)
            out[i * query_heads : (i + 1) * query_heads, :] = state_ref[pick, :]
            out[(own_queries + i) * query_heads : (own_queries + i + 1) * query_heads, :] = stat_ref[pick, :]


def merge_kernel(*refs):
    parts, out = refs[:-1], refs[-1]
    rows = parts[0].shape[0] // 2
    tops = [p[rows:, 0:1] for p in parts]
    top = tops[0]
    for t in tops[1:]:
        top = jnp.maximum(top, t)
    total = jnp.zeros((rows, 1), jnp.float32)
    numer = jnp.zeros((rows, LANES), jnp.float32)
    for p, t in zip(parts, tops):
        factor = jnp.exp(t - top)
        total += factor * p[rows:, LANES // 2 : LANES // 2 + 1]
        numer += factor * p[:rows, :]
    result = numer / total
    queries = out.shape[0]
    each = rows // queries
    lines = [
        jnp.concatenate([result[i * each + k : i * each + k + 1] for k in range(each)], 1)
        for i in range(queries)
    ]
    out[...] = jnp.concatenate(lines, 0).astype(jnp.bfloat16)


def exchange_plan(
    hidden,
    suffix_hidden,
    norm_gain,
    key_matrix,
    value_matrix,
    key_offset_bias,
    value_offset_bias,
    suffix_query_rows,
    slot_keys,
    slot_values,
    page_slot_table,
    split_page,
):
    n_ctx = GROUPS * PAIR
    ctx = lax.axis_index("ctx").astype(jnp.int32)
    core = lax.axis_index("tp").astype(jnp.int32)
    place = jnp.stack([core, ctx])
    rows, features = hidden.shape
    half_rows = rows // 2
    width = key_matrix.shape[1]
    query_width = suffix_query_rows.shape[1]
    prefix_len = page_slot_table.shape[0] * slot_keys.shape[1]
    smem = pl.BlockSpec(memory_space=pltpu.SMEM)
    vmem = pl.BlockSpec(memory_space=pltpu.VMEM)
    params = pltpu.CompilerParams(vmem_limit_bytes=48 * 1024 * 1024)

    def move(array, target):
        pairs = []
        for c in range(n_ctx):
            for t in range(2):
                to_c, to_t = target(c, t)
                pairs.append((c * 2 + t, to_c * 2 + to_t))
        return lax.ppermute(array, ("ctx", "tp"), pairs)

    def around(shift):
        return lambda c, t: ((c + shift) % n_ctx, t)

    def along(shift):
        return lambda c, t: ((c // PAIR + shift) % GROUPS * PAIR + c % PAIR, t)

    def beside(c, t):
        return (c ^ 1, t)

    def sibling(c, t):
        return (c, 1 - t)

    query_parts = [suffix_query_rows] + [move(suffix_query_rows, around(s)) for s in range(1, n_ctx)]
    far_key = move(key_matrix, beside)
    far_value = move(value_matrix, beside)

    steps = 4
    pieces = features // GROUPS // LANES
    block_rows = pieces * half_rows + pieces
    blocks = pl.pallas_call(
        norm_kernel,
        grid_spec=pltpu.PrefetchScalarGridSpec(
            num_scalar_prefetch=1,
            grid=(steps,),
            in_specs=[
                pl.BlockSpec((half_rows // steps, features), lambda i, place: (place[0] * steps + i, 0)),
                pl.BlockSpec((2, features), lambda i, place: (0, 0)),
                pl.BlockSpec((1, features), lambda i, place: (0, 0)),
            ],
            out_specs=[pl.BlockSpec((block_rows, LANES), lambda i, place: (0, 0))] * GROUPS,
            scratch_shapes=[pltpu.VMEM((1, features), jnp.float32)],
        ),
        out_shape=[jax.ShapeDtypeStruct((block_rows, LANES), jnp.bfloat16)] * GROUPS,
        compiler_params=params,
        cost_estimate=pl.CostEstimate(flops=4 * half_rows * features, bytes_accessed=2 * 2 * half_rows * features, transcendentals=0),
        name="norm_rows",
    )(place, hidden, suffix_hidden, norm_gain.reshape(1, features))

    mine = [blocks[0]] + [move(blocks[s], along(s)) for s in range(1, GROUPS)]
    lhs = []
    for block in mine:
        lhs += [block, move(block, sibling)]

    queries = jnp.concatenate(query_parts, 0)
    query_count = queries.shape[0]
    states = query_count * query_width // HEAD_SIZE
    state = jax.ShapeDtypeStruct((states, LANES), jnp.float32)
    top, total, numer = pl.pallas_call(
        loaded_kernel,
        in_specs=[smem, smem, smem, vmem, vmem, vmem],
        out_specs=[vmem] * 3,
        out_shape=[state] * 3,
        compiler_params=params,
        cost_estimate=pl.CostEstimate(flops=4 * states * slot_keys.shape[0] * slot_keys.shape[1] * HEAD_SIZE, bytes_accessed=4 * slot_keys.size, transcendentals=states * 512),
        name="loaded_attention",
    )(place, page_slot_table, split_page, queries, slot_keys, slot_values)

    inverse_freq = rope_base ** (
        -(jnp.arange(HEAD_SIZE // 2, dtype=jnp.float32) * (2.0 / HEAD_SIZE))
    )
    row = jnp.arange(rows + 16, dtype=jnp.int32)
    front_position = ctx * rows + (row + core * half_rows) % rows
    end_position = prefix_len + ctx * 2 + jnp.where(row == rows, core, 1 - core)
    position = jnp.where(row < rows, front_position, end_position)
    angles = position.astype(jnp.float32)[:, None] * inverse_freq[None, :]
    cosine, sine = jnp.cos(angles), jnp.sin(angles)
    cosine = jnp.concatenate([cosine, cosine], 1)
    sine = jnp.concatenate([-sine, sine], 1)

    part_rows = 3 * (width // LANES) * rows + 16
    partials = pl.pallas_call(
        project_kernel,
        in_specs=[vmem] * (2 * GROUPS + 4),
        out_specs=[vmem] * GROUPS,
        out_shape=[jax.ShapeDtypeStruct((part_rows, LANES), jnp.bfloat16)] * GROUPS,
        scratch_shapes=[pltpu.VMEM((GROUPS * rows + 16, PAIR * features // n_ctx), jnp.bfloat16)],
        compiler_params=params,
        cost_estimate=pl.CostEstimate(flops=2 * GROUPS * rows * 2 * width * features // GROUPS, bytes_accessed=6 * 1024 * 1024, transcendentals=0),
        name="project",
    )(*lhs, key_matrix, value_matrix, far_key, far_value)
    received = [move(partials[s], along(-s)) for s in range(1, GROUPS)]

    own_queries = suffix_query_rows.shape[0]
    payload = jax.ShapeDtypeStruct((2 * own_queries * query_width // HEAD_SIZE, LANES), jnp.float32)
    row_shape = jax.ShapeDtypeStruct((rows, width), jnp.bfloat16)
    front_key, front_value, *payloads = pl.pallas_call(
        front_kernel,
        in_specs=[smem, smem] + [vmem] * (GROUPS + 8),
        out_specs=[vmem] * (2 + n_ctx),
        out_shape=[row_shape] * 2 + [payload] * n_ctx,
        scratch_shapes=[pltpu.VMEM((states, LANES), jnp.float32)] * 2,
        compiler_params=params,
        cost_estimate=pl.CostEstimate(flops=4 * states * rows * HEAD_SIZE, bytes_accessed=2 * 1024 * 1024, transcendentals=states * rows),
        name="front_attention",
    )(
        place,
        split_page,
        partials[0],
        *received,
        key_offset_bias.reshape(1, width),
        value_offset_bias.reshape(1, width),
        cosine,
        sine,
        queries,
        top,
        total,
        numer,
    )
    parts = [payloads[0]] + [move(payloads[s], around(-s)) for s in range(1, n_ctx)]
    attended = pl.pallas_call(
        merge_kernel,
        in_specs=[vmem] * n_ctx,
        out_specs=vmem,
        out_shape=jax.ShapeDtypeStruct((own_queries, query_width), jnp.bfloat16),
        compiler_params=params,
        name="merge",
    )(*parts)
    return (front_key, front_value, attended)


def solution(mesh):
    per_device = exchange_plan if mesh.shape["ctx"] == GROUPS * PAIR else gathered_plan
    return jax.shard_map(
        per_device,
        mesh=mesh,
        in_specs=(
            P(("req", "ctx"), None),
            P(("req", "ctx"), None),
            P(),
            P("ctx", "tp"),
            P("ctx", "tp"),
            P("tp"),
            P("tp"),
            P(("req", "ctx"), "tp"),
            P(("req", "ctx"), None, "tp"),
            P(("req", "ctx"), None, "tp"),
            P("req"),
            P("req"),
        ),
        out_specs=(P(("req", "ctx"), "tp"), P(("req", "ctx"), "tp"), P(("req", "ctx"), "tp")),
        check_vma=False,
    )
```

```python
import math

import jax
import jax.numpy as jnp
from jax import lax
from jax.experimental import pallas as pl
from jax.experimental.pallas import tpu as pltpu
from jax.sharding import PartitionSpec as P

QUERY_HEADS = 32
KEY_VALUE_HEADS = 4
HEAD_SIZE = 128


epsilon = 1e-06
rope_base = 1000000.0
masked_score = -1e30


def rms_rows(matrix, norm_gain):
    widened = matrix.astype(jnp.float32)
    inverse = lax.rsqrt(jnp.mean(widened * widened, axis=-1, keepdims=True) + epsilon)
    return (widened * inverse * norm_gain).astype(jnp.bfloat16)


def rotate(key_rows, positions, head_dim):
    row_count = key_rows.shape[0]
    split_heads = key_rows.reshape(row_count, -1, head_dim)
    half_dim = head_dim // 2
    inverse_freq = rope_base ** (-(jnp.arange(half_dim, dtype=jnp.float32) * (2.0 / head_dim)))
    angles = positions.astype(jnp.float32)[:, None] * inverse_freq[None, :]
    cosine = jnp.concatenate([jnp.cos(angles), jnp.cos(angles)], -1)[:, None, :]
    sine = jnp.concatenate([jnp.sin(angles), jnp.sin(angles)], -1)[:, None, :]
    turned = jnp.concatenate([-split_heads[..., half_dim:], split_heads[..., :half_dim]], -1)
    return (split_heads * cosine + turned * sine).reshape(row_count, -1)


def gathered_plan(
    hidden,
    suffix_hidden,
    norm_gain,
    key_matrix,
    value_matrix,
    key_offset_bias,
    value_offset_bias,
    suffix_query_rows,
    slot_keys,
    slot_values,
    page_slot_table,
    split_page,
):
    ctx_index = lax.axis_index("ctx")
    queries = lax.all_gather(suffix_query_rows, "ctx", axis=0, tiled=True)
    front_rows = hidden.shape[0]
    suffix_rows = suffix_hidden.shape[0]
    page_size = slot_keys.shape[1]
    slot_count = slot_keys.shape[0]
    total_pages = page_slot_table.shape[0]
    prefix_len = total_pages * page_size
    normed = rms_rows(jnp.concatenate([hidden, suffix_hidden], 0), norm_gain)
    col_width = key_matrix.shape[1]

    def accumulate(block_rows):
        return jnp.dot(normed, block_rows, preferred_element_type=jnp.float32)

    key_acc = accumulate(lax.all_gather(key_matrix, "ctx", axis=0, tiled=True))
    value_acc = accumulate(lax.all_gather(value_matrix, "ctx", axis=0, tiled=True))
    front_pos = ctx_index * front_rows + jnp.arange(front_rows, dtype=jnp.int32)
    suffix_pos = prefix_len + ctx_index * suffix_rows + jnp.arange(suffix_rows, dtype=jnp.int32)
    new_keys = rotate(
        key_acc + key_offset_bias, jnp.concatenate([front_pos, suffix_pos], 0), HEAD_SIZE
    ).astype(jnp.bfloat16)
    new_values = (value_acc + value_offset_bias).astype(jnp.bfloat16)
    cut_pos = split_page[0] * page_size
    global_slot = ctx_index * slot_count + jnp.arange(slot_count, dtype=jnp.int32)
    page_index = jnp.arange(total_pages, dtype=jnp.int32)
    slot_hits = (page_slot_table[None, :] == global_slot[:, None]) & (
        page_index[None, :] >= split_page[0]
    )
    slot_live = jnp.max(slot_hits.astype(jnp.int32), axis=1) > 0
    every_key = jnp.concatenate(
        [new_keys[:front_rows], slot_keys.reshape(-1, col_width), new_keys[front_rows:]], 0
    )
    every_value = jnp.concatenate(
        [new_values[:front_rows], slot_values.reshape(-1, col_width), new_values[front_rows:]], 0
    )
    query_count = queries.shape[0]
    query_pos = prefix_len + jnp.arange(query_count, dtype=jnp.int32)
    prefix_seen = jnp.concatenate([front_pos < cut_pos, jnp.repeat(slot_live, page_size)], 0)
    suffix_seen = suffix_pos[None, :] <= query_pos[:, None]
    visible = jnp.concatenate(
        [jnp.broadcast_to(prefix_seen[None, :], (query_count, prefix_seen.shape[0])), suffix_seen],
        1,
    )
    visible_wide = visible[:, None, :]
    sharing_count = QUERY_HEADS // KEY_VALUE_HEADS
    local_heads = col_width // HEAD_SIZE
    grouped_heads = queries.reshape(query_count, local_heads, sharing_count, HEAD_SIZE)
    top_list = []
    total_list = []
    numer_list = []
    for current_head in range(local_heads):
        head_keys = every_key[:, current_head * HEAD_SIZE : (current_head + 1) * HEAD_SIZE]
        head_values = every_value[:, current_head * HEAD_SIZE : (current_head + 1) * HEAD_SIZE]
        scores = jnp.einsum(
            "qgd,ld->qgl",
            grouped_heads[:, current_head],
            head_keys,
            preferred_element_type=jnp.float32,
        ) * (1.0 / math.sqrt(HEAD_SIZE))
        scores = jnp.where(visible_wide, scores, masked_score)
        row_top = jnp.max(scores, axis=-1)
        expos = jnp.where(visible_wide, jnp.exp(scores - row_top[..., None]), 0.0)
        total_list.append(jnp.sum(expos, axis=-1))
        top_list.append(row_top)
        numer_list.append(
            jnp.einsum(
                "qgl,ld->qgd",
                expos.astype(jnp.bfloat16),
                head_values,
                preferred_element_type=jnp.float32,
            )
        )
    row_top = jnp.stack(top_list, 1)
    weight_total = jnp.stack(total_list, 1)
    numer = jnp.stack(numer_list, 1)
    global_top = lax.pmax(row_top, "ctx")
    factor = jnp.exp(row_top - global_top)
    own_total, own_numer = (
        lax.psum_scatter(
            (weight_total * factor).reshape(query_count, -1), "ctx", scatter_dimension=0, tiled=True
        ),
        lax.psum_scatter(
            (numer * factor[..., None]).reshape(query_count, -1),
            "ctx",
            scatter_dimension=0,
            tiled=True,
        ),
    )
    own_total = own_total.reshape(suffix_rows, local_heads, sharing_count)
    own_numer = own_numer.reshape(suffix_rows, local_heads, sharing_count, HEAD_SIZE)
    attended = (own_numer / own_total[..., None]).reshape(suffix_rows, -1).astype(jnp.bfloat16)
    return (new_keys[:front_rows], new_values[:front_rows], attended)

GROUPS = 4
PAIR = 2
LANES = 128
SCALE = 1.0 / math.sqrt(HEAD_SIZE)


def row_scale(values):
    mean = jnp.sum(values * values, axis=-1, keepdims=True) * (1.0 / values.shape[-1])
    return lax.rsqrt(mean + epsilon)


def pack_kernel(key_ref, value_ref, out_ref, sems):
    rows = key_ref.shape[0]
    copies = [
        pltpu.make_async_copy(key_ref, out_ref.at[:rows], sems.at[0]),
        pltpu.make_async_copy(value_ref, out_ref.at[rows:], sems.at[1]),
    ]
    for copy in copies:
        copy.start()
    for copy in copies:
        copy.wait()


CHUNKS = 4


def norm_kernel(place_ref, query_ref, beside_ref, hidden_any, suffix_any, gain_any, *rest):
    outs = rest[:GROUPS]
    hidden_ref, suffix_ref, gain_ref, tail_ref, sems = rest[GROUPS:]
    core, ctx = place_ref[0], place_ref[1]
    z, x = ctx // PAIR, ctx % PAIR
    half_rows, features = hidden_ref.shape
    rows = half_rows // CHUNKS
    block = features // (GROUPS * PAIR)
    per_block = block // LANES
    pieces = PAIR * per_block
    copies = [
        pltpu.make_async_copy(gain_any, gain_ref, sems.at[CHUNKS]),
        pltpu.make_async_copy(suffix_any, suffix_ref, sems.at[CHUNKS + 1]),
    ]
    for i in range(CHUNKS):
        start = pl.multiple_of(core * half_rows + i * rows, rows)
        copies.append(
            pltpu.make_async_copy(
                hidden_any.at[pl.ds(start, rows)], hidden_ref.at[i * rows : (i + 1) * rows], sems.at[i]
            )
        )
    for copy in copies:
        copy.start()

    def offset(shift, side, j):
        owner = lax.rem(z + shift, GROUPS) * PAIR + lax.rem(x + side, PAIR)
        return pl.multiple_of(owner * block + j * LANES, LANES)

    query_rows = jnp.concatenate(
        [query_ref[...].astype(jnp.float32), beside_ref[...].astype(jnp.float32)], 0
    )
    lines = query_rows.shape[1] // LANES
    for r in range(query_rows.shape[0]):
        tile = [query_rows[r : r + 1, j * LANES : (j + 1) * LANES] for j in range(lines)]
        tile = jnp.concatenate(tile, 0).astype(jnp.bfloat16)
        start = pieces * half_rows + pieces + r * lines
        for out in outs:
            out[start : start + lines, :] = tile

    copies[0].wait()
    copies[1].wait()
    both = suffix_ref[...].astype(jnp.float32)
    normed = both * row_scale(both) * gain_ref[...]
    tail_ref[...] = jnp.where(core == 0, normed[0:1], normed[1:2])
    for shift in range(GROUPS):
        ends = [
            tail_ref[:, pl.ds(offset(shift, side, j), LANES)]
            for side in range(PAIR)
            for j in range(per_block)
        ]
        start = pieces * half_rows
        outs[shift][start : start + pieces, :] = jnp.concatenate(ends, 0).astype(jnp.bfloat16)
    for i in range(CHUNKS):
        copies[2 + i].wait()
        at = slice(i * rows, (i + 1) * rows)
        inverse = row_scale(hidden_ref[at, :].astype(jnp.float32))
        for shift in range(GROUPS):
            for side in range(PAIR):
                for j in range(per_block):
                    columns = pl.ds(offset(shift, side, j), LANES)
                    piece = hidden_ref[at, columns].astype(jnp.float32) * inverse * gain_ref[:, columns]
                    start = (side * per_block + j) * half_rows + i * rows
                    outs[shift][start : start + rows, :] = piece.astype(jnp.bfloat16)


def project_kernel(*refs):
    blocks = refs[: 2 * GROUPS]
    near, far = refs[2 * GROUPS : 2 * GROUPS + 2]
    outs = refs[2 * GROUPS + 2 : 3 * GROUPS + 2]
    lhs_ref = refs[3 * GROUPS + 2]
    depth = near.shape[0] // 2
    pieces = 2 * depth // LANES
    half_rows = (lhs_ref.shape[0] - 16) // (2 * GROUPS)
    rows = 2 * half_rows
    tails = []
    for i, block in enumerate(blocks):
        for j in range(pieces):
            lhs_ref[i * half_rows : (i + 1) * half_rows, j * LANES : (j + 1) * LANES] = block[
                j * half_rows : (j + 1) * half_rows, :
            ]
        tail = block[pieces * half_rows : pieces * half_rows + pieces, :].astype(jnp.float32)
        tails.append(jnp.concatenate([tail[j : j + 1] for j in range(pieces)], 1))
    tails.append(jnp.zeros((16 - len(tails), 2 * depth), jnp.float32))
    total = GROUPS * rows
    lhs_ref[total : total + 16, :] = jnp.concatenate(tails, 0).astype(jnp.bfloat16)

    def product(at):
        return jnp.dot(
            lhs_ref[:, :depth], near[at, :], preferred_element_type=jnp.float32
        ) + jnp.dot(lhs_ref[:, depth:], far[at, :], preferred_element_type=jnp.float32)

    keys = product(slice(0, depth))
    values = product(slice(depth, 2 * depth))
    high = keys.astype(jnp.bfloat16).astype(jnp.float32)
    low = keys - high
    columns = []
    for array in (high, low, values):
        for j in range(array.shape[1] // LANES):
            columns.append(array[:, j * LANES : (j + 1) * LANES])
    for group in range(GROUPS):
        for t, column in enumerate(columns):
            outs[group][t * rows : (t + 1) * rows, :] = column[
                group * rows : (group + 1) * rows
            ].astype(jnp.bfloat16)
        ends = [c[total + 2 * group : total + 2 * group + 2] for c in columns]
        ends.append(jnp.zeros((16 - 2 * len(columns), LANES), jnp.float32))
        outs[group][len(columns) * rows :, :] = jnp.concatenate(ends, 0).astype(jnp.bfloat16)


def head_queries(blocks, head, width):
    sharing = QUERY_HEADS // KEY_VALUE_HEADS
    lines = sharing * width // HEAD_SIZE
    rows = blocks[0].shape[0]
    found = []
    for block in blocks:
        tiles = block[rows - 2 * PAIR * lines :, :].astype(jnp.float32)
        for r in range(2 * PAIR):
            start = r * lines + head * sharing
            found.append(tiles[start : start + sharing])
    return jnp.concatenate(found, 0).astype(jnp.bfloat16)


def times_transposed(a, b):
    return lax.dot_general(a, b, (((1,), (1,)), ((), ())), preferred_element_type=jnp.float32)


def loaded_kernel(place_ref, table_ref, split_ref, *refs):
    blocks = refs[:GROUPS]
    key_ref, value_ref, top_ref, total_ref, numer_ref, query_ref = refs[GROUPS:]
    ctx = place_ref[1]
    slots, page, width = key_ref.shape
    heads = width // HEAD_SIZE
    split = split_ref[0]
    live = []
    for s in range(slots):
        hit = jnp.int32(0)
        for p in range(table_ref.shape[0]):
            hit = hit | ((table_ref[p] == ctx * slots + s) & (p >= split)).astype(jnp.int32)
        live.append(hit)
    for head in range(heads):
        columns = slice(head * HEAD_SIZE, (head + 1) * HEAD_SIZE)
        queries = head_queries(blocks, head, width)
        count = queries.shape[0]
        query_ref[head * count : (head + 1) * count, :] = queries
        scores = [
            jnp.where(live[s] > 0, times_transposed(queries, key_ref[s, :, columns]) * SCALE, masked_score)
            for s in range(slots)
        ]
        top = scores[0].max(-1, keepdims=True)
        for s in range(1, slots):
            top = jnp.maximum(top, scores[s].max(-1, keepdims=True))
        total = jnp.zeros((count, 1), jnp.float32)
        numer = jnp.zeros((count, HEAD_SIZE), jnp.float32)
        for s in range(slots):
            expos = jnp.where(live[s] > 0, jnp.exp(scores[s] - top), 0.0)
            total += expos.sum(-1, keepdims=True)
            numer += jnp.dot(
                expos.astype(jnp.bfloat16), value_ref[s, :, columns], preferred_element_type=jnp.float32
            )
        rows = slice(head * count, (head + 1) * count)
        top_ref[rows, :] = jnp.broadcast_to(top, (count, LANES))
        total_ref[rows, :] = jnp.broadcast_to(total, (count, LANES))
        numer_ref[rows, :] = numer


def front_kernel(
    place_ref, split_ref, own, *refs
):
    received = refs[: GROUPS - 1]
    (key_bias, value_bias, cosine_ref, sine_ref, query_ref, top_ref, total_ref, numer_ref) = refs[
        GROUPS - 1 : GROUPS + 7
    ]
    front_key, front_value = refs[GROUPS + 7 : GROUPS + 9]
    (out,) = refs[GROUPS + 9 :]
    core, ctx = place_ref[0], place_ref[1]
    z, x = ctx // PAIR, ctx % PAIR
    rows, width = front_key.shape
    half_rows = rows // 2
    heads = width // HEAD_SIZE
    sharing = QUERY_HEADS // KEY_VALUE_HEADS
    count = query_ref.shape[0] // heads
    own_queries = count // sharing // (GROUPS * PAIR)
    lane = lax.broadcasted_iota(jnp.int32, (count, LANES), 1)

    def owner(slot):
        group, side = slot // PAIR, slot % PAIR
        return lax.rem(z - group + GROUPS, GROUPS) * PAIR + lax.rem(x + side, PAIR)

    visible = ctx < split_ref[0]

    def summed(start, size):
        value = own[start : start + size, :].astype(jnp.float32)
        for ref in received:
            value += ref[start : start + size, :].astype(jnp.float32)
        return value

    ends = summed(3 * heads * rows, 16)
    row_query = lax.broadcasted_iota(jnp.int32, (count, 16), 0) // sharing
    query_position = owner(row_query // own_queries) * own_queries + row_query % own_queries
    end_column = lax.broadcasted_iota(jnp.int32, (count, 16), 1)
    end_position = ctx * 2 + jnp.where(end_column == 0, core, 1 - core)
    end_seen = (end_column < 2) & (end_position <= query_position)
    pad = jnp.zeros((14, HEAD_SIZE), jnp.float32)
    for head in range(heads):
        columns = slice(head * HEAD_SIZE, (head + 1) * HEAD_SIZE)
        raw = summed(head * rows, rows) + summed((heads + head) * rows, rows)
        value = (summed((2 * heads + head) * rows, rows) + value_bias[:, columns]).astype(jnp.bfloat16)
        end_raw = ends[2 * head : 2 * head + 2] + ends[2 * (heads + head) : 2 * (heads + head) + 2]
        end_value = ends[2 * (2 * heads + head) : 2 * (2 * heads + head) + 2] + value_bias[:, columns]
        end_raw = jnp.concatenate([end_raw + key_bias[:, columns], pad], 0)
        end_value = jnp.concatenate([end_value, pad], 0).astype(jnp.bfloat16)
        raw = raw + key_bias[:, columns]

        def rotated(k, part):
            turned = pltpu.roll(k, HEAD_SIZE // 2, 1)
            return (k * cosine_ref[part, :] + turned * sine_ref[part, :]).astype(jnp.bfloat16)

        key = rotated(raw, slice(0, rows))
        end_key = rotated(end_raw, slice(rows, rows + 16))
        for half in range(2):
            to = pl.ds(pl.multiple_of(lax.rem(core + half, 2) * half_rows, half_rows), half_rows)
            front_key[to, columns] = key[half * half_rows : (half + 1) * half_rows]
            front_value[to, columns] = value[half * half_rows : (half + 1) * half_rows]
        part = slice(head * count, (head + 1) * count)
        queries = query_ref[part, :]
        scores = jnp.where(visible, times_transposed(queries, key) * SCALE, masked_score)
        end_scores = jnp.where(end_seen, times_transposed(queries, end_key) * SCALE, masked_score)
        old_top = top_ref[part, :]
        top = jnp.maximum(scores.max(-1, keepdims=True), end_scores.max(-1, keepdims=True))
        top = jnp.maximum(old_top, top)
        factor = jnp.exp(old_top - top)
        expos = jnp.where(visible, jnp.exp(scores - top), 0.0)
        end_expos = jnp.where(end_seen, jnp.exp(end_scores - top[:, :16]), 0.0)
        total = total_ref[part, :] * factor + (
            expos.sum(-1, keepdims=True) + end_expos.sum(-1, keepdims=True)
        )
        numer = (
            numer_ref[part, :] * factor
            + jnp.dot(expos.astype(jnp.bfloat16), value, preferred_element_type=jnp.float32)
            + jnp.dot(end_expos.astype(jnp.bfloat16), end_value, preferred_element_type=jnp.float32)
        )
        stats = jnp.where(lane < LANES // 2, top, total)
        each = own_queries * sharing
        for slot in range(GROUPS * PAIR):
            start = pl.multiple_of(owner(slot) * 2 * heads * each + head * each, each)
            at = slice(slot * each, (slot + 1) * each)
            out[pl.ds(start, each), :] = numer[at]
            out[pl.ds(start + heads * each, each), :] = stats[at]


def merge_kernel(parts_ref, out_ref):
    count = GROUPS * PAIR
    rows = parts_ref.shape[0] // count // 2
    numers = [parts_ref[2 * i * rows : (2 * i + 1) * rows, :] for i in range(count)]
    stats = [parts_ref[(2 * i + 1) * rows : (2 * i + 2) * rows, :] for i in range(count)]
    top = stats[0][:, 0:1]
    for s in stats[1:]:
        top = jnp.maximum(top, s[:, 0:1])
    total = jnp.zeros((rows, 1), jnp.float32)
    numer = jnp.zeros((rows, LANES), jnp.float32)
    for n, s in zip(numers, stats):
        factor = jnp.exp(s[:, 0:1] - top)
        total += factor * s[:, LANES // 2 : LANES // 2 + 1]
        numer += factor * n
    result = numer / total
    queries, width = out_ref.shape
    sharing = QUERY_HEADS // KEY_VALUE_HEADS
    heads = width // HEAD_SIZE // sharing
    lines = []
    for i in range(queries):
        starts = [(h * queries + i) * sharing + g for h in range(heads) for g in range(sharing)]
        lines.append(jnp.concatenate([result[s : s + 1] for s in starts], 1))
    out_ref[...] = jnp.concatenate(lines, 0).astype(jnp.bfloat16)


def exchange_plan(
    hidden,
    suffix_hidden,
    norm_gain,
    key_matrix,
    value_matrix,
    key_offset_bias,
    value_offset_bias,
    suffix_query_rows,
    slot_keys,
    slot_values,
    page_slot_table,
    split_page,
):
    n_ctx = GROUPS * PAIR
    ctx = lax.axis_index("ctx").astype(jnp.int32)
    core = lax.axis_index("tp").astype(jnp.int32)
    place = jnp.stack([core, ctx])
    rows, features = hidden.shape
    half_rows = rows // 2
    width = key_matrix.shape[1]
    query_width = suffix_query_rows.shape[1]
    prefix_len = page_slot_table.shape[0] * slot_keys.shape[1]
    smem = pl.BlockSpec(memory_space=pltpu.SMEM)
    vmem = pl.BlockSpec(memory_space=pltpu.VMEM)
    params = pltpu.CompilerParams(vmem_limit_bytes=48 * 1024 * 1024)

    def move(array, target):
        pairs = []
        for c in range(n_ctx):
            for t in range(2):
                to_c, to_t = target(c, t)
                pairs.append((c * 2 + t, to_c * 2 + to_t))
        return lax.ppermute(array, ("ctx", "tp"), pairs)

    def along(shift):
        return lambda c, t: ((c // PAIR + shift) % GROUPS * PAIR + c % PAIR, t)

    def beside(c, t):
        return (c ^ 1, t)

    def sibling(c, t):
        return (c, 1 - t)

    hbm = pl.BlockSpec(memory_space=pltpu.HBM)
    beside_queries = move(suffix_query_rows, beside)
    packed = pl.pallas_call(
        pack_kernel,
        in_specs=[hbm, hbm],
        out_specs=vmem,
        out_shape=jax.ShapeDtypeStruct((2 * key_matrix.shape[0], width), jnp.bfloat16),
        scratch_shapes=[pltpu.SemaphoreType.DMA((2,))],
        compiler_params=params,
        cost_estimate=pl.CostEstimate(flops=0, bytes_accessed=4 * key_matrix.size, transcendentals=0),
        name="pack_weights",
    )(key_matrix, value_matrix)
    far = move(packed, beside)

    pieces = features // GROUPS // LANES
    own_queries = suffix_query_rows.shape[0]
    lines = query_width // LANES
    block_rows = pieces * half_rows + pieces + own_queries * PAIR * lines
    blocks = pl.pallas_call(
        norm_kernel,
        in_specs=[smem, vmem, vmem, hbm, hbm, hbm],
        out_specs=[vmem] * GROUPS,
        out_shape=[jax.ShapeDtypeStruct((block_rows, LANES), jnp.bfloat16)] * GROUPS,
        scratch_shapes=[
            pltpu.VMEM((half_rows, features), jnp.bfloat16),
            pltpu.VMEM(suffix_hidden.shape, jnp.bfloat16),
            pltpu.VMEM((1, features), jnp.float32),
            pltpu.VMEM((1, features), jnp.float32),
            pltpu.SemaphoreType.DMA((CHUNKS + 2,)),
        ],
        compiler_params=params,
        cost_estimate=pl.CostEstimate(
            flops=4 * half_rows * features, bytes_accessed=4 * half_rows * features, transcendentals=0
        ),
        name="norm_rows",
    )(place, suffix_query_rows, beside_queries, hidden, suffix_hidden, norm_gain.reshape(1, features))

    mine = [blocks[0]] + [move(blocks[s], along(s)) for s in range(1, GROUPS)]
    lhs = []
    for block in mine:
        lhs += [block, move(block, sibling)]

    states = n_ctx * own_queries * query_width // HEAD_SIZE
    state = jax.ShapeDtypeStruct((states, LANES), jnp.float32)
    top, total, numer, queries = pl.pallas_call(
        loaded_kernel,
        in_specs=[smem, smem, smem] + [vmem] * (GROUPS + 2),
        out_specs=[vmem] * 4,
        out_shape=[state] * 3 + [jax.ShapeDtypeStruct((states, LANES), jnp.bfloat16)],
        compiler_params=params,
        cost_estimate=pl.CostEstimate(
            flops=4 * states * slot_keys.shape[0] * slot_keys.shape[1] * HEAD_SIZE,
            bytes_accessed=4 * slot_keys.size,
            transcendentals=states * slot_keys.shape[0] * slot_keys.shape[1],
        ),
        name="loaded_attention",
    )(place, page_slot_table, split_page, *mine, slot_keys, slot_values)

    inverse_freq = rope_base ** (
        -(jnp.arange(HEAD_SIZE // 2, dtype=jnp.float32) * (2.0 / HEAD_SIZE))
    )
    row = jnp.arange(rows + 16, dtype=jnp.int32)
    front_position = ctx * rows + (row + core * half_rows) % rows
    end_position = prefix_len + ctx * 2 + jnp.where(row == rows, core, 1 - core)
    position = jnp.where(row < rows, front_position, end_position)
    angles = position.astype(jnp.float32)[:, None] * inverse_freq[None, :]
    cosine, sine = jnp.cos(angles), jnp.sin(angles)
    cosine = jnp.concatenate([cosine, cosine], 1)
    sine = jnp.concatenate([-sine, sine], 1)

    part_rows = 3 * (width // LANES) * rows + 16
    partials = pl.pallas_call(
        project_kernel,
        in_specs=[vmem] * (2 * GROUPS + 2),
        out_specs=[vmem] * GROUPS,
        out_shape=[jax.ShapeDtypeStruct((part_rows, LANES), jnp.bfloat16)] * GROUPS,
        scratch_shapes=[pltpu.VMEM((GROUPS * rows + 16, PAIR * features // n_ctx), jnp.bfloat16)],
        compiler_params=params,
        cost_estimate=pl.CostEstimate(flops=2 * GROUPS * rows * 2 * width * features // GROUPS, bytes_accessed=6 * 1024 * 1024, transcendentals=0),
        name="project",
    )(*lhs, packed, far)
    received = [move(partials[s], along(-s)) for s in range(1, GROUPS)]

    payload_shape = jax.ShapeDtypeStruct((2 * states, LANES), jnp.float32)
    row_shape = jax.ShapeDtypeStruct((rows, width), jnp.bfloat16)
    front_key, front_value, payload = pl.pallas_call(
        front_kernel,
        in_specs=[smem, smem] + [vmem] * (GROUPS + 8),
        out_specs=[vmem] * 3,
        out_shape=[row_shape] * 2 + [payload_shape],
        compiler_params=params,
        cost_estimate=pl.CostEstimate(flops=4 * states * rows * HEAD_SIZE, bytes_accessed=2 * 1024 * 1024, transcendentals=states * rows),
        name="front_attention",
    )(
        place,
        split_page,
        partials[0],
        *received,
        key_offset_bias.reshape(1, width),
        value_offset_bias.reshape(1, width),
        cosine,
        sine,
        queries,
        top,
        total,
        numer,
    )
    parts = lax.all_to_all(payload, "ctx", 0, 0, tiled=True)
    attended = pl.pallas_call(
        merge_kernel,
        in_specs=[vmem],
        out_specs=vmem,
        out_shape=jax.ShapeDtypeStruct((own_queries, query_width), jnp.bfloat16),
        compiler_params=params,
        name="merge",
    )(parts)
    return (front_key, front_value, attended)


def solution(mesh):
    per_device = exchange_plan if mesh.shape["ctx"] == GROUPS * PAIR else gathered_plan
    return jax.shard_map(
        per_device,
        mesh=mesh,
        in_specs=(
            P(("req", "ctx"), None),
            P(("req", "ctx"), None),
            P(),
            P("ctx", "tp"),
            P("ctx", "tp"),
            P("tp"),
            P("tp"),
            P(("req", "ctx"), "tp"),
            P(("req", "ctx"), None, "tp"),
            P(("req", "ctx"), None, "tp"),
            P("req"),
            P("req"),
        ),
        out_specs=(P(("req", "ctx"), "tp"), P(("req", "ctx"), "tp"), P(("req", "ctx"), "tp")),
        check_vma=False,
    )
```

```python
import functools
import math

import jax
import jax.numpy as jnp
from jax import lax
from jax.experimental import pallas as pl
from jax.experimental.pallas import tpu as pltpu
from jax.sharding import PartitionSpec as P

QUERY_HEADS = 32
KEY_VALUE_HEADS = 4
HEAD_SIZE = 128


epsilon = 1e-06
rope_base = 1000000.0
masked_score = -1e30


def rms_rows(matrix, norm_gain):
    widened = matrix.astype(jnp.float32)
    inverse = lax.rsqrt(jnp.mean(widened * widened, axis=-1, keepdims=True) + epsilon)
    return (widened * inverse * norm_gain).astype(jnp.bfloat16)


def rotate(key_rows, positions, head_dim):
    row_count = key_rows.shape[0]
    split_heads = key_rows.reshape(row_count, -1, head_dim)
    half_dim = head_dim // 2
    inverse_freq = rope_base ** (-(jnp.arange(half_dim, dtype=jnp.float32) * (2.0 / head_dim)))
    angles = positions.astype(jnp.float32)[:, None] * inverse_freq[None, :]
    cosine = jnp.concatenate([jnp.cos(angles), jnp.cos(angles)], -1)[:, None, :]
    sine = jnp.concatenate([jnp.sin(angles), jnp.sin(angles)], -1)[:, None, :]
    turned = jnp.concatenate([-split_heads[..., half_dim:], split_heads[..., :half_dim]], -1)
    return (split_heads * cosine + turned * sine).reshape(row_count, -1)


def gathered_plan(
    hidden,
    suffix_hidden,
    norm_gain,
    key_matrix,
    value_matrix,
    key_offset_bias,
    value_offset_bias,
    suffix_query_rows,
    slot_keys,
    slot_values,
    page_slot_table,
    split_page,
):
    ctx_index = lax.axis_index("ctx")
    queries = lax.all_gather(suffix_query_rows, "ctx", axis=0, tiled=True)
    front_rows = hidden.shape[0]
    suffix_rows = suffix_hidden.shape[0]
    page_size = slot_keys.shape[1]
    slot_count = slot_keys.shape[0]
    total_pages = page_slot_table.shape[0]
    prefix_len = total_pages * page_size
    normed = rms_rows(jnp.concatenate([hidden, suffix_hidden], 0), norm_gain)
    col_width = key_matrix.shape[1]

    def accumulate(block_rows):
        return jnp.dot(normed, block_rows, preferred_element_type=jnp.float32)

    key_acc = accumulate(lax.all_gather(key_matrix, "ctx", axis=0, tiled=True))
    value_acc = accumulate(lax.all_gather(value_matrix, "ctx", axis=0, tiled=True))
    front_pos = ctx_index * front_rows + jnp.arange(front_rows, dtype=jnp.int32)
    suffix_pos = prefix_len + ctx_index * suffix_rows + jnp.arange(suffix_rows, dtype=jnp.int32)
    new_keys = rotate(
        key_acc + key_offset_bias, jnp.concatenate([front_pos, suffix_pos], 0), HEAD_SIZE
    ).astype(jnp.bfloat16)
    new_values = (value_acc + value_offset_bias).astype(jnp.bfloat16)
    cut_pos = split_page[0] * page_size
    global_slot = ctx_index * slot_count + jnp.arange(slot_count, dtype=jnp.int32)
    page_index = jnp.arange(total_pages, dtype=jnp.int32)
    slot_hits = (page_slot_table[None, :] == global_slot[:, None]) & (
        page_index[None, :] >= split_page[0]
    )
    slot_live = jnp.max(slot_hits.astype(jnp.int32), axis=1) > 0
    every_key = jnp.concatenate(
        [new_keys[:front_rows], slot_keys.reshape(-1, col_width), new_keys[front_rows:]], 0
    )
    every_value = jnp.concatenate(
        [new_values[:front_rows], slot_values.reshape(-1, col_width), new_values[front_rows:]], 0
    )
    query_count = queries.shape[0]
    query_pos = prefix_len + jnp.arange(query_count, dtype=jnp.int32)
    prefix_seen = jnp.concatenate([front_pos < cut_pos, jnp.repeat(slot_live, page_size)], 0)
    suffix_seen = suffix_pos[None, :] <= query_pos[:, None]
    visible = jnp.concatenate(
        [jnp.broadcast_to(prefix_seen[None, :], (query_count, prefix_seen.shape[0])), suffix_seen],
        1,
    )
    visible_wide = visible[:, None, :]
    sharing_count = QUERY_HEADS // KEY_VALUE_HEADS
    local_heads = col_width // HEAD_SIZE
    grouped_heads = queries.reshape(query_count, local_heads, sharing_count, HEAD_SIZE)
    top_list = []
    total_list = []
    numer_list = []
    for current_head in range(local_heads):
        head_keys = every_key[:, current_head * HEAD_SIZE : (current_head + 1) * HEAD_SIZE]
        head_values = every_value[:, current_head * HEAD_SIZE : (current_head + 1) * HEAD_SIZE]
        scores = jnp.einsum(
            "qgd,ld->qgl",
            grouped_heads[:, current_head],
            head_keys,
            preferred_element_type=jnp.float32,
        ) * (1.0 / math.sqrt(HEAD_SIZE))
        scores = jnp.where(visible_wide, scores, masked_score)
        row_top = jnp.max(scores, axis=-1)
        expos = jnp.where(visible_wide, jnp.exp(scores - row_top[..., None]), 0.0)
        total_list.append(jnp.sum(expos, axis=-1))
        top_list.append(row_top)
        numer_list.append(
            jnp.einsum(
                "qgl,ld->qgd",
                expos.astype(jnp.bfloat16),
                head_values,
                preferred_element_type=jnp.float32,
            )
        )
    row_top = jnp.stack(top_list, 1)
    weight_total = jnp.stack(total_list, 1)
    numer = jnp.stack(numer_list, 1)
    global_top = lax.pmax(row_top, "ctx")
    factor = jnp.exp(row_top - global_top)
    own_total, own_numer = (
        lax.psum_scatter(
            (weight_total * factor).reshape(query_count, -1), "ctx", scatter_dimension=0, tiled=True
        ),
        lax.psum_scatter(
            (numer * factor[..., None]).reshape(query_count, -1),
            "ctx",
            scatter_dimension=0,
            tiled=True,
        ),
    )
    own_total = own_total.reshape(suffix_rows, local_heads, sharing_count)
    own_numer = own_numer.reshape(suffix_rows, local_heads, sharing_count, HEAD_SIZE)
    attended = (own_numer / own_total[..., None]).reshape(suffix_rows, -1).astype(jnp.bfloat16)
    return (new_keys[:front_rows], new_values[:front_rows], attended)

GROUPS = 4
PAIR = 2
LANES = 128
SCALE = 1.0 / math.sqrt(HEAD_SIZE)


def row_scale(values):
    mean = jnp.sum(values * values, axis=-1, keepdims=True) * (1.0 / values.shape[-1])
    return lax.rsqrt(mean + epsilon)


CHUNKS = 4


def norm_kernel(place_ref, query_any, hidden_any, suffix_any, gain_any, key_any, value_any, *rest):
    outs, packed_any = rest[:GROUPS], rest[GROUPS]
    hidden_ref, suffix_ref, gain_ref, query_ref, tail_ref, sems = rest[GROUPS + 1 :]
    depth = key_any.shape[0]
    packing = [
        pltpu.make_async_copy(key_any, packed_any.at[:depth], sems.at[CHUNKS + 3]),
        pltpu.make_async_copy(value_any, packed_any.at[depth:], sems.at[CHUNKS + 4]),
    ]
    core, ctx = place_ref[0], place_ref[1]
    z, x = ctx // PAIR, ctx % PAIR
    half_rows, features = hidden_ref.shape
    rows = half_rows // CHUNKS
    block = features // (GROUPS * PAIR)
    per_block = block // LANES
    pieces = PAIR * per_block
    copies = [
        pltpu.make_async_copy(gain_any, gain_ref, sems.at[CHUNKS]),
        pltpu.make_async_copy(suffix_any, suffix_ref, sems.at[CHUNKS + 1]),
        pltpu.make_async_copy(query_any, query_ref, sems.at[CHUNKS + 2]),
    ]
    for i in range(CHUNKS):
        start = pl.multiple_of(core * half_rows + i * rows, rows)
        copies.append(
            pltpu.make_async_copy(
                hidden_any.at[pl.ds(start, rows)], hidden_ref.at[i * rows : (i + 1) * rows], sems.at[i]
            )
        )
    for copy in copies + packing:
        copy.start()

    def offset(shift, side, j):
        owner = (z ^ shift) * PAIR + (x ^ side)
        return pl.multiple_of(owner * block + j * LANES, LANES)

    copies[0].wait()
    copies[1].wait()
    copies[2].wait()
    query_rows = query_ref[...].astype(jnp.float32)
    lines = query_rows.shape[1] // LANES
    for r in range(query_rows.shape[0]):
        tile = [query_rows[r : r + 1, j * LANES : (j + 1) * LANES] for j in range(lines)]
        tile = jnp.concatenate(tile, 0).astype(jnp.bfloat16)
        start = pieces * half_rows + pieces + r * lines
        for out in outs:
            out[start : start + lines, :] = tile

    both = suffix_ref[...].astype(jnp.float32)
    normed = both * row_scale(both) * gain_ref[...]
    tail_ref[...] = jnp.where(core == 0, normed[0:1], normed[1:2])
    for shift in range(GROUPS):
        ends = [
            tail_ref[:, pl.ds(offset(shift, side, j), LANES)]
            for side in range(PAIR)
            for j in range(per_block)
        ]
        start = pieces * half_rows
        outs[shift][start : start + pieces, :] = jnp.concatenate(ends, 0).astype(jnp.bfloat16)
    for i in range(CHUNKS):
        copies[3 + i].wait()
        at = slice(i * rows, (i + 1) * rows)
        inverse = row_scale(hidden_ref[at, :].astype(jnp.float32))
        for shift in range(GROUPS):
            for side in range(PAIR):
                for j in range(per_block):
                    columns = pl.ds(offset(shift, side, j), LANES)
                    piece = hidden_ref[at, columns].astype(jnp.float32) * inverse * gain_ref[:, columns]
                    start = (side * per_block + j) * half_rows + i * rows
                    outs[shift][start : start + rows, :] = piece.astype(jnp.bfloat16)
    for copy in packing:
        copy.wait()


def project_kernel(*refs):
    blocks = refs[: 2 * GROUPS]
    near, far = refs[2 * GROUPS : 2 * GROUPS + 2]
    outs = refs[2 * GROUPS + 2 : 3 * GROUPS + 2]
    query_ref, lhs_ref = refs[3 * GROUPS + 2 :]
    depth = near.shape[0] // 2
    pieces = 2 * depth // LANES
    half_rows = (lhs_ref.shape[0] - 16) // (2 * GROUPS)
    rows = 2 * half_rows
    tails = []
    for i, block in enumerate(blocks):
        for j in range(pieces):
            lhs_ref[i * half_rows : (i + 1) * half_rows, j * LANES : (j + 1) * LANES] = block[
                j * half_rows : (j + 1) * half_rows, :
            ]
        tail = block[pieces * half_rows : pieces * half_rows + pieces, :].astype(jnp.float32)
        tails.append(jnp.concatenate([tail[j : j + 1] for j in range(pieces)], 1))
    tails.append(jnp.zeros((16 - len(tails), 2 * depth), jnp.float32))
    lines = query_ref.shape[0] // GROUPS
    for group in range(GROUPS):
        block = blocks[2 * group]
        query_ref[group * lines : (group + 1) * lines, :] = block[block.shape[0] - lines :, :]
    total = GROUPS * rows
    lhs_ref[total : total + 16, :] = jnp.concatenate(tails, 0).astype(jnp.bfloat16)

    def product(at):
        return jnp.dot(
            lhs_ref[:, :depth], near[at, :], preferred_element_type=jnp.float32
        ) + jnp.dot(lhs_ref[:, depth:], far[at, :], preferred_element_type=jnp.float32)

    keys = product(slice(0, depth))
    values = product(slice(depth, 2 * depth))
    high = keys.astype(jnp.bfloat16).astype(jnp.float32)
    low = keys - high
    columns = []
    for array in (high, low, values):
        for j in range(array.shape[1] // LANES):
            columns.append(array[:, j * LANES : (j + 1) * LANES])
    for group in range(GROUPS):
        for t, column in enumerate(columns):
            outs[group][t * rows : (t + 1) * rows, :] = column[
                group * rows : (group + 1) * rows
            ].astype(jnp.bfloat16)
        ends = [c[total + 2 * group : total + 2 * group + 2] for c in columns]
        ends.append(jnp.zeros((16 - 2 * len(columns), LANES), jnp.float32))
        outs[group][len(columns) * rows :, :] = jnp.concatenate(ends, 0).astype(jnp.bfloat16)


def head_queries(parts, head, width):
    sharing = QUERY_HEADS // KEY_VALUE_HEADS
    lines = sharing * width // HEAD_SIZE
    each = parts[0].shape[0] // GROUPS
    found = []
    for group in range(GROUPS):
        for part in parts:
            tiles = part[group * each : (group + 1) * each, :].astype(jnp.float32)
            for start in range(head * sharing, each, lines):
                found.append(tiles[start : start + sharing])
    return jnp.concatenate(found, 0).astype(jnp.bfloat16)


def times_transposed(a, b):
    return lax.dot_general(a, b, (((1,), (1,)), ((), ())), preferred_element_type=jnp.float32)


def loaded_kernel(place_ref, table_ref, split_ref, *refs):
    parts = refs[:PAIR]
    key_ref, value_ref, top_ref, total_ref, numer_ref, query_ref = refs[PAIR:]
    ctx = place_ref[1]
    slots, page, width = key_ref.shape
    heads = width // HEAD_SIZE
    split = split_ref[0]
    live = []
    for s in range(slots):
        hit = jnp.int32(0)
        for p in range(table_ref.shape[0]):
            hit = hit | ((table_ref[p] == ctx * slots + s) & (p >= split)).astype(jnp.int32)
        live.append(hit)
    for head in range(heads):
        columns = slice(head * HEAD_SIZE, (head + 1) * HEAD_SIZE)
        queries = head_queries(parts, head, width)
        count = queries.shape[0]
        query_ref[head * count : (head + 1) * count, :] = queries
        scores = [
            jnp.where(live[s] > 0, times_transposed(queries, key_ref[s, :, columns]) * SCALE, masked_score)
            for s in range(slots)
        ]
        top = scores[0].max(-1, keepdims=True)
        for s in range(1, slots):
            top = jnp.maximum(top, scores[s].max(-1, keepdims=True))
        total = jnp.zeros((count, 1), jnp.float32)
        numer = jnp.zeros((count, HEAD_SIZE), jnp.float32)
        for s in range(slots):
            expos = jnp.where(live[s] > 0, jnp.exp(scores[s] - top), 0.0)
            total += expos.sum(-1, keepdims=True)
            numer += jnp.dot(
                expos.astype(jnp.bfloat16), value_ref[s, :, columns], preferred_element_type=jnp.float32
            )
        rows = slice(head * count, (head + 1) * count)
        top_ref[rows, :] = jnp.broadcast_to(top, (count, LANES))
        total_ref[rows, :] = jnp.broadcast_to(total, (count, LANES))
        numer_ref[rows, :] = numer


def front_kernel(
    place_ref, split_ref, own, *refs
):
    received = refs[: GROUPS - 1]
    (key_bias, value_bias, cosine_ref, sine_ref, query_ref, top_ref, total_ref, numer_ref) = refs[
        GROUPS - 1 : GROUPS + 7
    ]
    front_key, front_value = refs[GROUPS + 7 : GROUPS + 9]
    outs = refs[GROUPS + 9 :]
    core, ctx = place_ref[0], place_ref[1]
    rows, width = front_key.shape
    half_rows = rows // 2
    heads = width // HEAD_SIZE
    sharing = QUERY_HEADS // KEY_VALUE_HEADS
    count = query_ref.shape[0] // heads
    own_queries = count // sharing // (GROUPS * PAIR)
    lane = lax.broadcasted_iota(jnp.int32, (count, LANES), 1)

    visible = ctx < split_ref[0]

    def summed(start, size):
        value = own[start : start + size, :].astype(jnp.float32)
        for ref in received:
            value += ref[start : start + size, :].astype(jnp.float32)
        return value

    ends = summed(3 * heads * rows, 16)
    row_query = lax.broadcasted_iota(jnp.int32, (count, 16), 0) // sharing
    query_position = (ctx ^ (row_query // own_queries)) * own_queries + row_query % own_queries
    end_column = lax.broadcasted_iota(jnp.int32, (count, 16), 1)
    end_position = ctx * 2 + jnp.where(end_column == 0, core, 1 - core)
    end_seen = (end_column < 2) & (end_position <= query_position)
    pad = jnp.zeros((14, HEAD_SIZE), jnp.float32)
    for head in range(heads):
        columns = slice(head * HEAD_SIZE, (head + 1) * HEAD_SIZE)
        raw = summed(head * rows, rows) + summed((heads + head) * rows, rows)
        value = (summed((2 * heads + head) * rows, rows) + value_bias[:, columns]).astype(jnp.bfloat16)
        end_raw = ends[2 * head : 2 * head + 2] + ends[2 * (heads + head) : 2 * (heads + head) + 2]
        end_value = ends[2 * (2 * heads + head) : 2 * (2 * heads + head) + 2] + value_bias[:, columns]
        end_raw = jnp.concatenate([end_raw + key_bias[:, columns], pad], 0)
        end_value = jnp.concatenate([end_value, pad], 0).astype(jnp.bfloat16)
        raw = raw + key_bias[:, columns]

        def rotated(k, part):
            turned = pltpu.roll(k, HEAD_SIZE // 2, 1)
            return (k * cosine_ref[part, :] + turned * sine_ref[part, :]).astype(jnp.bfloat16)

        key = rotated(raw, slice(0, rows))
        end_key = rotated(end_raw, slice(rows, rows + 16))
        for half in range(2):
            to = pl.ds(pl.multiple_of(lax.rem(core + half, 2) * half_rows, half_rows), half_rows)
            front_key[to, columns] = key[half * half_rows : (half + 1) * half_rows]
            front_value[to, columns] = value[half * half_rows : (half + 1) * half_rows]
        part = slice(head * count, (head + 1) * count)
        queries = query_ref[part, :]
        scores = jnp.where(visible, times_transposed(queries, key) * SCALE, masked_score)
        end_scores = jnp.where(end_seen, times_transposed(queries, end_key) * SCALE, masked_score)
        old_top = top_ref[part, :]
        top = jnp.maximum(scores.max(-1, keepdims=True), end_scores.max(-1, keepdims=True))
        top = jnp.maximum(old_top, top)
        factor = jnp.exp(old_top - top)
        expos = jnp.where(visible, jnp.exp(scores - top), 0.0)
        end_expos = jnp.where(end_seen, jnp.exp(end_scores - top[:, :16]), 0.0)
        total = total_ref[part, :] * factor + (
            expos.sum(-1, keepdims=True) + end_expos.sum(-1, keepdims=True)
        )
        numer = (
            numer_ref[part, :] * factor
            + jnp.dot(expos.astype(jnp.bfloat16), value, preferred_element_type=jnp.float32)
            + jnp.dot(end_expos.astype(jnp.bfloat16), end_value, preferred_element_type=jnp.float32)
        )
        stats = jnp.where(lane < LANES // 2, top, total)
        each = own_queries * sharing
        for slot in range(GROUPS * PAIR):
            start = (slot // PAIR * 2 * heads + head) * each
            at = slice(slot * each, (slot + 1) * each)
            out = outs[slot % PAIR]
            out[start : start + each, :] = numer[at]
            out[start + heads * each : start + (heads + 1) * each, :] = stats[at]


def merged(kept, other, start, rows):
    half = LANES // 2
    stats, other_stats = [ref[start + rows : start + 2 * rows, :] for ref in (kept, other)]
    top = jnp.maximum(stats[:, 0:1], other_stats[:, 0:1])
    factor = jnp.exp(stats[:, 0:1] - top)
    other_factor = jnp.exp(other_stats[:, 0:1] - top)
    total = factor * stats[:, half : half + 1] + other_factor * other_stats[:, half : half + 1]
    numer = factor * kept[start : start + rows, :] + other_factor * other[start : start + rows, :]
    return numer, top, total


def merge_kernel(each, kept, other, keep_ref, send_ref):
    rows = each // 2
    for slot in range(kept.shape[0] // each):
        numer, top, total = merged(kept, other, slot * each, rows)
        lane = lax.broadcasted_iota(jnp.int32, numer.shape, 1)
        out = (keep_ref, send_ref)[slot % 2]
        start = slot // 2 * each
        out[start : start + rows, :] = numer
        out[start + rows : start + each, :] = jnp.where(lane < LANES // 2, top, total)


def last_kernel(kept, other, out_ref):
    rows = kept.shape[0] // 2
    numer, _, total = merged(kept, other, 0, rows)
    result = numer / total
    queries, width = out_ref.shape
    sharing = QUERY_HEADS // KEY_VALUE_HEADS
    heads = width // HEAD_SIZE // sharing
    lines = []
    for i in range(queries):
        starts = [(h * queries + i) * sharing + g for h in range(heads) for g in range(sharing)]
        lines.append(jnp.concatenate([result[s : s + 1] for s in starts], 1))
    out_ref[...] = jnp.concatenate(lines, 0).astype(jnp.bfloat16)


def exchange_plan(
    hidden,
    suffix_hidden,
    norm_gain,
    key_matrix,
    value_matrix,
    key_offset_bias,
    value_offset_bias,
    suffix_query_rows,
    slot_keys,
    slot_values,
    page_slot_table,
    split_page,
):
    n_ctx = GROUPS * PAIR
    ctx = lax.axis_index("ctx").astype(jnp.int32)
    core = lax.axis_index("tp").astype(jnp.int32)
    place = jnp.stack([core, ctx])
    rows, features = hidden.shape
    half_rows = rows // 2
    width = key_matrix.shape[1]
    query_width = suffix_query_rows.shape[1]
    prefix_len = page_slot_table.shape[0] * slot_keys.shape[1]
    smem = pl.BlockSpec(memory_space=pltpu.SMEM)
    vmem = pl.BlockSpec(memory_space=pltpu.VMEM)
    params = pltpu.CompilerParams(vmem_limit_bytes=48 * 1024 * 1024)

    def move(array, target):
        pairs = []
        for c in range(n_ctx):
            for t in range(2):
                to_c, to_t = target(c, t)
                pairs.append((c * 2 + t, to_c * 2 + to_t))
        return lax.ppermute(array, ("ctx", "tp"), pairs)

    def along(shift):
        return lambda c, t: ((c // PAIR ^ shift) * PAIR + c % PAIR, t)

    def beside(c, t):
        return (c ^ 1, t)

    def sibling(c, t):
        return (c, 1 - t)

    hbm = pl.BlockSpec(memory_space=pltpu.HBM)
    pieces = features // GROUPS // LANES
    own_queries = suffix_query_rows.shape[0]
    lines = query_width // LANES
    block_rows = pieces * half_rows + pieces + own_queries * lines
    *blocks, packed = pl.pallas_call(
        norm_kernel,
        in_specs=[smem] + [hbm] * 6,
        out_specs=[vmem] * GROUPS + [hbm],
        out_shape=[jax.ShapeDtypeStruct((block_rows, LANES), jnp.bfloat16)] * GROUPS
        + [jax.ShapeDtypeStruct((2 * key_matrix.shape[0], width), jnp.bfloat16)],
        scratch_shapes=[
            pltpu.VMEM((half_rows, features), jnp.bfloat16),
            pltpu.VMEM(suffix_hidden.shape, jnp.bfloat16),
            pltpu.VMEM((1, features), jnp.float32),
            pltpu.VMEM(suffix_query_rows.shape, jnp.bfloat16),
            pltpu.VMEM((1, features), jnp.float32),
            pltpu.SemaphoreType.DMA((CHUNKS + 5,)),
        ],
        compiler_params=pltpu.CompilerParams(vmem_limit_bytes=60 * 1024 * 1024),
        cost_estimate=pl.CostEstimate(
            flops=4 * half_rows * features, bytes_accessed=4 * half_rows * features, transcendentals=0
        ),
        name="norm_rows",
    )(
        place,
        suffix_query_rows,
        hidden,
        suffix_hidden,
        norm_gain.reshape(1, features),
        key_matrix,
        value_matrix,
    )
    far = move(packed, beside)

    mine = [blocks[0]] + [move(blocks[s], along(s)) for s in range(1, GROUPS)]
    lhs = []
    for block in mine:
        lhs += [block, move(block, sibling)]

    inverse_freq = rope_base ** (
        -(jnp.arange(HEAD_SIZE // 2, dtype=jnp.float32) * (2.0 / HEAD_SIZE))
    )
    row = jnp.arange(rows + 16, dtype=jnp.int32)
    front_position = ctx * rows + (row + core * half_rows) % rows
    end_position = prefix_len + ctx * 2 + jnp.where(row == rows, core, 1 - core)
    position = jnp.where(row < rows, front_position, end_position)
    angles = position.astype(jnp.float32)[:, None] * inverse_freq[None, :]
    cosine, sine = jnp.cos(angles), jnp.sin(angles)
    cosine = jnp.concatenate([cosine, cosine], 1)
    sine = jnp.concatenate([-sine, sine], 1)

    part_rows = 3 * (width // LANES) * rows + 16
    *partials, own_tiles = pl.pallas_call(
        project_kernel,
        in_specs=[vmem] * (2 * GROUPS + 2),
        out_specs=[vmem] * (GROUPS + 1),
        out_shape=[jax.ShapeDtypeStruct((part_rows, LANES), jnp.bfloat16)] * GROUPS
        + [jax.ShapeDtypeStruct((GROUPS * own_queries * lines, LANES), jnp.bfloat16)],
        scratch_shapes=[pltpu.VMEM((GROUPS * rows + 16, PAIR * features // n_ctx), jnp.bfloat16)],
        compiler_params=params,
        cost_estimate=pl.CostEstimate(flops=2 * GROUPS * rows * 2 * width * features // GROUPS, bytes_accessed=6 * 1024 * 1024, transcendentals=0),
        name="project",
    )(*lhs, packed, far)
    received = [move(partials[s], along(s)) for s in range(1, GROUPS)]
    beside_tiles = move(own_tiles, beside)

    states = n_ctx * own_queries * query_width // HEAD_SIZE
    state = jax.ShapeDtypeStruct((states, LANES), jnp.float32)
    top, total, numer, queries = pl.pallas_call(
        loaded_kernel,
        in_specs=[smem, smem, smem] + [vmem] * (PAIR + 2),
        out_specs=[vmem] * 4,
        out_shape=[state] * 3 + [jax.ShapeDtypeStruct((states, LANES), jnp.bfloat16)],
        compiler_params=params,
        cost_estimate=pl.CostEstimate(
            flops=4 * states * slot_keys.shape[0] * slot_keys.shape[1] * HEAD_SIZE,
            bytes_accessed=4 * slot_keys.size,
            transcendentals=states * slot_keys.shape[0] * slot_keys.shape[1],
        ),
        name="loaded_attention",
    )(place, page_slot_table, split_page, own_tiles, beside_tiles, slot_keys, slot_values)


    payload_shape = jax.ShapeDtypeStruct((states, LANES), jnp.float32)
    row_shape = jax.ShapeDtypeStruct((rows, width), jnp.bfloat16)
    front_key, front_value, kept, sent = pl.pallas_call(
        front_kernel,
        in_specs=[smem, smem] + [vmem] * (GROUPS + 8),
        out_specs=[vmem] * 4,
        out_shape=[row_shape] * 2 + [payload_shape] * 2,
        compiler_params=params,
        cost_estimate=pl.CostEstimate(flops=4 * states * rows * HEAD_SIZE, bytes_accessed=2 * 1024 * 1024, transcendentals=states * rows),
        name="front_attention",
    )(
        place,
        split_page,
        partials[0],
        *received,
        key_offset_bias.reshape(1, width),
        value_offset_bias.reshape(1, width),
        cosine,
        sine,
        queries,
        top,
        total,
        numer,
    )
    for target in (beside, along(1)):
        half = jax.ShapeDtypeStruct((kept.shape[0] // 2, LANES), jnp.float32)
        kept, sent = pl.pallas_call(
            functools.partial(merge_kernel, states // GROUPS),
            in_specs=[vmem] * 2,
            out_specs=[vmem] * 2,
            out_shape=[half] * 2,
            compiler_params=params,
            name="merge",
        )(kept, move(sent, target))
    attended = pl.pallas_call(
        last_kernel,
        in_specs=[vmem] * 2,
        out_specs=vmem,
        out_shape=jax.ShapeDtypeStruct((own_queries, query_width), jnp.bfloat16),
        compiler_params=params,
        name="finish",
    )(kept, move(sent, along(2)))
    return (front_key, front_value, attended)


def solution(mesh):
    per_device = exchange_plan if mesh.shape["ctx"] == GROUPS * PAIR else gathered_plan
    return jax.shard_map(
        per_device,
        mesh=mesh,
        in_specs=(
            P(("req", "ctx"), None),
            P(("req", "ctx"), None),
            P(),
            P("ctx", "tp"),
            P("ctx", "tp"),
            P("tp"),
            P("tp"),
            P(("req", "ctx"), "tp"),
            P(("req", "ctx"), None, "tp"),
            P(("req", "ctx"), None, "tp"),
            P("req"),
            P("req"),
        ),
        out_specs=(P(("req", "ctx"), "tp"), P(("req", "ctx"), "tp"), P(("req", "ctx"), "tp")),
        check_vma=False,
    )
```

```python
import functools
import math

import jax
import jax.numpy as jnp
from jax import lax
from jax.experimental import pallas as pl
from jax.experimental.pallas import tpu as pltpu
from jax.sharding import PartitionSpec as P

QUERY_HEADS = 32
KEY_VALUE_HEADS = 4
HEAD_SIZE = 128


epsilon = 1e-06
rope_base = 1000000.0
masked_score = -1e30


def rms_rows(matrix, norm_gain):
    widened = matrix.astype(jnp.float32)
    inverse = lax.rsqrt(jnp.mean(widened * widened, axis=-1, keepdims=True) + epsilon)
    return (widened * inverse * norm_gain).astype(jnp.bfloat16)


def rotate(key_rows, positions, head_dim):
    row_count = key_rows.shape[0]
    split_heads = key_rows.reshape(row_count, -1, head_dim)
    half_dim = head_dim // 2
    inverse_freq = rope_base ** (-(jnp.arange(half_dim, dtype=jnp.float32) * (2.0 / head_dim)))
    angles = positions.astype(jnp.float32)[:, None] * inverse_freq[None, :]
    cosine = jnp.concatenate([jnp.cos(angles), jnp.cos(angles)], -1)[:, None, :]
    sine = jnp.concatenate([jnp.sin(angles), jnp.sin(angles)], -1)[:, None, :]
    turned = jnp.concatenate([-split_heads[..., half_dim:], split_heads[..., :half_dim]], -1)
    return (split_heads * cosine + turned * sine).reshape(row_count, -1)


def gathered_plan(
    hidden,
    suffix_hidden,
    norm_gain,
    key_matrix,
    value_matrix,
    key_offset_bias,
    value_offset_bias,
    suffix_query_rows,
    slot_keys,
    slot_values,
    page_slot_table,
    split_page,
):
    ctx_index = lax.axis_index("ctx")
    queries = lax.all_gather(suffix_query_rows, "ctx", axis=0, tiled=True)
    front_rows = hidden.shape[0]
    suffix_rows = suffix_hidden.shape[0]
    page_size = slot_keys.shape[1]
    slot_count = slot_keys.shape[0]
    total_pages = page_slot_table.shape[0]
    prefix_len = total_pages * page_size
    normed = rms_rows(jnp.concatenate([hidden, suffix_hidden], 0), norm_gain)
    col_width = key_matrix.shape[1]

    def accumulate(block_rows):
        return jnp.dot(normed, block_rows, preferred_element_type=jnp.float32)

    key_acc = accumulate(lax.all_gather(key_matrix, "ctx", axis=0, tiled=True))
    value_acc = accumulate(lax.all_gather(value_matrix, "ctx", axis=0, tiled=True))
    front_pos = ctx_index * front_rows + jnp.arange(front_rows, dtype=jnp.int32)
    suffix_pos = prefix_len + ctx_index * suffix_rows + jnp.arange(suffix_rows, dtype=jnp.int32)
    new_keys = rotate(
        key_acc + key_offset_bias, jnp.concatenate([front_pos, suffix_pos], 0), HEAD_SIZE
    ).astype(jnp.bfloat16)
    new_values = (value_acc + value_offset_bias).astype(jnp.bfloat16)
    cut_pos = split_page[0] * page_size
    global_slot = ctx_index * slot_count + jnp.arange(slot_count, dtype=jnp.int32)
    page_index = jnp.arange(total_pages, dtype=jnp.int32)
    slot_hits = (page_slot_table[None, :] == global_slot[:, None]) & (
        page_index[None, :] >= split_page[0]
    )
    slot_live = jnp.max(slot_hits.astype(jnp.int32), axis=1) > 0
    every_key = jnp.concatenate(
        [new_keys[:front_rows], slot_keys.reshape(-1, col_width), new_keys[front_rows:]], 0
    )
    every_value = jnp.concatenate(
        [new_values[:front_rows], slot_values.reshape(-1, col_width), new_values[front_rows:]], 0
    )
    query_count = queries.shape[0]
    query_pos = prefix_len + jnp.arange(query_count, dtype=jnp.int32)
    prefix_seen = jnp.concatenate([front_pos < cut_pos, jnp.repeat(slot_live, page_size)], 0)
    suffix_seen = suffix_pos[None, :] <= query_pos[:, None]
    visible = jnp.concatenate(
        [jnp.broadcast_to(prefix_seen[None, :], (query_count, prefix_seen.shape[0])), suffix_seen],
        1,
    )
    visible_wide = visible[:, None, :]
    sharing_count = QUERY_HEADS // KEY_VALUE_HEADS
    local_heads = col_width // HEAD_SIZE
    grouped_heads = queries.reshape(query_count, local_heads, sharing_count, HEAD_SIZE)
    top_list = []
    total_list = []
    numer_list = []
    for current_head in range(local_heads):
        head_keys = every_key[:, current_head * HEAD_SIZE : (current_head + 1) * HEAD_SIZE]
        head_values = every_value[:, current_head * HEAD_SIZE : (current_head + 1) * HEAD_SIZE]
        scores = jnp.einsum(
            "qgd,ld->qgl",
            grouped_heads[:, current_head],
            head_keys,
            preferred_element_type=jnp.float32,
        ) * (1.0 / math.sqrt(HEAD_SIZE))
        scores = jnp.where(visible_wide, scores, masked_score)
        row_top = jnp.max(scores, axis=-1)
        expos = jnp.where(visible_wide, jnp.exp(scores - row_top[..., None]), 0.0)
        total_list.append(jnp.sum(expos, axis=-1))
        top_list.append(row_top)
        numer_list.append(
            jnp.einsum(
                "qgl,ld->qgd",
                expos.astype(jnp.bfloat16),
                head_values,
                preferred_element_type=jnp.float32,
            )
        )
    row_top = jnp.stack(top_list, 1)
    weight_total = jnp.stack(total_list, 1)
    numer = jnp.stack(numer_list, 1)
    global_top = lax.pmax(row_top, "ctx")
    factor = jnp.exp(row_top - global_top)
    own_total, own_numer = (
        lax.psum_scatter(
            (weight_total * factor).reshape(query_count, -1), "ctx", scatter_dimension=0, tiled=True
        ),
        lax.psum_scatter(
            (numer * factor[..., None]).reshape(query_count, -1),
            "ctx",
            scatter_dimension=0,
            tiled=True,
        ),
    )
    own_total = own_total.reshape(suffix_rows, local_heads, sharing_count)
    own_numer = own_numer.reshape(suffix_rows, local_heads, sharing_count, HEAD_SIZE)
    attended = (own_numer / own_total[..., None]).reshape(suffix_rows, -1).astype(jnp.bfloat16)
    return (new_keys[:front_rows], new_values[:front_rows], attended)

GROUPS = 4
PAIR = 2
LANES = 128
SCALE = 1.0 / math.sqrt(HEAD_SIZE)


def row_scale(values):
    mean = jnp.sum(values * values, axis=-1, keepdims=True) * (1.0 / values.shape[-1])
    return lax.rsqrt(mean + epsilon)


CHUNKS = 4


def norm_kernel(query_any, hidden_any, suffix_any, gain_any, key_any, value_any, *rest):
    outs, packed_any, own_ref = rest[:GROUPS], rest[GROUPS], rest[GROUPS + 1]
    hidden_ref, suffix_ref, gain_ref, query_ref, packed_ref, tail_ref, sems = rest[GROUPS + 2 :]
    depth = key_any.shape[0]
    packing = [
        pltpu.make_async_copy(key_any, packed_ref.at[:depth], sems.at[CHUNKS + 3]),
        pltpu.make_async_copy(value_any, packed_ref.at[depth:], sems.at[CHUNKS + 4]),
    ]
    unpacking = pltpu.make_async_copy(packed_ref, packed_any, sems.at[CHUNKS + 5])
    core, ctx = lax.axis_index("tp"), lax.axis_index("ctx")
    z, x = ctx // PAIR, ctx % PAIR
    half_rows, features = hidden_ref.shape
    rows = half_rows // CHUNKS
    block = features // (GROUPS * PAIR)
    per_block = block // LANES
    pieces = PAIR * per_block
    copies = [
        pltpu.make_async_copy(gain_any, gain_ref, sems.at[CHUNKS]),
        pltpu.make_async_copy(suffix_any, suffix_ref, sems.at[CHUNKS + 1]),
        pltpu.make_async_copy(query_any, query_ref, sems.at[CHUNKS + 2]),
    ]
    for i in range(CHUNKS):
        start = pl.multiple_of(core * half_rows + i * rows, rows)
        copies.append(
            pltpu.make_async_copy(
                hidden_any.at[pl.ds(start, rows)], hidden_ref.at[i * rows : (i + 1) * rows], sems.at[i]
            )
        )
    for copy in copies + packing:
        copy.start()

    def offset(shift, side, j):
        owner = (z ^ shift) * PAIR + (x ^ side)
        return pl.multiple_of(owner * block + j * LANES, LANES)

    copies[0].wait()
    copies[1].wait()
    copies[2].wait()
    query_rows = query_ref[...].astype(jnp.float32)
    lines = query_rows.shape[1] // LANES
    for r in range(query_rows.shape[0]):
        tile = [query_rows[r : r + 1, j * LANES : (j + 1) * LANES] for j in range(lines)]
        tile = jnp.concatenate(tile, 0).astype(jnp.bfloat16)
        start = pieces * half_rows + pieces + r * lines
        for out in outs:
            out[start : start + lines, :] = tile

    both = suffix_ref[...].astype(jnp.float32)
    normed = both * row_scale(both) * gain_ref[...]
    tail_ref[...] = jnp.where(core == 0, normed[0:1], normed[1:2])
    for shift in range(GROUPS):
        ends = [
            tail_ref[:, pl.ds(offset(shift, side, j), LANES)]
            for side in range(PAIR)
            for j in range(per_block)
        ]
        start = pieces * half_rows
        outs[shift][start : start + pieces, :] = jnp.concatenate(ends, 0).astype(jnp.bfloat16)
    for copy in packing:
        copy.wait()
    unpacking.start()
    for i in range(CHUNKS):
        copies[3 + i].wait()
        at = slice(i * rows, (i + 1) * rows)
        inverse = row_scale(hidden_ref[at, :].astype(jnp.float32))
        for shift in range(GROUPS):
            for side in range(PAIR):
                for j in range(per_block):
                    columns = pl.ds(offset(shift, side, j), LANES)
                    piece = hidden_ref[at, columns].astype(jnp.float32) * inverse * gain_ref[:, columns]
                    start = (side * per_block + j) * half_rows + i * rows
                    outs[shift][start : start + rows, :] = piece.astype(jnp.bfloat16)
    own_ref[...] = outs[0][...]
    unpacking.wait()


def project_kernel(*refs):
    blocks = refs[: 2 * GROUPS]
    near_key, near_value, far = refs[2 * GROUPS : 2 * GROUPS + 3]
    outs = refs[2 * GROUPS + 3 : 3 * GROUPS + 3]
    query_ref, lhs_ref = refs[3 * GROUPS + 3 :]
    depth = near_key.shape[0]
    pieces = 2 * depth // LANES
    half_rows = (lhs_ref.shape[0] - 16) // (2 * GROUPS)
    rows = 2 * half_rows
    tails = []
    for i, block in enumerate(blocks):
        for j in range(pieces):
            lhs_ref[i * half_rows : (i + 1) * half_rows, j * LANES : (j + 1) * LANES] = block[
                j * half_rows : (j + 1) * half_rows, :
            ]
        tail = block[pieces * half_rows : pieces * half_rows + pieces, :].astype(jnp.float32)
        tails.append(jnp.concatenate([tail[j : j + 1] for j in range(pieces)], 1))
    tails.append(jnp.zeros((16 - len(tails), 2 * depth), jnp.float32))
    lines = query_ref.shape[0] // GROUPS
    for group in range(GROUPS):
        block = blocks[2 * group]
        query_ref[group * lines : (group + 1) * lines, :] = block[block.shape[0] - lines :, :]
    total = GROUPS * rows
    lhs_ref[total : total + 16, :] = jnp.concatenate(tails, 0).astype(jnp.bfloat16)

    def product(near, at):
        return jnp.dot(
            lhs_ref[:, :depth], near[...], preferred_element_type=jnp.float32
        ) + jnp.dot(lhs_ref[:, depth:], far[at, :], preferred_element_type=jnp.float32)

    keys = product(near_key, slice(0, depth))
    values = product(near_value, slice(depth, 2 * depth))
    high = keys.astype(jnp.bfloat16).astype(jnp.float32)
    low = keys - high
    columns = []
    for array in (high, low, values):
        for j in range(array.shape[1] // LANES):
            columns.append(array[:, j * LANES : (j + 1) * LANES])
    for group in range(GROUPS):
        for t, column in enumerate(columns):
            outs[group][t * rows : (t + 1) * rows, :] = column[
                group * rows : (group + 1) * rows
            ].astype(jnp.bfloat16)
        ends = [c[total + 2 * group : total + 2 * group + 2] for c in columns]
        ends.append(jnp.zeros((16 - 2 * len(columns), LANES), jnp.float32))
        outs[group][len(columns) * rows :, :] = jnp.concatenate(ends, 0).astype(jnp.bfloat16)


def head_queries(parts, head, width):
    sharing = QUERY_HEADS // KEY_VALUE_HEADS
    lines = sharing * width // HEAD_SIZE
    each = parts[0].shape[0] // GROUPS
    found = []
    for group in range(GROUPS):
        for part in parts:
            tiles = part[group * each : (group + 1) * each, :].astype(jnp.float32)
            for start in range(head * sharing, each, lines):
                found.append(tiles[start : start + sharing])
    return jnp.concatenate(found, 0).astype(jnp.bfloat16)


def times_transposed(a, b):
    return lax.dot_general(a, b, (((1,), (1,)), ((), ())), preferred_element_type=jnp.float32)


def loaded_kernel(place_ref, table_ref, split_ref, *refs):
    parts = refs[:PAIR]
    key_ref, value_ref, top_ref, total_ref, numer_ref, query_ref = refs[PAIR:]
    ctx = place_ref[1]
    slots, page, width = key_ref.shape
    heads = width // HEAD_SIZE
    split = split_ref[0]
    live = []
    for s in range(slots):
        hit = jnp.int32(0)
        for p in range(table_ref.shape[0]):
            hit = hit | ((table_ref[p] == ctx * slots + s) & (p >= split)).astype(jnp.int32)
        live.append(hit)
    for head in range(heads):
        columns = slice(head * HEAD_SIZE, (head + 1) * HEAD_SIZE)
        queries = head_queries(parts, head, width)
        count = queries.shape[0]
        query_ref[head * count : (head + 1) * count, :] = queries
        scores = [
            jnp.where(live[s] > 0, times_transposed(queries, key_ref[s, :, columns]) * SCALE, masked_score)
            for s in range(slots)
        ]
        top = scores[0].max(-1, keepdims=True)
        for s in range(1, slots):
            top = jnp.maximum(top, scores[s].max(-1, keepdims=True))
        total = jnp.zeros((count, 1), jnp.float32)
        numer = jnp.zeros((count, HEAD_SIZE), jnp.float32)
        for s in range(slots):
            expos = jnp.where(live[s] > 0, jnp.exp(scores[s] - top), 0.0)
            total += expos.sum(-1, keepdims=True)
            numer += jnp.dot(
                expos.astype(jnp.bfloat16), value_ref[s, :, columns], preferred_element_type=jnp.float32
            )
        rows = slice(head * count, (head + 1) * count)
        top_ref[rows, :] = jnp.broadcast_to(top, (count, LANES))
        total_ref[rows, :] = jnp.broadcast_to(total, (count, LANES))
        numer_ref[rows, :] = numer


def front_kernel(
    place_ref, split_ref, own, *refs
):
    received = refs[: GROUPS - 1]
    (key_bias, value_bias, cosine_ref, sine_ref, query_ref, top_ref, total_ref, numer_ref) = refs[
        GROUPS - 1 : GROUPS + 7
    ]
    front_key, front_value = refs[GROUPS + 7 : GROUPS + 9]
    outs = refs[GROUPS + 9 :]
    core, ctx = place_ref[0], place_ref[1]
    rows, width = front_key.shape
    half_rows = rows // 2
    heads = width // HEAD_SIZE
    sharing = QUERY_HEADS // KEY_VALUE_HEADS
    count = query_ref.shape[0] // heads
    own_queries = count // sharing // (GROUPS * PAIR)
    visible = ctx < split_ref[0]

    def summed(start, size):
        value = own[start : start + size, :].astype(jnp.float32)
        for ref in received:
            value += ref[start : start + size, :].astype(jnp.float32)
        return value

    ends = summed(3 * heads * rows, 16)
    row_query = lax.broadcasted_iota(jnp.int32, (count, 16), 0) // sharing
    query_position = (ctx ^ (row_query // own_queries)) * own_queries + row_query % own_queries
    end_column = lax.broadcasted_iota(jnp.int32, (count, 16), 1)
    end_position = ctx * 2 + jnp.where(end_column == 0, core, 1 - core)
    end_seen = (end_column < 2) & (end_position <= query_position)
    pad = jnp.zeros((14, HEAD_SIZE), jnp.float32)
    for head in range(heads):
        columns = slice(head * HEAD_SIZE, (head + 1) * HEAD_SIZE)
        raw = summed(head * rows, rows) + summed((heads + head) * rows, rows)
        value = (summed((2 * heads + head) * rows, rows) + value_bias[:, columns]).astype(jnp.bfloat16)
        end_raw = ends[2 * head : 2 * head + 2] + ends[2 * (heads + head) : 2 * (heads + head) + 2]
        end_value = ends[2 * (2 * heads + head) : 2 * (2 * heads + head) + 2] + value_bias[:, columns]
        end_raw = jnp.concatenate([end_raw + key_bias[:, columns], pad], 0)
        end_value = jnp.concatenate([end_value, pad], 0).astype(jnp.bfloat16)
        raw = raw + key_bias[:, columns]

        def rotated(k, part):
            turned = pltpu.roll(k, HEAD_SIZE // 2, 1)
            return (k * cosine_ref[part, :] + turned * sine_ref[part, :]).astype(jnp.bfloat16)

        key = rotated(raw, slice(0, rows))
        end_key = rotated(end_raw, slice(rows, rows + 16))
        for half in range(2):
            to = pl.ds(pl.multiple_of(lax.rem(core + half, 2) * half_rows, half_rows), half_rows)
            front_key[to, columns] = key[half * half_rows : (half + 1) * half_rows]
            front_value[to, columns] = value[half * half_rows : (half + 1) * half_rows]
        part = slice(head * count, (head + 1) * count)
        queries = query_ref[part, :]
        scores = jnp.where(visible, times_transposed(queries, key) * SCALE, masked_score)
        end_scores = jnp.where(end_seen, times_transposed(queries, end_key) * SCALE, masked_score)
        old_top = top_ref[part, :]
        top = jnp.maximum(scores.max(-1, keepdims=True), end_scores.max(-1, keepdims=True))
        top = jnp.maximum(old_top, top)
        factor = jnp.exp(old_top - top)
        expos = jnp.where(visible, jnp.exp(scores - top), 0.0)
        end_expos = jnp.where(end_seen, jnp.exp(end_scores - top[:, :16]), 0.0)
        total = total_ref[part, :] * factor + (
            expos.sum(-1, keepdims=True) + end_expos.sum(-1, keepdims=True)
        )
        numer = (
            numer_ref[part, :] * factor
            + jnp.dot(expos.astype(jnp.bfloat16), value, preferred_element_type=jnp.float32)
            + jnp.dot(end_expos.astype(jnp.bfloat16), end_value, preferred_element_type=jnp.float32)
        )
        stats = (kept_stats(top[:, 0:1], total[:, 0:1]), sent_stats(top[:, 0:1], total[:, 0:1]))
        each = own_queries * sharing
        for slot in range(GROUPS * PAIR):
            start = (slot // PAIR * 2 * heads + head) * each
            at = slice(slot * each, (slot + 1) * each)
            out = outs[slot % PAIR]
            out[start : start + each, :] = numer[at].astype(out.dtype)
            out[start + heads * each : start + (heads + 1) * each, :] = stats[slot % PAIR][at]


def kept_stats(top, total):
    lane = lax.broadcasted_iota(jnp.int32, (top.shape[0], LANES), 1)
    return jnp.where(lane < LANES // 2, top, total)


def sent_stats(top, total):
    terms = []
    for rest, count in ((top, 3), (total, 2)):
        for _ in range(count):
            term = rest.astype(jnp.bfloat16).astype(jnp.float32)
            terms.append(term)
            rest = rest - term
    part = lax.broadcasted_iota(jnp.int32, (top.shape[0], LANES), 1) // 16
    stats = jnp.broadcast_to(terms[-1], part.shape)
    for i, term in enumerate(terms[:-1]):
        stats = jnp.where(part == i, term, stats)
    return stats.astype(jnp.bfloat16)


def merged(kept, other, start, rows):
    half = LANES // 2
    stats = kept[start + rows : start + 2 * rows, :]
    top, total = stats[:, 0:1], stats[:, half : half + 1]
    terms = other[start + rows : start + 2 * rows, :].astype(jnp.float32)
    other_top = (terms[:, 0:1] + terms[:, 16:17]) + terms[:, 32:33]
    other_total = terms[:, 48:49] + terms[:, 64:65]
    both = jnp.maximum(top, other_top)
    factor, other_factor = jnp.exp(top - both), jnp.exp(other_top - both)
    total = factor * total + other_factor * other_total
    numer = factor * kept[start : start + rows, :]
    numer += other_factor * other[start : start + rows, :].astype(jnp.float32)
    return numer, both, total


def merge_kernel(each, kept, other, keep_ref, send_ref):
    rows = each // 2
    for slot in range(kept.shape[0] // each):
        numer, top, total = merged(kept, other, slot * each, rows)
        start = slot // 2 * each
        if slot % 2 == 0:
            keep_ref[start : start + rows, :] = numer
            keep_ref[start + rows : start + each, :] = kept_stats(top, total)
        else:
            send_ref[start : start + rows, :] = numer.astype(jnp.bfloat16)
            send_ref[start + rows : start + each, :] = sent_stats(top, total)


def last_kernel(kept, other, out_ref):
    rows = kept.shape[0] // 2
    numer, _, total = merged(kept, other, 0, rows)
    result = numer / total
    queries, width = out_ref.shape
    sharing = QUERY_HEADS // KEY_VALUE_HEADS
    heads = width // HEAD_SIZE // sharing
    lines = []
    for i in range(queries):
        starts = [(h * queries + i) * sharing + g for h in range(heads) for g in range(sharing)]
        lines.append(jnp.concatenate([result[s : s + 1] for s in starts], 1))
    out_ref[...] = jnp.concatenate(lines, 0).astype(jnp.bfloat16)


def exchange_plan(
    hidden,
    suffix_hidden,
    norm_gain,
    key_matrix,
    value_matrix,
    key_offset_bias,
    value_offset_bias,
    suffix_query_rows,
    slot_keys,
    slot_values,
    page_slot_table,
    split_page,
):
    n_ctx = GROUPS * PAIR
    ctx = lax.axis_index("ctx").astype(jnp.int32)
    core = lax.axis_index("tp").astype(jnp.int32)
    place = jnp.stack([core, ctx])
    rows, features = hidden.shape
    half_rows = rows // 2
    width = key_matrix.shape[1]
    query_width = suffix_query_rows.shape[1]
    prefix_len = page_slot_table.shape[0] * slot_keys.shape[1]
    smem = pl.BlockSpec(memory_space=pltpu.SMEM)
    vmem = pl.BlockSpec(memory_space=pltpu.VMEM)
    params = pltpu.CompilerParams(vmem_limit_bytes=48 * 1024 * 1024)

    def move(array, target):
        pairs = []
        for c in range(n_ctx):
            for t in range(2):
                to_c, to_t = target(c, t)
                pairs.append((c * 2 + t, to_c * 2 + to_t))
        return lax.ppermute(array, ("ctx", "tp"), pairs)

    def along(shift):
        return lambda c, t: ((c // PAIR ^ shift) * PAIR + c % PAIR, t)

    def beside(c, t):
        return (c ^ 1, t)

    def sibling(c, t):
        return (c, 1 - t)

    hbm = pl.BlockSpec(memory_space=pltpu.HBM)
    pieces = features // GROUPS // LANES
    own_queries = suffix_query_rows.shape[0]
    lines = query_width // LANES
    block_rows = pieces * half_rows + pieces + own_queries * lines
    *blocks, packed, own = pl.pallas_call(
        norm_kernel,
        in_specs=[hbm] * 6,
        out_specs=[vmem] * GROUPS + [hbm, vmem],
        out_shape=[jax.ShapeDtypeStruct((block_rows, LANES), jnp.bfloat16)] * GROUPS
        + [
            jax.ShapeDtypeStruct((2 * key_matrix.shape[0], width), jnp.bfloat16),
            jax.ShapeDtypeStruct((block_rows, LANES), jnp.bfloat16),
        ],
        scratch_shapes=[
            pltpu.VMEM((half_rows, features), jnp.bfloat16),
            pltpu.VMEM(suffix_hidden.shape, jnp.bfloat16),
            pltpu.VMEM((1, features), jnp.float32),
            pltpu.VMEM(suffix_query_rows.shape, jnp.bfloat16),
            pltpu.VMEM((2 * key_matrix.shape[0], width), jnp.bfloat16),
            pltpu.VMEM((1, features), jnp.float32),
            pltpu.SemaphoreType.DMA((CHUNKS + 6,)),
        ],
        compiler_params=pltpu.CompilerParams(vmem_limit_bytes=60 * 1024 * 1024),
        cost_estimate=pl.CostEstimate(
            flops=4 * half_rows * features, bytes_accessed=4 * half_rows * features, transcendentals=0
        ),
        name="norm_rows",
    )(
        suffix_query_rows,
        hidden,
        suffix_hidden,
        norm_gain.reshape(1, features),
        key_matrix,
        value_matrix,
    )
    far_first = sorted(range(1, GROUPS), key=lambda s: s < 2)
    far = move(packed, beside)

    mine = {s: move(blocks[s], along(s)) for s in far_first}
    theirs = {s: move(mine.get(s, blocks[0]), sibling) for s in [0] + far_first}
    mine[0] = own
    lhs = [part[s] for s in range(GROUPS) for part in (mine, theirs)]

    inverse_freq = rope_base ** (
        -(jnp.arange(HEAD_SIZE // 2, dtype=jnp.float32) * (2.0 / HEAD_SIZE))
    )
    row = jnp.arange(rows + 16, dtype=jnp.int32)
    front_position = ctx * rows + (row + core * half_rows) % rows
    end_position = prefix_len + ctx * 2 + jnp.where(row == rows, core, 1 - core)
    position = jnp.where(row < rows, front_position, end_position)
    angles = position.astype(jnp.float32)[:, None] * inverse_freq[None, :]
    cosine, sine = jnp.cos(angles), jnp.sin(angles)
    cosine = jnp.concatenate([cosine, cosine], 1)
    sine = jnp.concatenate([-sine, sine], 1)

    part_rows = 3 * (width // LANES) * rows + 16
    *partials, own_tiles = pl.pallas_call(
        project_kernel,
        in_specs=[vmem] * (2 * GROUPS + 3),
        out_specs=[vmem] * (GROUPS + 1),
        out_shape=[jax.ShapeDtypeStruct((part_rows, LANES), jnp.bfloat16)] * GROUPS
        + [jax.ShapeDtypeStruct((GROUPS * own_queries * lines, LANES), jnp.bfloat16)],
        scratch_shapes=[pltpu.VMEM((GROUPS * rows + 16, PAIR * features // n_ctx), jnp.bfloat16)],
        compiler_params=params,
        cost_estimate=pl.CostEstimate(flops=2 * GROUPS * rows * 2 * width * features // GROUPS, bytes_accessed=6 * 1024 * 1024, transcendentals=0),
        name="project",
    )(*lhs, key_matrix, value_matrix, far)
    received = [move(partials[s], along(s)) for s in far_first]
    beside_tiles = move(own_tiles, beside)

    states = n_ctx * own_queries * query_width // HEAD_SIZE
    state = jax.ShapeDtypeStruct((states, LANES), jnp.float32)
    top, total, numer, queries = pl.pallas_call(
        loaded_kernel,
        in_specs=[smem, smem, smem] + [vmem] * (PAIR + 2),
        out_specs=[vmem] * 4,
        out_shape=[state] * 3 + [jax.ShapeDtypeStruct((states, LANES), jnp.bfloat16)],
        compiler_params=params,
        cost_estimate=pl.CostEstimate(
            flops=4 * states * slot_keys.shape[0] * slot_keys.shape[1] * HEAD_SIZE,
            bytes_accessed=4 * slot_keys.size,
            transcendentals=states * slot_keys.shape[0] * slot_keys.shape[1],
        ),
        name="loaded_attention",
    )(place, page_slot_table, split_page, own_tiles, beside_tiles, slot_keys, slot_values)


    def payloads(size):
        return [jax.ShapeDtypeStruct((size, LANES), kind) for kind in (jnp.float32, jnp.bfloat16)]

    row_shape = jax.ShapeDtypeStruct((rows, width), jnp.bfloat16)
    front_key, front_value, kept, sent = pl.pallas_call(
        front_kernel,
        in_specs=[smem, smem] + [vmem] * (GROUPS + 8),
        out_specs=[vmem] * 4,
        out_shape=[row_shape] * 2 + payloads(states),
        compiler_params=params,
        cost_estimate=pl.CostEstimate(flops=4 * states * rows * HEAD_SIZE, bytes_accessed=2 * 1024 * 1024, transcendentals=states * rows),
        name="front_attention",
    )(
        place,
        split_page,
        partials[0],
        *received,
        key_offset_bias.reshape(1, width),
        value_offset_bias.reshape(1, width),
        cosine,
        sine,
        queries,
        top,
        total,
        numer,
    )
    for target in (beside, along(1)):
        kept, sent = pl.pallas_call(
            functools.partial(merge_kernel, states // GROUPS),
            in_specs=[vmem] * 2,
            out_specs=[vmem] * 2,
            out_shape=payloads(kept.shape[0] // 2),
            compiler_params=params,
            name="merge",
        )(kept, move(sent, target))
    attended = pl.pallas_call(
        last_kernel,
        in_specs=[vmem] * 2,
        out_specs=vmem,
        out_shape=jax.ShapeDtypeStruct((own_queries, query_width), jnp.bfloat16),
        compiler_params=params,
        name="finish",
    )(kept, move(sent, along(2)))
    return (front_key, front_value, attended)


def solution(mesh):
    per_device = exchange_plan if mesh.shape["ctx"] == GROUPS * PAIR else gathered_plan
    return jax.shard_map(
        per_device,
        mesh=mesh,
        in_specs=(
            P(("req", "ctx"), None),
            P(("req", "ctx"), None),
            P(),
            P("ctx", "tp"),
            P("ctx", "tp"),
            P("tp"),
            P("tp"),
            P(("req", "ctx"), "tp"),
            P(("req", "ctx"), None, "tp"),
            P(("req", "ctx"), None, "tp"),
            P("req"),
            P("req"),
        ),
        out_specs=(P(("req", "ctx"), "tp"), P(("req", "ctx"), "tp"), P(("req", "ctx"), "tp")),
        check_vma=False,
    )
```

```python
import functools
import math

import jax
import jax.numpy as jnp
from jax import lax
from jax.experimental import pallas as pl
from jax.experimental.pallas import tpu as pltpu
from jax.sharding import PartitionSpec as P

QUERY_HEADS = 32
KEY_VALUE_HEADS = 4
HEAD_SIZE = 128


epsilon = 1e-06
rope_base = 1000000.0
masked_score = -1e30


def rms_rows(matrix, norm_gain):
    widened = matrix.astype(jnp.float32)
    inverse = lax.rsqrt(jnp.mean(widened * widened, axis=-1, keepdims=True) + epsilon)
    return (widened * inverse * norm_gain).astype(jnp.bfloat16)


def rotate(key_rows, positions, head_dim):
    row_count = key_rows.shape[0]
    split_heads = key_rows.reshape(row_count, -1, head_dim)
    half_dim = head_dim // 2
    inverse_freq = rope_base ** (-(jnp.arange(half_dim, dtype=jnp.float32) * (2.0 / head_dim)))
    angles = positions.astype(jnp.float32)[:, None] * inverse_freq[None, :]
    cosine = jnp.concatenate([jnp.cos(angles), jnp.cos(angles)], -1)[:, None, :]
    sine = jnp.concatenate([jnp.sin(angles), jnp.sin(angles)], -1)[:, None, :]
    turned = jnp.concatenate([-split_heads[..., half_dim:], split_heads[..., :half_dim]], -1)
    return (split_heads * cosine + turned * sine).reshape(row_count, -1)


def gathered_plan(
    hidden,
    suffix_hidden,
    norm_gain,
    key_matrix,
    value_matrix,
    key_offset_bias,
    value_offset_bias,
    suffix_query_rows,
    slot_keys,
    slot_values,
    page_slot_table,
    split_page,
):
    ctx_index = lax.axis_index("ctx")
    queries = lax.all_gather(suffix_query_rows, "ctx", axis=0, tiled=True)
    front_rows = hidden.shape[0]
    suffix_rows = suffix_hidden.shape[0]
    page_size = slot_keys.shape[1]
    slot_count = slot_keys.shape[0]
    total_pages = page_slot_table.shape[0]
    prefix_len = total_pages * page_size
    normed = rms_rows(jnp.concatenate([hidden, suffix_hidden], 0), norm_gain)
    col_width = key_matrix.shape[1]

    def accumulate(block_rows):
        return jnp.dot(normed, block_rows, preferred_element_type=jnp.float32)

    key_acc = accumulate(lax.all_gather(key_matrix, "ctx", axis=0, tiled=True))
    value_acc = accumulate(lax.all_gather(value_matrix, "ctx", axis=0, tiled=True))
    front_pos = ctx_index * front_rows + jnp.arange(front_rows, dtype=jnp.int32)
    suffix_pos = prefix_len + ctx_index * suffix_rows + jnp.arange(suffix_rows, dtype=jnp.int32)
    new_keys = rotate(
        key_acc + key_offset_bias, jnp.concatenate([front_pos, suffix_pos], 0), HEAD_SIZE
    ).astype(jnp.bfloat16)
    new_values = (value_acc + value_offset_bias).astype(jnp.bfloat16)
    cut_pos = split_page[0] * page_size
    global_slot = ctx_index * slot_count + jnp.arange(slot_count, dtype=jnp.int32)
    page_index = jnp.arange(total_pages, dtype=jnp.int32)
    slot_hits = (page_slot_table[None, :] == global_slot[:, None]) & (
        page_index[None, :] >= split_page[0]
    )
    slot_live = jnp.max(slot_hits.astype(jnp.int32), axis=1) > 0
    every_key = jnp.concatenate(
        [new_keys[:front_rows], slot_keys.reshape(-1, col_width), new_keys[front_rows:]], 0
    )
    every_value = jnp.concatenate(
        [new_values[:front_rows], slot_values.reshape(-1, col_width), new_values[front_rows:]], 0
    )
    query_count = queries.shape[0]
    query_pos = prefix_len + jnp.arange(query_count, dtype=jnp.int32)
    prefix_seen = jnp.concatenate([front_pos < cut_pos, jnp.repeat(slot_live, page_size)], 0)
    suffix_seen = suffix_pos[None, :] <= query_pos[:, None]
    visible = jnp.concatenate(
        [jnp.broadcast_to(prefix_seen[None, :], (query_count, prefix_seen.shape[0])), suffix_seen],
        1,
    )
    visible_wide = visible[:, None, :]
    sharing_count = QUERY_HEADS // KEY_VALUE_HEADS
    local_heads = col_width // HEAD_SIZE
    grouped_heads = queries.reshape(query_count, local_heads, sharing_count, HEAD_SIZE)
    top_list = []
    total_list = []
    numer_list = []
    for current_head in range(local_heads):
        head_keys = every_key[:, current_head * HEAD_SIZE : (current_head + 1) * HEAD_SIZE]
        head_values = every_value[:, current_head * HEAD_SIZE : (current_head + 1) * HEAD_SIZE]
        scores = jnp.einsum(
            "qgd,ld->qgl",
            grouped_heads[:, current_head],
            head_keys,
            preferred_element_type=jnp.float32,
        ) * (1.0 / math.sqrt(HEAD_SIZE))
        scores = jnp.where(visible_wide, scores, masked_score)
        row_top = jnp.max(scores, axis=-1)
        expos = jnp.where(visible_wide, jnp.exp(scores - row_top[..., None]), 0.0)
        total_list.append(jnp.sum(expos, axis=-1))
        top_list.append(row_top)
        numer_list.append(
            jnp.einsum(
                "qgl,ld->qgd",
                expos.astype(jnp.bfloat16),
                head_values,
                preferred_element_type=jnp.float32,
            )
        )
    row_top = jnp.stack(top_list, 1)
    weight_total = jnp.stack(total_list, 1)
    numer = jnp.stack(numer_list, 1)
    global_top = lax.pmax(row_top, "ctx")
    factor = jnp.exp(row_top - global_top)
    own_total, own_numer = (
        lax.psum_scatter(
            (weight_total * factor).reshape(query_count, -1), "ctx", scatter_dimension=0, tiled=True
        ),
        lax.psum_scatter(
            (numer * factor[..., None]).reshape(query_count, -1),
            "ctx",
            scatter_dimension=0,
            tiled=True,
        ),
    )
    own_total = own_total.reshape(suffix_rows, local_heads, sharing_count)
    own_numer = own_numer.reshape(suffix_rows, local_heads, sharing_count, HEAD_SIZE)
    attended = (own_numer / own_total[..., None]).reshape(suffix_rows, -1).astype(jnp.bfloat16)
    return (new_keys[:front_rows], new_values[:front_rows], attended)

GROUPS = 4
PAIR = 2
LANES = 128
SCALE = 1.0 / math.sqrt(HEAD_SIZE)


def row_scale(values):
    mean = jnp.sum(values * values, axis=-1, keepdims=True) * (1.0 / values.shape[-1])
    return lax.rsqrt(mean + epsilon)


CHUNKS = 4


def far_first():
    return sorted(range(1, GROUPS), key=lambda s: s < GROUPS // 2)


def norm_kernel(query_any, hidden_any, suffix_any, gain_any, key_any, value_any, *rest):
    blocks_any, packed_any, own_any = rest[:GROUPS], rest[GROUPS], rest[GROUPS + 1]
    hidden_ref, suffix_ref, gain_ref, query_ref, packed_ref, tail_ref = rest[GROUPS + 2 : GROUPS + 8]
    outs, (sems, out_sems) = rest[GROUPS + 8 : -2], rest[-2:]
    depth = key_any.shape[0]
    packing = [
        pltpu.make_async_copy(key_any, packed_ref.at[:depth], sems.at[CHUNKS + 3]),
        pltpu.make_async_copy(value_any, packed_ref.at[depth:], sems.at[CHUNKS + 4]),
    ]
    unpacking = pltpu.make_async_copy(packed_ref, packed_any, sems.at[CHUNKS + 5])
    core, ctx = lax.axis_index("tp"), lax.axis_index("ctx")
    z, x = ctx // PAIR, ctx % PAIR
    half_rows, features = hidden_ref.shape
    rows = half_rows // CHUNKS
    block = features // (GROUPS * PAIR)
    per_block = block // LANES
    pieces = PAIR * per_block
    copies = [
        pltpu.make_async_copy(gain_any, gain_ref, sems.at[CHUNKS]),
        pltpu.make_async_copy(suffix_any, suffix_ref, sems.at[CHUNKS + 1]),
        pltpu.make_async_copy(query_any, query_ref, sems.at[CHUNKS + 2]),
    ]
    for i in range(CHUNKS):
        start = pl.multiple_of(core * half_rows + i * rows, rows)
        copies.append(
            pltpu.make_async_copy(
                hidden_any.at[pl.ds(start, rows)], hidden_ref.at[i * rows : (i + 1) * rows], sems.at[i]
            )
        )
    for copy in copies + packing:
        copy.start()

    def offset(shift, side, j):
        owner = (z ^ shift) * PAIR + (x ^ side)
        return pl.multiple_of(owner * block + j * LANES, LANES)

    copies[0].wait()
    copies[1].wait()
    copies[2].wait()
    query_rows = query_ref[...].astype(jnp.float32)
    lines = query_rows.shape[1] // LANES
    for r in range(query_rows.shape[0]):
        tile = [query_rows[r : r + 1, j * LANES : (j + 1) * LANES] for j in range(lines)]
        tile = jnp.concatenate(tile, 0).astype(jnp.bfloat16)
        start = pieces * half_rows + pieces + r * lines
        for out in outs:
            out[start : start + lines, :] = tile

    both = suffix_ref[...].astype(jnp.float32)
    normed = both * row_scale(both) * gain_ref[...]
    tail_ref[...] = jnp.where(core == 0, normed[0:1], normed[1:2])
    for shift in range(GROUPS):
        ends = [
            tail_ref[:, pl.ds(offset(shift, side, j), LANES)]
            for side in range(PAIR)
            for j in range(per_block)
        ]
        start = pieces * half_rows
        outs[shift][start : start + pieces, :] = jnp.concatenate(ends, 0).astype(jnp.bfloat16)
    inverses = []
    for i in range(CHUNKS):
        copies[3 + i].wait()
        inverses.append(row_scale(hidden_ref[i * rows : (i + 1) * rows, :].astype(jnp.float32)))
    for copy in packing:
        copy.wait()
    unpacking.start()
    leaving = []
    for shift in far_first() + [0]:
        for side in range(PAIR):
            for j in range(per_block):
                columns = pl.ds(offset(shift, side, j), LANES)
                for i in range(CHUNKS):
                    piece = hidden_ref[i * rows : (i + 1) * rows, columns].astype(jnp.float32)
                    piece = piece * inverses[i] * gain_ref[:, columns]
                    start = (side * per_block + j) * half_rows + i * rows
                    outs[shift][start : start + rows, :] = piece.astype(jnp.bfloat16)
        leaving.append(pltpu.make_async_copy(outs[shift], blocks_any[shift], out_sems.at[shift]))
        leaving[-1].start()
    leaving.append(pltpu.make_async_copy(outs[0], own_any, out_sems.at[GROUPS]))
    leaving[-1].start()
    for copy in leaving:
        copy.wait()
    unpacking.wait()


def fetch_kernel(from_any, to_ref, sem):
    copy = pltpu.make_async_copy(from_any, to_ref, sem)
    copy.start()
    copy.wait()


def project_kernel(*refs):
    blocks = refs[: 2 * GROUPS]
    near_key, near_value, far = refs[2 * GROUPS : 2 * GROUPS + 3]
    outs = refs[2 * GROUPS + 3 : 3 * GROUPS + 3]
    query_ref, lhs_ref = refs[3 * GROUPS + 3 :]
    depth = near_key.shape[0]
    pieces = 2 * depth // LANES
    half_rows = (lhs_ref.shape[0] - 16) // (2 * GROUPS)
    rows = 2 * half_rows
    tails = [None] * len(blocks)
    for i, block in enumerate(blocks):
        for j in range(pieces):
            lhs_ref[i * half_rows : (i + 1) * half_rows, j * LANES : (j + 1) * LANES] = block[
                j * half_rows : (j + 1) * half_rows, :
            ]
        tail = block[pieces * half_rows : pieces * half_rows + pieces, :].astype(jnp.float32)
        tails[i] = jnp.concatenate([tail[j : j + 1] for j in range(pieces)], 1)
    tails.append(jnp.zeros((16 - len(tails), 2 * depth), jnp.float32))
    lines = query_ref.shape[0] // GROUPS
    for group in range(GROUPS):
        block = blocks[2 * group]
        query_ref[group * lines : (group + 1) * lines, :] = block[block.shape[0] - lines :, :]
    total = GROUPS * rows
    lhs_ref[total : total + 16, :] = jnp.concatenate(tails, 0).astype(jnp.bfloat16)

    def product(near, at):
        return jnp.dot(
            lhs_ref[:, :depth], near[...], preferred_element_type=jnp.float32
        ) + jnp.dot(lhs_ref[:, depth:], far[at, :], preferred_element_type=jnp.float32)

    keys = product(near_key, slice(0, depth))
    values = product(near_value, slice(depth, 2 * depth))
    high = keys.astype(jnp.bfloat16).astype(jnp.float32)
    low = keys - high
    columns = []
    for array in (high, low, values):
        for j in range(array.shape[1] // LANES):
            columns.append(array[:, j * LANES : (j + 1) * LANES])
    for group in range(GROUPS):
        for t, column in enumerate(columns):
            outs[group][t * rows : (t + 1) * rows, :] = column[
                group * rows : (group + 1) * rows
            ].astype(jnp.bfloat16)
        ends = [c[total + 2 * group : total + 2 * group + 2] for c in columns]
        ends.append(jnp.zeros((16 - 2 * len(columns), LANES), jnp.float32))
        outs[group][len(columns) * rows :, :] = jnp.concatenate(ends, 0).astype(jnp.bfloat16)


def head_queries(parts, head, width):
    sharing = QUERY_HEADS // KEY_VALUE_HEADS
    lines = sharing * width // HEAD_SIZE
    each = parts[0].shape[0] // GROUPS
    found = []
    for group in range(GROUPS):
        for part in parts:
            tiles = part[group * each : (group + 1) * each, :].astype(jnp.float32)
            for start in range(head * sharing, each, lines):
                found.append(tiles[start : start + sharing])
    return jnp.concatenate(found, 0).astype(jnp.bfloat16)


def times_transposed(a, b):
    return lax.dot_general(a, b, (((1,), (1,)), ((), ())), preferred_element_type=jnp.float32)


def loaded_kernel(place_ref, table_ref, split_ref, *refs):
    parts = refs[:PAIR]
    key_ref, value_ref, top_ref, total_ref, numer_ref, query_ref = refs[PAIR:]
    ctx = place_ref[1]
    slots, page, width = key_ref.shape
    heads = width // HEAD_SIZE
    split = split_ref[0]
    live = []
    for s in range(slots):
        hit = jnp.int32(0)
        for p in range(table_ref.shape[0]):
            hit = hit | ((table_ref[p] == ctx * slots + s) & (p >= split)).astype(jnp.int32)
        live.append(hit)
    for head in range(heads):
        columns = slice(head * HEAD_SIZE, (head + 1) * HEAD_SIZE)
        queries = head_queries(parts, head, width)
        count = queries.shape[0]
        query_ref[head * count : (head + 1) * count, :] = queries
        scores = [
            jnp.where(live[s] > 0, times_transposed(queries, key_ref[s, :, columns]) * SCALE, masked_score)
            for s in range(slots)
        ]
        top = scores[0].max(-1, keepdims=True)
        for s in range(1, slots):
            top = jnp.maximum(top, scores[s].max(-1, keepdims=True))
        total = jnp.zeros((count, 1), jnp.float32)
        numer = jnp.zeros((count, HEAD_SIZE), jnp.float32)
        for s in range(slots):
            expos = jnp.where(live[s] > 0, jnp.exp(scores[s] - top), 0.0)
            total += expos.sum(-1, keepdims=True)
            numer += jnp.dot(
                expos.astype(jnp.bfloat16), value_ref[s, :, columns], preferred_element_type=jnp.float32
            )
        rows = slice(head * count, (head + 1) * count)
        top_ref[rows, :] = jnp.broadcast_to(top, (count, LANES))
        total_ref[rows, :] = jnp.broadcast_to(total, (count, LANES))
        numer_ref[rows, :] = numer


def front_kernel(
    place_ref, split_ref, own, *refs
):
    received = refs[: GROUPS - 1]
    (key_bias, value_bias, cosine_ref, sine_ref, query_ref, top_ref, total_ref, numer_ref) = refs[
        GROUPS - 1 : GROUPS + 7
    ]
    front_key, front_value = refs[GROUPS + 7 : GROUPS + 9]
    outs = refs[GROUPS + 9 :]
    core, ctx = place_ref[0], place_ref[1]
    rows, width = front_key.shape
    half_rows = rows // 2
    heads = width // HEAD_SIZE
    sharing = QUERY_HEADS // KEY_VALUE_HEADS
    count = query_ref.shape[0] // heads
    own_queries = count // sharing // (GROUPS * PAIR)
    visible = ctx < split_ref[0]

    def summed(start, size):
        value = own[start : start + size, :].astype(jnp.float32)
        for ref in received:
            value += ref[start : start + size, :].astype(jnp.float32)
        return value

    ends = summed(3 * heads * rows, 16)
    row_query = lax.broadcasted_iota(jnp.int32, (count, 16), 0) // sharing
    query_position = (ctx ^ (row_query // own_queries)) * own_queries + row_query % own_queries
    end_column = lax.broadcasted_iota(jnp.int32, (count, 16), 1)
    end_position = ctx * 2 + jnp.where(end_column == 0, core, 1 - core)
    end_seen = (end_column < 2) & (end_position <= query_position)
    pad = jnp.zeros((14, HEAD_SIZE), jnp.float32)
    for head in range(heads):
        columns = slice(head * HEAD_SIZE, (head + 1) * HEAD_SIZE)
        raw = summed(head * rows, rows) + summed((heads + head) * rows, rows)
        value = (summed((2 * heads + head) * rows, rows) + value_bias[:, columns]).astype(jnp.bfloat16)
        end_raw = ends[2 * head : 2 * head + 2] + ends[2 * (heads + head) : 2 * (heads + head) + 2]
        end_value = ends[2 * (2 * heads + head) : 2 * (2 * heads + head) + 2] + value_bias[:, columns]
        end_raw = jnp.concatenate([end_raw + key_bias[:, columns], pad], 0)
        end_value = jnp.concatenate([end_value, pad], 0).astype(jnp.bfloat16)
        raw = raw + key_bias[:, columns]

        def rotated(k, part):
            turned = pltpu.roll(k, HEAD_SIZE // 2, 1)
            return (k * cosine_ref[part, :] + turned * sine_ref[part, :]).astype(jnp.bfloat16)

        key = rotated(raw, slice(0, rows))
        end_key = rotated(end_raw, slice(rows, rows + 16))
        for half in range(2):
            to = pl.ds(pl.multiple_of(lax.rem(core + half, 2) * half_rows, half_rows), half_rows)
            front_key[to, columns] = key[half * half_rows : (half + 1) * half_rows]
            front_value[to, columns] = value[half * half_rows : (half + 1) * half_rows]
        part = slice(head * count, (head + 1) * count)
        queries = query_ref[part, :]
        scores = jnp.where(visible, times_transposed(queries, key) * SCALE, masked_score)
        end_scores = jnp.where(end_seen, times_transposed(queries, end_key) * SCALE, masked_score)
        old_top = top_ref[part, :]
        top = jnp.maximum(scores.max(-1, keepdims=True), end_scores.max(-1, keepdims=True))
        top = jnp.maximum(old_top, top)
        factor = jnp.exp(old_top - top)
        expos = jnp.where(visible, jnp.exp(scores - top), 0.0)
        end_expos = jnp.where(end_seen, jnp.exp(end_scores - top[:, :16]), 0.0)
        total = total_ref[part, :] * factor + (
            expos.sum(-1, keepdims=True) + end_expos.sum(-1, keepdims=True)
        )
        numer = (
            numer_ref[part, :] * factor
            + jnp.dot(expos.astype(jnp.bfloat16), value, preferred_element_type=jnp.float32)
            + jnp.dot(end_expos.astype(jnp.bfloat16), end_value, preferred_element_type=jnp.float32)
        )
        stats = (kept_stats(top[:, 0:1], total[:, 0:1]), sent_stats(top[:, 0:1], total[:, 0:1]))
        each = own_queries * sharing
        for slot in range(GROUPS * PAIR):
            start = (slot // PAIR * 2 * heads + head) * each
            at = slice(slot * each, (slot + 1) * each)
            out = outs[slot % PAIR]
            out[start : start + each, :] = numer[at].astype(out.dtype)
            out[start + heads * each : start + (heads + 1) * each, :] = stats[slot % PAIR][at]


def kept_stats(top, total):
    lane = lax.broadcasted_iota(jnp.int32, (top.shape[0], LANES), 1)
    return jnp.where(lane < LANES // 2, top, total)


def sent_stats(top, total):
    terms = []
    for rest, count in ((top, 3), (total, 2)):
        for _ in range(count):
            term = rest.astype(jnp.bfloat16).astype(jnp.float32)
            terms.append(term)
            rest = rest - term
    part = lax.broadcasted_iota(jnp.int32, (top.shape[0], LANES), 1) // 16
    stats = jnp.broadcast_to(terms[-1], part.shape)
    for i, term in enumerate(terms[:-1]):
        stats = jnp.where(part == i, term, stats)
    return stats.astype(jnp.bfloat16)


def merged(kept, others, start, rows):
    half = LANES // 2
    stats = kept[start + rows : start + 2 * rows, :]
    tops, totals = [stats[:, 0:1]], [stats[:, half : half + 1]]
    numers = [kept[start : start + rows, :]]
    for other in others:
        terms = other[start + rows : start + 2 * rows, :].astype(jnp.float32)
        tops.append((terms[:, 0:1] + terms[:, 16:17]) + terms[:, 32:33])
        totals.append(terms[:, 48:49] + terms[:, 64:65])
        numers.append(other[start : start + rows, :].astype(jnp.float32))
    top = functools.reduce(jnp.maximum, tops)
    factors = [jnp.exp(t - top) for t in tops]
    total = sum(f * t for f, t in zip(factors, totals))
    numer = sum(f * n for f, n in zip(factors, numers))
    return numer, top, total


def merge_kernel(kept, other, keep_ref, *send_refs):
    each = keep_ref.shape[0]
    rows = each // 2
    for slot in range(GROUPS):
        numer, top, total = merged(kept, [other], slot * each, rows)
        if slot == 0:
            keep_ref[:rows, :] = numer
            keep_ref[rows:, :] = kept_stats(top, total)
        else:
            send_refs[slot - 1][:rows, :] = numer.astype(jnp.bfloat16)
            send_refs[slot - 1][rows:, :] = sent_stats(top, total)


def last_kernel(kept, *refs):
    others, out_ref = refs[:-1], refs[-1]
    numer, _, total = merged(kept, others, 0, kept.shape[0] // 2)
    result = numer / total
    queries, width = out_ref.shape
    sharing = QUERY_HEADS // KEY_VALUE_HEADS
    heads = width // HEAD_SIZE // sharing
    lines = []
    for i in range(queries):
        starts = [(h * queries + i) * sharing + g for h in range(heads) for g in range(sharing)]
        lines.append(jnp.concatenate([result[s : s + 1] for s in starts], 1))
    out_ref[...] = jnp.concatenate(lines, 0).astype(jnp.bfloat16)


def exchange_plan(
    hidden,
    suffix_hidden,
    norm_gain,
    key_matrix,
    value_matrix,
    key_offset_bias,
    value_offset_bias,
    suffix_query_rows,
    slot_keys,
    slot_values,
    page_slot_table,
    split_page,
):
    n_ctx = GROUPS * PAIR
    ctx = lax.axis_index("ctx").astype(jnp.int32)
    core = lax.axis_index("tp").astype(jnp.int32)
    place = jnp.stack([core, ctx])
    rows, features = hidden.shape
    half_rows = rows // 2
    width = key_matrix.shape[1]
    query_width = suffix_query_rows.shape[1]
    prefix_len = page_slot_table.shape[0] * slot_keys.shape[1]
    smem = pl.BlockSpec(memory_space=pltpu.SMEM)
    vmem = pl.BlockSpec(memory_space=pltpu.VMEM)
    params = pltpu.CompilerParams(vmem_limit_bytes=48 * 1024 * 1024)

    def move(array, target):
        pairs = []
        for c in range(n_ctx):
            for t in range(2):
                to_c, to_t = target(c, t)
                pairs.append((c * 2 + t, to_c * 2 + to_t))
        return lax.ppermute(array, ("ctx", "tp"), pairs)

    def along(shift):
        return lambda c, t: ((c // PAIR ^ shift) * PAIR + c % PAIR, t)

    def beside(c, t):
        return (c ^ 1, t)

    def sibling(c, t):
        return (c, 1 - t)

    hbm = pl.BlockSpec(memory_space=pltpu.HBM)
    pieces = features // GROUPS // LANES
    own_queries = suffix_query_rows.shape[0]
    lines = query_width // LANES
    block_rows = pieces * half_rows + pieces + own_queries * lines
    *blocks, packed, own = pl.pallas_call(
        norm_kernel,
        in_specs=[hbm] * 6,
        out_specs=[hbm] * (GROUPS + 2),
        out_shape=[jax.ShapeDtypeStruct((block_rows, LANES), jnp.bfloat16)] * GROUPS
        + [
            jax.ShapeDtypeStruct((2 * key_matrix.shape[0], width), jnp.bfloat16),
            jax.ShapeDtypeStruct((block_rows, LANES), jnp.bfloat16),
        ],
        scratch_shapes=[
            pltpu.VMEM((half_rows, features), jnp.bfloat16),
            pltpu.VMEM(suffix_hidden.shape, jnp.bfloat16),
            pltpu.VMEM((1, features), jnp.float32),
            pltpu.VMEM(suffix_query_rows.shape, jnp.bfloat16),
            pltpu.VMEM((2 * key_matrix.shape[0], width), jnp.bfloat16),
            pltpu.VMEM((1, features), jnp.float32),
        ]
        + [pltpu.VMEM((block_rows, LANES), jnp.bfloat16)] * GROUPS
        + [
            pltpu.SemaphoreType.DMA((CHUNKS + 6,)),
            pltpu.SemaphoreType.DMA((GROUPS + 1,)),
        ],
        compiler_params=pltpu.CompilerParams(vmem_limit_bytes=60 * 1024 * 1024),
        cost_estimate=pl.CostEstimate(
            flops=4 * half_rows * features, bytes_accessed=4 * half_rows * features, transcendentals=0
        ),
        name="norm_rows",
    )(
        suffix_query_rows,
        hidden,
        suffix_hidden,
        norm_gain.reshape(1, features),
        key_matrix,
        value_matrix,
    )
    far = move(packed, beside)

    mine = {s: move(blocks[s], along(s)) for s in far_first()}
    theirs = {s: move(mine.get(s, blocks[0]), sibling) for s in [0] + far_first()}
    mine[0] = pl.pallas_call(
        fetch_kernel,
        in_specs=[hbm],
        out_specs=vmem,
        out_shape=jax.ShapeDtypeStruct(own.shape, own.dtype),
        scratch_shapes=[pltpu.SemaphoreType.DMA],
        compiler_params=params,
        cost_estimate=pl.CostEstimate(flops=0, bytes_accessed=16 * 1024 * 1024, transcendentals=0),
        name="fetch_own",
    )(own)
    lhs = [part[s] for s in range(GROUPS) for part in (mine, theirs)]

    inverse_freq = rope_base ** (
        -(jnp.arange(HEAD_SIZE // 2, dtype=jnp.float32) * (2.0 / HEAD_SIZE))
    )
    row = jnp.arange(rows + 16, dtype=jnp.int32)
    front_position = ctx * rows + (row + core * half_rows) % rows
    end_position = prefix_len + ctx * 2 + jnp.where(row == rows, core, 1 - core)
    position = jnp.where(row < rows, front_position, end_position)
    angles = position.astype(jnp.float32)[:, None] * inverse_freq[None, :]
    cosine, sine = jnp.cos(angles), jnp.sin(angles)
    cosine = jnp.concatenate([cosine, cosine], 1)
    sine = jnp.concatenate([-sine, sine], 1)

    part_rows = 3 * (width // LANES) * rows + 16
    *partials, own_tiles = pl.pallas_call(
        project_kernel,
        in_specs=[vmem] * (2 * GROUPS + 3),
        out_specs=[vmem] * (GROUPS + 1),
        out_shape=[jax.ShapeDtypeStruct((part_rows, LANES), jnp.bfloat16)] * GROUPS
        + [jax.ShapeDtypeStruct((GROUPS * own_queries * lines, LANES), jnp.bfloat16)],
        scratch_shapes=[pltpu.VMEM((GROUPS * rows + 16, PAIR * features // n_ctx), jnp.bfloat16)],
        compiler_params=params,
        cost_estimate=pl.CostEstimate(flops=2 * GROUPS * rows * 2 * width * features // GROUPS, bytes_accessed=6 * 1024 * 1024, transcendentals=0),
        name="project",
    )(*lhs, key_matrix, value_matrix, far)
    received = [move(partials[s], along(s)) for s in far_first()[1:] + far_first()[:1]]
    beside_tiles = move(own_tiles, beside)

    states = n_ctx * own_queries * query_width // HEAD_SIZE
    state = jax.ShapeDtypeStruct((states, LANES), jnp.float32)
    top, total, numer, queries = pl.pallas_call(
        loaded_kernel,
        in_specs=[smem, smem, smem] + [vmem] * (PAIR + 2),
        out_specs=[vmem] * 4,
        out_shape=[state] * 3 + [jax.ShapeDtypeStruct((states, LANES), jnp.bfloat16)],
        compiler_params=params,
        cost_estimate=pl.CostEstimate(
            flops=4 * states * slot_keys.shape[0] * slot_keys.shape[1] * HEAD_SIZE,
            bytes_accessed=4 * slot_keys.size,
            transcendentals=states * slot_keys.shape[0] * slot_keys.shape[1],
        ),
        name="loaded_attention",
    )(place, page_slot_table, split_page, own_tiles, beside_tiles, slot_keys, slot_values)


    def payloads(size):
        return [jax.ShapeDtypeStruct((size, LANES), kind) for kind in (jnp.float32, jnp.bfloat16)]

    row_shape = jax.ShapeDtypeStruct((rows, width), jnp.bfloat16)
    front_key, front_value, kept, sent = pl.pallas_call(
        front_kernel,
        in_specs=[smem, smem] + [vmem] * (GROUPS + 8),
        out_specs=[vmem] * 4,
        out_shape=[row_shape] * 2 + payloads(states),
        compiler_params=params,
        cost_estimate=pl.CostEstimate(flops=4 * states * rows * HEAD_SIZE, bytes_accessed=2 * 1024 * 1024, transcendentals=states * rows),
        name="front_attention",
    )(
        place,
        split_page,
        partials[0],
        *received,
        key_offset_bias.reshape(1, width),
        value_offset_bias.reshape(1, width),
        cosine,
        sine,
        queries,
        top,
        total,
        numer,
    )
    kept, *sent = pl.pallas_call(
        merge_kernel,
        in_specs=[vmem] * 2,
        out_specs=[vmem] * GROUPS,
        out_shape=payloads(states // GROUPS) + payloads(states // GROUPS)[1:] * (GROUPS - 2),
        compiler_params=params,
        name="merge",
    )(kept, move(sent, beside))
    attended = pl.pallas_call(
        last_kernel,
        in_specs=[vmem] * GROUPS,
        out_specs=vmem,
        out_shape=jax.ShapeDtypeStruct((own_queries, query_width), jnp.bfloat16),
        compiler_params=params,
        name="finish",
    )(kept, *[move(sent[s - 1], along(s)) for s in range(1, GROUPS)])
    return (front_key, front_value, attended)


def solution(mesh):
    per_device = exchange_plan if mesh.shape["ctx"] == GROUPS * PAIR else gathered_plan
    return jax.shard_map(
        per_device,
        mesh=mesh,
        in_specs=(
            P(("req", "ctx"), None),
            P(("req", "ctx"), None),
            P(),
            P("ctx", "tp"),
            P("ctx", "tp"),
            P("tp"),
            P("tp"),
            P(("req", "ctx"), "tp"),
            P(("req", "ctx"), None, "tp"),
            P(("req", "ctx"), None, "tp"),
            P("req"),
            P("req"),
        ),
        out_specs=(P(("req", "ctx"), "tp"), P(("req", "ctx"), "tp"), P(("req", "ctx"), "tp")),
        check_vma=False,
    )
```

```python
import functools
import math

import jax
import jax.numpy as jnp
from jax import lax
from jax.experimental import pallas as pl
from jax.experimental.pallas import tpu as pltpu
from jax.sharding import PartitionSpec as P

QUERY_HEADS = 32
KEY_VALUE_HEADS = 4
HEAD_SIZE = 128


epsilon = 1e-06
rope_base = 1000000.0
masked_score = -1e30


def rms_rows(matrix, norm_gain):
    widened = matrix.astype(jnp.float32)
    inverse = lax.rsqrt(jnp.mean(widened * widened, axis=-1, keepdims=True) + epsilon)
    return (widened * inverse * norm_gain).astype(jnp.bfloat16)


def rotate(key_rows, positions, head_dim):
    row_count = key_rows.shape[0]
    split_heads = key_rows.reshape(row_count, -1, head_dim)
    half_dim = head_dim // 2
    inverse_freq = rope_base ** (-(jnp.arange(half_dim, dtype=jnp.float32) * (2.0 / head_dim)))
    angles = positions.astype(jnp.float32)[:, None] * inverse_freq[None, :]
    cosine = jnp.concatenate([jnp.cos(angles), jnp.cos(angles)], -1)[:, None, :]
    sine = jnp.concatenate([jnp.sin(angles), jnp.sin(angles)], -1)[:, None, :]
    turned = jnp.concatenate([-split_heads[..., half_dim:], split_heads[..., :half_dim]], -1)
    return (split_heads * cosine + turned * sine).reshape(row_count, -1)


def gathered_plan(
    hidden,
    suffix_hidden,
    norm_gain,
    key_matrix,
    value_matrix,
    key_offset_bias,
    value_offset_bias,
    suffix_query_rows,
    slot_keys,
    slot_values,
    page_slot_table,
    split_page,
):
    ctx_index = lax.axis_index("ctx")
    queries = lax.all_gather(suffix_query_rows, "ctx", axis=0, tiled=True)
    front_rows = hidden.shape[0]
    suffix_rows = suffix_hidden.shape[0]
    page_size = slot_keys.shape[1]
    slot_count = slot_keys.shape[0]
    total_pages = page_slot_table.shape[0]
    prefix_len = total_pages * page_size
    normed = rms_rows(jnp.concatenate([hidden, suffix_hidden], 0), norm_gain)
    col_width = key_matrix.shape[1]

    def accumulate(block_rows):
        return jnp.dot(normed, block_rows, preferred_element_type=jnp.float32)

    key_acc = accumulate(lax.all_gather(key_matrix, "ctx", axis=0, tiled=True))
    value_acc = accumulate(lax.all_gather(value_matrix, "ctx", axis=0, tiled=True))
    front_pos = ctx_index * front_rows + jnp.arange(front_rows, dtype=jnp.int32)
    suffix_pos = prefix_len + ctx_index * suffix_rows + jnp.arange(suffix_rows, dtype=jnp.int32)
    new_keys = rotate(
        key_acc + key_offset_bias, jnp.concatenate([front_pos, suffix_pos], 0), HEAD_SIZE
    ).astype(jnp.bfloat16)
    new_values = (value_acc + value_offset_bias).astype(jnp.bfloat16)
    cut_pos = split_page[0] * page_size
    global_slot = ctx_index * slot_count + jnp.arange(slot_count, dtype=jnp.int32)
    page_index = jnp.arange(total_pages, dtype=jnp.int32)
    slot_hits = (page_slot_table[None, :] == global_slot[:, None]) & (
        page_index[None, :] >= split_page[0]
    )
    slot_live = jnp.max(slot_hits.astype(jnp.int32), axis=1) > 0
    every_key = jnp.concatenate(
        [new_keys[:front_rows], slot_keys.reshape(-1, col_width), new_keys[front_rows:]], 0
    )
    every_value = jnp.concatenate(
        [new_values[:front_rows], slot_values.reshape(-1, col_width), new_values[front_rows:]], 0
    )
    query_count = queries.shape[0]
    query_pos = prefix_len + jnp.arange(query_count, dtype=jnp.int32)
    prefix_seen = jnp.concatenate([front_pos < cut_pos, jnp.repeat(slot_live, page_size)], 0)
    suffix_seen = suffix_pos[None, :] <= query_pos[:, None]
    visible = jnp.concatenate(
        [jnp.broadcast_to(prefix_seen[None, :], (query_count, prefix_seen.shape[0])), suffix_seen],
        1,
    )
    visible_wide = visible[:, None, :]
    sharing_count = QUERY_HEADS // KEY_VALUE_HEADS
    local_heads = col_width // HEAD_SIZE
    grouped_heads = queries.reshape(query_count, local_heads, sharing_count, HEAD_SIZE)
    top_list = []
    total_list = []
    numer_list = []
    for current_head in range(local_heads):
        head_keys = every_key[:, current_head * HEAD_SIZE : (current_head + 1) * HEAD_SIZE]
        head_values = every_value[:, current_head * HEAD_SIZE : (current_head + 1) * HEAD_SIZE]
        scores = jnp.einsum(
            "qgd,ld->qgl",
            grouped_heads[:, current_head],
            head_keys,
            preferred_element_type=jnp.float32,
        ) * (1.0 / math.sqrt(HEAD_SIZE))
        scores = jnp.where(visible_wide, scores, masked_score)
        row_top = jnp.max(scores, axis=-1)
        expos = jnp.where(visible_wide, jnp.exp(scores - row_top[..., None]), 0.0)
        total_list.append(jnp.sum(expos, axis=-1))
        top_list.append(row_top)
        numer_list.append(
            jnp.einsum(
                "qgl,ld->qgd",
                expos.astype(jnp.bfloat16),
                head_values,
                preferred_element_type=jnp.float32,
            )
        )
    row_top = jnp.stack(top_list, 1)
    weight_total = jnp.stack(total_list, 1)
    numer = jnp.stack(numer_list, 1)
    global_top = lax.pmax(row_top, "ctx")
    factor = jnp.exp(row_top - global_top)
    own_total, own_numer = (
        lax.psum_scatter(
            (weight_total * factor).reshape(query_count, -1), "ctx", scatter_dimension=0, tiled=True
        ),
        lax.psum_scatter(
            (numer * factor[..., None]).reshape(query_count, -1),
            "ctx",
            scatter_dimension=0,
            tiled=True,
        ),
    )
    own_total = own_total.reshape(suffix_rows, local_heads, sharing_count)
    own_numer = own_numer.reshape(suffix_rows, local_heads, sharing_count, HEAD_SIZE)
    attended = (own_numer / own_total[..., None]).reshape(suffix_rows, -1).astype(jnp.bfloat16)
    return (new_keys[:front_rows], new_values[:front_rows], attended)

GROUPS = 4
PAIR = 2
LANES = 128
SCALE = 1.0 / math.sqrt(HEAD_SIZE)


def row_scale(values):
    mean = jnp.sum(values * values, axis=-1, keepdims=True) * (1.0 / values.shape[-1])
    return lax.rsqrt(mean + epsilon)


CHUNKS = 4


def far_first():
    return list(range(GROUPS - 1, 0, -1))


def norm_kernel(query_any, hidden_any, suffix_any, gain_any, key_any, value_any, *rest):
    blocks_any, packed_any, own_any = rest[:GROUPS], rest[GROUPS], rest[GROUPS + 1]
    hidden_ref, suffix_ref, gain_ref, query_ref, packed_ref, tail_ref = rest[GROUPS + 2 : GROUPS + 8]
    outs, (sems, out_sems) = rest[GROUPS + 8 : -2], rest[-2:]
    depth = key_any.shape[0]
    packing = [
        pltpu.make_async_copy(key_any, packed_ref.at[:depth], sems.at[CHUNKS + 3]),
        pltpu.make_async_copy(value_any, packed_ref.at[depth:], sems.at[CHUNKS + 4]),
    ]
    unpacking = pltpu.make_async_copy(packed_ref, packed_any, sems.at[CHUNKS + 5])
    core, ctx = lax.axis_index("tp"), lax.axis_index("ctx")
    z, x = ctx // PAIR, ctx % PAIR
    half_rows, features = hidden_ref.shape
    rows = half_rows // CHUNKS
    block = features // (GROUPS * PAIR)
    per_block = block // LANES
    pieces = PAIR * per_block
    copies = [
        pltpu.make_async_copy(gain_any, gain_ref, sems.at[CHUNKS]),
        pltpu.make_async_copy(suffix_any, suffix_ref, sems.at[CHUNKS + 1]),
        pltpu.make_async_copy(query_any, query_ref, sems.at[CHUNKS + 2]),
    ]
    for i in range(CHUNKS):
        start = pl.multiple_of(core * half_rows + i * rows, rows)
        copies.append(
            pltpu.make_async_copy(
                hidden_any.at[pl.ds(start, rows)], hidden_ref.at[i * rows : (i + 1) * rows], sems.at[i]
            )
        )
    for copy in copies + packing:
        copy.start()

    def offset(shift, side, j):
        owner = (z ^ shift) * PAIR + (x ^ side)
        return pl.multiple_of(owner * block + j * LANES, LANES)

    copies[0].wait()
    copies[1].wait()
    copies[2].wait()
    query_rows = query_ref[...].astype(jnp.float32)
    lines = query_rows.shape[1] // LANES
    for r in range(query_rows.shape[0]):
        tile = [query_rows[r : r + 1, j * LANES : (j + 1) * LANES] for j in range(lines)]
        tile = jnp.concatenate(tile, 0).astype(jnp.bfloat16)
        start = pieces * half_rows + pieces + r * lines
        for out in outs:
            out[start : start + lines, :] = tile

    both = suffix_ref[...].astype(jnp.float32)
    normed = both * row_scale(both) * gain_ref[...]
    tail_ref[...] = jnp.where(core == 0, normed[0:1], normed[1:2])
    for shift in range(GROUPS):
        ends = [
            tail_ref[:, pl.ds(offset(shift, side, j), LANES)]
            for side in range(PAIR)
            for j in range(per_block)
        ]
        start = pieces * half_rows
        outs[shift][start : start + pieces, :] = jnp.concatenate(ends, 0).astype(jnp.bfloat16)
    inverses = []
    for i in range(CHUNKS):
        copies[3 + i].wait()
        inverses.append(row_scale(hidden_ref[i * rows : (i + 1) * rows, :].astype(jnp.float32)))
    for copy in packing:
        copy.wait()
    unpacking.start()
    leaving = []
    for shift in far_first() + [0]:
        for side in range(PAIR):
            for j in range(per_block):
                columns = pl.ds(offset(shift, side, j), LANES)
                for i in range(CHUNKS):
                    piece = hidden_ref[i * rows : (i + 1) * rows, columns].astype(jnp.float32)
                    piece = piece * inverses[i] * gain_ref[:, columns]
                    start = (side * per_block + j) * half_rows + i * rows
                    outs[shift][start : start + rows, :] = piece.astype(jnp.bfloat16)
        leaving.append(pltpu.make_async_copy(outs[shift], blocks_any[shift], out_sems.at[shift]))
        leaving[-1].start()
    leaving.append(pltpu.make_async_copy(outs[0], own_any, out_sems.at[GROUPS]))
    leaving[-1].start()
    for copy in leaving:
        copy.wait()
    unpacking.wait()


def fetch_kernel(from_any, to_ref, sem):
    copy = pltpu.make_async_copy(from_any, to_ref, sem)
    copy.start()
    copy.wait()


def project_kernel(*refs):
    blocks = refs[: 2 * GROUPS]
    near_key, near_value, far = refs[2 * GROUPS : 2 * GROUPS + 3]
    outs = refs[2 * GROUPS + 3 : 3 * GROUPS + 3]
    query_ref, lhs_ref = refs[3 * GROUPS + 3 :]
    depth = near_key.shape[0]
    pieces = 2 * depth // LANES
    half_rows = (lhs_ref.shape[0] - 16) // (2 * GROUPS)
    rows = 2 * half_rows
    tails = [None] * len(blocks)
    for i, block in enumerate(blocks):
        for j in range(pieces):
            lhs_ref[i * half_rows : (i + 1) * half_rows, j * LANES : (j + 1) * LANES] = block[
                j * half_rows : (j + 1) * half_rows, :
            ]
        tail = block[pieces * half_rows : pieces * half_rows + pieces, :].astype(jnp.float32)
        tails[i] = jnp.concatenate([tail[j : j + 1] for j in range(pieces)], 1)
    tails.append(jnp.zeros((16 - len(tails), 2 * depth), jnp.float32))
    lines = query_ref.shape[0] // GROUPS
    for place, group in enumerate([0] + far_first()):
        block = blocks[2 * place]
        query_ref[group * lines : (group + 1) * lines, :] = block[block.shape[0] - lines :, :]
    total = GROUPS * rows
    lhs_ref[total : total + 16, :] = jnp.concatenate(tails, 0).astype(jnp.bfloat16)

    def product(near, at):
        return jnp.dot(
            lhs_ref[:, :depth], near[...], preferred_element_type=jnp.float32
        ) + jnp.dot(lhs_ref[:, depth:], far[at, :], preferred_element_type=jnp.float32)

    keys = product(near_key, slice(0, depth))
    values = product(near_value, slice(depth, 2 * depth))
    high = keys.astype(jnp.bfloat16).astype(jnp.float32)
    low = keys - high
    columns = []
    for array in (high, low, values):
        for j in range(array.shape[1] // LANES):
            columns.append(array[:, j * LANES : (j + 1) * LANES])
    for group in range(GROUPS):
        for t, column in enumerate(columns):
            outs[group][t * rows : (t + 1) * rows, :] = column[
                group * rows : (group + 1) * rows
            ].astype(jnp.bfloat16)
        ends = [c[total + 2 * group : total + 2 * group + 2] for c in columns]
        ends.append(jnp.zeros((16 - 2 * len(columns), LANES), jnp.float32))
        outs[group][len(columns) * rows :, :] = jnp.concatenate(ends, 0).astype(jnp.bfloat16)


def head_queries(parts, head, width):
    sharing = QUERY_HEADS // KEY_VALUE_HEADS
    lines = sharing * width // HEAD_SIZE
    each = parts[0].shape[0] // GROUPS
    found = []
    for group in range(GROUPS):
        for part in parts:
            tiles = part[group * each : (group + 1) * each, :].astype(jnp.float32)
            for start in range(head * sharing, each, lines):
                found.append(tiles[start : start + sharing])
    return jnp.concatenate(found, 0).astype(jnp.bfloat16)


def times_transposed(a, b):
    return lax.dot_general(a, b, (((1,), (1,)), ((), ())), preferred_element_type=jnp.float32)


def loaded_kernel(place_ref, table_ref, split_ref, *refs):
    parts = refs[:PAIR]
    key_ref, value_ref, top_ref, total_ref, numer_ref, query_ref = refs[PAIR:]
    ctx = place_ref[1]
    slots, page, width = key_ref.shape
    heads = width // HEAD_SIZE
    split = split_ref[0]
    live = []
    for s in range(slots):
        hit = jnp.int32(0)
        for p in range(table_ref.shape[0]):
            hit = hit | ((table_ref[p] == ctx * slots + s) & (p >= split)).astype(jnp.int32)
        live.append(hit)
    for head in range(heads):
        columns = slice(head * HEAD_SIZE, (head + 1) * HEAD_SIZE)
        queries = head_queries(parts, head, width)
        count = queries.shape[0]
        query_ref[head * count : (head + 1) * count, :] = queries
        scores = [
            jnp.where(live[s] > 0, times_transposed(queries, key_ref[s, :, columns]) * SCALE, masked_score)
            for s in range(slots)
        ]
        top = scores[0].max(-1, keepdims=True)
        for s in range(1, slots):
            top = jnp.maximum(top, scores[s].max(-1, keepdims=True))
        total = jnp.zeros((count, 1), jnp.float32)
        numer = jnp.zeros((count, HEAD_SIZE), jnp.float32)
        for s in range(slots):
            expos = jnp.where(live[s] > 0, jnp.exp(scores[s] - top), 0.0)
            total += expos.sum(-1, keepdims=True)
            numer += jnp.dot(
                expos.astype(jnp.bfloat16), value_ref[s, :, columns], preferred_element_type=jnp.float32
            )
        rows = slice(head * count, (head + 1) * count)
        top_ref[rows, :] = jnp.broadcast_to(top, (count, LANES))
        total_ref[rows, :] = jnp.broadcast_to(total, (count, LANES))
        numer_ref[rows, :] = numer


def front_kernel(
    place_ref, split_ref, own, *refs
):
    received = refs[: GROUPS - 1]
    (key_bias, value_bias, cosine_ref, sine_ref, query_ref, top_ref, total_ref, numer_ref) = refs[
        GROUPS - 1 : GROUPS + 7
    ]
    front_key, front_value = refs[GROUPS + 7 : GROUPS + 9]
    outs = refs[GROUPS + 9 :]
    core, ctx = place_ref[0], place_ref[1]
    rows, width = front_key.shape
    half_rows = rows // 2
    heads = width // HEAD_SIZE
    sharing = QUERY_HEADS // KEY_VALUE_HEADS
    count = query_ref.shape[0] // heads
    own_queries = count // sharing // (GROUPS * PAIR)
    visible = ctx < split_ref[0]

    def summed(start, size):
        value = own[start : start + size, :].astype(jnp.float32)
        for ref in received:
            value += ref[start : start + size, :].astype(jnp.float32)
        return value

    ends = summed(3 * heads * rows, 16)
    row_query = lax.broadcasted_iota(jnp.int32, (count, 16), 0) // sharing
    query_position = (ctx ^ (row_query // own_queries)) * own_queries + row_query % own_queries
    end_column = lax.broadcasted_iota(jnp.int32, (count, 16), 1)
    end_position = ctx * 2 + jnp.where(end_column == 0, core, 1 - core)
    end_seen = (end_column < 2) & (end_position <= query_position)
    pad = jnp.zeros((14, HEAD_SIZE), jnp.float32)
    for head in range(heads):
        columns = slice(head * HEAD_SIZE, (head + 1) * HEAD_SIZE)
        raw = summed(head * rows, rows) + summed((heads + head) * rows, rows)
        value = (summed((2 * heads + head) * rows, rows) + value_bias[:, columns]).astype(jnp.bfloat16)
        end_raw = ends[2 * head : 2 * head + 2] + ends[2 * (heads + head) : 2 * (heads + head) + 2]
        end_value = ends[2 * (2 * heads + head) : 2 * (2 * heads + head) + 2] + value_bias[:, columns]
        end_raw = jnp.concatenate([end_raw + key_bias[:, columns], pad], 0)
        end_value = jnp.concatenate([end_value, pad], 0).astype(jnp.bfloat16)
        raw = raw + key_bias[:, columns]

        def rotated(k, part):
            turned = pltpu.roll(k, HEAD_SIZE // 2, 1)
            return (k * cosine_ref[part, :] + turned * sine_ref[part, :]).astype(jnp.bfloat16)

        key = rotated(raw, slice(0, rows))
        end_key = rotated(end_raw, slice(rows, rows + 16))
        for half in range(2):
            to = pl.ds(pl.multiple_of(lax.rem(core + half, 2) * half_rows, half_rows), half_rows)
            front_key[to, columns] = key[half * half_rows : (half + 1) * half_rows]
            front_value[to, columns] = value[half * half_rows : (half + 1) * half_rows]
        part = slice(head * count, (head + 1) * count)
        queries = query_ref[part, :]
        scores = jnp.where(visible, times_transposed(queries, key) * SCALE, masked_score)
        end_scores = jnp.where(end_seen, times_transposed(queries, end_key) * SCALE, masked_score)
        old_top = top_ref[part, :]
        top = jnp.maximum(scores.max(-1, keepdims=True), end_scores.max(-1, keepdims=True))
        top = jnp.maximum(old_top, top)
        factor = jnp.exp(old_top - top)
        expos = jnp.where(visible, jnp.exp(scores - top), 0.0)
        end_expos = jnp.where(end_seen, jnp.exp(end_scores - top[:, :16]), 0.0)
        total = total_ref[part, :] * factor + (
            expos.sum(-1, keepdims=True) + end_expos.sum(-1, keepdims=True)
        )
        numer = (
            numer_ref[part, :] * factor
            + jnp.dot(expos.astype(jnp.bfloat16), value, preferred_element_type=jnp.float32)
            + jnp.dot(end_expos.astype(jnp.bfloat16), end_value, preferred_element_type=jnp.float32)
        )
        stats = (kept_stats(top[:, 0:1], total[:, 0:1]), sent_stats(top[:, 0:1], total[:, 0:1]))
        each = own_queries * sharing
        for slot in range(GROUPS * PAIR):
            start = (slot // PAIR * 2 * heads + head) * each
            at = slice(slot * each, (slot + 1) * each)
            out = outs[slot % PAIR]
            out[start : start + each, :] = numer[at].astype(out.dtype)
            out[start + heads * each : start + (heads + 1) * each, :] = stats[slot % PAIR][at]


def kept_stats(top, total):
    lane = lax.broadcasted_iota(jnp.int32, (top.shape[0], LANES), 1)
    return jnp.where(lane < LANES // 2, top, total)


def sent_stats(top, total):
    terms = []
    for rest, count in ((top, 3), (total, 2)):
        for _ in range(count):
            term = rest.astype(jnp.bfloat16).astype(jnp.float32)
            terms.append(term)
            rest = rest - term
    part = lax.broadcasted_iota(jnp.int32, (top.shape[0], LANES), 1) // 16
    stats = jnp.broadcast_to(terms[-1], part.shape)
    for i, term in enumerate(terms[:-1]):
        stats = jnp.where(part == i, term, stats)
    return stats.astype(jnp.bfloat16)


def merged(kept, others, start, rows):
    half = LANES // 2
    stats = kept[start + rows : start + 2 * rows, :]
    tops, totals = [stats[:, 0:1]], [stats[:, half : half + 1]]
    numers = [kept[start : start + rows, :]]
    for other in others:
        terms = other[start + rows : start + 2 * rows, :].astype(jnp.float32)
        tops.append((terms[:, 0:1] + terms[:, 16:17]) + terms[:, 32:33])
        totals.append(terms[:, 48:49] + terms[:, 64:65])
        numers.append(other[start : start + rows, :].astype(jnp.float32))
    top = functools.reduce(jnp.maximum, tops)
    factors = [jnp.exp(t - top) for t in tops]
    total = sum(f * t for f, t in zip(factors, totals))
    numer = sum(f * n for f, n in zip(factors, numers))
    return numer, top, total


def merge_kernel(kept, other, keep_ref, *send_refs):
    each = keep_ref.shape[0]
    rows = each // 2
    for slot in range(GROUPS):
        numer, top, total = merged(kept, [other], slot * each, rows)
        if slot == 0:
            keep_ref[:rows, :] = numer
            keep_ref[rows:, :] = kept_stats(top, total)
        else:
            send_refs[slot - 1][:rows, :] = numer.astype(jnp.bfloat16)
            send_refs[slot - 1][rows:, :] = sent_stats(top, total)


def last_kernel(kept, *refs):
    others, out_ref = refs[:-1], refs[-1]
    numer, _, total = merged(kept, others, 0, kept.shape[0] // 2)
    result = numer / total
    queries, width = out_ref.shape
    sharing = QUERY_HEADS // KEY_VALUE_HEADS
    heads = width // HEAD_SIZE // sharing
    lines = []
    for i in range(queries):
        starts = [(h * queries + i) * sharing + g for h in range(heads) for g in range(sharing)]
        lines.append(jnp.concatenate([result[s : s + 1] for s in starts], 1))
    out_ref[...] = jnp.concatenate(lines, 0).astype(jnp.bfloat16)


def exchange_plan(
    hidden,
    suffix_hidden,
    norm_gain,
    key_matrix,
    value_matrix,
    key_offset_bias,
    value_offset_bias,
    suffix_query_rows,
    slot_keys,
    slot_values,
    page_slot_table,
    split_page,
):
    n_ctx = GROUPS * PAIR
    ctx = lax.axis_index("ctx").astype(jnp.int32)
    core = lax.axis_index("tp").astype(jnp.int32)
    place = jnp.stack([core, ctx])
    rows, features = hidden.shape
    half_rows = rows // 2
    width = key_matrix.shape[1]
    query_width = suffix_query_rows.shape[1]
    prefix_len = page_slot_table.shape[0] * slot_keys.shape[1]
    smem = pl.BlockSpec(memory_space=pltpu.SMEM)
    vmem = pl.BlockSpec(memory_space=pltpu.VMEM)
    params = pltpu.CompilerParams(vmem_limit_bytes=48 * 1024 * 1024)

    def move(array, target):
        pairs = []
        for c in range(n_ctx):
            for t in range(2):
                to_c, to_t = target(c, t)
                pairs.append((c * 2 + t, to_c * 2 + to_t))
        return lax.ppermute(array, ("ctx", "tp"), pairs)

    def along(shift):
        return lambda c, t: ((c // PAIR ^ shift) * PAIR + c % PAIR, t)

    def beside(c, t):
        return (c ^ 1, t)

    def sibling(c, t):
        return (c, 1 - t)

    hbm = pl.BlockSpec(memory_space=pltpu.HBM)
    pieces = features // GROUPS // LANES
    own_queries = suffix_query_rows.shape[0]
    lines = query_width // LANES
    block_rows = pieces * half_rows + pieces + own_queries * lines
    *blocks, packed, own = pl.pallas_call(
        norm_kernel,
        in_specs=[hbm] * 6,
        out_specs=[hbm] * (GROUPS + 2),
        out_shape=[jax.ShapeDtypeStruct((block_rows, LANES), jnp.bfloat16)] * GROUPS
        + [
            jax.ShapeDtypeStruct((2 * key_matrix.shape[0], width), jnp.bfloat16),
            jax.ShapeDtypeStruct((block_rows, LANES), jnp.bfloat16),
        ],
        scratch_shapes=[
            pltpu.VMEM((half_rows, features), jnp.bfloat16),
            pltpu.VMEM(suffix_hidden.shape, jnp.bfloat16),
            pltpu.VMEM((1, features), jnp.float32),
            pltpu.VMEM(suffix_query_rows.shape, jnp.bfloat16),
            pltpu.VMEM((2 * key_matrix.shape[0], width), jnp.bfloat16),
            pltpu.VMEM((1, features), jnp.float32),
        ]
        + [pltpu.VMEM((block_rows, LANES), jnp.bfloat16)] * GROUPS
        + [
            pltpu.SemaphoreType.DMA((CHUNKS + 6,)),
            pltpu.SemaphoreType.DMA((GROUPS + 1,)),
        ],
        compiler_params=pltpu.CompilerParams(vmem_limit_bytes=60 * 1024 * 1024),
        cost_estimate=pl.CostEstimate(
            flops=4 * half_rows * features, bytes_accessed=4 * half_rows * features, transcendentals=0
        ),
        name="norm_rows",
    )(
        suffix_query_rows,
        hidden,
        suffix_hidden,
        norm_gain.reshape(1, features),
        key_matrix,
        value_matrix,
    )
    far = move(packed, beside)

    mine = {s: move(blocks[s], along(s)) for s in far_first()}
    inverse_freq = rope_base ** (
        -(jnp.arange(HEAD_SIZE // 2, dtype=jnp.float32) * (2.0 / HEAD_SIZE))
    )
    row = jnp.arange(rows + 16, dtype=jnp.int32)
    front_position = ctx * rows + (row + core * half_rows) % rows
    end_position = prefix_len + ctx * 2 + jnp.where(row == rows, core, 1 - core)
    position = jnp.where(row < rows, front_position, end_position)
    angles = position.astype(jnp.float32)[:, None] * inverse_freq[None, :]
    cosine, sine = jnp.cos(angles), jnp.sin(angles)
    cosine = jnp.concatenate([cosine, cosine], 1)
    sine = jnp.concatenate([-sine, sine], 1)

    mine[0] = pl.pallas_call(
        fetch_kernel,
        in_specs=[hbm],
        out_specs=vmem,
        out_shape=jax.ShapeDtypeStruct(own.shape, own.dtype),
        scratch_shapes=[pltpu.SemaphoreType.DMA],
        compiler_params=params,
        cost_estimate=pl.CostEstimate(flops=0, bytes_accessed=16 * 1024 * 1024, transcendentals=0),
        name="fetch_own",
    )(own)
    first = far_first()[0]
    mine[first], mine[0], cosine, sine = lax.optimization_barrier(
        (mine[first], mine[0], cosine, sine)
    )
    theirs = {s: move(blocks[0] if s == 0 else mine[s], sibling) for s in [0] + far_first()}
    lhs = [part[s] for s in [0] + far_first() for part in (mine, theirs)]

    part_rows = 3 * (width // LANES) * rows + 16
    *partials, own_tiles = pl.pallas_call(
        project_kernel,
        in_specs=[vmem] * (2 * GROUPS + 3),
        out_specs=[vmem] * (GROUPS + 1),
        out_shape=[jax.ShapeDtypeStruct((part_rows, LANES), jnp.bfloat16)] * GROUPS
        + [jax.ShapeDtypeStruct((GROUPS * own_queries * lines, LANES), jnp.bfloat16)],
        scratch_shapes=[pltpu.VMEM((GROUPS * rows + 16, PAIR * features // n_ctx), jnp.bfloat16)],
        compiler_params=params,
        cost_estimate=pl.CostEstimate(flops=2 * GROUPS * rows * 2 * width * features // GROUPS, bytes_accessed=6 * 1024 * 1024, transcendentals=0),
        name="project",
    )(*lhs, key_matrix, value_matrix, far)
    received = [move(partials[1 + i], along(s)) for i, s in enumerate(far_first())]
    beside_tiles = move(own_tiles, beside)

    states = n_ctx * own_queries * query_width // HEAD_SIZE
    state = jax.ShapeDtypeStruct((states, LANES), jnp.float32)
    top, total, numer, queries = pl.pallas_call(
        loaded_kernel,
        in_specs=[smem, smem, smem] + [vmem] * (PAIR + 2),
        out_specs=[vmem] * 4,
        out_shape=[state] * 3 + [jax.ShapeDtypeStruct((states, LANES), jnp.bfloat16)],
        compiler_params=params,
        cost_estimate=pl.CostEstimate(
            flops=4 * states * slot_keys.shape[0] * slot_keys.shape[1] * HEAD_SIZE,
            bytes_accessed=4 * slot_keys.size,
            transcendentals=states * slot_keys.shape[0] * slot_keys.shape[1],
        ),
        name="loaded_attention",
    )(place, page_slot_table, split_page, own_tiles, beside_tiles, slot_keys, slot_values)


    def payloads(size):
        return [jax.ShapeDtypeStruct((size, LANES), kind) for kind in (jnp.float32, jnp.bfloat16)]

    row_shape = jax.ShapeDtypeStruct((rows, width), jnp.bfloat16)
    front_key, front_value, kept, sent = pl.pallas_call(
        front_kernel,
        in_specs=[smem, smem] + [vmem] * (GROUPS + 8),
        out_specs=[vmem] * 4,
        out_shape=[row_shape] * 2 + payloads(states),
        compiler_params=params,
        cost_estimate=pl.CostEstimate(flops=4 * states * rows * HEAD_SIZE, bytes_accessed=2 * 1024 * 1024, transcendentals=states * rows),
        name="front_attention",
    )(
        place,
        split_page,
        partials[0],
        *received,
        key_offset_bias.reshape(1, width),
        value_offset_bias.reshape(1, width),
        cosine,
        sine,
        queries,
        top,
        total,
        numer,
    )
    kept, *sent = pl.pallas_call(
        merge_kernel,
        in_specs=[vmem] * 2,
        out_specs=[vmem] * GROUPS,
        out_shape=payloads(states // GROUPS) + payloads(states // GROUPS)[1:] * (GROUPS - 2),
        compiler_params=params,
        name="merge",
    )(kept, move(sent, beside))
    attended = pl.pallas_call(
        last_kernel,
        in_specs=[vmem] * GROUPS,
        out_specs=vmem,
        out_shape=jax.ShapeDtypeStruct((own_queries, query_width), jnp.bfloat16),
        compiler_params=params,
        name="finish",
    )(kept, *[move(sent[s - 1], along(s)) for s in far_first()])
    return (front_key, front_value, attended)


def solution(mesh):
    per_device = exchange_plan if mesh.shape["ctx"] == GROUPS * PAIR else gathered_plan
    return jax.shard_map(
        per_device,
        mesh=mesh,
        in_specs=(
            P(("req", "ctx"), None),
            P(("req", "ctx"), None),
            P(),
            P("ctx", "tp"),
            P("ctx", "tp"),
            P("tp"),
            P("tp"),
            P(("req", "ctx"), "tp"),
            P(("req", "ctx"), None, "tp"),
            P(("req", "ctx"), None, "tp"),
            P("req"),
            P("req"),
        ),
        out_specs=(P(("req", "ctx"), "tp"), P(("req", "ctx"), "tp"), P(("req", "ctx"), "tp")),
        check_vma=False,
    )
```

```python
import functools
import math

import jax
import jax.numpy as jnp
from jax import lax
from jax.experimental import pallas as pl
from jax.experimental.pallas import tpu as pltpu
from jax.sharding import PartitionSpec as P

QUERY_HEADS = 32
KEY_VALUE_HEADS = 4
HEAD_SIZE = 128


epsilon = 1e-06
rope_base = 1000000.0
masked_score = -1e30


def rms_rows(matrix, norm_gain):
    widened = matrix.astype(jnp.float32)
    inverse = lax.rsqrt(jnp.mean(widened * widened, axis=-1, keepdims=True) + epsilon)
    return (widened * inverse * norm_gain).astype(jnp.bfloat16)


def rotate(key_rows, positions, head_dim):
    row_count = key_rows.shape[0]
    split_heads = key_rows.reshape(row_count, -1, head_dim)
    half_dim = head_dim // 2
    inverse_freq = rope_base ** (-(jnp.arange(half_dim, dtype=jnp.float32) * (2.0 / head_dim)))
    angles = positions.astype(jnp.float32)[:, None] * inverse_freq[None, :]
    cosine = jnp.concatenate([jnp.cos(angles), jnp.cos(angles)], -1)[:, None, :]
    sine = jnp.concatenate([jnp.sin(angles), jnp.sin(angles)], -1)[:, None, :]
    turned = jnp.concatenate([-split_heads[..., half_dim:], split_heads[..., :half_dim]], -1)
    return (split_heads * cosine + turned * sine).reshape(row_count, -1)


def gathered_plan(
    hidden,
    suffix_hidden,
    norm_gain,
    key_matrix,
    value_matrix,
    key_offset_bias,
    value_offset_bias,
    suffix_query_rows,
    slot_keys,
    slot_values,
    page_slot_table,
    split_page,
):
    ctx_index = lax.axis_index("ctx")
    queries = lax.all_gather(suffix_query_rows, "ctx", axis=0, tiled=True)
    front_rows = hidden.shape[0]
    suffix_rows = suffix_hidden.shape[0]
    page_size = slot_keys.shape[1]
    slot_count = slot_keys.shape[0]
    total_pages = page_slot_table.shape[0]
    prefix_len = total_pages * page_size
    normed = rms_rows(jnp.concatenate([hidden, suffix_hidden], 0), norm_gain)
    col_width = key_matrix.shape[1]

    def accumulate(block_rows):
        return jnp.dot(normed, block_rows, preferred_element_type=jnp.float32)

    key_acc = accumulate(lax.all_gather(key_matrix, "ctx", axis=0, tiled=True))
    value_acc = accumulate(lax.all_gather(value_matrix, "ctx", axis=0, tiled=True))
    front_pos = ctx_index * front_rows + jnp.arange(front_rows, dtype=jnp.int32)
    suffix_pos = prefix_len + ctx_index * suffix_rows + jnp.arange(suffix_rows, dtype=jnp.int32)
    new_keys = rotate(
        key_acc + key_offset_bias, jnp.concatenate([front_pos, suffix_pos], 0), HEAD_SIZE
    ).astype(jnp.bfloat16)
    new_values = (value_acc + value_offset_bias).astype(jnp.bfloat16)
    cut_pos = split_page[0] * page_size
    global_slot = ctx_index * slot_count + jnp.arange(slot_count, dtype=jnp.int32)
    page_index = jnp.arange(total_pages, dtype=jnp.int32)
    slot_hits = (page_slot_table[None, :] == global_slot[:, None]) & (
        page_index[None, :] >= split_page[0]
    )
    slot_live = jnp.max(slot_hits.astype(jnp.int32), axis=1) > 0
    every_key = jnp.concatenate(
        [new_keys[:front_rows], slot_keys.reshape(-1, col_width), new_keys[front_rows:]], 0
    )
    every_value = jnp.concatenate(
        [new_values[:front_rows], slot_values.reshape(-1, col_width), new_values[front_rows:]], 0
    )
    query_count = queries.shape[0]
    query_pos = prefix_len + jnp.arange(query_count, dtype=jnp.int32)
    prefix_seen = jnp.concatenate([front_pos < cut_pos, jnp.repeat(slot_live, page_size)], 0)
    suffix_seen = suffix_pos[None, :] <= query_pos[:, None]
    visible = jnp.concatenate(
        [jnp.broadcast_to(prefix_seen[None, :], (query_count, prefix_seen.shape[0])), suffix_seen],
        1,
    )
    visible_wide = visible[:, None, :]
    sharing_count = QUERY_HEADS // KEY_VALUE_HEADS
    local_heads = col_width // HEAD_SIZE
    grouped_heads = queries.reshape(query_count, local_heads, sharing_count, HEAD_SIZE)
    top_list = []
    total_list = []
    numer_list = []
    for current_head in range(local_heads):
        head_keys = every_key[:, current_head * HEAD_SIZE : (current_head + 1) * HEAD_SIZE]
        head_values = every_value[:, current_head * HEAD_SIZE : (current_head + 1) * HEAD_SIZE]
        scores = jnp.einsum(
            "qgd,ld->qgl",
            grouped_heads[:, current_head],
            head_keys,
            preferred_element_type=jnp.float32,
        ) * (1.0 / math.sqrt(HEAD_SIZE))
        scores = jnp.where(visible_wide, scores, masked_score)
        row_top = jnp.max(scores, axis=-1)
        expos = jnp.where(visible_wide, jnp.exp(scores - row_top[..., None]), 0.0)
        total_list.append(jnp.sum(expos, axis=-1))
        top_list.append(row_top)
        numer_list.append(
            jnp.einsum(
                "qgl,ld->qgd",
                expos.astype(jnp.bfloat16),
                head_values,
                preferred_element_type=jnp.float32,
            )
        )
    row_top = jnp.stack(top_list, 1)
    weight_total = jnp.stack(total_list, 1)
    numer = jnp.stack(numer_list, 1)
    global_top = lax.pmax(row_top, "ctx")
    factor = jnp.exp(row_top - global_top)
    own_total, own_numer = (
        lax.psum_scatter(
            (weight_total * factor).reshape(query_count, -1), "ctx", scatter_dimension=0, tiled=True
        ),
        lax.psum_scatter(
            (numer * factor[..., None]).reshape(query_count, -1),
            "ctx",
            scatter_dimension=0,
            tiled=True,
        ),
    )
    own_total = own_total.reshape(suffix_rows, local_heads, sharing_count)
    own_numer = own_numer.reshape(suffix_rows, local_heads, sharing_count, HEAD_SIZE)
    attended = (own_numer / own_total[..., None]).reshape(suffix_rows, -1).astype(jnp.bfloat16)
    return (new_keys[:front_rows], new_values[:front_rows], attended)

GROUPS = 4
PAIR = 2
LANES = 128
SCALE = 1.0 / math.sqrt(HEAD_SIZE)


def row_scale(values):
    mean = jnp.sum(values * values, axis=-1, keepdims=True) * (1.0 / values.shape[-1])
    return lax.rsqrt(mean + epsilon)


CHUNKS = 4


def far_first():
    return list(range(GROUPS - 1, 0, -1))


def norm_kernel(query_any, hidden_any, suffix_any, gain_any, *rest):
    blocks_any, own_any = rest[:GROUPS], rest[GROUPS]
    hidden_ref, suffix_ref, gain_ref, query_ref, tail_ref = rest[GROUPS + 1 : GROUPS + 6]
    outs, (sems, out_sems) = rest[GROUPS + 6 : -2], rest[-2:]
    core, ctx = lax.axis_index("tp"), lax.axis_index("ctx")
    z, x = ctx // PAIR, ctx % PAIR
    half_rows, features = hidden_ref.shape
    rows = half_rows // CHUNKS
    block = features // (GROUPS * PAIR)
    per_block = block // LANES
    pieces = PAIR * per_block
    copies = [
        pltpu.make_async_copy(gain_any, gain_ref, sems.at[CHUNKS]),
        pltpu.make_async_copy(suffix_any, suffix_ref, sems.at[CHUNKS + 1]),
        pltpu.make_async_copy(query_any, query_ref, sems.at[CHUNKS + 2]),
    ]
    for i in range(CHUNKS):
        start = pl.multiple_of(core * half_rows + i * rows, rows)
        copies.append(
            pltpu.make_async_copy(
                hidden_any.at[pl.ds(start, rows)], hidden_ref.at[i * rows : (i + 1) * rows], sems.at[i]
            )
        )
    for copy in copies:
        copy.start()

    def offset(shift, side, j):
        owner = (z ^ shift) * PAIR + (x ^ side)
        return pl.multiple_of(owner * block + j * LANES, LANES)

    copies[0].wait()
    copies[1].wait()
    copies[2].wait()
    query_rows = query_ref[...].astype(jnp.float32)
    lines = query_rows.shape[1] // LANES
    for r in range(query_rows.shape[0]):
        tile = [query_rows[r : r + 1, j * LANES : (j + 1) * LANES] for j in range(lines)]
        tile = jnp.concatenate(tile, 0).astype(jnp.bfloat16)
        start = pieces * half_rows + pieces + r * lines
        for out in outs:
            out[start : start + lines, :] = tile

    both = suffix_ref[...].astype(jnp.float32)
    normed = both * row_scale(both) * gain_ref[...]
    tail_ref[...] = jnp.where(core == 0, normed[0:1], normed[1:2])
    for shift in range(GROUPS):
        ends = [
            tail_ref[:, pl.ds(offset(shift, side, j), LANES)]
            for side in range(PAIR)
            for j in range(per_block)
        ]
        start = pieces * half_rows
        outs[shift][start : start + pieces, :] = jnp.concatenate(ends, 0).astype(jnp.bfloat16)
    inverses = []
    for i in range(CHUNKS):
        copies[3 + i].wait()
        inverses.append(row_scale(hidden_ref[i * rows : (i + 1) * rows, :].astype(jnp.float32)))
    leaving = []
    for shift in far_first() + [0]:
        for side in range(PAIR):
            for j in range(per_block):
                columns = pl.ds(offset(shift, side, j), LANES)
                for i in range(CHUNKS):
                    piece = hidden_ref[i * rows : (i + 1) * rows, columns].astype(jnp.float32)
                    piece = piece * inverses[i] * gain_ref[:, columns]
                    start = (side * per_block + j) * half_rows + i * rows
                    outs[shift][start : start + rows, :] = piece.astype(jnp.bfloat16)
        leaving.append(pltpu.make_async_copy(outs[shift], blocks_any[shift], out_sems.at[shift]))
        leaving[-1].start()
    leaving.append(pltpu.make_async_copy(outs[0], own_any, out_sems.at[GROUPS]))
    leaving[-1].start()
    for copy in leaving:
        copy.wait()


def fetch_kernel(from_any, to_ref, sem):
    copy = pltpu.make_async_copy(from_any, to_ref, sem)
    copy.start()
    copy.wait()


def project_kernel(*refs):
    blocks = refs[: 2 * GROUPS]
    near_key, near_value, far_key, far_value = refs[2 * GROUPS : 2 * GROUPS + 4]
    outs = refs[2 * GROUPS + 4 : 3 * GROUPS + 4]
    query_ref, lhs_ref = refs[3 * GROUPS + 4 :]
    depth = near_key.shape[0]
    pieces = 2 * depth // LANES
    half_rows = (lhs_ref.shape[0] - 16) // (2 * GROUPS)
    rows = 2 * half_rows
    tails = [None] * len(blocks)
    for i, block in enumerate(blocks):
        for j in range(pieces):
            lhs_ref[i * half_rows : (i + 1) * half_rows, j * LANES : (j + 1) * LANES] = block[
                j * half_rows : (j + 1) * half_rows, :
            ]
        tail = block[pieces * half_rows : pieces * half_rows + pieces, :].astype(jnp.float32)
        tails[i] = jnp.concatenate([tail[j : j + 1] for j in range(pieces)], 1)
    tails.append(jnp.zeros((16 - len(tails), 2 * depth), jnp.float32))
    lines = query_ref.shape[0] // GROUPS
    for place, group in enumerate([0] + far_first()):
        block = blocks[2 * place]
        query_ref[group * lines : (group + 1) * lines, :] = block[block.shape[0] - lines :, :]
    total = GROUPS * rows
    lhs_ref[total : total + 16, :] = jnp.concatenate(tails, 0).astype(jnp.bfloat16)

    def product(near, far):
        return jnp.dot(
            lhs_ref[:, :depth], near[...], preferred_element_type=jnp.float32
        ) + jnp.dot(lhs_ref[:, depth:], far[...], preferred_element_type=jnp.float32)

    keys = product(near_key, far_key)
    values = product(near_value, far_value)
    high = keys.astype(jnp.bfloat16).astype(jnp.float32)
    low = keys - high
    columns = []
    for array in (high, low, values):
        for j in range(array.shape[1] // LANES):
            columns.append(array[:, j * LANES : (j + 1) * LANES])
    for group in range(GROUPS):
        for t, column in enumerate(columns):
            outs[group][t * rows : (t + 1) * rows, :] = column[
                group * rows : (group + 1) * rows
            ].astype(jnp.bfloat16)
        ends = [c[total + 2 * group : total + 2 * group + 2] for c in columns]
        ends.append(jnp.zeros((16 - 2 * len(columns), LANES), jnp.float32))
        outs[group][len(columns) * rows :, :] = jnp.concatenate(ends, 0).astype(jnp.bfloat16)


def head_queries(parts, head, width):
    sharing = QUERY_HEADS // KEY_VALUE_HEADS
    lines = sharing * width // HEAD_SIZE
    each = parts[0].shape[0] // GROUPS
    found = []
    for group in range(GROUPS):
        for part in parts:
            tiles = part[group * each : (group + 1) * each, :].astype(jnp.float32)
            for start in range(head * sharing, each, lines):
                found.append(tiles[start : start + sharing])
    return jnp.concatenate(found, 0).astype(jnp.bfloat16)


def times_transposed(a, b):
    return lax.dot_general(a, b, (((1,), (1,)), ((), ())), preferred_element_type=jnp.float32)


def loaded_kernel(place_ref, table_ref, split_ref, *refs):
    parts = refs[:PAIR]
    key_ref, value_ref, top_ref, total_ref, numer_ref, query_ref = refs[PAIR:]
    ctx = place_ref[1]
    slots, page, width = key_ref.shape
    heads = width // HEAD_SIZE
    split = split_ref[0]
    live = []
    for s in range(slots):
        hit = jnp.int32(0)
        for p in range(table_ref.shape[0]):
            hit = hit | ((table_ref[p] == ctx * slots + s) & (p >= split)).astype(jnp.int32)
        live.append(hit)
    for head in range(heads):
        columns = slice(head * HEAD_SIZE, (head + 1) * HEAD_SIZE)
        queries = head_queries(parts, head, width)
        count = queries.shape[0]
        query_ref[head * count : (head + 1) * count, :] = queries
        scores = [
            jnp.where(live[s] > 0, times_transposed(queries, key_ref[s, :, columns]) * SCALE, masked_score)
            for s in range(slots)
        ]
        top = scores[0].max(-1, keepdims=True)
        for s in range(1, slots):
            top = jnp.maximum(top, scores[s].max(-1, keepdims=True))
        total = jnp.zeros((count, 1), jnp.float32)
        numer = jnp.zeros((count, HEAD_SIZE), jnp.float32)
        for s in range(slots):
            expos = jnp.where(live[s] > 0, jnp.exp(scores[s] - top), 0.0)
            total += expos.sum(-1, keepdims=True)
            numer += jnp.dot(
                expos.astype(jnp.bfloat16), value_ref[s, :, columns], preferred_element_type=jnp.float32
            )
        rows = slice(head * count, (head + 1) * count)
        top_ref[rows, :] = jnp.broadcast_to(top, (count, LANES))
        total_ref[rows, :] = jnp.broadcast_to(total, (count, LANES))
        numer_ref[rows, :] = numer


def front_kernel(
    place_ref, split_ref, own, *refs
):
    received = refs[: GROUPS - 1]
    (key_bias, value_bias, cosine_ref, sine_ref, query_ref, top_ref, total_ref, numer_ref) = refs[
        GROUPS - 1 : GROUPS + 7
    ]
    front_key, front_value = refs[GROUPS + 7 : GROUPS + 9]
    outs = refs[GROUPS + 9 :]
    core, ctx = place_ref[0], place_ref[1]
    rows, width = front_key.shape
    half_rows = rows // 2
    heads = width // HEAD_SIZE
    sharing = QUERY_HEADS // KEY_VALUE_HEADS
    count = query_ref.shape[0] // heads
    own_queries = count // sharing // (GROUPS * PAIR)
    visible = ctx < split_ref[0]

    def summed(start, size):
        value = own[start : start + size, :].astype(jnp.float32)
        for ref in received:
            value += ref[start : start + size, :].astype(jnp.float32)
        return value

    ends = summed(3 * heads * rows, 16)
    row_query = lax.broadcasted_iota(jnp.int32, (count, 16), 0) // sharing
    query_position = (ctx ^ (row_query // own_queries)) * own_queries + row_query % own_queries
    end_column = lax.broadcasted_iota(jnp.int32, (count, 16), 1)
    end_position = ctx * 2 + jnp.where(end_column == 0, core, 1 - core)
    end_seen = (end_column < 2) & (end_position <= query_position)
    pad = jnp.zeros((14, HEAD_SIZE), jnp.float32)
    for head in range(heads):
        columns = slice(head * HEAD_SIZE, (head + 1) * HEAD_SIZE)
        raw = summed(head * rows, rows) + summed((heads + head) * rows, rows)
        value = (summed((2 * heads + head) * rows, rows) + value_bias[:, columns]).astype(jnp.bfloat16)
        end_raw = ends[2 * head : 2 * head + 2] + ends[2 * (heads + head) : 2 * (heads + head) + 2]
        end_value = ends[2 * (2 * heads + head) : 2 * (2 * heads + head) + 2] + value_bias[:, columns]
        end_raw = jnp.concatenate([end_raw + key_bias[:, columns], pad], 0)
        end_value = jnp.concatenate([end_value, pad], 0).astype(jnp.bfloat16)
        raw = raw + key_bias[:, columns]

        def rotated(k, part):
            turned = pltpu.roll(k, HEAD_SIZE // 2, 1)
            return (k * cosine_ref[part, :] + turned * sine_ref[part, :]).astype(jnp.bfloat16)

        key = rotated(raw, slice(0, rows))
        end_key = rotated(end_raw, slice(rows, rows + 16))
        for half in range(2):
            to = pl.ds(pl.multiple_of(lax.rem(core + half, 2) * half_rows, half_rows), half_rows)
            front_key[to, columns] = key[half * half_rows : (half + 1) * half_rows]
            front_value[to, columns] = value[half * half_rows : (half + 1) * half_rows]
        part = slice(head * count, (head + 1) * count)
        queries = query_ref[part, :]
        scores = jnp.where(visible, times_transposed(queries, key) * SCALE, masked_score)
        end_scores = jnp.where(end_seen, times_transposed(queries, end_key) * SCALE, masked_score)
        old_top = top_ref[part, :]
        top = jnp.maximum(scores.max(-1, keepdims=True), end_scores.max(-1, keepdims=True))
        top = jnp.maximum(old_top, top)
        factor = jnp.exp(old_top - top)
        expos = jnp.where(visible, jnp.exp(scores - top), 0.0)
        end_expos = jnp.where(end_seen, jnp.exp(end_scores - top[:, :16]), 0.0)
        total = total_ref[part, :] * factor + (
            expos.sum(-1, keepdims=True) + end_expos.sum(-1, keepdims=True)
        )
        numer = (
            numer_ref[part, :] * factor
            + jnp.dot(expos.astype(jnp.bfloat16), value, preferred_element_type=jnp.float32)
            + jnp.dot(end_expos.astype(jnp.bfloat16), end_value, preferred_element_type=jnp.float32)
        )
        stats = (kept_stats(top[:, 0:1], total[:, 0:1]), sent_stats(top[:, 0:1], total[:, 0:1]))
        each = own_queries * sharing
        for slot, out in enumerate(outs):
            at = slice(slot * each, (slot + 1) * each)
            out[head * each : (head + 1) * each, :] = numer[at].astype(out.dtype)
            out[(heads + head) * each : (heads + head + 1) * each, :] = stats[slot > 0][at]


def kept_stats(top, total):
    lane = lax.broadcasted_iota(jnp.int32, (top.shape[0], LANES), 1)
    return jnp.where(lane < LANES // 2, top, total)


def sent_stats(top, total):
    terms = []
    for rest, count in ((top, 3), (total, 2)):
        for _ in range(count):
            term = rest.astype(jnp.bfloat16).astype(jnp.float32)
            terms.append(term)
            rest = rest - term
    part = lax.broadcasted_iota(jnp.int32, (top.shape[0], LANES), 1) // 16
    stats = jnp.broadcast_to(terms[-1], part.shape)
    for i, term in enumerate(terms[:-1]):
        stats = jnp.where(part == i, term, stats)
    return stats.astype(jnp.bfloat16)


def merged(kept, others, start, rows):
    half = LANES // 2
    stats = kept[start + rows : start + 2 * rows, :]
    tops, totals = [stats[:, 0:1]], [stats[:, half : half + 1]]
    numers = [kept[start : start + rows, :]]
    for other in others:
        terms = other[start + rows : start + 2 * rows, :].astype(jnp.float32)
        tops.append((terms[:, 0:1] + terms[:, 16:17]) + terms[:, 32:33])
        totals.append(terms[:, 48:49] + terms[:, 64:65])
        numers.append(other[start : start + rows, :].astype(jnp.float32))
    top = functools.reduce(jnp.maximum, tops)
    factors = [jnp.exp(t - top) for t in tops]
    total = sum(f * t for f, t in zip(factors, totals))
    numer = sum(f * n for f, n in zip(factors, numers))
    return numer, top, total


def last_kernel(kept, *refs):
    others, out_ref = refs[:-1], refs[-1]
    numer, _, total = merged(kept, others, 0, kept.shape[0] // 2)
    result = numer / total
    queries, width = out_ref.shape
    sharing = QUERY_HEADS // KEY_VALUE_HEADS
    heads = width // HEAD_SIZE // sharing
    lines = []
    for i in range(queries):
        starts = [(h * queries + i) * sharing + g for h in range(heads) for g in range(sharing)]
        lines.append(jnp.concatenate([result[s : s + 1] for s in starts], 1))
    out_ref[...] = jnp.concatenate(lines, 0).astype(jnp.bfloat16)


def exchange_plan(
    hidden,
    suffix_hidden,
    norm_gain,
    key_matrix,
    value_matrix,
    key_offset_bias,
    value_offset_bias,
    suffix_query_rows,
    slot_keys,
    slot_values,
    page_slot_table,
    split_page,
):
    n_ctx = GROUPS * PAIR
    ctx = lax.axis_index("ctx").astype(jnp.int32)
    core = lax.axis_index("tp").astype(jnp.int32)
    place = jnp.stack([core, ctx])
    rows, features = hidden.shape
    half_rows = rows // 2
    width = key_matrix.shape[1]
    query_width = suffix_query_rows.shape[1]
    prefix_len = page_slot_table.shape[0] * slot_keys.shape[1]
    smem = pl.BlockSpec(memory_space=pltpu.SMEM)
    vmem = pl.BlockSpec(memory_space=pltpu.VMEM)
    params = pltpu.CompilerParams(vmem_limit_bytes=48 * 1024 * 1024)

    def move(array, target):
        pairs = []
        for c in range(n_ctx):
            for t in range(2):
                to_c, to_t = target(c, t)
                pairs.append((c * 2 + t, to_c * 2 + to_t))
        return lax.ppermute(array, ("ctx", "tp"), pairs)

    def partner(away):
        return lambda c, t: (c ^ away, t)

    def along(shift):
        return partner(shift * PAIR)

    def beside(c, t):
        return (c ^ 1, t)

    def sibling(c, t):
        return (c, 1 - t)

    hbm = pl.BlockSpec(memory_space=pltpu.HBM)
    pieces = features // GROUPS // LANES
    own_queries = suffix_query_rows.shape[0]
    lines = query_width // LANES
    block_rows = pieces * half_rows + pieces + own_queries * lines
    *blocks, own = pl.pallas_call(
        norm_kernel,
        in_specs=[hbm] * 4,
        out_specs=[hbm] * (GROUPS + 1),
        out_shape=[jax.ShapeDtypeStruct((block_rows, LANES), jnp.bfloat16)] * (GROUPS + 1),
        scratch_shapes=[
            pltpu.VMEM((half_rows, features), jnp.bfloat16),
            pltpu.VMEM(suffix_hidden.shape, jnp.bfloat16),
            pltpu.VMEM((1, features), jnp.float32),
            pltpu.VMEM(suffix_query_rows.shape, jnp.bfloat16),
            pltpu.VMEM((1, features), jnp.float32),
        ]
        + [pltpu.VMEM((block_rows, LANES), jnp.bfloat16)] * GROUPS
        + [
            pltpu.SemaphoreType.DMA((CHUNKS + 3,)),
            pltpu.SemaphoreType.DMA((GROUPS + 1,)),
        ],
        compiler_params=pltpu.CompilerParams(vmem_limit_bytes=60 * 1024 * 1024),
        cost_estimate=pl.CostEstimate(
            flops=4 * half_rows * features, bytes_accessed=4 * half_rows * features, transcendentals=0
        ),
        name="norm_rows",
    )(
        suffix_query_rows,
        hidden,
        suffix_hidden,
        norm_gain.reshape(1, features),
    )
    far = [move(key_matrix, beside), move(value_matrix, beside)]

    mine = {s: move(blocks[s], along(s)) for s in far_first()}
    inverse_freq = rope_base ** (
        -(jnp.arange(HEAD_SIZE // 2, dtype=jnp.float32) * (2.0 / HEAD_SIZE))
    )
    row = jnp.arange(rows + 16, dtype=jnp.int32)
    front_position = ctx * rows + (row + core * half_rows) % rows
    end_position = prefix_len + ctx * 2 + jnp.where(row == rows, core, 1 - core)
    position = jnp.where(row < rows, front_position, end_position)
    angles = position.astype(jnp.float32)[:, None] * inverse_freq[None, :]
    cosine, sine = jnp.cos(angles), jnp.sin(angles)
    cosine = jnp.concatenate([cosine, cosine], 1)
    sine = jnp.concatenate([-sine, sine], 1)

    first, second = far_first()[:2]
    mine[first], own = lax.optimization_barrier((mine[first], own))
    mine[0] = pl.pallas_call(
        fetch_kernel,
        in_specs=[hbm],
        out_specs=vmem,
        out_shape=jax.ShapeDtypeStruct(own.shape, own.dtype),
        scratch_shapes=[pltpu.SemaphoreType.DMA],
        compiler_params=params,
        cost_estimate=pl.CostEstimate(flops=0, bytes_accessed=64 * 1024 * 1024, transcendentals=0),
        name="fetch_own",
    )(own)
    mine[second], mine[0], cosine, sine = lax.optimization_barrier(
        (mine[second], mine[0], cosine, sine)
    )
    theirs = {s: move(blocks[0] if s == 0 else mine[s], sibling) for s in [0] + far_first()}
    lhs = [part[s] for s in [0] + far_first() for part in (mine, theirs)]

    part_rows = 3 * (width // LANES) * rows + 16
    *partials, own_tiles = pl.pallas_call(
        project_kernel,
        in_specs=[vmem] * (2 * GROUPS + 4),
        out_specs=[vmem] * (GROUPS + 1),
        out_shape=[jax.ShapeDtypeStruct((part_rows, LANES), jnp.bfloat16)] * GROUPS
        + [jax.ShapeDtypeStruct((GROUPS * own_queries * lines, LANES), jnp.bfloat16)],
        scratch_shapes=[pltpu.VMEM((GROUPS * rows + 16, PAIR * features // n_ctx), jnp.bfloat16)],
        compiler_params=params,
        cost_estimate=pl.CostEstimate(flops=2 * GROUPS * rows * 2 * width * features // GROUPS, bytes_accessed=6 * 1024 * 1024, transcendentals=0),
        name="project",
    )(*lhs, key_matrix, value_matrix, *far)
    received = [move(partials[1 + i], along(s)) for i, s in enumerate(far_first())]
    beside_tiles = move(own_tiles, beside)

    states = n_ctx * own_queries * query_width // HEAD_SIZE
    state = jax.ShapeDtypeStruct((states, LANES), jnp.float32)
    top, total, numer, queries = pl.pallas_call(
        loaded_kernel,
        in_specs=[smem, smem, smem] + [vmem] * (PAIR + 2),
        out_specs=[vmem] * 4,
        out_shape=[state] * 3 + [jax.ShapeDtypeStruct((states, LANES), jnp.bfloat16)],
        compiler_params=params,
        cost_estimate=pl.CostEstimate(
            flops=4 * states * slot_keys.shape[0] * slot_keys.shape[1] * HEAD_SIZE,
            bytes_accessed=4 * slot_keys.size,
            transcendentals=states * slot_keys.shape[0] * slot_keys.shape[1],
        ),
        name="loaded_attention",
    )(place, page_slot_table, split_page, own_tiles, beside_tiles, slot_keys, slot_values)


    def payload(kind):
        return jax.ShapeDtypeStruct((2 * states // n_ctx, LANES), kind)

    row_shape = jax.ShapeDtypeStruct((rows, width), jnp.bfloat16)
    front_key, front_value, kept, *sent = pl.pallas_call(
        front_kernel,
        in_specs=[smem, smem] + [vmem] * (GROUPS + 8),
        out_specs=[vmem] * (2 + n_ctx),
        out_shape=[row_shape] * 2 + [payload(jnp.float32)] + [payload(jnp.bfloat16)] * (n_ctx - 1),
        compiler_params=params,
        cost_estimate=pl.CostEstimate(flops=4 * states * rows * HEAD_SIZE, bytes_accessed=2 * 1024 * 1024, transcendentals=states * rows),
        name="front_attention",
    )(
        place,
        split_page,
        partials[0],
        *received,
        key_offset_bias.reshape(1, width),
        value_offset_bias.reshape(1, width),
        cosine,
        sine,
        queries,
        top,
        total,
        numer,
    )
    attended = pl.pallas_call(
        last_kernel,
        in_specs=[vmem] * n_ctx,
        out_specs=vmem,
        out_shape=jax.ShapeDtypeStruct((own_queries, query_width), jnp.bfloat16),
        compiler_params=params,
        name="finish",
    )(kept, *[move(sent[r - 1], partner(r)) for r in range(n_ctx - 1, 0, -1)])
    return (front_key, front_value, attended)


def solution(mesh):
    per_device = exchange_plan if mesh.shape["ctx"] == GROUPS * PAIR else gathered_plan
    return jax.shard_map(
        per_device,
        mesh=mesh,
        in_specs=(
            P(("req", "ctx"), None),
            P(("req", "ctx"), None),
            P(),
            P("ctx", "tp"),
            P("ctx", "tp"),
            P("tp"),
            P("tp"),
            P(("req", "ctx"), "tp"),
            P(("req", "ctx"), None, "tp"),
            P(("req", "ctx"), None, "tp"),
            P("req"),
            P("req"),
        ),
        out_specs=(P(("req", "ctx"), "tp"), P(("req", "ctx"), "tp"), P(("req", "ctx"), "tp")),
        check_vma=False,
    )
```

```python
import functools
import math

import jax
import jax.numpy as jnp
from jax import lax
from jax.experimental import pallas as pl
from jax.experimental.pallas import tpu as pltpu
from jax.sharding import PartitionSpec as P

QUERY_HEADS = 32
KEY_VALUE_HEADS = 4
HEAD_SIZE = 128


epsilon = 1e-06
rope_base = 1000000.0
masked_score = -1e30


def rms_rows(matrix, norm_gain):
    widened = matrix.astype(jnp.float32)
    inverse = lax.rsqrt(jnp.mean(widened * widened, axis=-1, keepdims=True) + epsilon)
    return (widened * inverse * norm_gain).astype(jnp.bfloat16)


def rotate(key_rows, positions, head_dim):
    row_count = key_rows.shape[0]
    split_heads = key_rows.reshape(row_count, -1, head_dim)
    half_dim = head_dim // 2
    inverse_freq = rope_base ** (-(jnp.arange(half_dim, dtype=jnp.float32) * (2.0 / head_dim)))
    angles = positions.astype(jnp.float32)[:, None] * inverse_freq[None, :]
    cosine = jnp.concatenate([jnp.cos(angles), jnp.cos(angles)], -1)[:, None, :]
    sine = jnp.concatenate([jnp.sin(angles), jnp.sin(angles)], -1)[:, None, :]
    turned = jnp.concatenate([-split_heads[..., half_dim:], split_heads[..., :half_dim]], -1)
    return (split_heads * cosine + turned * sine).reshape(row_count, -1)


def gathered_plan(
    hidden,
    suffix_hidden,
    norm_gain,
    key_matrix,
    value_matrix,
    key_offset_bias,
    value_offset_bias,
    suffix_query_rows,
    slot_keys,
    slot_values,
    page_slot_table,
    split_page,
):
    ctx_index = lax.axis_index("ctx")
    queries = lax.all_gather(suffix_query_rows, "ctx", axis=0, tiled=True)
    front_rows = hidden.shape[0]
    suffix_rows = suffix_hidden.shape[0]
    page_size = slot_keys.shape[1]
    slot_count = slot_keys.shape[0]
    total_pages = page_slot_table.shape[0]
    prefix_len = total_pages * page_size
    normed = rms_rows(jnp.concatenate([hidden, suffix_hidden], 0), norm_gain)
    col_width = key_matrix.shape[1]

    def accumulate(block_rows):
        return jnp.dot(normed, block_rows, preferred_element_type=jnp.float32)

    key_acc = accumulate(lax.all_gather(key_matrix, "ctx", axis=0, tiled=True))
    value_acc = accumulate(lax.all_gather(value_matrix, "ctx", axis=0, tiled=True))
    front_pos = ctx_index * front_rows + jnp.arange(front_rows, dtype=jnp.int32)
    suffix_pos = prefix_len + ctx_index * suffix_rows + jnp.arange(suffix_rows, dtype=jnp.int32)
    new_keys = rotate(
        key_acc + key_offset_bias, jnp.concatenate([front_pos, suffix_pos], 0), HEAD_SIZE
    ).astype(jnp.bfloat16)
    new_values = (value_acc + value_offset_bias).astype(jnp.bfloat16)
    cut_pos = split_page[0] * page_size
    global_slot = ctx_index * slot_count + jnp.arange(slot_count, dtype=jnp.int32)
    page_index = jnp.arange(total_pages, dtype=jnp.int32)
    slot_hits = (page_slot_table[None, :] == global_slot[:, None]) & (
        page_index[None, :] >= split_page[0]
    )
    slot_live = jnp.max(slot_hits.astype(jnp.int32), axis=1) > 0
    every_key = jnp.concatenate(
        [new_keys[:front_rows], slot_keys.reshape(-1, col_width), new_keys[front_rows:]], 0
    )
    every_value = jnp.concatenate(
        [new_values[:front_rows], slot_values.reshape(-1, col_width), new_values[front_rows:]], 0
    )
    query_count = queries.shape[0]
    query_pos = prefix_len + jnp.arange(query_count, dtype=jnp.int32)
    prefix_seen = jnp.concatenate([front_pos < cut_pos, jnp.repeat(slot_live, page_size)], 0)
    suffix_seen = suffix_pos[None, :] <= query_pos[:, None]
    visible = jnp.concatenate(
        [jnp.broadcast_to(prefix_seen[None, :], (query_count, prefix_seen.shape[0])), suffix_seen],
        1,
    )
    visible_wide = visible[:, None, :]
    sharing_count = QUERY_HEADS // KEY_VALUE_HEADS
    local_heads = col_width // HEAD_SIZE
    grouped_heads = queries.reshape(query_count, local_heads, sharing_count, HEAD_SIZE)
    top_list = []
    total_list = []
    numer_list = []
    for current_head in range(local_heads):
        head_keys = every_key[:, current_head * HEAD_SIZE : (current_head + 1) * HEAD_SIZE]
        head_values = every_value[:, current_head * HEAD_SIZE : (current_head + 1) * HEAD_SIZE]
        scores = jnp.einsum(
            "qgd,ld->qgl",
            grouped_heads[:, current_head],
            head_keys,
            preferred_element_type=jnp.float32,
        ) * (1.0 / math.sqrt(HEAD_SIZE))
        scores = jnp.where(visible_wide, scores, masked_score)
        row_top = jnp.max(scores, axis=-1)
        expos = jnp.where(visible_wide, jnp.exp(scores - row_top[..., None]), 0.0)
        total_list.append(jnp.sum(expos, axis=-1))
        top_list.append(row_top)
        numer_list.append(
            jnp.einsum(
                "qgl,ld->qgd",
                expos.astype(jnp.bfloat16),
                head_values,
                preferred_element_type=jnp.float32,
            )
        )
    row_top = jnp.stack(top_list, 1)
    weight_total = jnp.stack(total_list, 1)
    numer = jnp.stack(numer_list, 1)
    global_top = lax.pmax(row_top, "ctx")
    factor = jnp.exp(row_top - global_top)
    own_total, own_numer = (
        lax.psum_scatter(
            (weight_total * factor).reshape(query_count, -1), "ctx", scatter_dimension=0, tiled=True
        ),
        lax.psum_scatter(
            (numer * factor[..., None]).reshape(query_count, -1),
            "ctx",
            scatter_dimension=0,
            tiled=True,
        ),
    )
    own_total = own_total.reshape(suffix_rows, local_heads, sharing_count)
    own_numer = own_numer.reshape(suffix_rows, local_heads, sharing_count, HEAD_SIZE)
    attended = (own_numer / own_total[..., None]).reshape(suffix_rows, -1).astype(jnp.bfloat16)
    return (new_keys[:front_rows], new_values[:front_rows], attended)

GROUPS = 4
PAIR = 2
LANES = 128
SCALE = 1.0 / math.sqrt(HEAD_SIZE)


def row_scale(values):
    mean = jnp.sum(values * values, axis=-1, keepdims=True) * (1.0 / values.shape[-1])
    return lax.rsqrt(mean + epsilon)


CHUNKS = 4


def far_first():
    return list(range(GROUPS - 1, 0, -1))


def norm_kernel(query_any, hidden_any, suffix_any, gain_any, *rest):
    blocks_any, own_any = rest[:GROUPS], rest[GROUPS]
    hidden_ref, suffix_ref, gain_ref, query_ref, tail_ref = rest[GROUPS + 1 : GROUPS + 6]
    outs, (sems, out_sems) = rest[GROUPS + 6 : -2], rest[-2:]
    core, ctx = lax.axis_index("tp"), lax.axis_index("ctx")
    z, x = ctx // PAIR, ctx % PAIR
    half_rows, features = hidden_ref.shape
    rows = half_rows // CHUNKS
    block = features // (GROUPS * PAIR)
    per_block = block // LANES
    pieces = PAIR * per_block
    copies = [
        pltpu.make_async_copy(gain_any, gain_ref, sems.at[CHUNKS]),
        pltpu.make_async_copy(suffix_any, suffix_ref, sems.at[CHUNKS + 1]),
        pltpu.make_async_copy(query_any, query_ref, sems.at[CHUNKS + 2]),
    ]
    for i in range(CHUNKS):
        start = pl.multiple_of(core * half_rows + i * rows, rows)
        copies.append(
            pltpu.make_async_copy(
                hidden_any.at[pl.ds(start, rows)], hidden_ref.at[i * rows : (i + 1) * rows], sems.at[i]
            )
        )
    for copy in copies:
        copy.start()

    def offset(shift, side, j):
        owner = (z ^ shift) * PAIR + (x ^ side)
        return pl.multiple_of(owner * block + j * LANES, LANES)

    copies[0].wait()
    copies[1].wait()
    copies[2].wait()
    query_rows = query_ref[...].astype(jnp.float32)
    lines = query_rows.shape[1] // LANES
    for r in range(query_rows.shape[0]):
        tile = [query_rows[r : r + 1, j * LANES : (j + 1) * LANES] for j in range(lines)]
        tile = jnp.concatenate(tile, 0).astype(jnp.bfloat16)
        start = pieces * half_rows + pieces + r * lines
        for out in outs:
            out[start : start + lines, :] = tile

    both = suffix_ref[...].astype(jnp.float32)
    normed = both * row_scale(both) * gain_ref[...]
    tail_ref[...] = jnp.where(core == 0, normed[0:1], normed[1:2])
    for shift in range(GROUPS):
        ends = [
            tail_ref[:, pl.ds(offset(shift, side, j), LANES)]
            for side in range(PAIR)
            for j in range(per_block)
        ]
        start = pieces * half_rows
        outs[shift][start : start + pieces, :] = jnp.concatenate(ends, 0).astype(jnp.bfloat16)
    inverses = []
    for i in range(CHUNKS):
        copies[3 + i].wait()
        inverses.append(row_scale(hidden_ref[i * rows : (i + 1) * rows, :].astype(jnp.float32)))
    leaving = []
    for shift in far_first() + [0]:
        for side in range(PAIR):
            for j in range(per_block):
                columns = pl.ds(offset(shift, side, j), LANES)
                for i in range(CHUNKS):
                    piece = hidden_ref[i * rows : (i + 1) * rows, columns].astype(jnp.float32)
                    piece = piece * inverses[i] * gain_ref[:, columns]
                    start = (side * per_block + j) * half_rows + i * rows
                    outs[shift][start : start + rows, :] = piece.astype(jnp.bfloat16)
        leaving.append(pltpu.make_async_copy(outs[shift], blocks_any[shift], out_sems.at[shift]))
        leaving[-1].start()
    leaving.append(pltpu.make_async_copy(outs[0], own_any, out_sems.at[GROUPS]))
    leaving[-1].start()
    for copy in leaving:
        copy.wait()


def fetch_kernel(from_any, to_ref, sem):
    copy = pltpu.make_async_copy(from_any, to_ref, sem)
    copy.start()
    copy.wait()


def project_kernel(*refs):
    blocks = refs[: 2 * GROUPS]
    near_key, near_value, far_key, far_value = refs[2 * GROUPS : 2 * GROUPS + 4]
    outs = refs[2 * GROUPS + 4 : 3 * GROUPS + 4]
    query_ref, lhs_ref = refs[3 * GROUPS + 4 :]
    depth = near_key.shape[0]
    pieces = 2 * depth // LANES
    half_rows = (lhs_ref.shape[0] - 16) // (2 * GROUPS)
    rows = 2 * half_rows
    tails = [None] * len(blocks)
    for i, block in enumerate(blocks):
        for j in range(pieces):
            lhs_ref[i * half_rows : (i + 1) * half_rows, j * LANES : (j + 1) * LANES] = block[
                j * half_rows : (j + 1) * half_rows, :
            ]
        tail = block[pieces * half_rows : pieces * half_rows + pieces, :].astype(jnp.float32)
        tails[i] = jnp.concatenate([tail[j : j + 1] for j in range(pieces)], 1)
    tails.append(jnp.zeros((16 - len(tails), 2 * depth), jnp.float32))
    lines = query_ref.shape[0] // GROUPS
    for place, group in enumerate([0] + far_first()):
        block = blocks[2 * place]
        query_ref[group * lines : (group + 1) * lines, :] = block[block.shape[0] - lines :, :]
    total = GROUPS * rows
    lhs_ref[total : total + 16, :] = jnp.concatenate(tails, 0).astype(jnp.bfloat16)

    def product(near, far):
        return jnp.dot(
            lhs_ref[:, :depth], near[...], preferred_element_type=jnp.float32
        ) + jnp.dot(lhs_ref[:, depth:], far[...], preferred_element_type=jnp.float32)

    keys = product(near_key, far_key)
    values = product(near_value, far_value)
    high = keys.astype(jnp.bfloat16).astype(jnp.float32)
    low = keys - high
    columns = []
    for array in (high, low, values):
        for j in range(array.shape[1] // LANES):
            columns.append(array[:, j * LANES : (j + 1) * LANES])
    for group in range(GROUPS):
        for t, column in enumerate(columns):
            outs[group][t * rows : (t + 1) * rows, :] = column[
                group * rows : (group + 1) * rows
            ].astype(jnp.bfloat16)
        ends = [c[total + 2 * group : total + 2 * group + 2] for c in columns]
        ends.append(jnp.zeros((16 - 2 * len(columns), LANES), jnp.float32))
        outs[group][len(columns) * rows :, :] = jnp.concatenate(ends, 0).astype(jnp.bfloat16)


def head_queries(parts, head, width):
    sharing = QUERY_HEADS // KEY_VALUE_HEADS
    lines = sharing * width // HEAD_SIZE
    each = parts[0].shape[0] // GROUPS
    found = []
    for group in range(GROUPS):
        for part in parts:
            tiles = part[group * each : (group + 1) * each, :].astype(jnp.float32)
            for start in range(head * sharing, each, lines):
                found.append(tiles[start : start + sharing])
    return jnp.concatenate(found, 0).astype(jnp.bfloat16)


def times_transposed(a, b):
    return lax.dot_general(a, b, (((1,), (1,)), ((), ())), preferred_element_type=jnp.float32)


def loaded_kernel(place_ref, table_ref, split_ref, *refs):
    parts = refs[:PAIR]
    key_ref, value_ref, top_ref, total_ref, numer_ref, query_ref = refs[PAIR:]
    ctx = place_ref[1]
    slots, page, width = key_ref.shape
    heads = width // HEAD_SIZE
    split = split_ref[0]
    live = []
    for s in range(slots):
        hit = jnp.int32(0)
        for p in range(table_ref.shape[0]):
            hit = hit | ((table_ref[p] == ctx * slots + s) & (p >= split)).astype(jnp.int32)
        live.append(hit)
    for head in range(heads):
        columns = slice(head * HEAD_SIZE, (head + 1) * HEAD_SIZE)
        queries = head_queries(parts, head, width)
        count = queries.shape[0]
        query_ref[head * count : (head + 1) * count, :] = queries
        scores = [
            jnp.where(live[s] > 0, times_transposed(queries, key_ref[s, :, columns]) * SCALE, masked_score)
            for s in range(slots)
        ]
        top = scores[0].max(-1, keepdims=True)
        for s in range(1, slots):
            top = jnp.maximum(top, scores[s].max(-1, keepdims=True))
        total = jnp.zeros((count, 1), jnp.float32)
        numer = jnp.zeros((count, HEAD_SIZE), jnp.float32)
        for s in range(slots):
            expos = jnp.where(live[s] > 0, jnp.exp(scores[s] - top), 0.0)
            total += expos.sum(-1, keepdims=True)
            numer += jnp.dot(
                expos.astype(jnp.bfloat16), value_ref[s, :, columns], preferred_element_type=jnp.float32
            )
        rows = slice(head * count, (head + 1) * count)
        top_ref[rows, :] = jnp.broadcast_to(top, (count, LANES))
        total_ref[rows, :] = jnp.broadcast_to(total, (count, LANES))
        numer_ref[rows, :] = numer


def front_kernel(
    place_ref, split_ref, own, *refs
):
    received = refs[: GROUPS - 1]
    (key_bias, value_bias, cosine_ref, sine_ref, query_ref, top_ref, total_ref, numer_ref) = refs[
        GROUPS - 1 : GROUPS + 7
    ]
    front_key, front_value = refs[GROUPS + 7 : GROUPS + 9]
    outs = refs[GROUPS + 9 :]
    core, ctx = place_ref[0], place_ref[1]
    rows, width = front_key.shape
    half_rows = rows // 2
    heads = width // HEAD_SIZE
    sharing = QUERY_HEADS // KEY_VALUE_HEADS
    count = query_ref.shape[0] // heads
    own_queries = count // sharing // (GROUPS * PAIR)
    visible = ctx < split_ref[0]

    def summed(start, size):
        value = own[start : start + size, :].astype(jnp.float32)
        for ref in received:
            value += ref[start : start + size, :].astype(jnp.float32)
        return value

    ends = summed(3 * heads * rows, 16)
    row_query = lax.broadcasted_iota(jnp.int32, (count, 16), 0) // sharing
    query_position = (ctx ^ (row_query // own_queries)) * own_queries + row_query % own_queries
    end_column = lax.broadcasted_iota(jnp.int32, (count, 16), 1)
    end_position = ctx * 2 + jnp.where(end_column == 0, core, 1 - core)
    end_seen = (end_column < 2) & (end_position <= query_position)
    pad = jnp.zeros((14, HEAD_SIZE), jnp.float32)
    for head in range(heads):
        columns = slice(head * HEAD_SIZE, (head + 1) * HEAD_SIZE)
        raw = summed(head * rows, rows) + summed((heads + head) * rows, rows)
        value = (summed((2 * heads + head) * rows, rows) + value_bias[:, columns]).astype(jnp.bfloat16)
        end_raw = ends[2 * head : 2 * head + 2] + ends[2 * (heads + head) : 2 * (heads + head) + 2]
        end_value = ends[2 * (2 * heads + head) : 2 * (2 * heads + head) + 2] + value_bias[:, columns]
        end_raw = jnp.concatenate([end_raw + key_bias[:, columns], pad], 0)
        end_value = jnp.concatenate([end_value, pad], 0).astype(jnp.bfloat16)
        raw = raw + key_bias[:, columns]

        def rotated(k, part):
            turned = pltpu.roll(k, HEAD_SIZE // 2, 1)
            return (k * cosine_ref[part, :] + turned * sine_ref[part, :]).astype(jnp.bfloat16)

        key = rotated(raw, slice(0, rows))
        end_key = rotated(end_raw, slice(rows, rows + 16))
        for half in range(2):
            to = pl.ds(pl.multiple_of(lax.rem(core + half, 2) * half_rows, half_rows), half_rows)
            front_key[to, columns] = key[half * half_rows : (half + 1) * half_rows]
            front_value[to, columns] = value[half * half_rows : (half + 1) * half_rows]
        part = slice(head * count, (head + 1) * count)
        queries = query_ref[part, :]
        scores = jnp.where(visible, times_transposed(queries, key) * SCALE, masked_score)
        end_scores = jnp.where(end_seen, times_transposed(queries, end_key) * SCALE, masked_score)
        old_top = top_ref[part, :]
        top = jnp.maximum(scores.max(-1, keepdims=True), end_scores.max(-1, keepdims=True))
        top = jnp.maximum(old_top, top)
        factor = jnp.exp(old_top - top)
        expos = jnp.where(visible, jnp.exp(scores - top), 0.0)
        end_expos = jnp.where(end_seen, jnp.exp(end_scores - top[:, :16]), 0.0)
        total = total_ref[part, :] * factor + (
            expos.sum(-1, keepdims=True) + end_expos.sum(-1, keepdims=True)
        )
        numer = (
            numer_ref[part, :] * factor
            + jnp.dot(expos.astype(jnp.bfloat16), value, preferred_element_type=jnp.float32)
            + jnp.dot(end_expos.astype(jnp.bfloat16), end_value, preferred_element_type=jnp.float32)
        )
        stats = (kept_stats(top[:, 0:1], total[:, 0:1]), sent_stats(top[:, 0:1], total[:, 0:1]))
        each = own_queries * sharing
        for slot in range(GROUPS * PAIR):
            start = (slot // PAIR * 2 * heads + head) * each
            at = slice(slot * each, (slot + 1) * each)
            out = outs[slot % PAIR]
            out[start : start + each, :] = numer[at].astype(out.dtype)
            out[start + heads * each : start + (heads + 1) * each, :] = stats[slot % PAIR][at]


def kept_stats(top, total):
    lane = lax.broadcasted_iota(jnp.int32, (top.shape[0], LANES), 1)
    return jnp.where(lane < LANES // 2, top, total)


def sent_stats(top, total):
    terms = []
    for rest, count in ((top, 3), (total, 2)):
        for _ in range(count):
            term = rest.astype(jnp.bfloat16).astype(jnp.float32)
            terms.append(term)
            rest = rest - term
    part = lax.broadcasted_iota(jnp.int32, (top.shape[0], LANES), 1) // 16
    stats = jnp.broadcast_to(terms[-1], part.shape)
    for i, term in enumerate(terms[:-1]):
        stats = jnp.where(part == i, term, stats)
    return stats.astype(jnp.bfloat16)


def merged(kept, others, start, rows):
    half = LANES // 2
    stats = kept[start + rows : start + 2 * rows, :]
    tops, totals = [stats[:, 0:1]], [stats[:, half : half + 1]]
    numers = [kept[start : start + rows, :]]
    for other in others:
        terms = other[start + rows : start + 2 * rows, :].astype(jnp.float32)
        tops.append((terms[:, 0:1] + terms[:, 16:17]) + terms[:, 32:33])
        totals.append(terms[:, 48:49] + terms[:, 64:65])
        numers.append(other[start : start + rows, :].astype(jnp.float32))
    top = functools.reduce(jnp.maximum, tops)
    factors = [jnp.exp(t - top) for t in tops]
    total = sum(f * t for f, t in zip(factors, totals))
    numer = sum(f * n for f, n in zip(factors, numers))
    return numer, top, total


def merge_kernel(kept, other, keep_ref, *send_refs):
    each = keep_ref.shape[0]
    rows = each // 2
    for slot in range(GROUPS):
        numer, top, total = merged(kept, [other], slot * each, rows)
        if slot == 0:
            keep_ref[:rows, :] = numer
            keep_ref[rows:, :] = kept_stats(top, total)
        else:
            send_refs[slot - 1][:rows, :] = numer.astype(jnp.bfloat16)
            send_refs[slot - 1][rows:, :] = sent_stats(top, total)


def last_kernel(kept, *refs):
    others, out_ref = refs[:-1], refs[-1]
    numer, _, total = merged(kept, others, 0, kept.shape[0] // 2)
    result = numer / total
    queries, width = out_ref.shape
    sharing = QUERY_HEADS // KEY_VALUE_HEADS
    heads = width // HEAD_SIZE // sharing
    lines = []
    for i in range(queries):
        starts = [(h * queries + i) * sharing + g for h in range(heads) for g in range(sharing)]
        lines.append(jnp.concatenate([result[s : s + 1] for s in starts], 1))
    out_ref[...] = jnp.concatenate(lines, 0).astype(jnp.bfloat16)


def exchange_plan(
    hidden,
    suffix_hidden,
    norm_gain,
    key_matrix,
    value_matrix,
    key_offset_bias,
    value_offset_bias,
    suffix_query_rows,
    slot_keys,
    slot_values,
    page_slot_table,
    split_page,
):
    n_ctx = GROUPS * PAIR
    ctx = lax.axis_index("ctx").astype(jnp.int32)
    core = lax.axis_index("tp").astype(jnp.int32)
    place = jnp.stack([core, ctx])
    rows, features = hidden.shape
    half_rows = rows // 2
    width = key_matrix.shape[1]
    query_width = suffix_query_rows.shape[1]
    prefix_len = page_slot_table.shape[0] * slot_keys.shape[1]
    smem = pl.BlockSpec(memory_space=pltpu.SMEM)
    vmem = pl.BlockSpec(memory_space=pltpu.VMEM)
    params = pltpu.CompilerParams(vmem_limit_bytes=48 * 1024 * 1024)

    def move(array, target):
        pairs = []
        for c in range(n_ctx):
            for t in range(2):
                to_c, to_t = target(c, t)
                pairs.append((c * 2 + t, to_c * 2 + to_t))
        return lax.ppermute(array, ("ctx", "tp"), pairs)

    def partner(away):
        return lambda c, t: (c ^ away, t)

    def along(shift):
        return partner(shift * PAIR)

    def beside(c, t):
        return (c ^ 1, t)

    def sibling(c, t):
        return (c, 1 - t)

    hbm = pl.BlockSpec(memory_space=pltpu.HBM)
    pieces = features // GROUPS // LANES
    own_queries = suffix_query_rows.shape[0]
    lines = query_width // LANES
    block_rows = pieces * half_rows + pieces + own_queries * lines
    *blocks, own = pl.pallas_call(
        norm_kernel,
        in_specs=[hbm] * 4,
        out_specs=[hbm] * (GROUPS + 1),
        out_shape=[jax.ShapeDtypeStruct((block_rows, LANES), jnp.bfloat16)] * (GROUPS + 1),
        scratch_shapes=[
            pltpu.VMEM((half_rows, features), jnp.bfloat16),
            pltpu.VMEM(suffix_hidden.shape, jnp.bfloat16),
            pltpu.VMEM((1, features), jnp.float32),
            pltpu.VMEM(suffix_query_rows.shape, jnp.bfloat16),
            pltpu.VMEM((1, features), jnp.float32),
        ]
        + [pltpu.VMEM((block_rows, LANES), jnp.bfloat16)] * GROUPS
        + [
            pltpu.SemaphoreType.DMA((CHUNKS + 3,)),
            pltpu.SemaphoreType.DMA((GROUPS + 1,)),
        ],
        compiler_params=pltpu.CompilerParams(vmem_limit_bytes=60 * 1024 * 1024),
        cost_estimate=pl.CostEstimate(
            flops=4 * half_rows * features, bytes_accessed=4 * half_rows * features, transcendentals=0
        ),
        name="norm_rows",
    )(
        suffix_query_rows,
        hidden,
        suffix_hidden,
        norm_gain.reshape(1, features),
    )
    far = [move(key_matrix, beside), move(value_matrix, beside)]

    mine = {s: move(blocks[s], along(s)) for s in far_first()}
    inverse_freq = rope_base ** (
        -(jnp.arange(HEAD_SIZE // 2, dtype=jnp.float32) * (2.0 / HEAD_SIZE))
    )
    row = jnp.arange(rows + 16, dtype=jnp.int32)
    front_position = ctx * rows + (row + core * half_rows) % rows
    end_position = prefix_len + ctx * 2 + jnp.where(row == rows, core, 1 - core)
    position = jnp.where(row < rows, front_position, end_position)
    angles = position.astype(jnp.float32)[:, None] * inverse_freq[None, :]
    cosine, sine = jnp.cos(angles), jnp.sin(angles)
    cosine = jnp.concatenate([cosine, cosine], 1)
    sine = jnp.concatenate([-sine, sine], 1)

    first = far_first()[0]
    mine[0] = pl.pallas_call(
        fetch_kernel,
        in_specs=[hbm],
        out_specs=vmem,
        out_shape=jax.ShapeDtypeStruct(own.shape, own.dtype),
        scratch_shapes=[pltpu.SemaphoreType.DMA],
        compiler_params=params,
        cost_estimate=pl.CostEstimate(flops=0, bytes_accessed=64 * 1024 * 1024, transcendentals=0),
        name="fetch_own",
    )(own)
    mine[first], mine[0], cosine, sine = lax.optimization_barrier(
        (mine[first], mine[0], cosine, sine)
    )
    blocks[0], far[0] = lax.optimization_barrier((blocks[0], far[0]))
    theirs = {s: move(blocks[0] if s == 0 else mine[s], sibling) for s in [0] + far_first()}
    lhs = [part[s] for s in [0] + far_first() for part in (mine, theirs)]

    part_rows = 3 * (width // LANES) * rows + 16
    *partials, own_tiles = pl.pallas_call(
        project_kernel,
        in_specs=[vmem] * (2 * GROUPS + 4),
        out_specs=[vmem] * (GROUPS + 1),
        out_shape=[jax.ShapeDtypeStruct((part_rows, LANES), jnp.bfloat16)] * GROUPS
        + [jax.ShapeDtypeStruct((GROUPS * own_queries * lines, LANES), jnp.bfloat16)],
        scratch_shapes=[pltpu.VMEM((GROUPS * rows + 16, PAIR * features // n_ctx), jnp.bfloat16)],
        compiler_params=params,
        cost_estimate=pl.CostEstimate(flops=2 * GROUPS * rows * 2 * width * features // GROUPS, bytes_accessed=6 * 1024 * 1024, transcendentals=0),
        name="project",
    )(*lhs, key_matrix, value_matrix, *far)
    received = [move(partials[1 + i], along(s)) for i, s in enumerate(far_first())]
    beside_tiles = move(own_tiles, beside)

    states = n_ctx * own_queries * query_width // HEAD_SIZE
    state = jax.ShapeDtypeStruct((states, LANES), jnp.float32)
    top, total, numer, queries = pl.pallas_call(
        loaded_kernel,
        in_specs=[smem, smem, smem] + [vmem] * (PAIR + 2),
        out_specs=[vmem] * 4,
        out_shape=[state] * 3 + [jax.ShapeDtypeStruct((states, LANES), jnp.bfloat16)],
        compiler_params=params,
        cost_estimate=pl.CostEstimate(
            flops=4 * states * slot_keys.shape[0] * slot_keys.shape[1] * HEAD_SIZE,
            bytes_accessed=4 * slot_keys.size,
            transcendentals=states * slot_keys.shape[0] * slot_keys.shape[1],
        ),
        name="loaded_attention",
    )(place, page_slot_table, split_page, own_tiles, beside_tiles, slot_keys, slot_values)


    def payloads(size):
        return [jax.ShapeDtypeStruct((size, LANES), kind) for kind in (jnp.float32, jnp.bfloat16)]

    row_shape = jax.ShapeDtypeStruct((rows, width), jnp.bfloat16)
    front_key, front_value, kept, sent = pl.pallas_call(
        front_kernel,
        in_specs=[smem, smem] + [vmem] * (GROUPS + 8),
        out_specs=[vmem] * 4,
        out_shape=[row_shape] * 2 + payloads(states),
        compiler_params=params,
        cost_estimate=pl.CostEstimate(flops=4 * states * rows * HEAD_SIZE, bytes_accessed=2 * 1024 * 1024, transcendentals=states * rows),
        name="front_attention",
    )(
        place,
        split_page,
        partials[0],
        *received,
        key_offset_bias.reshape(1, width),
        value_offset_bias.reshape(1, width),
        cosine,
        sine,
        queries,
        top,
        total,
        numer,
    )
    kept, *sent = pl.pallas_call(
        merge_kernel,
        in_specs=[vmem] * 2,
        out_specs=[vmem] * GROUPS,
        out_shape=payloads(states // GROUPS) + payloads(states // GROUPS)[1:] * (GROUPS - 2),
        compiler_params=params,
        name="merge",
    )(kept, move(sent, beside))
    attended = pl.pallas_call(
        last_kernel,
        in_specs=[vmem] * GROUPS,
        out_specs=vmem,
        out_shape=jax.ShapeDtypeStruct((own_queries, query_width), jnp.bfloat16),
        compiler_params=params,
        name="finish",
    )(kept, *[move(sent[s - 1], along(s)) for s in far_first()])
    return (front_key, front_value, attended)


def solution(mesh):
    per_device = exchange_plan if mesh.shape["ctx"] == GROUPS * PAIR else gathered_plan
    return jax.shard_map(
        per_device,
        mesh=mesh,
        in_specs=(
            P(("req", "ctx"), None),
            P(("req", "ctx"), None),
            P(),
            P("ctx", "tp"),
            P("ctx", "tp"),
            P("tp"),
            P("tp"),
            P(("req", "ctx"), "tp"),
            P(("req", "ctx"), None, "tp"),
            P(("req", "ctx"), None, "tp"),
            P("req"),
            P("req"),
        ),
        out_specs=(P(("req", "ctx"), "tp"), P(("req", "ctx"), "tp"), P(("req", "ctx"), "tp")),
        check_vma=False,
    )
```

```python
import functools
import math

import jax
import jax.numpy as jnp
from jax import lax
from jax.experimental import pallas as pl
from jax.experimental.pallas import tpu as pltpu
from jax.sharding import PartitionSpec as P

QUERY_HEADS = 32
KEY_VALUE_HEADS = 4
HEAD_SIZE = 128


epsilon = 1e-06
rope_base = 1000000.0
masked_score = -1e30


def rms_rows(matrix, norm_gain):
    widened = matrix.astype(jnp.float32)
    inverse = lax.rsqrt(jnp.mean(widened * widened, axis=-1, keepdims=True) + epsilon)
    return (widened * inverse * norm_gain).astype(jnp.bfloat16)


def rotate(key_rows, positions, head_dim):
    row_count = key_rows.shape[0]
    split_heads = key_rows.reshape(row_count, -1, head_dim)
    half_dim = head_dim // 2
    inverse_freq = rope_base ** (-(jnp.arange(half_dim, dtype=jnp.float32) * (2.0 / head_dim)))
    angles = positions.astype(jnp.float32)[:, None] * inverse_freq[None, :]
    cosine = jnp.concatenate([jnp.cos(angles), jnp.cos(angles)], -1)[:, None, :]
    sine = jnp.concatenate([jnp.sin(angles), jnp.sin(angles)], -1)[:, None, :]
    turned = jnp.concatenate([-split_heads[..., half_dim:], split_heads[..., :half_dim]], -1)
    return (split_heads * cosine + turned * sine).reshape(row_count, -1)


def gathered_plan(
    hidden,
    suffix_hidden,
    norm_gain,
    key_matrix,
    value_matrix,
    key_offset_bias,
    value_offset_bias,
    suffix_query_rows,
    slot_keys,
    slot_values,
    page_slot_table,
    split_page,
):
    ctx_index = lax.axis_index("ctx")
    queries = lax.all_gather(suffix_query_rows, "ctx", axis=0, tiled=True)
    front_rows = hidden.shape[0]
    suffix_rows = suffix_hidden.shape[0]
    page_size = slot_keys.shape[1]
    slot_count = slot_keys.shape[0]
    total_pages = page_slot_table.shape[0]
    prefix_len = total_pages * page_size
    normed = rms_rows(jnp.concatenate([hidden, suffix_hidden], 0), norm_gain)
    col_width = key_matrix.shape[1]

    def accumulate(block_rows):
        return jnp.dot(normed, block_rows, preferred_element_type=jnp.float32)

    key_acc = accumulate(lax.all_gather(key_matrix, "ctx", axis=0, tiled=True))
    value_acc = accumulate(lax.all_gather(value_matrix, "ctx", axis=0, tiled=True))
    front_pos = ctx_index * front_rows + jnp.arange(front_rows, dtype=jnp.int32)
    suffix_pos = prefix_len + ctx_index * suffix_rows + jnp.arange(suffix_rows, dtype=jnp.int32)
    new_keys = rotate(
        key_acc + key_offset_bias, jnp.concatenate([front_pos, suffix_pos], 0), HEAD_SIZE
    ).astype(jnp.bfloat16)
    new_values = (value_acc + value_offset_bias).astype(jnp.bfloat16)
    cut_pos = split_page[0] * page_size
    global_slot = ctx_index * slot_count + jnp.arange(slot_count, dtype=jnp.int32)
    page_index = jnp.arange(total_pages, dtype=jnp.int32)
    slot_hits = (page_slot_table[None, :] == global_slot[:, None]) & (
        page_index[None, :] >= split_page[0]
    )
    slot_live = jnp.max(slot_hits.astype(jnp.int32), axis=1) > 0
    every_key = jnp.concatenate(
        [new_keys[:front_rows], slot_keys.reshape(-1, col_width), new_keys[front_rows:]], 0
    )
    every_value = jnp.concatenate(
        [new_values[:front_rows], slot_values.reshape(-1, col_width), new_values[front_rows:]], 0
    )
    query_count = queries.shape[0]
    query_pos = prefix_len + jnp.arange(query_count, dtype=jnp.int32)
    prefix_seen = jnp.concatenate([front_pos < cut_pos, jnp.repeat(slot_live, page_size)], 0)
    suffix_seen = suffix_pos[None, :] <= query_pos[:, None]
    visible = jnp.concatenate(
        [jnp.broadcast_to(prefix_seen[None, :], (query_count, prefix_seen.shape[0])), suffix_seen],
        1,
    )
    visible_wide = visible[:, None, :]
    sharing_count = QUERY_HEADS // KEY_VALUE_HEADS
    local_heads = col_width // HEAD_SIZE
    grouped_heads = queries.reshape(query_count, local_heads, sharing_count, HEAD_SIZE)
    top_list = []
    total_list = []
    numer_list = []
    for current_head in range(local_heads):
        head_keys = every_key[:, current_head * HEAD_SIZE : (current_head + 1) * HEAD_SIZE]
        head_values = every_value[:, current_head * HEAD_SIZE : (current_head + 1) * HEAD_SIZE]
        scores = jnp.einsum(
            "qgd,ld->qgl",
            grouped_heads[:, current_head],
            head_keys,
            preferred_element_type=jnp.float32,
        ) * (1.0 / math.sqrt(HEAD_SIZE))
        scores = jnp.where(visible_wide, scores, masked_score)
        row_top = jnp.max(scores, axis=-1)
        expos = jnp.where(visible_wide, jnp.exp(scores - row_top[..., None]), 0.0)
        total_list.append(jnp.sum(expos, axis=-1))
        top_list.append(row_top)
        numer_list.append(
            jnp.einsum(
                "qgl,ld->qgd",
                expos.astype(jnp.bfloat16),
                head_values,
                preferred_element_type=jnp.float32,
            )
        )
    row_top = jnp.stack(top_list, 1)
    weight_total = jnp.stack(total_list, 1)
    numer = jnp.stack(numer_list, 1)
    global_top = lax.pmax(row_top, "ctx")
    factor = jnp.exp(row_top - global_top)
    own_total, own_numer = (
        lax.psum_scatter(
            (weight_total * factor).reshape(query_count, -1), "ctx", scatter_dimension=0, tiled=True
        ),
        lax.psum_scatter(
            (numer * factor[..., None]).reshape(query_count, -1),
            "ctx",
            scatter_dimension=0,
            tiled=True,
        ),
    )
    own_total = own_total.reshape(suffix_rows, local_heads, sharing_count)
    own_numer = own_numer.reshape(suffix_rows, local_heads, sharing_count, HEAD_SIZE)
    attended = (own_numer / own_total[..., None]).reshape(suffix_rows, -1).astype(jnp.bfloat16)
    return (new_keys[:front_rows], new_values[:front_rows], attended)

GROUPS = 4
PAIR = 2
LANES = 128
SCALE = 1.0 / math.sqrt(HEAD_SIZE)


def row_scale(values):
    mean = jnp.sum(values * values, axis=-1, keepdims=True) * (1.0 / values.shape[-1])
    return lax.rsqrt(mean + epsilon)


CHUNKS = 4


def far_first():
    return list(range(GROUPS - 1, 0, -1))


def norm_kernel(query_any, hidden_any, suffix_any, gain_any, *rest):
    blocks_any, own_any = rest[:GROUPS], rest[GROUPS]
    hidden_ref, suffix_ref, gain_ref, query_ref, tail_ref = rest[GROUPS + 1 : GROUPS + 6]
    outs, (sems, out_sems) = rest[GROUPS + 6 : -2], rest[-2:]
    core, ctx = lax.axis_index("tp"), lax.axis_index("ctx")
    z, x = ctx // PAIR, ctx % PAIR
    half_rows, features = hidden_ref.shape
    rows = half_rows // CHUNKS
    block = features // (GROUPS * PAIR)
    per_block = block // LANES
    pieces = PAIR * per_block
    copies = [
        pltpu.make_async_copy(gain_any, gain_ref, sems.at[CHUNKS]),
        pltpu.make_async_copy(suffix_any, suffix_ref, sems.at[CHUNKS + 1]),
        pltpu.make_async_copy(query_any, query_ref, sems.at[CHUNKS + 2]),
    ]
    for i in range(CHUNKS):
        start = pl.multiple_of(core * half_rows + i * rows, rows)
        copies.append(
            pltpu.make_async_copy(
                hidden_any.at[pl.ds(start, rows)], hidden_ref.at[i * rows : (i + 1) * rows], sems.at[i]
            )
        )
    for copy in copies:
        copy.start()

    def offset(shift, side, j):
        owner = (z ^ shift) * PAIR + (x ^ side)
        return pl.multiple_of(owner * block + j * LANES, LANES)

    copies[0].wait()
    copies[1].wait()
    copies[2].wait()
    query_rows = query_ref[...].astype(jnp.float32)
    lines = query_rows.shape[1] // LANES
    for r in range(query_rows.shape[0]):
        tile = [query_rows[r : r + 1, j * LANES : (j + 1) * LANES] for j in range(lines)]
        tile = jnp.concatenate(tile, 0).astype(jnp.bfloat16)
        start = pieces * half_rows + pieces + r * lines
        for out in outs:
            out[start : start + lines, :] = tile

    both = suffix_ref[...].astype(jnp.float32)
    normed = both * row_scale(both) * gain_ref[...]
    tail_ref[...] = jnp.where(core == 0, normed[0:1], normed[1:2])
    for shift in range(GROUPS):
        ends = [
            tail_ref[:, pl.ds(offset(shift, side, j), LANES)]
            for side in range(PAIR)
            for j in range(per_block)
        ]
        start = pieces * half_rows
        outs[shift][start : start + pieces, :] = jnp.concatenate(ends, 0).astype(jnp.bfloat16)
    inverses = []
    for i in range(CHUNKS):
        copies[3 + i].wait()
        inverses.append(row_scale(hidden_ref[i * rows : (i + 1) * rows, :].astype(jnp.float32)))
    leaving = []
    for shift in far_first() + [0]:
        for side in range(PAIR):
            for j in range(per_block):
                columns = pl.ds(offset(shift, side, j), LANES)
                for i in range(CHUNKS):
                    piece = hidden_ref[i * rows : (i + 1) * rows, columns].astype(jnp.float32)
                    piece = piece * inverses[i] * gain_ref[:, columns]
                    start = (side * per_block + j) * half_rows + i * rows
                    outs[shift][start : start + rows, :] = piece.astype(jnp.bfloat16)
        leaving.append(pltpu.make_async_copy(outs[shift], blocks_any[shift], out_sems.at[shift]))
        leaving[-1].start()
    leaving.append(pltpu.make_async_copy(outs[0], own_any, out_sems.at[GROUPS]))
    leaving[-1].start()
    for copy in leaving:
        copy.wait()


def fetch_kernel(from_any, to_ref, sem):
    copy = pltpu.make_async_copy(from_any, to_ref, sem)
    copy.start()
    copy.wait()


def project_kernel(shifts, *refs):
    count = len(shifts)
    blocks, rest = refs[: 2 * count], refs[2 * count :]
    near_key, near_value, far_key, far_value = rest[:4]
    earlier, outs, (query_ref, lhs_ref) = rest[4 : -2 - count], rest[-2 - count : -2], rest[-2:]
    depth = near_key.shape[0]
    pieces = 2 * depth // LANES
    half_rows = (lhs_ref.shape[0] - 16) // (2 * count)
    rows = 2 * half_rows
    tails = []
    for i, block in enumerate(blocks):
        for j in range(pieces):
            lhs_ref[i * half_rows : (i + 1) * half_rows, j * LANES : (j + 1) * LANES] = block[
                j * half_rows : (j + 1) * half_rows, :
            ]
        tail = block[pieces * half_rows : pieces * half_rows + pieces, :].astype(jnp.float32)
        tails.append(jnp.concatenate([tail[j : j + 1] for j in range(pieces)], 1))
    tails.append(jnp.zeros((16 - len(tails), 2 * depth), jnp.float32))
    lines = query_ref.shape[0] // GROUPS
    if earlier:
        query_ref[...] = earlier[0][...]
    for i, shift in enumerate(shifts):
        block = blocks[2 * i]
        query_ref[shift * lines : (shift + 1) * lines, :] = block[block.shape[0] - lines :, :]
    total = count * rows
    lhs_ref[total : total + 16, :] = jnp.concatenate(tails, 0).astype(jnp.bfloat16)

    def product(near, far):
        return jnp.dot(
            lhs_ref[:, :depth], near[...], preferred_element_type=jnp.float32
        ) + jnp.dot(lhs_ref[:, depth:], far[...], preferred_element_type=jnp.float32)

    keys = product(near_key, far_key)
    values = product(near_value, far_value)
    high = keys.astype(jnp.bfloat16).astype(jnp.float32)
    low = keys - high
    columns = []
    for array in (high, low, values):
        for j in range(array.shape[1] // LANES):
            columns.append(array[:, j * LANES : (j + 1) * LANES])
    for i, out in enumerate(outs):
        for k, column in enumerate(columns):
            out[k * rows : (k + 1) * rows, :] = column[i * rows : (i + 1) * rows].astype(jnp.bfloat16)
        ends = [c[total + 2 * i : total + 2 * i + 2] for c in columns]
        ends.append(jnp.zeros((16 - 2 * len(columns), LANES), jnp.float32))
        out[len(columns) * rows :, :] = jnp.concatenate(ends, 0).astype(jnp.bfloat16)


def head_queries(parts, head, width):
    sharing = QUERY_HEADS // KEY_VALUE_HEADS
    lines = sharing * width // HEAD_SIZE
    each = parts[0].shape[0] // GROUPS
    found = []
    for group in range(GROUPS):
        for part in parts:
            tiles = part[group * each : (group + 1) * each, :].astype(jnp.float32)
            for start in range(head * sharing, each, lines):
                found.append(tiles[start : start + sharing])
    return jnp.concatenate(found, 0).astype(jnp.bfloat16)


def times_transposed(a, b):
    return lax.dot_general(a, b, (((1,), (1,)), ((), ())), preferred_element_type=jnp.float32)


def loaded_kernel(place_ref, table_ref, split_ref, *refs):
    parts = refs[:PAIR]
    key_ref, value_ref, top_ref, total_ref, numer_ref, query_ref = refs[PAIR:]
    ctx = place_ref[1]
    slots, page, width = key_ref.shape
    heads = width // HEAD_SIZE
    split = split_ref[0]
    live = []
    for s in range(slots):
        hit = jnp.int32(0)
        for p in range(table_ref.shape[0]):
            hit = hit | ((table_ref[p] == ctx * slots + s) & (p >= split)).astype(jnp.int32)
        live.append(hit)
    for head in range(heads):
        columns = slice(head * HEAD_SIZE, (head + 1) * HEAD_SIZE)
        queries = head_queries(parts, head, width)
        count = queries.shape[0]
        query_ref[head * count : (head + 1) * count, :] = queries
        scores = [
            jnp.where(live[s] > 0, times_transposed(queries, key_ref[s, :, columns]) * SCALE, masked_score)
            for s in range(slots)
        ]
        top = scores[0].max(-1, keepdims=True)
        for s in range(1, slots):
            top = jnp.maximum(top, scores[s].max(-1, keepdims=True))
        total = jnp.zeros((count, 1), jnp.float32)
        numer = jnp.zeros((count, HEAD_SIZE), jnp.float32)
        for s in range(slots):
            expos = jnp.where(live[s] > 0, jnp.exp(scores[s] - top), 0.0)
            total += expos.sum(-1, keepdims=True)
            numer += jnp.dot(
                expos.astype(jnp.bfloat16), value_ref[s, :, columns], preferred_element_type=jnp.float32
            )
        rows = slice(head * count, (head + 1) * count)
        top_ref[rows, :] = jnp.broadcast_to(top, (count, LANES))
        total_ref[rows, :] = jnp.broadcast_to(total, (count, LANES))
        numer_ref[rows, :] = numer


def front_kernel(
    place_ref, split_ref, own, *refs
):
    received = refs[: GROUPS - 1]
    (key_bias, value_bias, cosine_ref, sine_ref, query_ref, top_ref, total_ref, numer_ref) = refs[
        GROUPS - 1 : GROUPS + 7
    ]
    front_key, front_value = refs[GROUPS + 7 : GROUPS + 9]
    outs = refs[GROUPS + 9 :]
    core, ctx = place_ref[0], place_ref[1]
    rows, width = front_key.shape
    half_rows = rows // 2
    heads = width // HEAD_SIZE
    sharing = QUERY_HEADS // KEY_VALUE_HEADS
    count = query_ref.shape[0] // heads
    own_queries = count // sharing // (GROUPS * PAIR)
    visible = ctx < split_ref[0]

    def summed(start, size):
        value = own[start : start + size, :].astype(jnp.float32)
        for ref in received:
            value += ref[start : start + size, :].astype(jnp.float32)
        return value

    ends = summed(3 * heads * rows, 16)
    row_query = lax.broadcasted_iota(jnp.int32, (count, 16), 0) // sharing
    query_position = (ctx ^ (row_query // own_queries)) * own_queries + row_query % own_queries
    end_column = lax.broadcasted_iota(jnp.int32, (count, 16), 1)
    end_position = ctx * 2 + jnp.where(end_column == 0, core, 1 - core)
    end_seen = (end_column < 2) & (end_position <= query_position)
    pad = jnp.zeros((14, HEAD_SIZE), jnp.float32)
    for head in range(heads):
        columns = slice(head * HEAD_SIZE, (head + 1) * HEAD_SIZE)
        raw = summed(head * rows, rows) + summed((heads + head) * rows, rows)
        value = (summed((2 * heads + head) * rows, rows) + value_bias[:, columns]).astype(jnp.bfloat16)
        end_raw = ends[2 * head : 2 * head + 2] + ends[2 * (heads + head) : 2 * (heads + head) + 2]
        end_value = ends[2 * (2 * heads + head) : 2 * (2 * heads + head) + 2] + value_bias[:, columns]
        end_raw = jnp.concatenate([end_raw + key_bias[:, columns], pad], 0)
        end_value = jnp.concatenate([end_value, pad], 0).astype(jnp.bfloat16)
        raw = raw + key_bias[:, columns]

        def rotated(k, part):
            turned = pltpu.roll(k, HEAD_SIZE // 2, 1)
            return (k * cosine_ref[part, :] + turned * sine_ref[part, :]).astype(jnp.bfloat16)

        key = rotated(raw, slice(0, rows))
        end_key = rotated(end_raw, slice(rows, rows + 16))
        for half in range(2):
            to = pl.ds(pl.multiple_of(lax.rem(core + half, 2) * half_rows, half_rows), half_rows)
            front_key[to, columns] = key[half * half_rows : (half + 1) * half_rows]
            front_value[to, columns] = value[half * half_rows : (half + 1) * half_rows]
        part = slice(head * count, (head + 1) * count)
        queries = query_ref[part, :]
        scores = jnp.where(visible, times_transposed(queries, key) * SCALE, masked_score)
        end_scores = jnp.where(end_seen, times_transposed(queries, end_key) * SCALE, masked_score)
        old_top = top_ref[part, :]
        top = jnp.maximum(scores.max(-1, keepdims=True), end_scores.max(-1, keepdims=True))
        top = jnp.maximum(old_top, top)
        factor = jnp.exp(old_top - top)
        expos = jnp.where(visible, jnp.exp(scores - top), 0.0)
        end_expos = jnp.where(end_seen, jnp.exp(end_scores - top[:, :16]), 0.0)
        total = total_ref[part, :] * factor + (
            expos.sum(-1, keepdims=True) + end_expos.sum(-1, keepdims=True)
        )
        numer = (
            numer_ref[part, :] * factor
            + jnp.dot(expos.astype(jnp.bfloat16), value, preferred_element_type=jnp.float32)
            + jnp.dot(end_expos.astype(jnp.bfloat16), end_value, preferred_element_type=jnp.float32)
        )
        stats = (kept_stats(top[:, 0:1], total[:, 0:1]), sent_stats(top[:, 0:1], total[:, 0:1]))
        each = own_queries * sharing
        for slot in range(GROUPS * PAIR):
            start = (slot // PAIR * 2 * heads + head) * each
            at = slice(slot * each, (slot + 1) * each)
            out = outs[slot % PAIR]
            out[start : start + each, :] = numer[at].astype(out.dtype)
            out[start + heads * each : start + (heads + 1) * each, :] = stats[slot % PAIR][at]


def kept_stats(top, total):
    lane = lax.broadcasted_iota(jnp.int32, (top.shape[0], LANES), 1)
    return jnp.where(lane < LANES // 2, top, total)


def sent_stats(top, total):
    terms = []
    for rest, count in ((top, 3), (total, 2)):
        for _ in range(count):
            term = rest.astype(jnp.bfloat16).astype(jnp.float32)
            terms.append(term)
            rest = rest - term
    part = lax.broadcasted_iota(jnp.int32, (top.shape[0], LANES), 1) // 16
    stats = jnp.broadcast_to(terms[-1], part.shape)
    for i, term in enumerate(terms[:-1]):
        stats = jnp.where(part == i, term, stats)
    return stats.astype(jnp.bfloat16)


def merged(kept, others, start, rows):
    half = LANES // 2
    stats = kept[start + rows : start + 2 * rows, :]
    tops, totals = [stats[:, 0:1]], [stats[:, half : half + 1]]
    numers = [kept[start : start + rows, :]]
    for other in others:
        terms = other[start + rows : start + 2 * rows, :].astype(jnp.float32)
        tops.append((terms[:, 0:1] + terms[:, 16:17]) + terms[:, 32:33])
        totals.append(terms[:, 48:49] + terms[:, 64:65])
        numers.append(other[start : start + rows, :].astype(jnp.float32))
    top = functools.reduce(jnp.maximum, tops)
    factors = [jnp.exp(t - top) for t in tops]
    total = sum(f * t for f, t in zip(factors, totals))
    numer = sum(f * n for f, n in zip(factors, numers))
    return numer, top, total


def merge_kernel(kept, other, keep_ref, *send_refs):
    each = keep_ref.shape[0]
    rows = each // 2
    for slot in range(GROUPS):
        numer, top, total = merged(kept, [other], slot * each, rows)
        if slot == 0:
            keep_ref[:rows, :] = numer
            keep_ref[rows:, :] = kept_stats(top, total)
        else:
            send_refs[slot - 1][:rows, :] = numer.astype(jnp.bfloat16)
            send_refs[slot - 1][rows:, :] = sent_stats(top, total)


def last_kernel(kept, *refs):
    others, out_ref = refs[:-1], refs[-1]
    numer, _, total = merged(kept, others, 0, kept.shape[0] // 2)
    result = numer / total
    queries, width = out_ref.shape
    sharing = QUERY_HEADS // KEY_VALUE_HEADS
    heads = width // HEAD_SIZE // sharing
    lines = []
    for i in range(queries):
        starts = [(h * queries + i) * sharing + g for h in range(heads) for g in range(sharing)]
        lines.append(jnp.concatenate([result[s : s + 1] for s in starts], 1))
    out_ref[...] = jnp.concatenate(lines, 0).astype(jnp.bfloat16)


def exchange_plan(
    hidden,
    suffix_hidden,
    norm_gain,
    key_matrix,
    value_matrix,
    key_offset_bias,
    value_offset_bias,
    suffix_query_rows,
    slot_keys,
    slot_values,
    page_slot_table,
    split_page,
):
    n_ctx = GROUPS * PAIR
    ctx = lax.axis_index("ctx").astype(jnp.int32)
    core = lax.axis_index("tp").astype(jnp.int32)
    place = jnp.stack([core, ctx])
    rows, features = hidden.shape
    half_rows = rows // 2
    width = key_matrix.shape[1]
    query_width = suffix_query_rows.shape[1]
    prefix_len = page_slot_table.shape[0] * slot_keys.shape[1]
    smem = pl.BlockSpec(memory_space=pltpu.SMEM)
    vmem = pl.BlockSpec(memory_space=pltpu.VMEM)
    params = pltpu.CompilerParams(vmem_limit_bytes=48 * 1024 * 1024)

    def move(array, target):
        pairs = []
        for c in range(n_ctx):
            for t in range(2):
                to_c, to_t = target(c, t)
                pairs.append((c * 2 + t, to_c * 2 + to_t))
        return lax.ppermute(array, ("ctx", "tp"), pairs)

    def partner(away):
        return lambda c, t: (c ^ away, t)

    def along(shift):
        return partner(shift * PAIR)

    def beside(c, t):
        return (c ^ 1, t)

    def sibling(c, t):
        return (c, 1 - t)

    hbm = pl.BlockSpec(memory_space=pltpu.HBM)
    pieces = features // GROUPS // LANES
    own_queries = suffix_query_rows.shape[0]
    lines = query_width // LANES
    block_rows = pieces * half_rows + pieces + own_queries * lines
    *blocks, own = pl.pallas_call(
        norm_kernel,
        in_specs=[hbm] * 4,
        out_specs=[hbm] * (GROUPS + 1),
        out_shape=[jax.ShapeDtypeStruct((block_rows, LANES), jnp.bfloat16)] * (GROUPS + 1),
        scratch_shapes=[
            pltpu.VMEM((half_rows, features), jnp.bfloat16),
            pltpu.VMEM(suffix_hidden.shape, jnp.bfloat16),
            pltpu.VMEM((1, features), jnp.float32),
            pltpu.VMEM(suffix_query_rows.shape, jnp.bfloat16),
            pltpu.VMEM((1, features), jnp.float32),
        ]
        + [pltpu.VMEM((block_rows, LANES), jnp.bfloat16)] * GROUPS
        + [
            pltpu.SemaphoreType.DMA((CHUNKS + 3,)),
            pltpu.SemaphoreType.DMA((GROUPS + 1,)),
        ],
        compiler_params=pltpu.CompilerParams(vmem_limit_bytes=60 * 1024 * 1024),
        cost_estimate=pl.CostEstimate(
            flops=4 * half_rows * features, bytes_accessed=4 * half_rows * features, transcendentals=0
        ),
        name="norm_rows",
    )(
        suffix_query_rows,
        hidden,
        suffix_hidden,
        norm_gain.reshape(1, features),
    )
    far = [move(key_matrix, beside), move(value_matrix, beside)]

    mine = {s: move(blocks[s], along(s)) for s in far_first()}
    inverse_freq = rope_base ** (
        -(jnp.arange(HEAD_SIZE // 2, dtype=jnp.float32) * (2.0 / HEAD_SIZE))
    )
    row = jnp.arange(rows + 16, dtype=jnp.int32)
    front_position = ctx * rows + (row + core * half_rows) % rows
    end_position = prefix_len + ctx * 2 + jnp.where(row == rows, core, 1 - core)
    position = jnp.where(row < rows, front_position, end_position)
    angles = position.astype(jnp.float32)[:, None] * inverse_freq[None, :]
    cosine, sine = jnp.cos(angles), jnp.sin(angles)
    cosine = jnp.concatenate([cosine, cosine], 1)
    sine = jnp.concatenate([-sine, sine], 1)

    first = far_first()[0]
    mine[0] = pl.pallas_call(
        fetch_kernel,
        in_specs=[hbm],
        out_specs=vmem,
        out_shape=jax.ShapeDtypeStruct(own.shape, own.dtype),
        scratch_shapes=[pltpu.SemaphoreType.DMA],
        compiler_params=params,
        cost_estimate=pl.CostEstimate(flops=0, bytes_accessed=64 * 1024 * 1024, transcendentals=0),
        name="fetch_own",
    )(own)
    mine[first], mine[0], cosine, sine = lax.optimization_barrier(
        (mine[first], mine[0], cosine, sine)
    )
    blocks[0], far[0] = lax.optimization_barrier((blocks[0], far[0]))
    theirs = {s: move(blocks[0] if s == 0 else mine[s], sibling) for s in [0] + far_first()}

    part_rows = 3 * (width // LANES) * rows + 16
    partials, own_tiles = {}, []
    for shifts in ((0, first), tuple(far_first()[1:])):
        *found, tiles = pl.pallas_call(
            functools.partial(project_kernel, shifts),
            in_specs=[vmem] * (2 * len(shifts) + 4 + len(own_tiles)),
            out_specs=[vmem] * (len(shifts) + 1),
            out_shape=[jax.ShapeDtypeStruct((part_rows, LANES), jnp.bfloat16)] * len(shifts)
            + [jax.ShapeDtypeStruct((GROUPS * own_queries * lines, LANES), jnp.bfloat16)],
            scratch_shapes=[
                pltpu.VMEM((len(shifts) * rows + 16, PAIR * features // n_ctx), jnp.bfloat16)
            ],
            compiler_params=params,
            cost_estimate=pl.CostEstimate(
                flops=2 * len(shifts) * rows * 2 * width * features // GROUPS,
                bytes_accessed=6 * 1024 * 1024,
                transcendentals=0,
            ),
            name="project",
        )(
            *[part[s] for s in shifts for part in (mine, theirs)],
            key_matrix,
            value_matrix,
            *far,
            *own_tiles,
        )
        partials.update(zip(shifts, found))
        own_tiles = [tiles]
    (own_tiles,) = own_tiles
    received = [move(partials[s], along(s)) for s in far_first()]
    beside_tiles = move(own_tiles, beside)

    states = n_ctx * own_queries * query_width // HEAD_SIZE
    state = jax.ShapeDtypeStruct((states, LANES), jnp.float32)
    top, total, numer, queries = pl.pallas_call(
        loaded_kernel,
        in_specs=[smem, smem, smem] + [vmem] * (PAIR + 2),
        out_specs=[vmem] * 4,
        out_shape=[state] * 3 + [jax.ShapeDtypeStruct((states, LANES), jnp.bfloat16)],
        compiler_params=params,
        cost_estimate=pl.CostEstimate(
            flops=4 * states * slot_keys.shape[0] * slot_keys.shape[1] * HEAD_SIZE,
            bytes_accessed=4 * slot_keys.size,
            transcendentals=states * slot_keys.shape[0] * slot_keys.shape[1],
        ),
        name="loaded_attention",
    )(place, page_slot_table, split_page, own_tiles, beside_tiles, slot_keys, slot_values)


    def payloads(size):
        return [jax.ShapeDtypeStruct((size, LANES), kind) for kind in (jnp.float32, jnp.bfloat16)]

    row_shape = jax.ShapeDtypeStruct((rows, width), jnp.bfloat16)
    front_key, front_value, kept, sent = pl.pallas_call(
        front_kernel,
        in_specs=[smem, smem] + [vmem] * (GROUPS + 8),
        out_specs=[vmem] * 4,
        out_shape=[row_shape] * 2 + payloads(states),
        compiler_params=params,
        cost_estimate=pl.CostEstimate(flops=4 * states * rows * HEAD_SIZE, bytes_accessed=2 * 1024 * 1024, transcendentals=states * rows),
        name="front_attention",
    )(
        place,
        split_page,
        partials[0],
        *received,
        key_offset_bias.reshape(1, width),
        value_offset_bias.reshape(1, width),
        cosine,
        sine,
        queries,
        top,
        total,
        numer,
    )
    kept, *sent = pl.pallas_call(
        merge_kernel,
        in_specs=[vmem] * 2,
        out_specs=[vmem] * GROUPS,
        out_shape=payloads(states // GROUPS) + payloads(states // GROUPS)[1:] * (GROUPS - 2),
        compiler_params=params,
        name="merge",
    )(kept, move(sent, beside))
    attended = pl.pallas_call(
        last_kernel,
        in_specs=[vmem] * GROUPS,
        out_specs=vmem,
        out_shape=jax.ShapeDtypeStruct((own_queries, query_width), jnp.bfloat16),
        compiler_params=params,
        name="finish",
    )(kept, *[move(sent[s - 1], along(s)) for s in far_first()])
    return (front_key, front_value, attended)


def solution(mesh):
    per_device = exchange_plan if mesh.shape["ctx"] == GROUPS * PAIR else gathered_plan
    return jax.shard_map(
        per_device,
        mesh=mesh,
        in_specs=(
            P(("req", "ctx"), None),
            P(("req", "ctx"), None),
            P(),
            P("ctx", "tp"),
            P("ctx", "tp"),
            P("tp"),
            P("tp"),
            P(("req", "ctx"), "tp"),
            P(("req", "ctx"), None, "tp"),
            P(("req", "ctx"), None, "tp"),
            P("req"),
            P("req"),
        ),
        out_specs=(P(("req", "ctx"), "tp"), P(("req", "ctx"), "tp"), P(("req", "ctx"), "tp")),
        check_vma=False,
    )
```

```python
import functools
import math

import jax
import jax.numpy as jnp
from jax import lax
from jax.experimental import pallas as pl
from jax.experimental.pallas import tpu as pltpu
from jax.sharding import PartitionSpec as P

QUERY_HEADS = 32
KEY_VALUE_HEADS = 4
HEAD_SIZE = 128


epsilon = 1e-06
rope_base = 1000000.0
masked_score = -1e30


def rms_rows(matrix, norm_gain):
    widened = matrix.astype(jnp.float32)
    inverse = lax.rsqrt(jnp.mean(widened * widened, axis=-1, keepdims=True) + epsilon)
    return (widened * inverse * norm_gain).astype(jnp.bfloat16)


def rotate(key_rows, positions, head_dim):
    row_count = key_rows.shape[0]
    split_heads = key_rows.reshape(row_count, -1, head_dim)
    half_dim = head_dim // 2
    inverse_freq = rope_base ** (-(jnp.arange(half_dim, dtype=jnp.float32) * (2.0 / head_dim)))
    angles = positions.astype(jnp.float32)[:, None] * inverse_freq[None, :]
    cosine = jnp.concatenate([jnp.cos(angles), jnp.cos(angles)], -1)[:, None, :]
    sine = jnp.concatenate([jnp.sin(angles), jnp.sin(angles)], -1)[:, None, :]
    turned = jnp.concatenate([-split_heads[..., half_dim:], split_heads[..., :half_dim]], -1)
    return (split_heads * cosine + turned * sine).reshape(row_count, -1)


def gathered_plan(
    hidden,
    suffix_hidden,
    norm_gain,
    key_matrix,
    value_matrix,
    key_offset_bias,
    value_offset_bias,
    suffix_query_rows,
    slot_keys,
    slot_values,
    page_slot_table,
    split_page,
):
    ctx_index = lax.axis_index("ctx")
    queries = lax.all_gather(suffix_query_rows, "ctx", axis=0, tiled=True)
    front_rows = hidden.shape[0]
    suffix_rows = suffix_hidden.shape[0]
    page_size = slot_keys.shape[1]
    slot_count = slot_keys.shape[0]
    total_pages = page_slot_table.shape[0]
    prefix_len = total_pages * page_size
    normed = rms_rows(jnp.concatenate([hidden, suffix_hidden], 0), norm_gain)
    col_width = key_matrix.shape[1]

    def accumulate(block_rows):
        return jnp.dot(normed, block_rows, preferred_element_type=jnp.float32)

    key_acc = accumulate(lax.all_gather(key_matrix, "ctx", axis=0, tiled=True))
    value_acc = accumulate(lax.all_gather(value_matrix, "ctx", axis=0, tiled=True))
    front_pos = ctx_index * front_rows + jnp.arange(front_rows, dtype=jnp.int32)
    suffix_pos = prefix_len + ctx_index * suffix_rows + jnp.arange(suffix_rows, dtype=jnp.int32)
    new_keys = rotate(
        key_acc + key_offset_bias, jnp.concatenate([front_pos, suffix_pos], 0), HEAD_SIZE
    ).astype(jnp.bfloat16)
    new_values = (value_acc + value_offset_bias).astype(jnp.bfloat16)
    cut_pos = split_page[0] * page_size
    global_slot = ctx_index * slot_count + jnp.arange(slot_count, dtype=jnp.int32)
    page_index = jnp.arange(total_pages, dtype=jnp.int32)
    slot_hits = (page_slot_table[None, :] == global_slot[:, None]) & (
        page_index[None, :] >= split_page[0]
    )
    slot_live = jnp.max(slot_hits.astype(jnp.int32), axis=1) > 0
    every_key = jnp.concatenate(
        [new_keys[:front_rows], slot_keys.reshape(-1, col_width), new_keys[front_rows:]], 0
    )
    every_value = jnp.concatenate(
        [new_values[:front_rows], slot_values.reshape(-1, col_width), new_values[front_rows:]], 0
    )
    query_count = queries.shape[0]
    query_pos = prefix_len + jnp.arange(query_count, dtype=jnp.int32)
    prefix_seen = jnp.concatenate([front_pos < cut_pos, jnp.repeat(slot_live, page_size)], 0)
    suffix_seen = suffix_pos[None, :] <= query_pos[:, None]
    visible = jnp.concatenate(
        [jnp.broadcast_to(prefix_seen[None, :], (query_count, prefix_seen.shape[0])), suffix_seen],
        1,
    )
    visible_wide = visible[:, None, :]
    sharing_count = QUERY_HEADS // KEY_VALUE_HEADS
    local_heads = col_width // HEAD_SIZE
    grouped_heads = queries.reshape(query_count, local_heads, sharing_count, HEAD_SIZE)
    top_list = []
    total_list = []
    numer_list = []
    for current_head in range(local_heads):
        head_keys = every_key[:, current_head * HEAD_SIZE : (current_head + 1) * HEAD_SIZE]
        head_values = every_value[:, current_head * HEAD_SIZE : (current_head + 1) * HEAD_SIZE]
        scores = jnp.einsum(
            "qgd,ld->qgl",
            grouped_heads[:, current_head],
            head_keys,
            preferred_element_type=jnp.float32,
        ) * (1.0 / math.sqrt(HEAD_SIZE))
        scores = jnp.where(visible_wide, scores, masked_score)
        row_top = jnp.max(scores, axis=-1)
        expos = jnp.where(visible_wide, jnp.exp(scores - row_top[..., None]), 0.0)
        total_list.append(jnp.sum(expos, axis=-1))
        top_list.append(row_top)
        numer_list.append(
            jnp.einsum(
                "qgl,ld->qgd",
                expos.astype(jnp.bfloat16),
                head_values,
                preferred_element_type=jnp.float32,
            )
        )
    row_top = jnp.stack(top_list, 1)
    weight_total = jnp.stack(total_list, 1)
    numer = jnp.stack(numer_list, 1)
    global_top = lax.pmax(row_top, "ctx")
    factor = jnp.exp(row_top - global_top)
    own_total, own_numer = (
        lax.psum_scatter(
            (weight_total * factor).reshape(query_count, -1), "ctx", scatter_dimension=0, tiled=True
        ),
        lax.psum_scatter(
            (numer * factor[..., None]).reshape(query_count, -1),
            "ctx",
            scatter_dimension=0,
            tiled=True,
        ),
    )
    own_total = own_total.reshape(suffix_rows, local_heads, sharing_count)
    own_numer = own_numer.reshape(suffix_rows, local_heads, sharing_count, HEAD_SIZE)
    attended = (own_numer / own_total[..., None]).reshape(suffix_rows, -1).astype(jnp.bfloat16)
    return (new_keys[:front_rows], new_values[:front_rows], attended)

GROUPS = 4
PAIR = 2
LANES = 128
SCALE = 1.0 / math.sqrt(HEAD_SIZE)


def row_scale(values):
    mean = jnp.sum(values * values, axis=-1, keepdims=True) * (1.0 / values.shape[-1])
    return lax.rsqrt(mean + epsilon)


CHUNKS = 4


def far_first():
    return sorted(range(1, GROUPS), key=lambda s: s < GROUPS // 2)


def norm_kernel(query_any, hidden_any, suffix_any, gain_any, *rest):
    blocks_any, own_any = rest[:GROUPS], rest[GROUPS]
    hidden_ref, suffix_ref, gain_ref, query_ref, tail_ref = rest[GROUPS + 1 : GROUPS + 6]
    outs, (sems, out_sems) = rest[GROUPS + 6 : -2], rest[-2:]
    core, ctx = lax.axis_index("tp"), lax.axis_index("ctx")
    z, x = ctx // PAIR, ctx % PAIR
    half_rows, features = hidden_ref.shape
    rows = half_rows // CHUNKS
    block = features // (GROUPS * PAIR)
    per_block = block // LANES
    pieces = PAIR * per_block
    copies = [
        pltpu.make_async_copy(gain_any, gain_ref, sems.at[CHUNKS]),
        pltpu.make_async_copy(suffix_any, suffix_ref, sems.at[CHUNKS + 1]),
        pltpu.make_async_copy(query_any, query_ref, sems.at[CHUNKS + 2]),
    ]
    for i in range(CHUNKS):
        start = pl.multiple_of(core * half_rows + i * rows, rows)
        copies.append(
            pltpu.make_async_copy(
                hidden_any.at[pl.ds(start, rows)], hidden_ref.at[i * rows : (i + 1) * rows], sems.at[i]
            )
        )
    for copy in copies:
        copy.start()

    def offset(shift, side, j):
        owner = (z ^ shift) * PAIR + (x ^ side)
        return pl.multiple_of(owner * block + j * LANES, LANES)

    copies[0].wait()
    copies[1].wait()
    copies[2].wait()
    query_rows = query_ref[...].astype(jnp.float32)
    lines = query_rows.shape[1] // LANES
    for r in range(query_rows.shape[0]):
        tile = [query_rows[r : r + 1, j * LANES : (j + 1) * LANES] for j in range(lines)]
        tile = jnp.concatenate(tile, 0).astype(jnp.bfloat16)
        start = pieces * half_rows + pieces + r * lines
        for out in outs:
            out[start : start + lines, :] = tile

    both = suffix_ref[...].astype(jnp.float32)
    normed = both * row_scale(both) * gain_ref[...]
    tail_ref[...] = jnp.where(core == 0, normed[0:1], normed[1:2])
    for shift in range(GROUPS):
        ends = [
            tail_ref[:, pl.ds(offset(shift, side, j), LANES)]
            for side in range(PAIR)
            for j in range(per_block)
        ]
        start = pieces * half_rows
        outs[shift][start : start + pieces, :] = jnp.concatenate(ends, 0).astype(jnp.bfloat16)
    inverses = []
    for i in range(CHUNKS):
        copies[3 + i].wait()
        inverses.append(row_scale(hidden_ref[i * rows : (i + 1) * rows, :].astype(jnp.float32)))
    leaving = []
    for shift in far_first() + [0]:
        for side in range(PAIR):
            for j in range(per_block):
                columns = pl.ds(offset(shift, side, j), LANES)
                for i in range(CHUNKS):
                    piece = hidden_ref[i * rows : (i + 1) * rows, columns].astype(jnp.float32)
                    piece = piece * inverses[i] * gain_ref[:, columns]
                    start = (side * per_block + j) * half_rows + i * rows
                    outs[shift][start : start + rows, :] = piece.astype(jnp.bfloat16)
        leaving.append(pltpu.make_async_copy(outs[shift], blocks_any[shift], out_sems.at[shift]))
        leaving[-1].start()
    leaving.append(pltpu.make_async_copy(outs[0], own_any, out_sems.at[GROUPS]))
    leaving[-1].start()
    for copy in leaving:
        copy.wait()


def fetch_kernel(from_any, to_ref, sem):
    copy = pltpu.make_async_copy(from_any, to_ref, sem)
    copy.start()
    copy.wait()


def project_kernel(shifts, *refs):
    count = len(shifts)
    blocks, rest = refs[: 2 * count], refs[2 * count :]
    near_key, near_value, far_key, far_value = rest[:4]
    earlier, outs, (query_ref, lhs_ref) = rest[4 : -2 - count], rest[-2 - count : -2], rest[-2:]
    depth = near_key.shape[0]
    pieces = 2 * depth // LANES
    half_rows = (lhs_ref.shape[0] - 16) // (2 * count)
    rows = 2 * half_rows
    tails = []
    for i, block in enumerate(blocks):
        for j in range(pieces):
            lhs_ref[i * half_rows : (i + 1) * half_rows, j * LANES : (j + 1) * LANES] = block[
                j * half_rows : (j + 1) * half_rows, :
            ]
        tail = block[pieces * half_rows : pieces * half_rows + pieces, :].astype(jnp.float32)
        tails.append(jnp.concatenate([tail[j : j + 1] for j in range(pieces)], 1))
    tails.append(jnp.zeros((16 - len(tails), 2 * depth), jnp.float32))
    lines = query_ref.shape[0] // GROUPS
    if earlier:
        query_ref[...] = earlier[0][...]
    for i, shift in enumerate(shifts):
        block = blocks[2 * i]
        query_ref[shift * lines : (shift + 1) * lines, :] = block[block.shape[0] - lines :, :]
    total = count * rows
    lhs_ref[total : total + 16, :] = jnp.concatenate(tails, 0).astype(jnp.bfloat16)

    def product(near, far):
        return jnp.dot(
            lhs_ref[:, :depth], near[...], preferred_element_type=jnp.float32
        ) + jnp.dot(lhs_ref[:, depth:], far[...], preferred_element_type=jnp.float32)

    keys = product(near_key, far_key)
    values = product(near_value, far_value)
    high = keys.astype(jnp.bfloat16).astype(jnp.float32)
    low = keys - high
    columns = []
    for array in (high, low, values):
        for j in range(array.shape[1] // LANES):
            columns.append(array[:, j * LANES : (j + 1) * LANES])
    for i, out in enumerate(outs):
        for k, column in enumerate(columns):
            out[k * rows : (k + 1) * rows, :] = column[i * rows : (i + 1) * rows].astype(jnp.bfloat16)
        ends = [c[total + 2 * i : total + 2 * i + 2] for c in columns]
        ends.append(jnp.zeros((16 - 2 * len(columns), LANES), jnp.float32))
        out[len(columns) * rows :, :] = jnp.concatenate(ends, 0).astype(jnp.bfloat16)


def head_queries(parts, head, width):
    sharing = QUERY_HEADS // KEY_VALUE_HEADS
    lines = sharing * width // HEAD_SIZE
    each = parts[0].shape[0] // GROUPS
    found = []
    for group in range(GROUPS):
        for part in parts:
            tiles = part[group * each : (group + 1) * each, :].astype(jnp.float32)
            for start in range(head * sharing, each, lines):
                found.append(tiles[start : start + sharing])
    return jnp.concatenate(found, 0).astype(jnp.bfloat16)


def times_transposed(a, b):
    return lax.dot_general(a, b, (((1,), (1,)), ((), ())), preferred_element_type=jnp.float32)


def loaded_kernel(place_ref, table_ref, split_ref, *refs):
    parts = refs[:PAIR]
    key_ref, value_ref, top_ref, total_ref, numer_ref, query_ref = refs[PAIR:]
    ctx = place_ref[1]
    slots, page, width = key_ref.shape
    heads = width // HEAD_SIZE
    split = split_ref[0]
    live = []
    for s in range(slots):
        hit = jnp.int32(0)
        for p in range(table_ref.shape[0]):
            hit = hit | ((table_ref[p] == ctx * slots + s) & (p >= split)).astype(jnp.int32)
        live.append(hit)
    for head in range(heads):
        columns = slice(head * HEAD_SIZE, (head + 1) * HEAD_SIZE)
        queries = head_queries(parts, head, width)
        count = queries.shape[0]
        query_ref[head * count : (head + 1) * count, :] = queries
        scores = [
            jnp.where(live[s] > 0, times_transposed(queries, key_ref[s, :, columns]) * SCALE, masked_score)
            for s in range(slots)
        ]
        top = scores[0].max(-1, keepdims=True)
        for s in range(1, slots):
            top = jnp.maximum(top, scores[s].max(-1, keepdims=True))
        total = jnp.zeros((count, 1), jnp.float32)
        numer = jnp.zeros((count, HEAD_SIZE), jnp.float32)
        for s in range(slots):
            expos = jnp.where(live[s] > 0, jnp.exp(scores[s] - top), 0.0)
            total += expos.sum(-1, keepdims=True)
            numer += jnp.dot(
                expos.astype(jnp.bfloat16), value_ref[s, :, columns], preferred_element_type=jnp.float32
            )
        rows = slice(head * count, (head + 1) * count)
        top_ref[rows, :] = jnp.broadcast_to(top, (count, LANES))
        total_ref[rows, :] = jnp.broadcast_to(total, (count, LANES))
        numer_ref[rows, :] = numer


def sum_kernel(one, other, out):
    out[...] = one[...].astype(jnp.float32) + other[...].astype(jnp.float32)


def front_kernel(
    place_ref, split_ref, early, *refs
):
    received = refs[: GROUPS - 2]
    (key_bias, value_bias, cosine_ref, sine_ref, query_ref, top_ref, total_ref, numer_ref) = refs[
        GROUPS - 2 : GROUPS + 6
    ]
    front_key, front_value = refs[GROUPS + 6 : GROUPS + 8]
    outs = refs[GROUPS + 8 :]
    core, ctx = place_ref[0], place_ref[1]
    rows, width = front_key.shape
    half_rows = rows // 2
    heads = width // HEAD_SIZE
    sharing = QUERY_HEADS // KEY_VALUE_HEADS
    count = query_ref.shape[0] // heads
    own_queries = count // sharing // (GROUPS * PAIR)
    visible = ctx < split_ref[0]

    def summed(start, size):
        value = early[start : start + size, :]
        for ref in received:
            value += ref[start : start + size, :].astype(jnp.float32)
        return value

    ends = summed(3 * heads * rows, 16)
    row_query = lax.broadcasted_iota(jnp.int32, (count, 16), 0) // sharing
    query_position = (ctx ^ (row_query // own_queries)) * own_queries + row_query % own_queries
    end_column = lax.broadcasted_iota(jnp.int32, (count, 16), 1)
    end_position = ctx * 2 + jnp.where(end_column == 0, core, 1 - core)
    end_seen = (end_column < 2) & (end_position <= query_position)
    pad = jnp.zeros((14, HEAD_SIZE), jnp.float32)
    for head in range(heads):
        columns = slice(head * HEAD_SIZE, (head + 1) * HEAD_SIZE)
        raw = summed(head * rows, rows) + summed((heads + head) * rows, rows)
        value = (summed((2 * heads + head) * rows, rows) + value_bias[:, columns]).astype(jnp.bfloat16)
        end_raw = ends[2 * head : 2 * head + 2] + ends[2 * (heads + head) : 2 * (heads + head) + 2]
        end_value = ends[2 * (2 * heads + head) : 2 * (2 * heads + head) + 2] + value_bias[:, columns]
        end_raw = jnp.concatenate([end_raw + key_bias[:, columns], pad], 0)
        end_value = jnp.concatenate([end_value, pad], 0).astype(jnp.bfloat16)
        raw = raw + key_bias[:, columns]

        def rotated(k, part):
            turned = pltpu.roll(k, HEAD_SIZE // 2, 1)
            return (k * cosine_ref[part, :] + turned * sine_ref[part, :]).astype(jnp.bfloat16)

        key = rotated(raw, slice(0, rows))
        end_key = rotated(end_raw, slice(rows, rows + 16))
        for half in range(2):
            to = pl.ds(pl.multiple_of(lax.rem(core + half, 2) * half_rows, half_rows), half_rows)
            front_key[to, columns] = key[half * half_rows : (half + 1) * half_rows]
            front_value[to, columns] = value[half * half_rows : (half + 1) * half_rows]
        part = slice(head * count, (head + 1) * count)
        queries = query_ref[part, :]
        scores = jnp.where(visible, times_transposed(queries, key) * SCALE, masked_score)
        end_scores = jnp.where(end_seen, times_transposed(queries, end_key) * SCALE, masked_score)
        old_top = top_ref[part, :]
        top = jnp.maximum(scores.max(-1, keepdims=True), end_scores.max(-1, keepdims=True))
        top = jnp.maximum(old_top, top)
        factor = jnp.exp(old_top - top)
        expos = jnp.where(visible, jnp.exp(scores - top), 0.0)
        end_expos = jnp.where(end_seen, jnp.exp(end_scores - top[:, :16]), 0.0)
        total = total_ref[part, :] * factor + (
            expos.sum(-1, keepdims=True) + end_expos.sum(-1, keepdims=True)
        )
        numer = (
            numer_ref[part, :] * factor
            + jnp.dot(expos.astype(jnp.bfloat16), value, preferred_element_type=jnp.float32)
            + jnp.dot(end_expos.astype(jnp.bfloat16), end_value, preferred_element_type=jnp.float32)
        )
        stats = (kept_stats(top[:, 0:1], total[:, 0:1]), sent_stats(top[:, 0:1], total[:, 0:1]))
        each = own_queries * sharing
        for slot in range(GROUPS * PAIR):
            start = (slot // PAIR * 2 * heads + head) * each
            at = slice(slot * each, (slot + 1) * each)
            out = outs[slot % PAIR]
            out[start : start + each, :] = numer[at].astype(out.dtype)
            out[start + heads * each : start + (heads + 1) * each, :] = stats[slot % PAIR][at]


def kept_stats(top, total):
    lane = lax.broadcasted_iota(jnp.int32, (top.shape[0], LANES), 1)
    return jnp.where(lane < LANES // 2, top, total)


def sent_stats(top, total):
    terms = []
    for rest, count in ((top, 3), (total, 2)):
        for _ in range(count):
            term = rest.astype(jnp.bfloat16).astype(jnp.float32)
            terms.append(term)
            rest = rest - term
    part = lax.broadcasted_iota(jnp.int32, (top.shape[0], LANES), 1) // 16
    stats = jnp.broadcast_to(terms[-1], part.shape)
    for i, term in enumerate(terms[:-1]):
        stats = jnp.where(part == i, term, stats)
    return stats.astype(jnp.bfloat16)


def merged(kept, others, start, rows):
    half = LANES // 2
    stats = kept[start + rows : start + 2 * rows, :]
    tops, totals = [stats[:, 0:1]], [stats[:, half : half + 1]]
    numers = [kept[start : start + rows, :]]
    for other in others:
        terms = other[start + rows : start + 2 * rows, :].astype(jnp.float32)
        tops.append((terms[:, 0:1] + terms[:, 16:17]) + terms[:, 32:33])
        totals.append(terms[:, 48:49] + terms[:, 64:65])
        numers.append(other[start : start + rows, :].astype(jnp.float32))
    top = functools.reduce(jnp.maximum, tops)
    factors = [jnp.exp(t - top) for t in tops]
    total = sum(f * t for f, t in zip(factors, totals))
    numer = sum(f * n for f, n in zip(factors, numers))
    return numer, top, total


def merge_kernel(kept, other, keep_ref, *send_refs):
    each = keep_ref.shape[0]
    rows = each // 2
    for slot in range(GROUPS):
        numer, top, total = merged(kept, [other], slot * each, rows)
        if slot == 0:
            keep_ref[:rows, :] = numer
            keep_ref[rows:, :] = kept_stats(top, total)
        else:
            send_refs[slot - 1][:rows, :] = numer.astype(jnp.bfloat16)
            send_refs[slot - 1][rows:, :] = sent_stats(top, total)


def last_kernel(kept, *refs):
    others, out_ref = refs[:-1], refs[-1]
    numer, _, total = merged(kept, others, 0, kept.shape[0] // 2)
    result = numer / total
    queries, width = out_ref.shape
    sharing = QUERY_HEADS // KEY_VALUE_HEADS
    heads = width // HEAD_SIZE // sharing
    lines = []
    for i in range(queries):
        starts = [(h * queries + i) * sharing + g for h in range(heads) for g in range(sharing)]
        lines.append(jnp.concatenate([result[s : s + 1] for s in starts], 1))
    out_ref[...] = jnp.concatenate(lines, 0).astype(jnp.bfloat16)


def exchange_plan(
    hidden,
    suffix_hidden,
    norm_gain,
    key_matrix,
    value_matrix,
    key_offset_bias,
    value_offset_bias,
    suffix_query_rows,
    slot_keys,
    slot_values,
    page_slot_table,
    split_page,
):
    n_ctx = GROUPS * PAIR
    ctx = lax.axis_index("ctx").astype(jnp.int32)
    core = lax.axis_index("tp").astype(jnp.int32)
    place = jnp.stack([core, ctx])
    rows, features = hidden.shape
    half_rows = rows // 2
    width = key_matrix.shape[1]
    query_width = suffix_query_rows.shape[1]
    prefix_len = page_slot_table.shape[0] * slot_keys.shape[1]
    smem = pl.BlockSpec(memory_space=pltpu.SMEM)
    vmem = pl.BlockSpec(memory_space=pltpu.VMEM)
    params = pltpu.CompilerParams(vmem_limit_bytes=48 * 1024 * 1024)

    def move(array, target):
        pairs = []
        for c in range(n_ctx):
            for t in range(2):
                to_c, to_t = target(c, t)
                pairs.append((c * 2 + t, to_c * 2 + to_t))
        return lax.ppermute(array, ("ctx", "tp"), pairs)

    def partner(away):
        return lambda c, t: (c ^ away, t)

    def along(shift):
        return partner(shift * PAIR)

    def beside(c, t):
        return (c ^ 1, t)

    def sibling(c, t):
        return (c, 1 - t)

    hbm = pl.BlockSpec(memory_space=pltpu.HBM)
    pieces = features // GROUPS // LANES
    own_queries = suffix_query_rows.shape[0]
    lines = query_width // LANES
    block_rows = pieces * half_rows + pieces + own_queries * lines
    *blocks, own = pl.pallas_call(
        norm_kernel,
        in_specs=[hbm] * 4,
        out_specs=[hbm] * (GROUPS + 1),
        out_shape=[jax.ShapeDtypeStruct((block_rows, LANES), jnp.bfloat16)] * (GROUPS + 1),
        scratch_shapes=[
            pltpu.VMEM((half_rows, features), jnp.bfloat16),
            pltpu.VMEM(suffix_hidden.shape, jnp.bfloat16),
            pltpu.VMEM((1, features), jnp.float32),
            pltpu.VMEM(suffix_query_rows.shape, jnp.bfloat16),
            pltpu.VMEM((1, features), jnp.float32),
        ]
        + [pltpu.VMEM((block_rows, LANES), jnp.bfloat16)] * GROUPS
        + [
            pltpu.SemaphoreType.DMA((CHUNKS + 3,)),
            pltpu.SemaphoreType.DMA((GROUPS + 1,)),
        ],
        compiler_params=pltpu.CompilerParams(vmem_limit_bytes=60 * 1024 * 1024),
        cost_estimate=pl.CostEstimate(
            flops=4 * half_rows * features, bytes_accessed=4 * half_rows * features, transcendentals=0
        ),
        name="norm_rows",
    )(
        suffix_query_rows,
        hidden,
        suffix_hidden,
        norm_gain.reshape(1, features),
    )
    *weights, blocks[1] = lax.optimization_barrier((key_matrix, value_matrix, blocks[1]))
    far = [move(matrix, beside) for matrix in weights]

    mine = {s: move(blocks[s], along(s)) for s in far_first()}
    inverse_freq = rope_base ** (
        -(jnp.arange(HEAD_SIZE // 2, dtype=jnp.float32) * (2.0 / HEAD_SIZE))
    )
    row = jnp.arange(rows + 16, dtype=jnp.int32)
    front_position = ctx * rows + (row + core * half_rows) % rows
    end_position = prefix_len + ctx * 2 + jnp.where(row == rows, core, 1 - core)
    position = jnp.where(row < rows, front_position, end_position)
    angles = position.astype(jnp.float32)[:, None] * inverse_freq[None, :]
    cosine, sine = jnp.cos(angles), jnp.sin(angles)
    cosine = jnp.concatenate([cosine, cosine], 1)
    sine = jnp.concatenate([-sine, sine], 1)

    first = far_first()[0]
    mine[0] = pl.pallas_call(
        fetch_kernel,
        in_specs=[hbm],
        out_specs=vmem,
        out_shape=jax.ShapeDtypeStruct(own.shape, own.dtype),
        scratch_shapes=[pltpu.SemaphoreType.DMA],
        compiler_params=params,
        cost_estimate=pl.CostEstimate(flops=0, bytes_accessed=64 * 1024 * 1024, transcendentals=0),
        name="fetch_own",
    )(own)
    mine[first], mine[0], cosine, sine = lax.optimization_barrier(
        (mine[first], mine[0], cosine, sine)
    )
    blocks[0], far[0] = lax.optimization_barrier((blocks[0], far[0]))
    theirs = {s: move(blocks[0] if s == 0 else mine[s], sibling) for s in [0] + far_first()}

    part_rows = 3 * (width // LANES) * rows + 16
    partials, own_tiles = {}, []
    for shifts in ((0, first), tuple(far_first()[1:])):
        *found, tiles = pl.pallas_call(
            functools.partial(project_kernel, shifts),
            in_specs=[vmem] * (2 * len(shifts) + 4 + len(own_tiles)),
            out_specs=[vmem] * (len(shifts) + 1),
            out_shape=[jax.ShapeDtypeStruct((part_rows, LANES), jnp.bfloat16)] * len(shifts)
            + [jax.ShapeDtypeStruct((GROUPS * own_queries * lines, LANES), jnp.bfloat16)],
            scratch_shapes=[
                pltpu.VMEM((len(shifts) * rows + 16, PAIR * features // n_ctx), jnp.bfloat16)
            ],
            compiler_params=params,
            cost_estimate=pl.CostEstimate(
                flops=2 * len(shifts) * rows * 2 * width * features // GROUPS,
                bytes_accessed=6 * 1024 * 1024,
                transcendentals=0,
            ),
            name="project",
        )(
            *[part[s] for s in shifts for part in (mine, theirs)],
            key_matrix,
            value_matrix,
            *far,
            *own_tiles,
        )
        partials.update(zip(shifts, found))
        own_tiles = [tiles]
    (own_tiles,) = own_tiles
    received = [move(partials[s], along(s)) for s in far_first()]
    early = pl.pallas_call(
        sum_kernel,
        in_specs=[vmem] * 2,
        out_specs=vmem,
        out_shape=jax.ShapeDtypeStruct((part_rows, LANES), jnp.float32),
        compiler_params=params,
        cost_estimate=pl.CostEstimate(flops=0, bytes_accessed=16 * 1024 * 1024, transcendentals=0),
        name="sum_early",
    )(partials[0], received[0])
    beside_tiles = move(own_tiles, beside)

    states = n_ctx * own_queries * query_width // HEAD_SIZE
    state = jax.ShapeDtypeStruct((states, LANES), jnp.float32)
    top, total, numer, queries = pl.pallas_call(
        loaded_kernel,
        in_specs=[smem, smem, smem] + [vmem] * (PAIR + 2),
        out_specs=[vmem] * 4,
        out_shape=[state] * 3 + [jax.ShapeDtypeStruct((states, LANES), jnp.bfloat16)],
        compiler_params=params,
        cost_estimate=pl.CostEstimate(
            flops=4 * states * slot_keys.shape[0] * slot_keys.shape[1] * HEAD_SIZE,
            bytes_accessed=4 * slot_keys.size,
            transcendentals=states * slot_keys.shape[0] * slot_keys.shape[1],
        ),
        name="loaded_attention",
    )(place, page_slot_table, split_page, own_tiles, beside_tiles, slot_keys, slot_values)


    def payloads(size):
        return [jax.ShapeDtypeStruct((size, LANES), kind) for kind in (jnp.float32, jnp.bfloat16)]

    row_shape = jax.ShapeDtypeStruct((rows, width), jnp.bfloat16)
    front_key, front_value, kept, sent = pl.pallas_call(
        front_kernel,
        in_specs=[smem, smem] + [vmem] * (GROUPS + 7),
        out_specs=[vmem] * 4,
        out_shape=[row_shape] * 2 + payloads(states),
        compiler_params=params,
        cost_estimate=pl.CostEstimate(flops=4 * states * rows * HEAD_SIZE, bytes_accessed=2 * 1024 * 1024, transcendentals=states * rows),
        name="front_attention",
    )(
        place,
        split_page,
        early,
        *received[1:],
        key_offset_bias.reshape(1, width),
        value_offset_bias.reshape(1, width),
        cosine,
        sine,
        queries,
        top,
        total,
        numer,
    )
    kept, *sent = pl.pallas_call(
        merge_kernel,
        in_specs=[vmem] * 2,
        out_specs=[vmem] * GROUPS,
        out_shape=payloads(states // GROUPS) + payloads(states // GROUPS)[1:] * (GROUPS - 2),
        compiler_params=params,
        name="merge",
    )(kept, move(sent, beside))
    attended = pl.pallas_call(
        last_kernel,
        in_specs=[vmem] * GROUPS,
        out_specs=vmem,
        out_shape=jax.ShapeDtypeStruct((own_queries, query_width), jnp.bfloat16),
        compiler_params=params,
        name="finish",
    )(kept, *[move(sent[s - 1], along(s)) for s in range(GROUPS - 1, 0, -1)])
    return (front_key, front_value, attended)


def solution(mesh):
    per_device = exchange_plan if mesh.shape["ctx"] == GROUPS * PAIR else gathered_plan
    return jax.shard_map(
        per_device,
        mesh=mesh,
        in_specs=(
            P(("req", "ctx"), None),
            P(("req", "ctx"), None),
            P(),
            P("ctx", "tp"),
            P("ctx", "tp"),
            P("tp"),
            P("tp"),
            P(("req", "ctx"), "tp"),
            P(("req", "ctx"), None, "tp"),
            P(("req", "ctx"), None, "tp"),
            P("req"),
            P("req"),
        ),
        out_specs=(P(("req", "ctx"), "tp"), P(("req", "ctx"), "tp"), P(("req", "ctx"), "tp")),
        check_vma=False,
    )
```

```python
import functools
import math

import jax
import jax.numpy as jnp
from jax import lax
from jax.experimental import pallas as pl
from jax.experimental.pallas import tpu as pltpu
from jax.sharding import PartitionSpec as P

QUERY_HEADS = 32
KEY_VALUE_HEADS = 4
HEAD_SIZE = 128


epsilon = 1e-06
rope_base = 1000000.0
masked_score = -1e30


def rms_rows(matrix, norm_gain):
    widened = matrix.astype(jnp.float32)
    inverse = lax.rsqrt(jnp.mean(widened * widened, axis=-1, keepdims=True) + epsilon)
    return (widened * inverse * norm_gain).astype(jnp.bfloat16)


def rotate(key_rows, positions, head_dim):
    row_count = key_rows.shape[0]
    split_heads = key_rows.reshape(row_count, -1, head_dim)
    half_dim = head_dim // 2
    inverse_freq = rope_base ** (-(jnp.arange(half_dim, dtype=jnp.float32) * (2.0 / head_dim)))
    angles = positions.astype(jnp.float32)[:, None] * inverse_freq[None, :]
    cosine = jnp.concatenate([jnp.cos(angles), jnp.cos(angles)], -1)[:, None, :]
    sine = jnp.concatenate([jnp.sin(angles), jnp.sin(angles)], -1)[:, None, :]
    turned = jnp.concatenate([-split_heads[..., half_dim:], split_heads[..., :half_dim]], -1)
    return (split_heads * cosine + turned * sine).reshape(row_count, -1)


def gathered_plan(
    hidden,
    suffix_hidden,
    norm_gain,
    key_matrix,
    value_matrix,
    key_offset_bias,
    value_offset_bias,
    suffix_query_rows,
    slot_keys,
    slot_values,
    page_slot_table,
    split_page,
):
    ctx_index = lax.axis_index("ctx")
    queries = lax.all_gather(suffix_query_rows, "ctx", axis=0, tiled=True)
    front_rows = hidden.shape[0]
    suffix_rows = suffix_hidden.shape[0]
    page_size = slot_keys.shape[1]
    slot_count = slot_keys.shape[0]
    total_pages = page_slot_table.shape[0]
    prefix_len = total_pages * page_size
    normed = rms_rows(jnp.concatenate([hidden, suffix_hidden], 0), norm_gain)
    col_width = key_matrix.shape[1]

    def accumulate(block_rows):
        return jnp.dot(normed, block_rows, preferred_element_type=jnp.float32)

    key_acc = accumulate(lax.all_gather(key_matrix, "ctx", axis=0, tiled=True))
    value_acc = accumulate(lax.all_gather(value_matrix, "ctx", axis=0, tiled=True))
    front_pos = ctx_index * front_rows + jnp.arange(front_rows, dtype=jnp.int32)
    suffix_pos = prefix_len + ctx_index * suffix_rows + jnp.arange(suffix_rows, dtype=jnp.int32)
    new_keys = rotate(
        key_acc + key_offset_bias, jnp.concatenate([front_pos, suffix_pos], 0), HEAD_SIZE
    ).astype(jnp.bfloat16)
    new_values = (value_acc + value_offset_bias).astype(jnp.bfloat16)
    cut_pos = split_page[0] * page_size
    global_slot = ctx_index * slot_count + jnp.arange(slot_count, dtype=jnp.int32)
    page_index = jnp.arange(total_pages, dtype=jnp.int32)
    slot_hits = (page_slot_table[None, :] == global_slot[:, None]) & (
        page_index[None, :] >= split_page[0]
    )
    slot_live = jnp.max(slot_hits.astype(jnp.int32), axis=1) > 0
    every_key = jnp.concatenate(
        [new_keys[:front_rows], slot_keys.reshape(-1, col_width), new_keys[front_rows:]], 0
    )
    every_value = jnp.concatenate(
        [new_values[:front_rows], slot_values.reshape(-1, col_width), new_values[front_rows:]], 0
    )
    query_count = queries.shape[0]
    query_pos = prefix_len + jnp.arange(query_count, dtype=jnp.int32)
    prefix_seen = jnp.concatenate([front_pos < cut_pos, jnp.repeat(slot_live, page_size)], 0)
    suffix_seen = suffix_pos[None, :] <= query_pos[:, None]
    visible = jnp.concatenate(
        [jnp.broadcast_to(prefix_seen[None, :], (query_count, prefix_seen.shape[0])), suffix_seen],
        1,
    )
    visible_wide = visible[:, None, :]
    sharing_count = QUERY_HEADS // KEY_VALUE_HEADS
    local_heads = col_width // HEAD_SIZE
    grouped_heads = queries.reshape(query_count, local_heads, sharing_count, HEAD_SIZE)
    top_list = []
    total_list = []
    numer_list = []
    for current_head in range(local_heads):
        head_keys = every_key[:, current_head * HEAD_SIZE : (current_head + 1) * HEAD_SIZE]
        head_values = every_value[:, current_head * HEAD_SIZE : (current_head + 1) * HEAD_SIZE]
        scores = jnp.einsum(
            "qgd,ld->qgl",
            grouped_heads[:, current_head],
            head_keys,
            preferred_element_type=jnp.float32,
        ) * (1.0 / math.sqrt(HEAD_SIZE))
        scores = jnp.where(visible_wide, scores, masked_score)
        row_top = jnp.max(scores, axis=-1)
        expos = jnp.where(visible_wide, jnp.exp(scores - row_top[..., None]), 0.0)
        total_list.append(jnp.sum(expos, axis=-1))
        top_list.append(row_top)
        numer_list.append(
            jnp.einsum(
                "qgl,ld->qgd",
                expos.astype(jnp.bfloat16),
                head_values,
                preferred_element_type=jnp.float32,
            )
        )
    row_top = jnp.stack(top_list, 1)
    weight_total = jnp.stack(total_list, 1)
    numer = jnp.stack(numer_list, 1)
    global_top = lax.pmax(row_top, "ctx")
    factor = jnp.exp(row_top - global_top)
    own_total, own_numer = (
        lax.psum_scatter(
            (weight_total * factor).reshape(query_count, -1), "ctx", scatter_dimension=0, tiled=True
        ),
        lax.psum_scatter(
            (numer * factor[..., None]).reshape(query_count, -1),
            "ctx",
            scatter_dimension=0,
            tiled=True,
        ),
    )
    own_total = own_total.reshape(suffix_rows, local_heads, sharing_count)
    own_numer = own_numer.reshape(suffix_rows, local_heads, sharing_count, HEAD_SIZE)
    attended = (own_numer / own_total[..., None]).reshape(suffix_rows, -1).astype(jnp.bfloat16)
    return (new_keys[:front_rows], new_values[:front_rows], attended)

GROUPS = 4
PAIR = 2
LANES = 128
SCALE = 1.0 / math.sqrt(HEAD_SIZE)


def row_scale(values):
    mean = jnp.sum(values * values, axis=-1, keepdims=True) * (1.0 / values.shape[-1])
    return lax.rsqrt(mean + epsilon)


CHUNKS = 4


def far_first():
    return sorted(range(1, GROUPS), key=lambda s: s < GROUPS // 2)


def norm_kernel(query_any, hidden_any, suffix_any, gain_any, *rest):
    blocks_any, own_any = rest[:GROUPS], rest[GROUPS]
    hidden_ref, suffix_ref, gain_ref, query_ref, tail_ref = rest[GROUPS + 1 : GROUPS + 6]
    outs, (sems, out_sems) = rest[GROUPS + 6 : -2], rest[-2:]
    core, ctx = lax.axis_index("tp"), lax.axis_index("ctx")
    z, x = ctx // PAIR, ctx % PAIR
    half_rows, features = hidden_ref.shape
    rows = half_rows // CHUNKS
    block = features // (GROUPS * PAIR)
    per_block = block // LANES
    pieces = PAIR * per_block
    copies = [
        pltpu.make_async_copy(gain_any, gain_ref, sems.at[CHUNKS]),
        pltpu.make_async_copy(suffix_any, suffix_ref, sems.at[CHUNKS + 1]),
        pltpu.make_async_copy(query_any, query_ref, sems.at[CHUNKS + 2]),
    ]
    for i in range(CHUNKS):
        start = pl.multiple_of(core * half_rows + i * rows, rows)
        copies.append(
            pltpu.make_async_copy(
                hidden_any.at[pl.ds(start, rows)], hidden_ref.at[i * rows : (i + 1) * rows], sems.at[i]
            )
        )
    for copy in copies:
        copy.start()

    def offset(shift, side, j):
        owner = (z ^ shift) * PAIR + (x ^ side)
        return pl.multiple_of(owner * block + j * LANES, LANES)

    copies[0].wait()
    copies[1].wait()
    copies[2].wait()
    query_rows = query_ref[...].astype(jnp.float32)
    lines = query_rows.shape[1] // LANES
    for r in range(query_rows.shape[0]):
        tile = [query_rows[r : r + 1, j * LANES : (j + 1) * LANES] for j in range(lines)]
        tile = jnp.concatenate(tile, 0).astype(jnp.bfloat16)
        start = pieces * half_rows + pieces + r * lines
        for out in outs:
            out[start : start + lines, :] = tile

    both = suffix_ref[...].astype(jnp.float32)
    normed = both * row_scale(both) * gain_ref[...]
    tail_ref[...] = jnp.where(core == 0, normed[0:1], normed[1:2])
    for shift in range(GROUPS):
        ends = [
            tail_ref[:, pl.ds(offset(shift, side, j), LANES)]
            for side in range(PAIR)
            for j in range(per_block)
        ]
        start = pieces * half_rows
        outs[shift][start : start + pieces, :] = jnp.concatenate(ends, 0).astype(jnp.bfloat16)
    inverses = []
    for i in range(CHUNKS):
        copies[3 + i].wait()
        inverses.append(row_scale(hidden_ref[i * rows : (i + 1) * rows, :].astype(jnp.float32)))
    leaving = []
    for shift in far_first() + [0]:
        for side in range(PAIR):
            for j in range(per_block):
                columns = pl.ds(offset(shift, side, j), LANES)
                for i in range(CHUNKS):
                    piece = hidden_ref[i * rows : (i + 1) * rows, columns].astype(jnp.float32)
                    piece = piece * inverses[i] * gain_ref[:, columns]
                    start = (side * per_block + j) * half_rows + i * rows
                    outs[shift][start : start + rows, :] = piece.astype(jnp.bfloat16)
        leaving.append(pltpu.make_async_copy(outs[shift], blocks_any[shift], out_sems.at[shift]))
        leaving[-1].start()
    leaving.append(pltpu.make_async_copy(outs[0], own_any, out_sems.at[GROUPS]))
    leaving[-1].start()
    for copy in leaving:
        copy.wait()


def fetch_kernel(from_any, to_ref, sem):
    copy = pltpu.make_async_copy(from_any, to_ref, sem)
    copy.start()
    copy.wait()


def project_kernel(shifts, *refs):
    count = len(shifts)
    blocks, rest = refs[: 2 * count], refs[2 * count :]
    near_key, near_value, far_key, far_value = rest[:4]
    earlier, outs, (query_ref, lhs_ref) = rest[4 : -2 - count], rest[-2 - count : -2], rest[-2:]
    depth = near_key.shape[0]
    pieces = 2 * depth // LANES
    half_rows = (lhs_ref.shape[0] - 16) // (2 * count)
    rows = 2 * half_rows
    tails = []
    for i, block in enumerate(blocks):
        for j in range(pieces):
            lhs_ref[i * half_rows : (i + 1) * half_rows, j * LANES : (j + 1) * LANES] = block[
                j * half_rows : (j + 1) * half_rows, :
            ]
        tail = block[pieces * half_rows : pieces * half_rows + pieces, :].astype(jnp.float32)
        tails.append(jnp.concatenate([tail[j : j + 1] for j in range(pieces)], 1))
    tails.append(jnp.zeros((16 - len(tails), 2 * depth), jnp.float32))
    lines = query_ref.shape[0] // GROUPS
    if earlier:
        query_ref[...] = earlier[0][...]
    for i, shift in enumerate(shifts):
        block = blocks[2 * i]
        query_ref[shift * lines : (shift + 1) * lines, :] = block[block.shape[0] - lines :, :]
    total = count * rows
    lhs_ref[total : total + 16, :] = jnp.concatenate(tails, 0).astype(jnp.bfloat16)

    def product(near, far):
        return jnp.dot(
            lhs_ref[:, :depth], near[...], preferred_element_type=jnp.float32
        ) + jnp.dot(lhs_ref[:, depth:], far[...], preferred_element_type=jnp.float32)

    keys = product(near_key, far_key)
    values = product(near_value, far_value)
    high = keys.astype(jnp.bfloat16).astype(jnp.float32)
    low = keys - high
    columns = []
    for array in (high, low, values):
        for j in range(array.shape[1] // LANES):
            columns.append(array[:, j * LANES : (j + 1) * LANES])
    for i, out in enumerate(outs):
        for k, column in enumerate(columns):
            out[k * rows : (k + 1) * rows, :] = column[i * rows : (i + 1) * rows].astype(jnp.bfloat16)
        ends = [c[total + 2 * i : total + 2 * i + 2] for c in columns]
        ends.append(jnp.zeros((16 - 2 * len(columns), LANES), jnp.float32))
        out[len(columns) * rows :, :] = jnp.concatenate(ends, 0).astype(jnp.bfloat16)


def head_queries(parts, head, width):
    sharing = QUERY_HEADS // KEY_VALUE_HEADS
    lines = sharing * width // HEAD_SIZE
    each = parts[0].shape[0] // GROUPS
    found = []
    for group in range(GROUPS):
        for part in parts:
            tiles = part[group * each : (group + 1) * each, :].astype(jnp.float32)
            for line in range(head * sharing, (head + 1) * sharing):
                found += [tiles[start : start + 1] for start in range(line, each, lines)]
    return jnp.concatenate(found, 0).astype(jnp.bfloat16)


def times_transposed(a, b):
    return lax.dot_general(a, b, (((1,), (1,)), ((), ())), preferred_element_type=jnp.float32)


def loaded_kernel(place_ref, table_ref, split_ref, *refs):
    parts = refs[:PAIR]
    key_ref, value_ref, top_ref, total_ref, numer_ref, query_ref = refs[PAIR:]
    ctx = place_ref[1]
    slots, page, width = key_ref.shape
    heads = width // HEAD_SIZE
    split = split_ref[0]
    live = []
    for s in range(slots):
        hit = jnp.int32(0)
        for p in range(table_ref.shape[0]):
            hit = hit | ((table_ref[p] == ctx * slots + s) & (p >= split)).astype(jnp.int32)
        live.append(hit)
    for head in range(heads):
        columns = slice(head * HEAD_SIZE, (head + 1) * HEAD_SIZE)
        queries = head_queries(parts, head, width)
        count = queries.shape[0]
        query_ref[head * count : (head + 1) * count, :] = queries
        scores = [
            jnp.where(live[s] > 0, times_transposed(queries, key_ref[s, :, columns]) * SCALE, masked_score)
            for s in range(slots)
        ]
        top = scores[0].max(-1, keepdims=True)
        for s in range(1, slots):
            top = jnp.maximum(top, scores[s].max(-1, keepdims=True))
        total = jnp.zeros((count, 1), jnp.float32)
        numer = jnp.zeros((count, HEAD_SIZE), jnp.float32)
        for s in range(slots):
            expos = jnp.where(live[s] > 0, jnp.exp(scores[s] - top), 0.0)
            total += expos.sum(-1, keepdims=True)
            numer += jnp.dot(
                expos.astype(jnp.bfloat16), value_ref[s, :, columns], preferred_element_type=jnp.float32
            )
        rows = slice(head * count, (head + 1) * count)
        top_ref[rows, :] = jnp.broadcast_to(top, (count, LANES))
        total_ref[rows, :] = jnp.broadcast_to(total, (count, LANES))
        numer_ref[rows, :] = numer


def sum_kernel(one, other, out):
    out[...] = one[...].astype(jnp.float32) + other[...].astype(jnp.float32)


def front_kernel(
    place_ref, split_ref, early, *refs
):
    received = refs[: GROUPS - 2]
    (key_bias, value_bias, cosine_ref, sine_ref, query_ref, top_ref, total_ref, numer_ref) = refs[
        GROUPS - 2 : GROUPS + 6
    ]
    front_key, front_value = refs[GROUPS + 6 : GROUPS + 8]
    outs = refs[GROUPS + 8 :]
    core, ctx = place_ref[0], place_ref[1]
    rows, width = front_key.shape
    half_rows = rows // 2
    heads = width // HEAD_SIZE
    sharing = QUERY_HEADS // KEY_VALUE_HEADS
    count = query_ref.shape[0] // heads
    own_queries = count // sharing // (GROUPS * PAIR)
    visible = ctx < split_ref[0]

    def summed(start, size):
        value = early[start : start + size, :]
        for ref in received:
            value += ref[start : start + size, :].astype(jnp.float32)
        return value

    ends = summed(3 * heads * rows, 16)
    row = lax.broadcasted_iota(jnp.int32, (count, 16), 0)
    query_position = (ctx ^ (row // (own_queries * sharing))) * own_queries + row % own_queries
    end_column = lax.broadcasted_iota(jnp.int32, (count, 16), 1)
    end_position = ctx * 2 + jnp.where(end_column == 0, core, 1 - core)
    end_seen = (end_column < 2) & (end_position <= query_position)
    pad = jnp.zeros((14, HEAD_SIZE), jnp.float32)
    for head in range(heads):
        columns = slice(head * HEAD_SIZE, (head + 1) * HEAD_SIZE)
        raw = summed(head * rows, rows) + summed((heads + head) * rows, rows)
        value = (summed((2 * heads + head) * rows, rows) + value_bias[:, columns]).astype(jnp.bfloat16)
        end_raw = ends[2 * head : 2 * head + 2] + ends[2 * (heads + head) : 2 * (heads + head) + 2]
        end_value = ends[2 * (2 * heads + head) : 2 * (2 * heads + head) + 2] + value_bias[:, columns]
        end_raw = jnp.concatenate([end_raw + key_bias[:, columns], pad], 0)
        end_value = jnp.concatenate([end_value, pad], 0).astype(jnp.bfloat16)
        raw = raw + key_bias[:, columns]

        def rotated(k, part):
            turned = pltpu.roll(k, HEAD_SIZE // 2, 1)
            return (k * cosine_ref[part, :] + turned * sine_ref[part, :]).astype(jnp.bfloat16)

        key = rotated(raw, slice(0, rows))
        end_key = rotated(end_raw, slice(rows, rows + 16))
        for half in range(2):
            to = pl.ds(pl.multiple_of(lax.rem(core + half, 2) * half_rows, half_rows), half_rows)
            front_key[to, columns] = key[half * half_rows : (half + 1) * half_rows]
            front_value[to, columns] = value[half * half_rows : (half + 1) * half_rows]
        part = slice(head * count, (head + 1) * count)
        queries = query_ref[part, :]
        scores = jnp.where(visible, times_transposed(queries, key) * SCALE, masked_score)
        end_scores = jnp.where(end_seen, times_transposed(queries, end_key) * SCALE, masked_score)
        old_top = top_ref[part, :]
        top = jnp.maximum(scores.max(-1, keepdims=True), end_scores.max(-1, keepdims=True))
        top = jnp.maximum(old_top, top)
        factor = jnp.exp(old_top - top)
        expos = jnp.where(visible, jnp.exp(scores - top), 0.0)
        end_expos = jnp.where(end_seen, jnp.exp(end_scores - top[:, :16]), 0.0)
        total = total_ref[part, :] * factor + (
            expos.sum(-1, keepdims=True) + end_expos.sum(-1, keepdims=True)
        )
        numer = (
            numer_ref[part, :] * factor
            + jnp.dot(expos.astype(jnp.bfloat16), value, preferred_element_type=jnp.float32)
            + jnp.dot(end_expos.astype(jnp.bfloat16), end_value, preferred_element_type=jnp.float32)
        )
        stats = (kept_stats(top[:, 0:1], total[:, 0:1]), sent_stats(top[:, 0:1], total[:, 0:1]))
        each = own_queries * sharing
        for slot in range(GROUPS * PAIR):
            start = (slot % PAIR * 2 * heads + head) * each
            at = slice(slot * each, (slot + 1) * each)
            out = outs[slot // PAIR]
            out[start : start + each, :] = numer[at].astype(out.dtype)
            out[start + heads * each : start + (heads + 1) * each, :] = stats[slot >= PAIR][at]


def kept_stats(top, total):
    lane = lax.broadcasted_iota(jnp.int32, (top.shape[0], LANES), 1)
    return jnp.where(lane < LANES // 2, top, total)


def sent_stats(top, total):
    terms = []
    for rest, count in ((top, 3), (total, 2)):
        for _ in range(count):
            term = rest.astype(jnp.bfloat16).astype(jnp.float32)
            terms.append(term)
            rest = rest - term
    part = lax.broadcasted_iota(jnp.int32, (top.shape[0], LANES), 1) // 16
    stats = jnp.broadcast_to(terms[-1], part.shape)
    for i, term in enumerate(terms[:-1]):
        stats = jnp.where(part == i, term, stats)
    return stats.astype(jnp.bfloat16)


def merged(kept, others, start, rows):
    half = LANES // 2
    stats = kept[start + rows : start + 2 * rows, :]
    tops, totals = [stats[:, 0:1]], [stats[:, half : half + 1]]
    numers = [kept[start : start + rows, :]]
    for other in others:
        terms = other[start + rows : start + 2 * rows, :].astype(jnp.float32)
        tops.append((terms[:, 0:1] + terms[:, 16:17]) + terms[:, 32:33])
        totals.append(terms[:, 48:49] + terms[:, 64:65])
        numers.append(other[start : start + rows, :].astype(jnp.float32))
    top = functools.reduce(jnp.maximum, tops)
    factors = [jnp.exp(t - top) for t in tops]
    total = sum(f * t for f, t in zip(factors, totals))
    numer = sum(f * n for f, n in zip(factors, numers))
    return numer, top, total


def merge_kernel(kept, *refs):
    others, (keep_ref, send_ref) = refs[:-2], refs[-2:]
    each = keep_ref.shape[0]
    rows = each // 2
    numer, top, total = merged(kept, others, 0, rows)
    keep_ref[:rows, :] = numer
    keep_ref[rows:, :] = kept_stats(top, total)
    numer, top, total = merged(kept, others, each, rows)
    send_ref[:rows, :] = numer.astype(jnp.bfloat16)
    send_ref[rows:, :] = sent_stats(top, total)


def last_kernel(kept, *refs):
    others, out_ref = refs[:-1], refs[-1]
    numer, _, total = merged(kept, others, 0, kept.shape[0] // 2)
    result = numer / total
    queries = out_ref.shape[0]
    pieces = [result[s : s + queries] for s in range(0, result.shape[0], queries)]
    out_ref[...] = jnp.concatenate(pieces, 1).astype(jnp.bfloat16)


def exchange_plan(
    hidden,
    suffix_hidden,
    norm_gain,
    key_matrix,
    value_matrix,
    key_offset_bias,
    value_offset_bias,
    suffix_query_rows,
    slot_keys,
    slot_values,
    page_slot_table,
    split_page,
):
    n_ctx = GROUPS * PAIR
    ctx = lax.axis_index("ctx").astype(jnp.int32)
    core = lax.axis_index("tp").astype(jnp.int32)
    place = jnp.stack([core, ctx])
    rows, features = hidden.shape
    half_rows = rows // 2
    width = key_matrix.shape[1]
    query_width = suffix_query_rows.shape[1]
    prefix_len = page_slot_table.shape[0] * slot_keys.shape[1]
    smem = pl.BlockSpec(memory_space=pltpu.SMEM)
    vmem = pl.BlockSpec(memory_space=pltpu.VMEM)
    params = pltpu.CompilerParams(vmem_limit_bytes=48 * 1024 * 1024)

    def move(array, target):
        pairs = []
        for c in range(n_ctx):
            for t in range(2):
                to_c, to_t = target(c, t)
                pairs.append((c * 2 + t, to_c * 2 + to_t))
        return lax.ppermute(array, ("ctx", "tp"), pairs)

    def partner(away):
        return lambda c, t: (c ^ away, t)

    def along(shift):
        return partner(shift * PAIR)

    def beside(c, t):
        return (c ^ 1, t)

    def sibling(c, t):
        return (c, 1 - t)

    hbm = pl.BlockSpec(memory_space=pltpu.HBM)
    pieces = features // GROUPS // LANES
    own_queries = suffix_query_rows.shape[0]
    lines = query_width // LANES
    block_rows = pieces * half_rows + pieces + own_queries * lines
    *blocks, own = pl.pallas_call(
        norm_kernel,
        in_specs=[hbm] * 4,
        out_specs=[hbm] * (GROUPS + 1),
        out_shape=[jax.ShapeDtypeStruct((block_rows, LANES), jnp.bfloat16)] * (GROUPS + 1),
        scratch_shapes=[
            pltpu.VMEM((half_rows, features), jnp.bfloat16),
            pltpu.VMEM(suffix_hidden.shape, jnp.bfloat16),
            pltpu.VMEM((1, features), jnp.float32),
            pltpu.VMEM(suffix_query_rows.shape, jnp.bfloat16),
            pltpu.VMEM((1, features), jnp.float32),
        ]
        + [pltpu.VMEM((block_rows, LANES), jnp.bfloat16)] * GROUPS
        + [
            pltpu.SemaphoreType.DMA((CHUNKS + 3,)),
            pltpu.SemaphoreType.DMA((GROUPS + 1,)),
        ],
        compiler_params=pltpu.CompilerParams(vmem_limit_bytes=60 * 1024 * 1024),
        cost_estimate=pl.CostEstimate(
            flops=4 * half_rows * features, bytes_accessed=4 * half_rows * features, transcendentals=0
        ),
        name="norm_rows",
    )(
        suffix_query_rows,
        hidden,
        suffix_hidden,
        norm_gain.reshape(1, features),
    )
    *weights, blocks[1] = lax.optimization_barrier((key_matrix, value_matrix, blocks[1]))
    far = [move(matrix, beside) for matrix in weights]

    mine = {s: move(blocks[s], along(s)) for s in far_first()}
    inverse_freq = rope_base ** (
        -(jnp.arange(HEAD_SIZE // 2, dtype=jnp.float32) * (2.0 / HEAD_SIZE))
    )
    row = jnp.arange(rows + 16, dtype=jnp.int32)
    front_position = ctx * rows + (row + core * half_rows) % rows
    end_position = prefix_len + ctx * 2 + jnp.where(row == rows, core, 1 - core)
    position = jnp.where(row < rows, front_position, end_position)
    angles = position.astype(jnp.float32)[:, None] * inverse_freq[None, :]
    cosine, sine = jnp.cos(angles), jnp.sin(angles)
    cosine = jnp.concatenate([cosine, cosine], 1)
    sine = jnp.concatenate([-sine, sine], 1)

    first = far_first()[0]
    mine[0] = pl.pallas_call(
        fetch_kernel,
        in_specs=[hbm],
        out_specs=vmem,
        out_shape=jax.ShapeDtypeStruct(own.shape, own.dtype),
        scratch_shapes=[pltpu.SemaphoreType.DMA],
        compiler_params=params,
        cost_estimate=pl.CostEstimate(flops=0, bytes_accessed=64 * 1024 * 1024, transcendentals=0),
        name="fetch_own",
    )(own)
    mine[first], mine[0], cosine, sine = lax.optimization_barrier(
        (mine[first], mine[0], cosine, sine)
    )
    blocks[0], far[0] = lax.optimization_barrier((blocks[0], far[0]))
    theirs = {s: move(blocks[0] if s == 0 else mine[s], sibling) for s in [0] + far_first()}

    part_rows = 3 * (width // LANES) * rows + 16
    partials, own_tiles = {}, []
    for shifts in ((0, first), tuple(far_first()[1:])):
        *found, tiles = pl.pallas_call(
            functools.partial(project_kernel, shifts),
            in_specs=[vmem] * (2 * len(shifts) + 4 + len(own_tiles)),
            out_specs=[vmem] * (len(shifts) + 1),
            out_shape=[jax.ShapeDtypeStruct((part_rows, LANES), jnp.bfloat16)] * len(shifts)
            + [jax.ShapeDtypeStruct((GROUPS * own_queries * lines, LANES), jnp.bfloat16)],
            scratch_shapes=[
                pltpu.VMEM((len(shifts) * rows + 16, PAIR * features // n_ctx), jnp.bfloat16)
            ],
            compiler_params=params,
            cost_estimate=pl.CostEstimate(
                flops=2 * len(shifts) * rows * 2 * width * features // GROUPS,
                bytes_accessed=6 * 1024 * 1024,
                transcendentals=0,
            ),
            name="project",
        )(
            *[part[s] for s in shifts for part in (mine, theirs)],
            key_matrix,
            value_matrix,
            *far,
            *own_tiles,
        )
        partials.update(zip(shifts, found))
        own_tiles = [tiles]
    (own_tiles,) = own_tiles
    received = [move(partials[s], along(s)) for s in far_first()]
    early = pl.pallas_call(
        sum_kernel,
        in_specs=[vmem] * 2,
        out_specs=vmem,
        out_shape=jax.ShapeDtypeStruct((part_rows, LANES), jnp.float32),
        compiler_params=params,
        cost_estimate=pl.CostEstimate(flops=0, bytes_accessed=16 * 1024 * 1024, transcendentals=0),
        name="sum_early",
    )(partials[0], received[0])
    beside_tiles = move(own_tiles, beside)

    states = n_ctx * own_queries * query_width // HEAD_SIZE
    state = jax.ShapeDtypeStruct((states, LANES), jnp.float32)
    top, total, numer, queries = pl.pallas_call(
        loaded_kernel,
        in_specs=[smem, smem, smem] + [vmem] * (PAIR + 2),
        out_specs=[vmem] * 4,
        out_shape=[state] * 3 + [jax.ShapeDtypeStruct((states, LANES), jnp.bfloat16)],
        compiler_params=params,
        cost_estimate=pl.CostEstimate(
            flops=4 * states * slot_keys.shape[0] * slot_keys.shape[1] * HEAD_SIZE,
            bytes_accessed=4 * slot_keys.size,
            transcendentals=states * slot_keys.shape[0] * slot_keys.shape[1],
        ),
        name="loaded_attention",
    )(place, page_slot_table, split_page, own_tiles, beside_tiles, slot_keys, slot_values)


    def payload(kind, slots):
        return jax.ShapeDtypeStruct((2 * slots * states // n_ctx, LANES), kind)

    row_shape = jax.ShapeDtypeStruct((rows, width), jnp.bfloat16)
    front_key, front_value, kept, *sent = pl.pallas_call(
        front_kernel,
        in_specs=[smem, smem] + [vmem] * (GROUPS + 7),
        out_specs=[vmem] * (2 + GROUPS),
        out_shape=[row_shape] * 2 + [payload(jnp.float32, PAIR)] + [payload(jnp.bfloat16, PAIR)] * (GROUPS - 1),
        compiler_params=params,
        cost_estimate=pl.CostEstimate(flops=4 * states * rows * HEAD_SIZE, bytes_accessed=2 * 1024 * 1024, transcendentals=states * rows),
        name="front_attention",
    )(
        place,
        split_page,
        early,
        *received[1:],
        key_offset_bias.reshape(1, width),
        value_offset_bias.reshape(1, width),
        cosine,
        sine,
        queries,
        top,
        total,
        numer,
    )
    kept, sent = pl.pallas_call(
        merge_kernel,
        in_specs=[vmem] * GROUPS,
        out_specs=[vmem] * 2,
        out_shape=[payload(jnp.float32, 1), payload(jnp.bfloat16, 1)],
        compiler_params=params,
        name="merge",
    )(kept, *[move(sent[s - 1], along(s)) for s in range(GROUPS - 1, 0, -1)])
    attended = pl.pallas_call(
        last_kernel,
        in_specs=[vmem] * 2,
        out_specs=vmem,
        out_shape=jax.ShapeDtypeStruct((own_queries, query_width), jnp.bfloat16),
        compiler_params=params,
        name="finish",
    )(kept, move(sent, beside))
    return (front_key, front_value, attended)


def solution(mesh):
    per_device = exchange_plan if mesh.shape["ctx"] == GROUPS * PAIR else gathered_plan
    return jax.shard_map(
        per_device,
        mesh=mesh,
        in_specs=(
            P(("req", "ctx"), None),
            P(("req", "ctx"), None),
            P(),
            P("ctx", "tp"),
            P("ctx", "tp"),
            P("tp"),
            P("tp"),
            P(("req", "ctx"), "tp"),
            P(("req", "ctx"), None, "tp"),
            P(("req", "ctx"), None, "tp"),
            P("req"),
            P("req"),
        ),
        out_specs=(P(("req", "ctx"), "tp"), P(("req", "ctx"), "tp"), P(("req", "ctx"), "tp")),
        check_vma=False,
    )
```

```python
import functools
import math

import jax
import jax.numpy as jnp
from jax import lax
from jax.experimental import pallas as pl
from jax.experimental.pallas import tpu as pltpu
from jax.sharding import PartitionSpec as P

QUERY_HEADS = 32
KEY_VALUE_HEADS = 4
HEAD_SIZE = 128


epsilon = 1e-06
rope_base = 1000000.0
masked_score = -1e30


def rms_rows(matrix, norm_gain):
    widened = matrix.astype(jnp.float32)
    inverse = lax.rsqrt(jnp.mean(widened * widened, axis=-1, keepdims=True) + epsilon)
    return (widened * inverse * norm_gain).astype(jnp.bfloat16)


def rotate(key_rows, positions, head_dim):
    row_count = key_rows.shape[0]
    split_heads = key_rows.reshape(row_count, -1, head_dim)
    half_dim = head_dim // 2
    inverse_freq = rope_base ** (-(jnp.arange(half_dim, dtype=jnp.float32) * (2.0 / head_dim)))
    angles = positions.astype(jnp.float32)[:, None] * inverse_freq[None, :]
    cosine = jnp.concatenate([jnp.cos(angles), jnp.cos(angles)], -1)[:, None, :]
    sine = jnp.concatenate([jnp.sin(angles), jnp.sin(angles)], -1)[:, None, :]
    turned = jnp.concatenate([-split_heads[..., half_dim:], split_heads[..., :half_dim]], -1)
    return (split_heads * cosine + turned * sine).reshape(row_count, -1)


def gathered_plan(
    hidden,
    suffix_hidden,
    norm_gain,
    key_matrix,
    value_matrix,
    key_offset_bias,
    value_offset_bias,
    suffix_query_rows,
    slot_keys,
    slot_values,
    page_slot_table,
    split_page,
):
    ctx_index = lax.axis_index("ctx")
    queries = lax.all_gather(suffix_query_rows, "ctx", axis=0, tiled=True)
    front_rows = hidden.shape[0]
    suffix_rows = suffix_hidden.shape[0]
    page_size = slot_keys.shape[1]
    slot_count = slot_keys.shape[0]
    total_pages = page_slot_table.shape[0]
    prefix_len = total_pages * page_size
    normed = rms_rows(jnp.concatenate([hidden, suffix_hidden], 0), norm_gain)
    col_width = key_matrix.shape[1]

    def accumulate(block_rows):
        return jnp.dot(normed, block_rows, preferred_element_type=jnp.float32)

    key_acc = accumulate(lax.all_gather(key_matrix, "ctx", axis=0, tiled=True))
    value_acc = accumulate(lax.all_gather(value_matrix, "ctx", axis=0, tiled=True))
    front_pos = ctx_index * front_rows + jnp.arange(front_rows, dtype=jnp.int32)
    suffix_pos = prefix_len + ctx_index * suffix_rows + jnp.arange(suffix_rows, dtype=jnp.int32)
    new_keys = rotate(
        key_acc + key_offset_bias, jnp.concatenate([front_pos, suffix_pos], 0), HEAD_SIZE
    ).astype(jnp.bfloat16)
    new_values = (value_acc + value_offset_bias).astype(jnp.bfloat16)
    cut_pos = split_page[0] * page_size
    global_slot = ctx_index * slot_count + jnp.arange(slot_count, dtype=jnp.int32)
    page_index = jnp.arange(total_pages, dtype=jnp.int32)
    slot_hits = (page_slot_table[None, :] == global_slot[:, None]) & (
        page_index[None, :] >= split_page[0]
    )
    slot_live = jnp.max(slot_hits.astype(jnp.int32), axis=1) > 0
    every_key = jnp.concatenate(
        [new_keys[:front_rows], slot_keys.reshape(-1, col_width), new_keys[front_rows:]], 0
    )
    every_value = jnp.concatenate(
        [new_values[:front_rows], slot_values.reshape(-1, col_width), new_values[front_rows:]], 0
    )
    query_count = queries.shape[0]
    query_pos = prefix_len + jnp.arange(query_count, dtype=jnp.int32)
    prefix_seen = jnp.concatenate([front_pos < cut_pos, jnp.repeat(slot_live, page_size)], 0)
    suffix_seen = suffix_pos[None, :] <= query_pos[:, None]
    visible = jnp.concatenate(
        [jnp.broadcast_to(prefix_seen[None, :], (query_count, prefix_seen.shape[0])), suffix_seen],
        1,
    )
    visible_wide = visible[:, None, :]
    sharing_count = QUERY_HEADS // KEY_VALUE_HEADS
    local_heads = col_width // HEAD_SIZE
    grouped_heads = queries.reshape(query_count, local_heads, sharing_count, HEAD_SIZE)
    top_list = []
    total_list = []
    numer_list = []
    for current_head in range(local_heads):
        head_keys = every_key[:, current_head * HEAD_SIZE : (current_head + 1) * HEAD_SIZE]
        head_values = every_value[:, current_head * HEAD_SIZE : (current_head + 1) * HEAD_SIZE]
        scores = jnp.einsum(
            "qgd,ld->qgl",
            grouped_heads[:, current_head],
            head_keys,
            preferred_element_type=jnp.float32,
        ) * (1.0 / math.sqrt(HEAD_SIZE))
        scores = jnp.where(visible_wide, scores, masked_score)
        row_top = jnp.max(scores, axis=-1)
        expos = jnp.where(visible_wide, jnp.exp(scores - row_top[..., None]), 0.0)
        total_list.append(jnp.sum(expos, axis=-1))
        top_list.append(row_top)
        numer_list.append(
            jnp.einsum(
                "qgl,ld->qgd",
                expos.astype(jnp.bfloat16),
                head_values,
                preferred_element_type=jnp.float32,
            )
        )
    row_top = jnp.stack(top_list, 1)
    weight_total = jnp.stack(total_list, 1)
    numer = jnp.stack(numer_list, 1)
    global_top = lax.pmax(row_top, "ctx")
    factor = jnp.exp(row_top - global_top)
    own_total, own_numer = (
        lax.psum_scatter(
            (weight_total * factor).reshape(query_count, -1), "ctx", scatter_dimension=0, tiled=True
        ),
        lax.psum_scatter(
            (numer * factor[..., None]).reshape(query_count, -1),
            "ctx",
            scatter_dimension=0,
            tiled=True,
        ),
    )
    own_total = own_total.reshape(suffix_rows, local_heads, sharing_count)
    own_numer = own_numer.reshape(suffix_rows, local_heads, sharing_count, HEAD_SIZE)
    attended = (own_numer / own_total[..., None]).reshape(suffix_rows, -1).astype(jnp.bfloat16)
    return (new_keys[:front_rows], new_values[:front_rows], attended)

GROUPS = 4
PAIR = 2
LANES = 128
SCALE = 1.0 / math.sqrt(HEAD_SIZE)


def row_scale(values):
    mean = jnp.sum(values * values, axis=-1, keepdims=True) * (1.0 / values.shape[-1])
    return lax.rsqrt(mean + epsilon)


CHUNKS = 4


def far_first():
    return sorted(range(1, GROUPS), key=lambda s: s < GROUPS // 2)


def norm_kernel(query_any, hidden_any, suffix_any, gain_any, *rest):
    blocks_any, own_any = rest[:GROUPS], rest[GROUPS]
    hidden_ref, suffix_ref, gain_ref, query_ref, tail_ref = rest[GROUPS + 1 : GROUPS + 6]
    outs, (sems, out_sems) = rest[GROUPS + 6 : -2], rest[-2:]
    core, ctx = lax.axis_index("tp"), lax.axis_index("ctx")
    z, x = ctx // PAIR, ctx % PAIR
    half_rows, features = hidden_ref.shape
    rows = half_rows // CHUNKS
    block = features // (GROUPS * PAIR)
    per_block = block // LANES
    pieces = PAIR * per_block
    copies = [
        pltpu.make_async_copy(gain_any, gain_ref, sems.at[CHUNKS]),
        pltpu.make_async_copy(suffix_any, suffix_ref, sems.at[CHUNKS + 1]),
        pltpu.make_async_copy(query_any, query_ref, sems.at[CHUNKS + 2]),
    ]
    for i in range(CHUNKS):
        start = pl.multiple_of(core * half_rows + i * rows, rows)
        copies.append(
            pltpu.make_async_copy(
                hidden_any.at[pl.ds(start, rows)], hidden_ref.at[i * rows : (i + 1) * rows], sems.at[i]
            )
        )
    for copy in copies:
        copy.start()

    def offset(shift, side, j):
        owner = (z ^ shift) * PAIR + (x ^ side)
        return pl.multiple_of(owner * block + j * LANES, LANES)

    copies[0].wait()
    copies[1].wait()
    copies[2].wait()
    query_rows = query_ref[...].astype(jnp.float32)
    lines = query_rows.shape[1] // LANES
    for r in range(query_rows.shape[0]):
        tile = [query_rows[r : r + 1, j * LANES : (j + 1) * LANES] for j in range(lines)]
        tile = jnp.concatenate(tile, 0).astype(jnp.bfloat16)
        start = pieces * half_rows + pieces + r * lines
        for out in outs:
            out[start : start + lines, :] = tile

    both = suffix_ref[...].astype(jnp.float32)
    normed = both * row_scale(both) * gain_ref[...]
    tail_ref[...] = jnp.where(core == 0, normed[0:1], normed[1:2])
    for shift in range(GROUPS):
        ends = [
            tail_ref[:, pl.ds(offset(shift, side, j), LANES)]
            for side in range(PAIR)
            for j in range(per_block)
        ]
        start = pieces * half_rows
        outs[shift][start : start + pieces, :] = jnp.concatenate(ends, 0).astype(jnp.bfloat16)
    inverses = []
    for i in range(CHUNKS):
        copies[3 + i].wait()
        inverses.append(row_scale(hidden_ref[i * rows : (i + 1) * rows, :].astype(jnp.float32)))
    leaving = []
    for shift in far_first() + [0]:
        for side in range(PAIR):
            for j in range(per_block):
                columns = pl.ds(offset(shift, side, j), LANES)
                for i in range(CHUNKS):
                    piece = hidden_ref[i * rows : (i + 1) * rows, columns].astype(jnp.float32)
                    piece = piece * inverses[i] * gain_ref[:, columns]
                    start = (side * per_block + j) * half_rows + i * rows
                    outs[shift][start : start + rows, :] = piece.astype(jnp.bfloat16)
        leaving.append(pltpu.make_async_copy(outs[shift], blocks_any[shift], out_sems.at[shift]))
        leaving[-1].start()
    leaving.append(pltpu.make_async_copy(outs[0], own_any, out_sems.at[GROUPS]))
    leaving[-1].start()
    for copy in leaving:
        copy.wait()


def fetch_kernel(from_any, to_ref, sem):
    copy = pltpu.make_async_copy(from_any, to_ref, sem)
    copy.start()
    copy.wait()


def project_kernel(shifts, *refs):
    count = len(shifts)
    blocks, rest = refs[: 2 * count], refs[2 * count :]
    near_key, near_value, far_key, far_value = rest[:4]
    earlier, outs, (query_ref, lhs_ref) = rest[4 : -2 - count], rest[-2 - count : -2], rest[-2:]
    depth = near_key.shape[0]
    pieces = 2 * depth // LANES
    half_rows = (lhs_ref.shape[0] - 16) // (2 * count)
    rows = 2 * half_rows
    tails = []
    for i, block in enumerate(blocks):
        for j in range(pieces):
            lhs_ref[i * half_rows : (i + 1) * half_rows, j * LANES : (j + 1) * LANES] = block[
                j * half_rows : (j + 1) * half_rows, :
            ]
        tail = block[pieces * half_rows : pieces * half_rows + pieces, :].astype(jnp.float32)
        tails.append(jnp.concatenate([tail[j : j + 1] for j in range(pieces)], 1))
    tails.append(jnp.zeros((16 - len(tails), 2 * depth), jnp.float32))
    lines = query_ref.shape[0] // GROUPS
    if earlier:
        query_ref[...] = earlier[0][...]
    for i, shift in enumerate(shifts):
        block = blocks[2 * i]
        query_ref[shift * lines : (shift + 1) * lines, :] = block[block.shape[0] - lines :, :]
    total = count * rows
    lhs_ref[total : total + 16, :] = jnp.concatenate(tails, 0).astype(jnp.bfloat16)

    def product(near, far):
        return jnp.dot(
            lhs_ref[:, :depth], near[...], preferred_element_type=jnp.float32
        ) + jnp.dot(lhs_ref[:, depth:], far[...], preferred_element_type=jnp.float32)

    keys = product(near_key, far_key)
    values = product(near_value, far_value)
    high = keys.astype(jnp.bfloat16).astype(jnp.float32)
    low = keys - high
    columns = []
    for array in (high, low, values):
        for j in range(array.shape[1] // LANES):
            columns.append(array[:, j * LANES : (j + 1) * LANES])
    for i, out in enumerate(outs):
        for k, column in enumerate(columns):
            out[k * rows : (k + 1) * rows, :] = column[i * rows : (i + 1) * rows].astype(jnp.bfloat16)
        ends = [c[total + 2 * i : total + 2 * i + 2] for c in columns]
        ends.append(jnp.zeros((16 - 2 * len(columns), LANES), jnp.float32))
        out[len(columns) * rows :, :] = jnp.concatenate(ends, 0).astype(jnp.bfloat16)


def head_queries(parts, head, width):
    sharing = QUERY_HEADS // KEY_VALUE_HEADS
    lines = sharing * width // HEAD_SIZE
    each = parts[0].shape[0] // GROUPS
    found = []
    for group in range(GROUPS):
        for part in parts:
            tiles = part[group * each : (group + 1) * each, :].astype(jnp.float32)
            for line in range(head * sharing, (head + 1) * sharing):
                found += [tiles[start : start + 1] for start in range(line, each, lines)]
    return jnp.concatenate(found, 0).astype(jnp.bfloat16)


def times_transposed(a, b):
    return lax.dot_general(a, b, (((1,), (1,)), ((), ())), preferred_element_type=jnp.float32)


def loaded_kernel(place_ref, table_ref, split_ref, *refs):
    parts = refs[:PAIR]
    key_ref, value_ref, top_ref, total_ref, numer_ref, query_ref = refs[PAIR:]
    ctx = place_ref[1]
    slots, page, width = key_ref.shape
    heads = width // HEAD_SIZE
    split = split_ref[0]
    live = []
    for s in range(slots):
        hit = jnp.int32(0)
        for p in range(table_ref.shape[0]):
            hit = hit | ((table_ref[p] == ctx * slots + s) & (p >= split)).astype(jnp.int32)
        live.append(hit)
    for head in range(heads):
        columns = slice(head * HEAD_SIZE, (head + 1) * HEAD_SIZE)
        queries = head_queries(parts, head, width)
        count = queries.shape[0]
        query_ref[head * count : (head + 1) * count, :] = queries
        scores = [
            jnp.where(live[s] > 0, times_transposed(queries, key_ref[s, :, columns]) * SCALE, masked_score)
            for s in range(slots)
        ]
        top = scores[0].max(-1, keepdims=True)
        for s in range(1, slots):
            top = jnp.maximum(top, scores[s].max(-1, keepdims=True))
        total = jnp.zeros((count, 1), jnp.float32)
        numer = jnp.zeros((count, HEAD_SIZE), jnp.float32)
        for s in range(slots):
            expos = jnp.where(live[s] > 0, jnp.exp(scores[s] - top), 0.0)
            total += expos.sum(-1, keepdims=True)
            numer += jnp.dot(
                expos.astype(jnp.bfloat16), value_ref[s, :, columns], preferred_element_type=jnp.float32
            )
        rows = slice(head * count, (head + 1) * count)
        top_ref[rows, :] = jnp.broadcast_to(top, (count, LANES))
        total_ref[rows, :] = jnp.broadcast_to(total, (count, LANES))
        numer_ref[rows, :] = numer


def sum_kernel(one, other, out):
    out[...] = one[...].astype(jnp.float32) + other[...].astype(jnp.float32)


def front_kernel(
    place_ref, split_ref, early, *refs
):
    received = refs[: GROUPS - 2]
    (key_bias, value_bias, cosine_ref, sine_ref, query_ref, top_ref, total_ref, numer_ref) = refs[
        GROUPS - 2 : GROUPS + 6
    ]
    key_any, value_any, *outs = refs[GROUPS + 6 : -3]
    front_key, front_value, sems = refs[-3:]
    core, ctx = place_ref[0], place_ref[1]
    rows, width = front_key.shape
    half_rows = rows // 2
    heads = width // HEAD_SIZE
    sharing = QUERY_HEADS // KEY_VALUE_HEADS
    count = query_ref.shape[0] // heads
    own_queries = count // sharing // (GROUPS * PAIR)
    visible = ctx < split_ref[0]

    def summed(start, size):
        value = early[start : start + size, :]
        for ref in received:
            value += ref[start : start + size, :].astype(jnp.float32)
        return value

    ends = summed(3 * heads * rows, 16)
    row = lax.broadcasted_iota(jnp.int32, (count, 16), 0)
    query_position = (ctx ^ (row // (own_queries * sharing))) * own_queries + row % own_queries
    end_column = lax.broadcasted_iota(jnp.int32, (count, 16), 1)
    end_position = ctx * 2 + jnp.where(end_column == 0, core, 1 - core)
    end_seen = (end_column < 2) & (end_position <= query_position)
    pad = jnp.zeros((14, HEAD_SIZE), jnp.float32)
    end_pairs = []
    for head in range(heads):
        columns = slice(head * HEAD_SIZE, (head + 1) * HEAD_SIZE)
        raw = summed(head * rows, rows) + summed((heads + head) * rows, rows)
        value = (summed((2 * heads + head) * rows, rows) + value_bias[:, columns]).astype(jnp.bfloat16)
        end_raw = ends[2 * head : 2 * head + 2] + ends[2 * (heads + head) : 2 * (heads + head) + 2]
        end_value = ends[2 * (2 * heads + head) : 2 * (2 * heads + head) + 2] + value_bias[:, columns]
        end_raw = jnp.concatenate([end_raw + key_bias[:, columns], pad], 0)
        end_value = jnp.concatenate([end_value, pad], 0).astype(jnp.bfloat16)
        raw = raw + key_bias[:, columns]

        def rotated(k, part):
            turned = pltpu.roll(k, HEAD_SIZE // 2, 1)
            return (k * cosine_ref[part, :] + turned * sine_ref[part, :]).astype(jnp.bfloat16)

        key = rotated(raw, slice(0, rows))
        end_key = rotated(end_raw, slice(rows, rows + 16))
        for half in range(2):
            to = pl.ds(pl.multiple_of(lax.rem(core + half, 2) * half_rows, half_rows), half_rows)
            front_key[to, columns] = key[half * half_rows : (half + 1) * half_rows]
            front_value[to, columns] = value[half * half_rows : (half + 1) * half_rows]
        end_pairs.append((key, value, end_key, end_value))
    leaving = [
        pltpu.make_async_copy(front_key, key_any, sems.at[0]),
        pltpu.make_async_copy(front_value, value_any, sems.at[1]),
    ]
    for copy in leaving:
        copy.start()
    for head, (key, value, end_key, end_value) in enumerate(end_pairs):
        part = slice(head * count, (head + 1) * count)
        queries = query_ref[part, :]
        scores = jnp.where(visible, times_transposed(queries, key) * SCALE, masked_score)
        end_scores = jnp.where(end_seen, times_transposed(queries, end_key) * SCALE, masked_score)
        old_top = top_ref[part, :]
        top = jnp.maximum(scores.max(-1, keepdims=True), end_scores.max(-1, keepdims=True))
        top = jnp.maximum(old_top, top)
        factor = jnp.exp(old_top - top)
        expos = jnp.where(visible, jnp.exp(scores - top), 0.0)
        end_expos = jnp.where(end_seen, jnp.exp(end_scores - top[:, :16]), 0.0)
        total = total_ref[part, :] * factor + (
            expos.sum(-1, keepdims=True) + end_expos.sum(-1, keepdims=True)
        )
        numer = (
            numer_ref[part, :] * factor
            + jnp.dot(expos.astype(jnp.bfloat16), value, preferred_element_type=jnp.float32)
            + jnp.dot(end_expos.astype(jnp.bfloat16), end_value, preferred_element_type=jnp.float32)
        )
        each = own_queries * sharing
        split = PAIR * each
        stats = jnp.concatenate(
            [
                kept_stats(top[:split, 0:1], total[:split, 0:1]),
                sent_stats(top[split:, 0:1], total[split:, 0:1]).astype(jnp.float32),
            ],
            0,
        )
        for slot in range(GROUPS * PAIR):
            start = (slot % PAIR * 2 * heads + head) * each
            at = slice(slot * each, (slot + 1) * each)
            out = outs[slot // PAIR]
            out[start : start + each, :] = numer[at].astype(out.dtype)
            out[start + heads * each : start + (heads + 1) * each, :] = stats[at].astype(out.dtype)
    for copy in leaving:
        copy.wait()


def kept_stats(top, total):
    lane = lax.broadcasted_iota(jnp.int32, (top.shape[0], LANES), 1)
    return jnp.where(lane < LANES // 2, top, total)


def sent_stats(top, total):
    terms = []
    for rest, count in ((top, 3), (total, 2)):
        for _ in range(count):
            term = rest.astype(jnp.bfloat16).astype(jnp.float32)
            terms.append(term)
            rest = rest - term
    part = lax.broadcasted_iota(jnp.int32, (top.shape[0], LANES), 1) // 16
    stats = jnp.broadcast_to(terms[-1], part.shape)
    for i, term in enumerate(terms[:-1]):
        stats = jnp.where(part == i, term, stats)
    return stats.astype(jnp.bfloat16)


def merged(kept, others, start, rows):
    half = LANES // 2
    stats = kept[start + rows : start + 2 * rows, :]
    tops, totals = [stats[:, 0:1]], [stats[:, half : half + 1]]
    numers = [kept[start : start + rows, :]]
    for other in others:
        terms = other[start + rows : start + 2 * rows, :].astype(jnp.float32)
        tops.append((terms[:, 0:1] + terms[:, 16:17]) + terms[:, 32:33])
        totals.append(terms[:, 48:49] + terms[:, 64:65])
        numers.append(other[start : start + rows, :].astype(jnp.float32))
    top = functools.reduce(jnp.maximum, tops)
    factors = [jnp.exp(t - top) for t in tops]
    total = sum(f * t for f, t in zip(factors, totals))
    numer = sum(f * n for f, n in zip(factors, numers))
    return numer, top, total


def merge_kernel(kept, *refs):
    others, (keep_ref, send_ref) = refs[:-2], refs[-2:]
    each = keep_ref.shape[0]
    rows = each // 2
    numer, top, total = merged(kept, others, 0, rows)
    keep_ref[:rows, :] = numer
    keep_ref[rows:, :] = kept_stats(top, total)
    numer, top, total = merged(kept, others, each, rows)
    send_ref[:rows, :] = numer.astype(jnp.bfloat16)
    send_ref[rows:, :] = sent_stats(top, total)


def last_kernel(kept, *refs):
    others, out_ref = refs[:-1], refs[-1]
    numer, _, total = merged(kept, others, 0, kept.shape[0] // 2)
    result = numer / total
    queries = out_ref.shape[0]
    pieces = [result[s : s + queries] for s in range(0, result.shape[0], queries)]
    out_ref[...] = jnp.concatenate(pieces, 1).astype(jnp.bfloat16)


def exchange_plan(
    hidden,
    suffix_hidden,
    norm_gain,
    key_matrix,
    value_matrix,
    key_offset_bias,
    value_offset_bias,
    suffix_query_rows,
    slot_keys,
    slot_values,
    page_slot_table,
    split_page,
):
    n_ctx = GROUPS * PAIR
    ctx = lax.axis_index("ctx").astype(jnp.int32)
    core = lax.axis_index("tp").astype(jnp.int32)
    place = jnp.stack([core, ctx])
    rows, features = hidden.shape
    half_rows = rows // 2
    width = key_matrix.shape[1]
    query_width = suffix_query_rows.shape[1]
    prefix_len = page_slot_table.shape[0] * slot_keys.shape[1]
    smem = pl.BlockSpec(memory_space=pltpu.SMEM)
    vmem = pl.BlockSpec(memory_space=pltpu.VMEM)
    params = pltpu.CompilerParams(vmem_limit_bytes=48 * 1024 * 1024)

    def move(array, target):
        pairs = []
        for c in range(n_ctx):
            for t in range(2):
                to_c, to_t = target(c, t)
                pairs.append((c * 2 + t, to_c * 2 + to_t))
        return lax.ppermute(array, ("ctx", "tp"), pairs)

    def partner(away):
        return lambda c, t: (c ^ away, t)

    def along(shift):
        return partner(shift * PAIR)

    def beside(c, t):
        return (c ^ 1, t)

    def sibling(c, t):
        return (c, 1 - t)

    hbm = pl.BlockSpec(memory_space=pltpu.HBM)
    pieces = features // GROUPS // LANES
    own_queries = suffix_query_rows.shape[0]
    lines = query_width // LANES
    block_rows = pieces * half_rows + pieces + own_queries * lines
    *blocks, own = pl.pallas_call(
        norm_kernel,
        in_specs=[hbm] * 4,
        out_specs=[hbm] * (GROUPS + 1),
        out_shape=[jax.ShapeDtypeStruct((block_rows, LANES), jnp.bfloat16)] * (GROUPS + 1),
        scratch_shapes=[
            pltpu.VMEM((half_rows, features), jnp.bfloat16),
            pltpu.VMEM(suffix_hidden.shape, jnp.bfloat16),
            pltpu.VMEM((1, features), jnp.float32),
            pltpu.VMEM(suffix_query_rows.shape, jnp.bfloat16),
            pltpu.VMEM((1, features), jnp.float32),
        ]
        + [pltpu.VMEM((block_rows, LANES), jnp.bfloat16)] * GROUPS
        + [
            pltpu.SemaphoreType.DMA((CHUNKS + 3,)),
            pltpu.SemaphoreType.DMA((GROUPS + 1,)),
        ],
        compiler_params=pltpu.CompilerParams(vmem_limit_bytes=60 * 1024 * 1024),
        cost_estimate=pl.CostEstimate(
            flops=4 * half_rows * features, bytes_accessed=4 * half_rows * features, transcendentals=0
        ),
        name="norm_rows",
    )(
        suffix_query_rows,
        hidden,
        suffix_hidden,
        norm_gain.reshape(1, features),
    )
    *weights, blocks[1] = lax.optimization_barrier((key_matrix, value_matrix, blocks[1]))
    far = [move(matrix, beside) for matrix in weights]

    mine = {s: move(blocks[s], along(s)) for s in far_first()}
    inverse_freq = rope_base ** (
        -(jnp.arange(HEAD_SIZE // 2, dtype=jnp.float32) * (2.0 / HEAD_SIZE))
    )
    row = jnp.arange(rows + 16, dtype=jnp.int32)
    front_position = ctx * rows + (row + core * half_rows) % rows
    end_position = prefix_len + ctx * 2 + jnp.where(row == rows, core, 1 - core)
    position = jnp.where(row < rows, front_position, end_position)
    angles = position.astype(jnp.float32)[:, None] * inverse_freq[None, :]
    cosine, sine = jnp.cos(angles), jnp.sin(angles)
    cosine = jnp.concatenate([cosine, cosine], 1)
    sine = jnp.concatenate([-sine, sine], 1)

    first = far_first()[0]
    mine[0] = pl.pallas_call(
        fetch_kernel,
        in_specs=[hbm],
        out_specs=vmem,
        out_shape=jax.ShapeDtypeStruct(own.shape, own.dtype),
        scratch_shapes=[pltpu.SemaphoreType.DMA],
        compiler_params=params,
        cost_estimate=pl.CostEstimate(flops=0, bytes_accessed=64 * 1024 * 1024, transcendentals=0),
        name="fetch_own",
    )(own)
    mine[first], mine[0], cosine, sine = lax.optimization_barrier(
        (mine[first], mine[0], cosine, sine)
    )
    blocks[0], far[0] = lax.optimization_barrier((blocks[0], far[0]))
    theirs = {s: move(blocks[0] if s == 0 else mine[s], sibling) for s in [0] + far_first()}

    part_rows = 3 * (width // LANES) * rows + 16
    partials, own_tiles = {}, []
    for shifts in ((0, first), tuple(far_first()[1:])):
        *found, tiles = pl.pallas_call(
            functools.partial(project_kernel, shifts),
            in_specs=[vmem] * (2 * len(shifts) + 4 + len(own_tiles)),
            out_specs=[vmem] * (len(shifts) + 1),
            out_shape=[jax.ShapeDtypeStruct((part_rows, LANES), jnp.bfloat16)] * len(shifts)
            + [jax.ShapeDtypeStruct((GROUPS * own_queries * lines, LANES), jnp.bfloat16)],
            scratch_shapes=[
                pltpu.VMEM((len(shifts) * rows + 16, PAIR * features // n_ctx), jnp.bfloat16)
            ],
            compiler_params=params,
            cost_estimate=pl.CostEstimate(
                flops=2 * len(shifts) * rows * 2 * width * features // GROUPS,
                bytes_accessed=6 * 1024 * 1024,
                transcendentals=0,
            ),
            name="project",
        )(
            *[part[s] for s in shifts for part in (mine, theirs)],
            key_matrix,
            value_matrix,
            *far,
            *own_tiles,
        )
        partials.update(zip(shifts, found))
        own_tiles = [tiles]
    (own_tiles,) = own_tiles
    received = [move(partials[s], along(s)) for s in far_first()]
    early = pl.pallas_call(
        sum_kernel,
        in_specs=[vmem] * 2,
        out_specs=vmem,
        out_shape=jax.ShapeDtypeStruct((part_rows, LANES), jnp.float32),
        compiler_params=params,
        cost_estimate=pl.CostEstimate(flops=0, bytes_accessed=16 * 1024 * 1024, transcendentals=0),
        name="sum_early",
    )(partials[0], received[0])
    beside_tiles = move(own_tiles, beside)

    states = n_ctx * own_queries * query_width // HEAD_SIZE
    state = jax.ShapeDtypeStruct((states, LANES), jnp.float32)
    top, total, numer, queries = pl.pallas_call(
        loaded_kernel,
        in_specs=[smem, smem, smem] + [vmem] * (PAIR + 2),
        out_specs=[vmem] * 4,
        out_shape=[state] * 3 + [jax.ShapeDtypeStruct((states, LANES), jnp.bfloat16)],
        compiler_params=params,
        cost_estimate=pl.CostEstimate(
            flops=4 * states * slot_keys.shape[0] * slot_keys.shape[1] * HEAD_SIZE,
            bytes_accessed=4 * slot_keys.size,
            transcendentals=states * slot_keys.shape[0] * slot_keys.shape[1],
        ),
        name="loaded_attention",
    )(place, page_slot_table, split_page, own_tiles, beside_tiles, slot_keys, slot_values)


    def payload(kind, slots):
        return jax.ShapeDtypeStruct((2 * slots * states // n_ctx, LANES), kind)

    row_shape = jax.ShapeDtypeStruct((rows, width), jnp.bfloat16)
    front_key, front_value, kept, *sent = pl.pallas_call(
        front_kernel,
        in_specs=[smem, smem] + [vmem] * (GROUPS + 7),
        out_specs=[hbm] * 2 + [vmem] * GROUPS,
        scratch_shapes=[pltpu.VMEM((rows, width), jnp.bfloat16)] * 2 + [pltpu.SemaphoreType.DMA((2,))],
        out_shape=[row_shape] * 2 + [payload(jnp.float32, PAIR)] + [payload(jnp.bfloat16, PAIR)] * (GROUPS - 1),
        compiler_params=params,
        cost_estimate=pl.CostEstimate(flops=4 * states * rows * HEAD_SIZE, bytes_accessed=2 * 1024 * 1024, transcendentals=states * rows),
        name="front_attention",
    )(
        place,
        split_page,
        early,
        *received[1:],
        key_offset_bias.reshape(1, width),
        value_offset_bias.reshape(1, width),
        cosine,
        sine,
        queries,
        top,
        total,
        numer,
    )
    kept, sent = pl.pallas_call(
        merge_kernel,
        in_specs=[vmem] * GROUPS,
        out_specs=[vmem] * 2,
        out_shape=[payload(jnp.float32, 1), payload(jnp.bfloat16, 1)],
        compiler_params=params,
        name="merge",
    )(kept, *[move(sent[s - 1], along(s)) for s in range(GROUPS - 1, 0, -1)])
    attended = pl.pallas_call(
        last_kernel,
        in_specs=[vmem] * 2,
        out_specs=vmem,
        out_shape=jax.ShapeDtypeStruct((own_queries, query_width), jnp.bfloat16),
        compiler_params=params,
        name="finish",
    )(kept, move(sent, beside))
    return (front_key, front_value, attended)


def solution(mesh):
    per_device = exchange_plan if mesh.shape["ctx"] == GROUPS * PAIR else gathered_plan
    return jax.shard_map(
        per_device,
        mesh=mesh,
        in_specs=(
            P(("req", "ctx"), None),
            P(("req", "ctx"), None),
            P(),
            P("ctx", "tp"),
            P("ctx", "tp"),
            P("tp"),
            P("tp"),
            P(("req", "ctx"), "tp"),
            P(("req", "ctx"), None, "tp"),
            P(("req", "ctx"), None, "tp"),
            P("req"),
            P("req"),
        ),
        out_specs=(P(("req", "ctx"), "tp"), P(("req", "ctx"), "tp"), P(("req", "ctx"), "tp")),
        check_vma=False,
    )
```

```python
import functools
import math

import jax
import jax.numpy as jnp
from jax import lax
from jax.experimental import pallas as pl
from jax.experimental.pallas import tpu as pltpu
from jax.sharding import PartitionSpec as P

QUERY_HEADS = 32
KEY_VALUE_HEADS = 4
HEAD_SIZE = 128


epsilon = 1e-06
rope_base = 1000000.0
masked_score = -1e30


def rms_rows(matrix, norm_gain):
    widened = matrix.astype(jnp.float32)
    inverse = lax.rsqrt(jnp.mean(widened * widened, axis=-1, keepdims=True) + epsilon)
    return (widened * inverse * norm_gain).astype(jnp.bfloat16)


def rotate(key_rows, positions, head_dim):
    row_count = key_rows.shape[0]
    split_heads = key_rows.reshape(row_count, -1, head_dim)
    half_dim = head_dim // 2
    inverse_freq = rope_base ** (-(jnp.arange(half_dim, dtype=jnp.float32) * (2.0 / head_dim)))
    angles = positions.astype(jnp.float32)[:, None] * inverse_freq[None, :]
    cosine = jnp.concatenate([jnp.cos(angles), jnp.cos(angles)], -1)[:, None, :]
    sine = jnp.concatenate([jnp.sin(angles), jnp.sin(angles)], -1)[:, None, :]
    turned = jnp.concatenate([-split_heads[..., half_dim:], split_heads[..., :half_dim]], -1)
    return (split_heads * cosine + turned * sine).reshape(row_count, -1)


def gathered_plan(
    hidden,
    suffix_hidden,
    norm_gain,
    key_matrix,
    value_matrix,
    key_offset_bias,
    value_offset_bias,
    suffix_query_rows,
    slot_keys,
    slot_values,
    page_slot_table,
    split_page,
):
    ctx_index = lax.axis_index("ctx")
    queries = lax.all_gather(suffix_query_rows, "ctx", axis=0, tiled=True)
    front_rows = hidden.shape[0]
    suffix_rows = suffix_hidden.shape[0]
    page_size = slot_keys.shape[1]
    slot_count = slot_keys.shape[0]
    total_pages = page_slot_table.shape[0]
    prefix_len = total_pages * page_size
    normed = rms_rows(jnp.concatenate([hidden, suffix_hidden], 0), norm_gain)
    col_width = key_matrix.shape[1]

    def accumulate(block_rows):
        return jnp.dot(normed, block_rows, preferred_element_type=jnp.float32)

    key_acc = accumulate(lax.all_gather(key_matrix, "ctx", axis=0, tiled=True))
    value_acc = accumulate(lax.all_gather(value_matrix, "ctx", axis=0, tiled=True))
    front_pos = ctx_index * front_rows + jnp.arange(front_rows, dtype=jnp.int32)
    suffix_pos = prefix_len + ctx_index * suffix_rows + jnp.arange(suffix_rows, dtype=jnp.int32)
    new_keys = rotate(
        key_acc + key_offset_bias, jnp.concatenate([front_pos, suffix_pos], 0), HEAD_SIZE
    ).astype(jnp.bfloat16)
    new_values = (value_acc + value_offset_bias).astype(jnp.bfloat16)
    cut_pos = split_page[0] * page_size
    global_slot = ctx_index * slot_count + jnp.arange(slot_count, dtype=jnp.int32)
    page_index = jnp.arange(total_pages, dtype=jnp.int32)
    slot_hits = (page_slot_table[None, :] == global_slot[:, None]) & (
        page_index[None, :] >= split_page[0]
    )
    slot_live = jnp.max(slot_hits.astype(jnp.int32), axis=1) > 0
    every_key = jnp.concatenate(
        [new_keys[:front_rows], slot_keys.reshape(-1, col_width), new_keys[front_rows:]], 0
    )
    every_value = jnp.concatenate(
        [new_values[:front_rows], slot_values.reshape(-1, col_width), new_values[front_rows:]], 0
    )
    query_count = queries.shape[0]
    query_pos = prefix_len + jnp.arange(query_count, dtype=jnp.int32)
    prefix_seen = jnp.concatenate([front_pos < cut_pos, jnp.repeat(slot_live, page_size)], 0)
    suffix_seen = suffix_pos[None, :] <= query_pos[:, None]
    visible = jnp.concatenate(
        [jnp.broadcast_to(prefix_seen[None, :], (query_count, prefix_seen.shape[0])), suffix_seen],
        1,
    )
    visible_wide = visible[:, None, :]
    sharing_count = QUERY_HEADS // KEY_VALUE_HEADS
    local_heads = col_width // HEAD_SIZE
    grouped_heads = queries.reshape(query_count, local_heads, sharing_count, HEAD_SIZE)
    top_list = []
    total_list = []
    numer_list = []
    for current_head in range(local_heads):
        head_keys = every_key[:, current_head * HEAD_SIZE : (current_head + 1) * HEAD_SIZE]
        head_values = every_value[:, current_head * HEAD_SIZE : (current_head + 1) * HEAD_SIZE]
        scores = jnp.einsum(
            "qgd,ld->qgl",
            grouped_heads[:, current_head],
            head_keys,
            preferred_element_type=jnp.float32,
        ) * (1.0 / math.sqrt(HEAD_SIZE))
        scores = jnp.where(visible_wide, scores, masked_score)
        row_top = jnp.max(scores, axis=-1)
        expos = jnp.where(visible_wide, jnp.exp(scores - row_top[..., None]), 0.0)
        total_list.append(jnp.sum(expos, axis=-1))
        top_list.append(row_top)
        numer_list.append(
            jnp.einsum(
                "qgl,ld->qgd",
                expos.astype(jnp.bfloat16),
                head_values,
                preferred_element_type=jnp.float32,
            )
        )
    row_top = jnp.stack(top_list, 1)
    weight_total = jnp.stack(total_list, 1)
    numer = jnp.stack(numer_list, 1)
    global_top = lax.pmax(row_top, "ctx")
    factor = jnp.exp(row_top - global_top)
    own_total, own_numer = (
        lax.psum_scatter(
            (weight_total * factor).reshape(query_count, -1), "ctx", scatter_dimension=0, tiled=True
        ),
        lax.psum_scatter(
            (numer * factor[..., None]).reshape(query_count, -1),
            "ctx",
            scatter_dimension=0,
            tiled=True,
        ),
    )
    own_total = own_total.reshape(suffix_rows, local_heads, sharing_count)
    own_numer = own_numer.reshape(suffix_rows, local_heads, sharing_count, HEAD_SIZE)
    attended = (own_numer / own_total[..., None]).reshape(suffix_rows, -1).astype(jnp.bfloat16)
    return (new_keys[:front_rows], new_values[:front_rows], attended)

GROUPS = 4
PAIR = 2
LANES = 128
SCALE = 1.0 / math.sqrt(HEAD_SIZE)


def row_scale(values):
    mean = jnp.sum(values * values, axis=-1, keepdims=True) * (1.0 / values.shape[-1])
    return lax.rsqrt(mean + epsilon)


CHUNKS = 4


def far_first():
    return sorted(range(1, GROUPS), key=lambda s: s < GROUPS // 2)


def norm_kernel(shifts, query_any, hidden_any, suffix_any, gain_any, *rest):
    count = len(shifts)
    blocks_any, rest = rest[:count], rest[count:]
    (hidden_ref, suffix_ref, gain_ref, query_ref, tail_ref), rest = rest[:5], rest[5:]
    outs, (sems, out_sems) = rest[:count], rest[count:]
    core, ctx = lax.axis_index("tp"), lax.axis_index("ctx")
    z, x = ctx // PAIR, ctx % PAIR
    half_rows, features = hidden_ref.shape
    rows = half_rows // CHUNKS
    block = features // (GROUPS * PAIR)
    per_block = block // LANES
    pieces = PAIR * per_block
    copies = [
        pltpu.make_async_copy(gain_any, gain_ref, sems.at[CHUNKS]),
        pltpu.make_async_copy(suffix_any, suffix_ref, sems.at[CHUNKS + 1]),
        pltpu.make_async_copy(query_any, query_ref, sems.at[CHUNKS + 2]),
    ]
    for i in range(CHUNKS):
        start = pl.multiple_of(core * half_rows + i * rows, rows)
        copies.append(
            pltpu.make_async_copy(
                hidden_any.at[pl.ds(start, rows)], hidden_ref.at[i * rows : (i + 1) * rows], sems.at[i]
            )
        )
    for copy in copies:
        copy.start()

    def offset(shift, side, j):
        owner = (z ^ shift) * PAIR + (x ^ side)
        return pl.multiple_of(owner * block + j * LANES, LANES)

    copies[0].wait()
    copies[1].wait()
    copies[2].wait()
    query_rows = query_ref[...].astype(jnp.float32)
    lines = query_rows.shape[1] // LANES
    for r in range(query_rows.shape[0]):
        tile = [query_rows[r : r + 1, j * LANES : (j + 1) * LANES] for j in range(lines)]
        tile = jnp.concatenate(tile, 0).astype(jnp.bfloat16)
        start = pieces * half_rows + pieces + r * lines
        for out in outs:
            out[start : start + lines, :] = tile

    both = suffix_ref[...].astype(jnp.float32)
    normed = both * row_scale(both) * gain_ref[...]
    tail_ref[...] = jnp.where(core == 0, normed[0:1], normed[1:2])
    for shift, out in zip(shifts, outs):
        ends = [
            tail_ref[:, pl.ds(offset(shift, side, j), LANES)]
            for side in range(PAIR)
            for j in range(per_block)
        ]
        start = pieces * half_rows
        out[start : start + pieces, :] = jnp.concatenate(ends, 0).astype(jnp.bfloat16)
    inverses = []
    for i in range(CHUNKS):
        copies[3 + i].wait()
        inverses.append(row_scale(hidden_ref[i * rows : (i + 1) * rows, :].astype(jnp.float32)))
    leaving = []
    for place, (shift, out) in enumerate(zip(shifts, outs)):
        for side in range(PAIR):
            for j in range(per_block):
                columns = pl.ds(offset(shift, side, j), LANES)
                for i in range(CHUNKS):
                    piece = hidden_ref[i * rows : (i + 1) * rows, columns].astype(jnp.float32)
                    piece = piece * inverses[i] * gain_ref[:, columns]
                    start = (side * per_block + j) * half_rows + i * rows
                    out[start : start + rows, :] = piece.astype(jnp.bfloat16)
        leaving.append(pltpu.make_async_copy(out, blocks_any[place], out_sems.at[place]))
        leaving[-1].start()
    for copy in leaving:
        copy.wait()


def fetch_kernel(from_any, to_ref, sem):
    copy = pltpu.make_async_copy(from_any, to_ref, sem)
    copy.start()
    copy.wait()


def project_kernel(shifts, *refs):
    count = len(shifts)
    blocks, rest = refs[: 2 * count], refs[2 * count :]
    near_key, near_value, far_key, far_value = rest[:4]
    earlier, outs, (query_ref, lhs_ref) = rest[4 : -2 - count], rest[-2 - count : -2], rest[-2:]
    depth = near_key.shape[0]
    pieces = 2 * depth // LANES
    half_rows = (lhs_ref.shape[0] - 16) // (2 * count)
    rows = 2 * half_rows
    tails = []
    for i, block in enumerate(blocks):
        for j in range(pieces):
            lhs_ref[i * half_rows : (i + 1) * half_rows, j * LANES : (j + 1) * LANES] = block[
                j * half_rows : (j + 1) * half_rows, :
            ]
        tail = block[pieces * half_rows : pieces * half_rows + pieces, :].astype(jnp.float32)
        tails.append(jnp.concatenate([tail[j : j + 1] for j in range(pieces)], 1))
    tails.append(jnp.zeros((16 - len(tails), 2 * depth), jnp.float32))
    lines = query_ref.shape[0] // GROUPS
    if earlier:
        query_ref[...] = earlier[0][...]
    for i, shift in enumerate(shifts):
        block = blocks[2 * i]
        query_ref[shift * lines : (shift + 1) * lines, :] = block[block.shape[0] - lines :, :]
    total = count * rows
    lhs_ref[total : total + 16, :] = jnp.concatenate(tails, 0).astype(jnp.bfloat16)

    def product(near, far):
        return jnp.dot(
            lhs_ref[:, :depth], near[...], preferred_element_type=jnp.float32
        ) + jnp.dot(lhs_ref[:, depth:], far[...], preferred_element_type=jnp.float32)

    keys = product(near_key, far_key)
    values = product(near_value, far_value)
    high = keys.astype(jnp.bfloat16).astype(jnp.float32)
    low = keys - high
    columns = []
    for array in (high, low, values):
        for j in range(array.shape[1] // LANES):
            columns.append(array[:, j * LANES : (j + 1) * LANES])
    for i, out in enumerate(outs):
        for k, column in enumerate(columns):
            out[k * rows : (k + 1) * rows, :] = column[i * rows : (i + 1) * rows].astype(jnp.bfloat16)
        ends = [c[total + 2 * i : total + 2 * i + 2] for c in columns]
        ends.append(jnp.zeros((16 - 2 * len(columns), LANES), jnp.float32))
        out[len(columns) * rows :, :] = jnp.concatenate(ends, 0).astype(jnp.bfloat16)


def head_queries(parts, head, width):
    sharing = QUERY_HEADS // KEY_VALUE_HEADS
    lines = sharing * width // HEAD_SIZE
    each = parts[0].shape[0] // GROUPS
    found = []
    for group in range(GROUPS):
        for part in parts:
            tiles = part[group * each : (group + 1) * each, :].astype(jnp.float32)
            for line in range(head * sharing, (head + 1) * sharing):
                found += [tiles[start : start + 1] for start in range(line, each, lines)]
    return jnp.concatenate(found, 0).astype(jnp.bfloat16)


def times_transposed(a, b):
    return lax.dot_general(a, b, (((1,), (1,)), ((), ())), preferred_element_type=jnp.float32)


def loaded_kernel(place_ref, table_ref, split_ref, *refs):
    parts = refs[:PAIR]
    key_ref, value_ref, top_ref, total_ref, numer_ref, query_ref = refs[PAIR:]
    ctx = place_ref[1]
    slots, page, width = key_ref.shape
    heads = width // HEAD_SIZE
    split = split_ref[0]
    live = []
    for s in range(slots):
        hit = jnp.int32(0)
        for p in range(table_ref.shape[0]):
            hit = hit | ((table_ref[p] == ctx * slots + s) & (p >= split)).astype(jnp.int32)
        live.append(hit)
    for head in range(heads):
        columns = slice(head * HEAD_SIZE, (head + 1) * HEAD_SIZE)
        queries = head_queries(parts, head, width)
        count = queries.shape[0]
        query_ref[head * count : (head + 1) * count, :] = queries
        scores = [
            jnp.where(live[s] > 0, times_transposed(queries, key_ref[s, :, columns]) * SCALE, masked_score)
            for s in range(slots)
        ]
        top = scores[0].max(-1, keepdims=True)
        for s in range(1, slots):
            top = jnp.maximum(top, scores[s].max(-1, keepdims=True))
        total = jnp.zeros((count, 1), jnp.float32)
        numer = jnp.zeros((count, HEAD_SIZE), jnp.float32)
        for s in range(slots):
            expos = jnp.where(live[s] > 0, jnp.exp(scores[s] - top), 0.0)
            total += expos.sum(-1, keepdims=True)
            numer += jnp.dot(
                expos.astype(jnp.bfloat16), value_ref[s, :, columns], preferred_element_type=jnp.float32
            )
        rows = slice(head * count, (head + 1) * count)
        top_ref[rows, :] = jnp.broadcast_to(top, (count, LANES))
        total_ref[rows, :] = jnp.broadcast_to(total, (count, LANES))
        numer_ref[rows, :] = numer


def sum_kernel(one, other, out):
    out[...] = one[...].astype(jnp.float32) + other[...].astype(jnp.float32)


def front_kernel(
    place_ref, split_ref, early, *refs
):
    received = refs[: GROUPS - 2]
    (key_bias, value_bias, cosine_ref, sine_ref, query_ref, top_ref, total_ref, numer_ref) = refs[
        GROUPS - 2 : GROUPS + 6
    ]
    key_any, value_any, *outs = refs[GROUPS + 6 : -3]
    front_key, front_value, sems = refs[-3:]
    core, ctx = place_ref[0], place_ref[1]
    rows, width = front_key.shape
    half_rows = rows // 2
    heads = width // HEAD_SIZE
    sharing = QUERY_HEADS // KEY_VALUE_HEADS
    count = query_ref.shape[0] // heads
    own_queries = count // sharing // (GROUPS * PAIR)
    visible = ctx < split_ref[0]

    def summed(start, size):
        value = early[start : start + size, :]
        for ref in received:
            value += ref[start : start + size, :].astype(jnp.float32)
        return value

    ends = summed(3 * heads * rows, 16)
    row = lax.broadcasted_iota(jnp.int32, (count, 16), 0)
    query_position = (ctx ^ (row // (own_queries * sharing))) * own_queries + row % own_queries
    end_column = lax.broadcasted_iota(jnp.int32, (count, 16), 1)
    end_position = ctx * 2 + jnp.where(end_column == 0, core, 1 - core)
    end_seen = (end_column < 2) & (end_position <= query_position)
    pad = jnp.zeros((14, HEAD_SIZE), jnp.float32)
    end_pairs = []
    for head in range(heads):
        columns = slice(head * HEAD_SIZE, (head + 1) * HEAD_SIZE)
        raw = summed(head * rows, rows) + summed((heads + head) * rows, rows)
        value = (summed((2 * heads + head) * rows, rows) + value_bias[:, columns]).astype(jnp.bfloat16)
        end_raw = ends[2 * head : 2 * head + 2] + ends[2 * (heads + head) : 2 * (heads + head) + 2]
        end_value = ends[2 * (2 * heads + head) : 2 * (2 * heads + head) + 2] + value_bias[:, columns]
        end_raw = jnp.concatenate([end_raw + key_bias[:, columns], pad], 0)
        end_value = jnp.concatenate([end_value, pad], 0).astype(jnp.bfloat16)
        raw = raw + key_bias[:, columns]

        def rotated(k, part):
            turned = pltpu.roll(k, HEAD_SIZE // 2, 1)
            return (k * cosine_ref[part, :] + turned * sine_ref[part, :]).astype(jnp.bfloat16)

        key = rotated(raw, slice(0, rows))
        end_key = rotated(end_raw, slice(rows, rows + 16))
        for half in range(2):
            to = pl.ds(pl.multiple_of(lax.rem(core + half, 2) * half_rows, half_rows), half_rows)
            front_key[to, columns] = key[half * half_rows : (half + 1) * half_rows]
            front_value[to, columns] = value[half * half_rows : (half + 1) * half_rows]
        end_pairs.append((key, value, end_key, end_value))
    leaving = [
        pltpu.make_async_copy(front_key, key_any, sems.at[0]),
        pltpu.make_async_copy(front_value, value_any, sems.at[1]),
    ]
    for copy in leaving:
        copy.start()
    for head, (key, value, end_key, end_value) in enumerate(end_pairs):
        part = slice(head * count, (head + 1) * count)
        queries = query_ref[part, :]
        scores = jnp.where(visible, times_transposed(queries, key) * SCALE, masked_score)
        end_scores = jnp.where(end_seen, times_transposed(queries, end_key) * SCALE, masked_score)
        old_top = top_ref[part, :]
        top = jnp.maximum(scores.max(-1, keepdims=True), end_scores.max(-1, keepdims=True))
        top = jnp.maximum(old_top, top)
        factor = jnp.exp(old_top - top)
        expos = jnp.where(visible, jnp.exp(scores - top), 0.0)
        end_expos = jnp.where(end_seen, jnp.exp(end_scores - top[:, :16]), 0.0)
        total = total_ref[part, :] * factor + (
            expos.sum(-1, keepdims=True) + end_expos.sum(-1, keepdims=True)
        )
        numer = (
            numer_ref[part, :] * factor
            + jnp.dot(expos.astype(jnp.bfloat16), value, preferred_element_type=jnp.float32)
            + jnp.dot(end_expos.astype(jnp.bfloat16), end_value, preferred_element_type=jnp.float32)
        )
        each = own_queries * sharing
        split = PAIR * each
        stats = jnp.concatenate(
            [
                kept_stats(top[:split, 0:1], total[:split, 0:1]),
                sent_stats(top[split:, 0:1], total[split:, 0:1]).astype(jnp.float32),
            ],
            0,
        )
        for slot in range(GROUPS * PAIR):
            start = (slot % PAIR * 2 * heads + head) * each
            at = slice(slot * each, (slot + 1) * each)
            out = outs[slot // PAIR]
            out[start : start + each, :] = numer[at].astype(out.dtype)
            out[start + heads * each : start + (heads + 1) * each, :] = stats[at].astype(out.dtype)
    for copy in leaving:
        copy.wait()


def kept_stats(top, total):
    lane = lax.broadcasted_iota(jnp.int32, (top.shape[0], LANES), 1)
    return jnp.where(lane < LANES // 2, top, total)


def sent_stats(top, total):
    terms = []
    for rest, count in ((top, 3), (total, 2)):
        for _ in range(count):
            term = rest.astype(jnp.bfloat16).astype(jnp.float32)
            terms.append(term)
            rest = rest - term
    part = lax.broadcasted_iota(jnp.int32, (top.shape[0], LANES), 1) // 16
    stats = jnp.broadcast_to(terms[-1], part.shape)
    for i, term in enumerate(terms[:-1]):
        stats = jnp.where(part == i, term, stats)
    return stats.astype(jnp.bfloat16)


def merged(kept, others, start, rows):
    half = LANES // 2
    stats = kept[start + rows : start + 2 * rows, :]
    tops, totals = [stats[:, 0:1]], [stats[:, half : half + 1]]
    numers = [kept[start : start + rows, :]]
    for other in others:
        terms = other[start + rows : start + 2 * rows, :].astype(jnp.float32)
        tops.append((terms[:, 0:1] + terms[:, 16:17]) + terms[:, 32:33])
        totals.append(terms[:, 48:49] + terms[:, 64:65])
        numers.append(other[start : start + rows, :].astype(jnp.float32))
    top = functools.reduce(jnp.maximum, tops)
    factors = [jnp.exp(t - top) for t in tops]
    total = sum(f * t for f, t in zip(factors, totals))
    numer = sum(f * n for f, n in zip(factors, numers))
    return numer, top, total


def merge_kernel(kept, *refs):
    others, (keep_ref, send_ref) = refs[:-2], refs[-2:]
    each = keep_ref.shape[0]
    rows = each // 2
    numer, top, total = merged(kept, others, 0, rows)
    keep_ref[:rows, :] = numer
    keep_ref[rows:, :] = kept_stats(top, total)
    numer, top, total = merged(kept, others, each, rows)
    send_ref[:rows, :] = numer.astype(jnp.bfloat16)
    send_ref[rows:, :] = sent_stats(top, total)


def last_kernel(kept, *refs):
    others, out_ref = refs[:-1], refs[-1]
    numer, _, total = merged(kept, others, 0, kept.shape[0] // 2)
    result = numer / total
    queries = out_ref.shape[0]
    pieces = [result[s : s + queries] for s in range(0, result.shape[0], queries)]
    out_ref[...] = jnp.concatenate(pieces, 1).astype(jnp.bfloat16)


def exchange_plan(
    hidden,
    suffix_hidden,
    norm_gain,
    key_matrix,
    value_matrix,
    key_offset_bias,
    value_offset_bias,
    suffix_query_rows,
    slot_keys,
    slot_values,
    page_slot_table,
    split_page,
):
    n_ctx = GROUPS * PAIR
    ctx = lax.axis_index("ctx").astype(jnp.int32)
    core = lax.axis_index("tp").astype(jnp.int32)
    place = jnp.stack([core, ctx])
    rows, features = hidden.shape
    half_rows = rows // 2
    width = key_matrix.shape[1]
    query_width = suffix_query_rows.shape[1]
    prefix_len = page_slot_table.shape[0] * slot_keys.shape[1]
    smem = pl.BlockSpec(memory_space=pltpu.SMEM)
    vmem = pl.BlockSpec(memory_space=pltpu.VMEM)
    params = pltpu.CompilerParams(vmem_limit_bytes=48 * 1024 * 1024)

    def move(array, target):
        pairs = []
        for c in range(n_ctx):
            for t in range(2):
                to_c, to_t = target(c, t)
                pairs.append((c * 2 + t, to_c * 2 + to_t))
        return lax.ppermute(array, ("ctx", "tp"), pairs)

    def partner(away):
        return lambda c, t: (c ^ away, t)

    def along(shift):
        return partner(shift * PAIR)

    def beside(c, t):
        return (c ^ 1, t)

    def sibling(c, t):
        return (c, 1 - t)

    hbm = pl.BlockSpec(memory_space=pltpu.HBM)
    pieces = features // GROUPS // LANES
    own_queries = suffix_query_rows.shape[0]
    lines = query_width // LANES
    block_rows = pieces * half_rows + pieces + own_queries * lines
    blocks = {}
    for shifts in (tuple(far_first()[:1]), tuple(far_first()[1:]) + (0,)):
        found = pl.pallas_call(
            functools.partial(norm_kernel, shifts),
            in_specs=[hbm] * 4,
            out_specs=[hbm] * len(shifts),
            out_shape=[jax.ShapeDtypeStruct((block_rows, LANES), jnp.bfloat16)] * len(shifts),
            scratch_shapes=[
                pltpu.VMEM((half_rows, features), jnp.bfloat16),
                pltpu.VMEM(suffix_hidden.shape, jnp.bfloat16),
                pltpu.VMEM((1, features), jnp.float32),
                pltpu.VMEM(suffix_query_rows.shape, jnp.bfloat16),
                pltpu.VMEM((1, features), jnp.float32),
            ]
            + [pltpu.VMEM((block_rows, LANES), jnp.bfloat16)] * len(shifts)
            + [pltpu.SemaphoreType.DMA((CHUNKS + 3,)), pltpu.SemaphoreType.DMA((len(shifts),))],
            compiler_params=pltpu.CompilerParams(vmem_limit_bytes=60 * 1024 * 1024),
            cost_estimate=pl.CostEstimate(
                flops=4 * half_rows * features,
                bytes_accessed=4 * half_rows * features,
                transcendentals=0,
            ),
            name="norm_rows",
        )(suffix_query_rows, hidden, suffix_hidden, norm_gain.reshape(1, features))
        blocks.update(zip(shifts, found))
    own = blocks[0]
    *weights, blocks[2] = lax.optimization_barrier((key_matrix, value_matrix, blocks[2]))
    far = [move(matrix, beside) for matrix in weights]

    mine = {s: move(blocks[s], along(s)) for s in far_first()}
    inverse_freq = rope_base ** (
        -(jnp.arange(HEAD_SIZE // 2, dtype=jnp.float32) * (2.0 / HEAD_SIZE))
    )
    row = jnp.arange(rows + 16, dtype=jnp.int32)
    front_position = ctx * rows + (row + core * half_rows) % rows
    end_position = prefix_len + ctx * 2 + jnp.where(row == rows, core, 1 - core)
    position = jnp.where(row < rows, front_position, end_position)
    angles = position.astype(jnp.float32)[:, None] * inverse_freq[None, :]
    cosine, sine = jnp.cos(angles), jnp.sin(angles)
    cosine = jnp.concatenate([cosine, cosine], 1)
    sine = jnp.concatenate([-sine, sine], 1)

    first = far_first()[0]
    mine[0] = pl.pallas_call(
        fetch_kernel,
        in_specs=[hbm],
        out_specs=vmem,
        out_shape=jax.ShapeDtypeStruct(own.shape, own.dtype),
        scratch_shapes=[pltpu.SemaphoreType.DMA],
        compiler_params=params,
        cost_estimate=pl.CostEstimate(flops=0, bytes_accessed=64 * 1024 * 1024, transcendentals=0),
        name="fetch_own",
    )(own)
    mine[first], mine[0], cosine, sine = lax.optimization_barrier(
        (mine[first], mine[0], cosine, sine)
    )
    blocks[0], far[0] = lax.optimization_barrier((blocks[0], far[0]))
    theirs = {s: move(blocks[0] if s == 0 else mine[s], sibling) for s in [0] + far_first()}

    part_rows = 3 * (width // LANES) * rows + 16
    partials, own_tiles = {}, []
    for shifts in ((0, first), tuple(far_first()[1:])):
        *found, tiles = pl.pallas_call(
            functools.partial(project_kernel, shifts),
            in_specs=[vmem] * (2 * len(shifts) + 4 + len(own_tiles)),
            out_specs=[vmem] * (len(shifts) + 1),
            out_shape=[jax.ShapeDtypeStruct((part_rows, LANES), jnp.bfloat16)] * len(shifts)
            + [jax.ShapeDtypeStruct((GROUPS * own_queries * lines, LANES), jnp.bfloat16)],
            scratch_shapes=[
                pltpu.VMEM((len(shifts) * rows + 16, PAIR * features // n_ctx), jnp.bfloat16)
            ],
            compiler_params=params,
            cost_estimate=pl.CostEstimate(
                flops=2 * len(shifts) * rows * 2 * width * features // GROUPS,
                bytes_accessed=6 * 1024 * 1024,
                transcendentals=0,
            ),
            name="project",
        )(
            *[part[s] for s in shifts for part in (mine, theirs)],
            key_matrix,
            value_matrix,
            *far,
            *own_tiles,
        )
        partials.update(zip(shifts, found))
        own_tiles = [tiles]
    (own_tiles,) = own_tiles
    received = [move(partials[s], along(s)) for s in far_first()]
    early = pl.pallas_call(
        sum_kernel,
        in_specs=[vmem] * 2,
        out_specs=vmem,
        out_shape=jax.ShapeDtypeStruct((part_rows, LANES), jnp.float32),
        compiler_params=params,
        cost_estimate=pl.CostEstimate(flops=0, bytes_accessed=16 * 1024 * 1024, transcendentals=0),
        name="sum_early",
    )(partials[0], received[0])
    beside_tiles = move(own_tiles, beside)

    states = n_ctx * own_queries * query_width // HEAD_SIZE
    state = jax.ShapeDtypeStruct((states, LANES), jnp.float32)
    top, total, numer, queries = pl.pallas_call(
        loaded_kernel,
        in_specs=[smem, smem, smem] + [vmem] * (PAIR + 2),
        out_specs=[vmem] * 4,
        out_shape=[state] * 3 + [jax.ShapeDtypeStruct((states, LANES), jnp.bfloat16)],
        compiler_params=params,
        cost_estimate=pl.CostEstimate(
            flops=4 * states * slot_keys.shape[0] * slot_keys.shape[1] * HEAD_SIZE,
            bytes_accessed=4 * slot_keys.size,
            transcendentals=states * slot_keys.shape[0] * slot_keys.shape[1],
        ),
        name="loaded_attention",
    )(place, page_slot_table, split_page, own_tiles, beside_tiles, slot_keys, slot_values)


    def payload(kind, slots):
        return jax.ShapeDtypeStruct((2 * slots * states // n_ctx, LANES), kind)

    row_shape = jax.ShapeDtypeStruct((rows, width), jnp.bfloat16)
    front_key, front_value, kept, *sent = pl.pallas_call(
        front_kernel,
        in_specs=[smem, smem] + [vmem] * (GROUPS + 7),
        out_specs=[hbm] * 2 + [vmem] * GROUPS,
        scratch_shapes=[pltpu.VMEM((rows, width), jnp.bfloat16)] * 2 + [pltpu.SemaphoreType.DMA((2,))],
        out_shape=[row_shape] * 2 + [payload(jnp.float32, PAIR)] + [payload(jnp.bfloat16, PAIR)] * (GROUPS - 1),
        compiler_params=params,
        cost_estimate=pl.CostEstimate(flops=4 * states * rows * HEAD_SIZE, bytes_accessed=2 * 1024 * 1024, transcendentals=states * rows),
        name="front_attention",
    )(
        place,
        split_page,
        early,
        *received[1:],
        key_offset_bias.reshape(1, width),
        value_offset_bias.reshape(1, width),
        cosine,
        sine,
        queries,
        top,
        total,
        numer,
    )
    kept, sent = pl.pallas_call(
        merge_kernel,
        in_specs=[vmem] * GROUPS,
        out_specs=[vmem] * 2,
        out_shape=[payload(jnp.float32, 1), payload(jnp.bfloat16, 1)],
        compiler_params=params,
        name="merge",
    )(kept, *[move(sent[s - 1], along(s)) for s in range(GROUPS - 1, 0, -1)])
    attended = pl.pallas_call(
        last_kernel,
        in_specs=[vmem] * 2,
        out_specs=vmem,
        out_shape=jax.ShapeDtypeStruct((own_queries, query_width), jnp.bfloat16),
        compiler_params=params,
        name="finish",
    )(kept, move(sent, beside))
    return (front_key, front_value, attended)


def solution(mesh):
    per_device = exchange_plan if mesh.shape["ctx"] == GROUPS * PAIR else gathered_plan
    return jax.shard_map(
        per_device,
        mesh=mesh,
        in_specs=(
            P(("req", "ctx"), None),
            P(("req", "ctx"), None),
            P(),
            P("ctx", "tp"),
            P("ctx", "tp"),
            P("tp"),
            P("tp"),
            P(("req", "ctx"), "tp"),
            P(("req", "ctx"), None, "tp"),
            P(("req", "ctx"), None, "tp"),
            P("req"),
            P("req"),
        ),
        out_specs=(P(("req", "ctx"), "tp"), P(("req", "ctx"), "tp"), P(("req", "ctx"), "tp")),
        check_vma=False,
    )
```

```python
import functools
import math

import jax
import jax.numpy as jnp
from jax import lax
from jax.experimental import pallas as pl
from jax.experimental.pallas import tpu as pltpu
from jax.sharding import PartitionSpec as P

QUERY_HEADS = 32
KEY_VALUE_HEADS = 4
HEAD_SIZE = 128


epsilon = 1e-06
rope_base = 1000000.0
masked_score = -1e30


def rms_rows(matrix, norm_gain):
    widened = matrix.astype(jnp.float32)
    inverse = lax.rsqrt(jnp.mean(widened * widened, axis=-1, keepdims=True) + epsilon)
    return (widened * inverse * norm_gain).astype(jnp.bfloat16)


def rotate(key_rows, positions, head_dim):
    row_count = key_rows.shape[0]
    split_heads = key_rows.reshape(row_count, -1, head_dim)
    half_dim = head_dim // 2
    inverse_freq = rope_base ** (-(jnp.arange(half_dim, dtype=jnp.float32) * (2.0 / head_dim)))
    angles = positions.astype(jnp.float32)[:, None] * inverse_freq[None, :]
    cosine = jnp.concatenate([jnp.cos(angles), jnp.cos(angles)], -1)[:, None, :]
    sine = jnp.concatenate([jnp.sin(angles), jnp.sin(angles)], -1)[:, None, :]
    turned = jnp.concatenate([-split_heads[..., half_dim:], split_heads[..., :half_dim]], -1)
    return (split_heads * cosine + turned * sine).reshape(row_count, -1)


def gathered_plan(
    hidden,
    suffix_hidden,
    norm_gain,
    key_matrix,
    value_matrix,
    key_offset_bias,
    value_offset_bias,
    suffix_query_rows,
    slot_keys,
    slot_values,
    page_slot_table,
    split_page,
):
    ctx_index = lax.axis_index("ctx")
    queries = lax.all_gather(suffix_query_rows, "ctx", axis=0, tiled=True)
    front_rows = hidden.shape[0]
    suffix_rows = suffix_hidden.shape[0]
    page_size = slot_keys.shape[1]
    slot_count = slot_keys.shape[0]
    total_pages = page_slot_table.shape[0]
    prefix_len = total_pages * page_size
    normed = rms_rows(jnp.concatenate([hidden, suffix_hidden], 0), norm_gain)
    col_width = key_matrix.shape[1]

    def accumulate(block_rows):
        return jnp.dot(normed, block_rows, preferred_element_type=jnp.float32)

    key_acc = accumulate(lax.all_gather(key_matrix, "ctx", axis=0, tiled=True))
    value_acc = accumulate(lax.all_gather(value_matrix, "ctx", axis=0, tiled=True))
    front_pos = ctx_index * front_rows + jnp.arange(front_rows, dtype=jnp.int32)
    suffix_pos = prefix_len + ctx_index * suffix_rows + jnp.arange(suffix_rows, dtype=jnp.int32)
    new_keys = rotate(
        key_acc + key_offset_bias, jnp.concatenate([front_pos, suffix_pos], 0), HEAD_SIZE
    ).astype(jnp.bfloat16)
    new_values = (value_acc + value_offset_bias).astype(jnp.bfloat16)
    cut_pos = split_page[0] * page_size
    global_slot = ctx_index * slot_count + jnp.arange(slot_count, dtype=jnp.int32)
    page_index = jnp.arange(total_pages, dtype=jnp.int32)
    slot_hits = (page_slot_table[None, :] == global_slot[:, None]) & (
        page_index[None, :] >= split_page[0]
    )
    slot_live = jnp.max(slot_hits.astype(jnp.int32), axis=1) > 0
    every_key = jnp.concatenate(
        [new_keys[:front_rows], slot_keys.reshape(-1, col_width), new_keys[front_rows:]], 0
    )
    every_value = jnp.concatenate(
        [new_values[:front_rows], slot_values.reshape(-1, col_width), new_values[front_rows:]], 0
    )
    query_count = queries.shape[0]
    query_pos = prefix_len + jnp.arange(query_count, dtype=jnp.int32)
    prefix_seen = jnp.concatenate([front_pos < cut_pos, jnp.repeat(slot_live, page_size)], 0)
    suffix_seen = suffix_pos[None, :] <= query_pos[:, None]
    visible = jnp.concatenate(
        [jnp.broadcast_to(prefix_seen[None, :], (query_count, prefix_seen.shape[0])), suffix_seen],
        1,
    )
    visible_wide = visible[:, None, :]
    sharing_count = QUERY_HEADS // KEY_VALUE_HEADS
    local_heads = col_width // HEAD_SIZE
    grouped_heads = queries.reshape(query_count, local_heads, sharing_count, HEAD_SIZE)
    top_list = []
    total_list = []
    numer_list = []
    for current_head in range(local_heads):
        head_keys = every_key[:, current_head * HEAD_SIZE : (current_head + 1) * HEAD_SIZE]
        head_values = every_value[:, current_head * HEAD_SIZE : (current_head + 1) * HEAD_SIZE]
        scores = jnp.einsum(
            "qgd,ld->qgl",
            grouped_heads[:, current_head],
            head_keys,
            preferred_element_type=jnp.float32,
        ) * (1.0 / math.sqrt(HEAD_SIZE))
        scores = jnp.where(visible_wide, scores, masked_score)
        row_top = jnp.max(scores, axis=-1)
        expos = jnp.where(visible_wide, jnp.exp(scores - row_top[..., None]), 0.0)
        total_list.append(jnp.sum(expos, axis=-1))
        top_list.append(row_top)
        numer_list.append(
            jnp.einsum(
                "qgl,ld->qgd",
                expos.astype(jnp.bfloat16),
                head_values,
                preferred_element_type=jnp.float32,
            )
        )
    row_top = jnp.stack(top_list, 1)
    weight_total = jnp.stack(total_list, 1)
    numer = jnp.stack(numer_list, 1)
    global_top = lax.pmax(row_top, "ctx")
    factor = jnp.exp(row_top - global_top)
    own_total, own_numer = (
        lax.psum_scatter(
            (weight_total * factor).reshape(query_count, -1), "ctx", scatter_dimension=0, tiled=True
        ),
        lax.psum_scatter(
            (numer * factor[..., None]).reshape(query_count, -1),
            "ctx",
            scatter_dimension=0,
            tiled=True,
        ),
    )
    own_total = own_total.reshape(suffix_rows, local_heads, sharing_count)
    own_numer = own_numer.reshape(suffix_rows, local_heads, sharing_count, HEAD_SIZE)
    attended = (own_numer / own_total[..., None]).reshape(suffix_rows, -1).astype(jnp.bfloat16)
    return (new_keys[:front_rows], new_values[:front_rows], attended)

GROUPS = 4
PAIR = 2
LANES = 128
SCALE = 1.0 / math.sqrt(HEAD_SIZE)


def row_scale(values):
    mean = jnp.sum(values * values, axis=-1, keepdims=True) * (1.0 / values.shape[-1])
    return lax.rsqrt(mean + epsilon)


CHUNKS = 4


def far_first():
    return sorted(range(1, GROUPS), key=lambda s: s < GROUPS // 2)


def norm_kernel(shifts, query_any, hidden_any, suffix_any, gain_any, *rest):
    count = len(shifts)
    blocks_any, rest = rest[:count], rest[count:]
    (hidden_ref, suffix_ref, gain_ref, query_ref, tail_ref), rest = rest[:5], rest[5:]
    outs, (sems, out_sems) = rest[:count], rest[count:]
    core, ctx = lax.axis_index("tp"), lax.axis_index("ctx")
    z, x = ctx // PAIR, ctx % PAIR
    half_rows, features = hidden_ref.shape
    rows = half_rows // CHUNKS
    block = features // (GROUPS * PAIR)
    per_block = block // LANES
    pieces = PAIR * per_block
    copies = [
        pltpu.make_async_copy(gain_any, gain_ref, sems.at[CHUNKS]),
        pltpu.make_async_copy(suffix_any, suffix_ref, sems.at[CHUNKS + 1]),
        pltpu.make_async_copy(query_any, query_ref, sems.at[CHUNKS + 2]),
    ]
    for i in range(CHUNKS):
        start = pl.multiple_of(core * half_rows + i * rows, rows)
        copies.append(
            pltpu.make_async_copy(
                hidden_any.at[pl.ds(start, rows)], hidden_ref.at[i * rows : (i + 1) * rows], sems.at[i]
            )
        )
    for copy in copies:
        copy.start()

    def offset(shift, side, j):
        owner = (z ^ shift) * PAIR + (x ^ side)
        return pl.multiple_of(owner * block + j * LANES, LANES)

    copies[0].wait()
    copies[1].wait()
    copies[2].wait()
    query_rows = query_ref[...].astype(jnp.float32)
    lines = query_rows.shape[1] // LANES
    for r in range(query_rows.shape[0]):
        tile = [query_rows[r : r + 1, j * LANES : (j + 1) * LANES] for j in range(lines)]
        tile = jnp.concatenate(tile, 0).astype(jnp.bfloat16)
        start = pieces * half_rows + pieces + r * lines
        for out in outs:
            out[start : start + lines, :] = tile

    both = suffix_ref[...].astype(jnp.float32)
    normed = both * row_scale(both) * gain_ref[...]
    tail_ref[...] = jnp.where(core == 0, normed[0:1], normed[1:2])
    for shift, out in zip(shifts, outs):
        ends = [
            tail_ref[:, pl.ds(offset(shift, side, j), LANES)]
            for side in range(PAIR)
            for j in range(per_block)
        ]
        start = pieces * half_rows
        out[start : start + pieces, :] = jnp.concatenate(ends, 0).astype(jnp.bfloat16)
    inverses = []
    for i in range(CHUNKS):
        copies[3 + i].wait()
        inverses.append(row_scale(hidden_ref[i * rows : (i + 1) * rows, :].astype(jnp.float32)))
    leaving = []
    for place, (shift, out) in enumerate(zip(shifts, outs)):
        for side in range(PAIR):
            for j in range(per_block):
                columns = pl.ds(offset(shift, side, j), LANES)
                for i in range(CHUNKS):
                    piece = hidden_ref[i * rows : (i + 1) * rows, columns].astype(jnp.float32)
                    piece = piece * inverses[i] * gain_ref[:, columns]
                    start = (side * per_block + j) * half_rows + i * rows
                    out[start : start + rows, :] = piece.astype(jnp.bfloat16)
        leaving.append(pltpu.make_async_copy(out, blocks_any[place], out_sems.at[place]))
        leaving[-1].start()
    for copy in leaving:
        copy.wait()


def fetch_kernel(from_any, to_ref, sem):
    copy = pltpu.make_async_copy(from_any, to_ref, sem)
    copy.start()
    copy.wait()


def project_kernel(shifts, *refs):
    count = len(shifts)
    blocks, rest = refs[: 2 * count], refs[2 * count :]
    near_key, near_value, far_key, far_value = rest[:4]
    earlier, outs, (query_ref, lhs_ref) = rest[4 : -2 - count], rest[-2 - count : -2], rest[-2:]
    depth = near_key.shape[0]
    pieces = 2 * depth // LANES
    half_rows = (lhs_ref.shape[0] - 16) // (2 * count)
    rows = 2 * half_rows
    tails = []
    for i, block in enumerate(blocks):
        for j in range(pieces):
            lhs_ref[i * half_rows : (i + 1) * half_rows, j * LANES : (j + 1) * LANES] = block[
                j * half_rows : (j + 1) * half_rows, :
            ]
        tail = block[pieces * half_rows : pieces * half_rows + pieces, :].astype(jnp.float32)
        tails.append(jnp.concatenate([tail[j : j + 1] for j in range(pieces)], 1))
    tails.append(jnp.zeros((16 - len(tails), 2 * depth), jnp.float32))
    lines = query_ref.shape[0] // GROUPS
    if earlier:
        query_ref[...] = earlier[0][...]
    for i, shift in enumerate(shifts):
        block = blocks[2 * i]
        query_ref[shift * lines : (shift + 1) * lines, :] = block[block.shape[0] - lines :, :]
    total = count * rows
    lhs_ref[total : total + 16, :] = jnp.concatenate(tails, 0).astype(jnp.bfloat16)

    def product(near, far):
        return jnp.dot(
            lhs_ref[:, :depth], near[...], preferred_element_type=jnp.float32
        ) + jnp.dot(lhs_ref[:, depth:], far[...], preferred_element_type=jnp.float32)

    keys = product(near_key, far_key)
    values = product(near_value, far_value)
    high = keys.astype(jnp.bfloat16).astype(jnp.float32)
    low = keys - high
    columns = []
    for array in (high, low, values):
        for j in range(array.shape[1] // LANES):
            columns.append(array[:, j * LANES : (j + 1) * LANES])
    for i, out in enumerate(outs):
        for k, column in enumerate(columns):
            out[k * rows : (k + 1) * rows, :] = column[i * rows : (i + 1) * rows].astype(jnp.bfloat16)
        ends = [c[total + 2 * i : total + 2 * i + 2] for c in columns]
        ends.append(jnp.zeros((16 - 2 * len(columns), LANES), jnp.float32))
        out[len(columns) * rows :, :] = jnp.concatenate(ends, 0).astype(jnp.bfloat16)


def head_queries(parts, head, width):
    sharing = QUERY_HEADS // KEY_VALUE_HEADS
    lines = sharing * width // HEAD_SIZE
    each = parts[0].shape[0] // GROUPS
    found = []
    for group in range(GROUPS):
        for part in parts:
            tiles = part[group * each : (group + 1) * each, :].astype(jnp.float32)
            for line in range(head * sharing, (head + 1) * sharing):
                found += [tiles[start : start + 1] for start in range(line, each, lines)]
    return jnp.concatenate(found, 0).astype(jnp.bfloat16)


def times_transposed(a, b):
    return lax.dot_general(a, b, (((1,), (1,)), ((), ())), preferred_element_type=jnp.float32)


def loaded_kernel(table_ref, split_ref, *refs):
    parts = refs[:PAIR]
    key_ref, value_ref, top_ref, total_ref, numer_ref, query_ref = refs[PAIR:]
    ctx = lax.axis_index("ctx")
    slots, page, width = key_ref.shape
    heads = width // HEAD_SIZE
    split = split_ref[0]
    live = []
    for s in range(slots):
        hit = jnp.int32(0)
        for p in range(table_ref.shape[0]):
            hit = hit | ((table_ref[p] == ctx * slots + s) & (p >= split)).astype(jnp.int32)
        live.append(hit)
    for head in range(heads):
        columns = slice(head * HEAD_SIZE, (head + 1) * HEAD_SIZE)
        queries = head_queries(parts, head, width)
        count = queries.shape[0]
        query_ref[head * count : (head + 1) * count, :] = queries
        scores = [
            jnp.where(live[s] > 0, times_transposed(queries, key_ref[s, :, columns]) * SCALE, masked_score)
            for s in range(slots)
        ]
        top = scores[0].max(-1, keepdims=True)
        for s in range(1, slots):
            top = jnp.maximum(top, scores[s].max(-1, keepdims=True))
        total = jnp.zeros((count, 1), jnp.float32)
        numer = jnp.zeros((count, HEAD_SIZE), jnp.float32)
        for s in range(slots):
            expos = jnp.where(live[s] > 0, jnp.exp(scores[s] - top), 0.0)
            total += expos.sum(-1, keepdims=True)
            numer += jnp.dot(
                expos.astype(jnp.bfloat16), value_ref[s, :, columns], preferred_element_type=jnp.float32
            )
        rows = slice(head * count, (head + 1) * count)
        top_ref[rows, :] = jnp.broadcast_to(top, (count, LANES))
        total_ref[rows, :] = jnp.broadcast_to(total, (count, LANES))
        numer_ref[rows, :] = numer


def sum_kernel(one, other, out):
    out[...] = one[...].astype(jnp.float32) + other[...].astype(jnp.float32)


def front_kernel(split_ref, early, *refs):
    received = refs[: GROUPS - 2]
    (key_bias, value_bias, cosine_ref, sine_ref, query_ref, top_ref, total_ref, numer_ref) = refs[
        GROUPS - 2 : GROUPS + 6
    ]
    key_any, value_any, *outs = refs[GROUPS + 6 : -3]
    front_key, front_value, sems = refs[-3:]
    core, ctx = lax.axis_index("tp"), lax.axis_index("ctx")
    rows, width = front_key.shape
    half_rows = rows // 2
    heads = width // HEAD_SIZE
    sharing = QUERY_HEADS // KEY_VALUE_HEADS
    count = query_ref.shape[0] // heads
    own_queries = count // sharing // (GROUPS * PAIR)
    visible = ctx < split_ref[0]

    def summed(start, size):
        value = early[start : start + size, :]
        for ref in received:
            value += ref[start : start + size, :].astype(jnp.float32)
        return value

    ends = summed(3 * heads * rows, 16)
    row = lax.broadcasted_iota(jnp.int32, (count, 16), 0)
    query_position = (ctx ^ (row // (own_queries * sharing))) * own_queries + row % own_queries
    end_column = lax.broadcasted_iota(jnp.int32, (count, 16), 1)
    end_position = ctx * 2 + jnp.where(end_column == 0, core, 1 - core)
    end_seen = (end_column < 2) & (end_position <= query_position)
    pad = jnp.zeros((14, HEAD_SIZE), jnp.float32)
    end_pairs = []
    for head in range(heads):
        columns = slice(head * HEAD_SIZE, (head + 1) * HEAD_SIZE)
        raw = summed(head * rows, rows) + summed((heads + head) * rows, rows)
        value = (summed((2 * heads + head) * rows, rows) + value_bias[:, columns]).astype(jnp.bfloat16)
        end_raw = ends[2 * head : 2 * head + 2] + ends[2 * (heads + head) : 2 * (heads + head) + 2]
        end_value = ends[2 * (2 * heads + head) : 2 * (2 * heads + head) + 2] + value_bias[:, columns]
        end_raw = jnp.concatenate([end_raw + key_bias[:, columns], pad], 0)
        end_value = jnp.concatenate([end_value, pad], 0).astype(jnp.bfloat16)
        raw = raw + key_bias[:, columns]

        def rotated(k, part):
            turned = pltpu.roll(k, HEAD_SIZE // 2, 1)
            return (k * cosine_ref[part, :] + turned * sine_ref[part, :]).astype(jnp.bfloat16)

        key = rotated(raw, slice(0, rows))
        end_key = rotated(end_raw, slice(rows, rows + 16))
        for half in range(2):
            to = pl.ds(pl.multiple_of(lax.rem(core + half, 2) * half_rows, half_rows), half_rows)
            front_key[to, columns] = key[half * half_rows : (half + 1) * half_rows]
            front_value[to, columns] = value[half * half_rows : (half + 1) * half_rows]
        end_pairs.append((key, value, end_key, end_value))
    leaving = [
        pltpu.make_async_copy(front_key, key_any, sems.at[0]),
        pltpu.make_async_copy(front_value, value_any, sems.at[1]),
    ]
    for copy in leaving:
        copy.start()
    for head, (key, value, end_key, end_value) in enumerate(end_pairs):
        part = slice(head * count, (head + 1) * count)
        queries = query_ref[part, :]
        scores = jnp.where(visible, times_transposed(queries, key) * SCALE, masked_score)
        end_scores = jnp.where(end_seen, times_transposed(queries, end_key) * SCALE, masked_score)
        old_top = top_ref[part, :]
        top = jnp.maximum(scores.max(-1, keepdims=True), end_scores.max(-1, keepdims=True))
        top = jnp.maximum(old_top, top)
        factor = jnp.exp(old_top - top)
        expos = jnp.where(visible, jnp.exp(scores - top), 0.0)
        end_expos = jnp.where(end_seen, jnp.exp(end_scores - top[:, :16]), 0.0)
        total = total_ref[part, :] * factor + (
            expos.sum(-1, keepdims=True) + end_expos.sum(-1, keepdims=True)
        )
        numer = (
            numer_ref[part, :] * factor
            + jnp.dot(expos.astype(jnp.bfloat16), value, preferred_element_type=jnp.float32)
            + jnp.dot(end_expos.astype(jnp.bfloat16), end_value, preferred_element_type=jnp.float32)
        )
        each = own_queries * sharing
        split = PAIR * each
        stats = jnp.concatenate(
            [
                kept_stats(top[:split, 0:1], total[:split, 0:1]),
                sent_stats(top[split:, 0:1], total[split:, 0:1]).astype(jnp.float32),
            ],
            0,
        )
        for slot in range(GROUPS * PAIR):
            start = (slot % PAIR * 2 * heads + head) * each
            at = slice(slot * each, (slot + 1) * each)
            out = outs[slot // PAIR]
            out[start : start + each, :] = numer[at].astype(out.dtype)
            out[start + heads * each : start + (heads + 1) * each, :] = stats[at].astype(out.dtype)
    for copy in leaving:
        copy.wait()


def kept_stats(top, total):
    lane = lax.broadcasted_iota(jnp.int32, (top.shape[0], LANES), 1)
    return jnp.where(lane < LANES // 2, top, total)


def sent_stats(top, total):
    terms = []
    for rest, count in ((top, 3), (total, 2)):
        for _ in range(count):
            term = rest.astype(jnp.bfloat16).astype(jnp.float32)
            terms.append(term)
            rest = rest - term
    part = lax.broadcasted_iota(jnp.int32, (top.shape[0], LANES), 1) // 16
    stats = jnp.broadcast_to(terms[-1], part.shape)
    for i, term in enumerate(terms[:-1]):
        stats = jnp.where(part == i, term, stats)
    return stats.astype(jnp.bfloat16)


def merged(kept, others, start, rows):
    half = LANES // 2
    stats = kept[start + rows : start + 2 * rows, :]
    tops, totals = [stats[:, 0:1]], [stats[:, half : half + 1]]
    numers = [kept[start : start + rows, :]]
    for other in others:
        terms = other[start + rows : start + 2 * rows, :].astype(jnp.float32)
        tops.append((terms[:, 0:1] + terms[:, 16:17]) + terms[:, 32:33])
        totals.append(terms[:, 48:49] + terms[:, 64:65])
        numers.append(other[start : start + rows, :].astype(jnp.float32))
    top = functools.reduce(jnp.maximum, tops)
    factors = [jnp.exp(t - top) for t in tops]
    total = sum(f * t for f, t in zip(factors, totals))
    numer = sum(f * n for f, n in zip(factors, numers))
    return numer, top, total


def merge_kernel(kept, *refs):
    others, (keep_ref, send_ref) = refs[:-2], refs[-2:]
    each = keep_ref.shape[0]
    rows = each // 2
    numer, top, total = merged(kept, others, 0, rows)
    keep_ref[:rows, :] = numer
    keep_ref[rows:, :] = kept_stats(top, total)
    numer, top, total = merged(kept, others, each, rows)
    send_ref[:rows, :] = numer.astype(jnp.bfloat16)
    send_ref[rows:, :] = sent_stats(top, total)


def last_kernel(kept, *refs):
    others, out_ref = refs[:-1], refs[-1]
    numer, _, total = merged(kept, others, 0, kept.shape[0] // 2)
    result = numer / total
    queries = out_ref.shape[0]
    pieces = [result[s : s + queries] for s in range(0, result.shape[0], queries)]
    out_ref[...] = jnp.concatenate(pieces, 1).astype(jnp.bfloat16)


def exchange_plan(
    hidden,
    suffix_hidden,
    norm_gain,
    key_matrix,
    value_matrix,
    key_offset_bias,
    value_offset_bias,
    suffix_query_rows,
    slot_keys,
    slot_values,
    page_slot_table,
    split_page,
):
    n_ctx = GROUPS * PAIR
    ctx = lax.axis_index("ctx").astype(jnp.int32)
    core = lax.axis_index("tp").astype(jnp.int32)
    rows, features = hidden.shape
    half_rows = rows // 2
    width = key_matrix.shape[1]
    query_width = suffix_query_rows.shape[1]
    prefix_len = page_slot_table.shape[0] * slot_keys.shape[1]
    smem = pl.BlockSpec(memory_space=pltpu.SMEM)
    vmem = pl.BlockSpec(memory_space=pltpu.VMEM)
    params = pltpu.CompilerParams(vmem_limit_bytes=48 * 1024 * 1024)

    def move(array, target):
        pairs = []
        for c in range(n_ctx):
            for t in range(2):
                to_c, to_t = target(c, t)
                pairs.append((c * 2 + t, to_c * 2 + to_t))
        return lax.ppermute(array, ("ctx", "tp"), pairs)

    def partner(away):
        return lambda c, t: (c ^ away, t)

    def along(shift):
        return partner(shift * PAIR)

    def beside(c, t):
        return (c ^ 1, t)

    def sibling(c, t):
        return (c, 1 - t)

    hbm = pl.BlockSpec(memory_space=pltpu.HBM)
    pieces = features // GROUPS // LANES
    own_queries = suffix_query_rows.shape[0]
    lines = query_width // LANES
    block_rows = pieces * half_rows + pieces + own_queries * lines
    blocks = {}
    for shifts in (tuple(far_first()[:1]), tuple(far_first()[1:]) + (0,)):
        found = pl.pallas_call(
            functools.partial(norm_kernel, shifts),
            in_specs=[hbm] * 4,
            out_specs=[hbm] * len(shifts),
            out_shape=[jax.ShapeDtypeStruct((block_rows, LANES), jnp.bfloat16)] * len(shifts),
            scratch_shapes=[
                pltpu.VMEM((half_rows, features), jnp.bfloat16),
                pltpu.VMEM(suffix_hidden.shape, jnp.bfloat16),
                pltpu.VMEM((1, features), jnp.float32),
                pltpu.VMEM(suffix_query_rows.shape, jnp.bfloat16),
                pltpu.VMEM((1, features), jnp.float32),
            ]
            + [pltpu.VMEM((block_rows, LANES), jnp.bfloat16)] * len(shifts)
            + [pltpu.SemaphoreType.DMA((CHUNKS + 3,)), pltpu.SemaphoreType.DMA((len(shifts),))],
            compiler_params=pltpu.CompilerParams(vmem_limit_bytes=60 * 1024 * 1024),
            cost_estimate=pl.CostEstimate(
                flops=4 * half_rows * features,
                bytes_accessed=4 * half_rows * features,
                transcendentals=0,
            ),
            name="norm_rows",
        )(suffix_query_rows, hidden, suffix_hidden, norm_gain.reshape(1, features))
        blocks.update(zip(shifts, found))
    own = blocks[0]
    *weights, blocks[2] = lax.optimization_barrier((key_matrix, value_matrix, blocks[2]))
    far = [move(matrix, beside) for matrix in weights]

    mine = {s: move(blocks[s], along(s)) for s in far_first()}
    inverse_freq = rope_base ** (
        -(jnp.arange(HEAD_SIZE // 2, dtype=jnp.float32) * (2.0 / HEAD_SIZE))
    )
    row = jnp.arange(rows + 16, dtype=jnp.int32)
    front_position = ctx * rows + (row + core * half_rows) % rows
    end_position = prefix_len + ctx * 2 + jnp.where(row == rows, core, 1 - core)
    position = jnp.where(row < rows, front_position, end_position)
    angles = position.astype(jnp.float32)[:, None] * inverse_freq[None, :]
    cosine, sine = jnp.cos(angles), jnp.sin(angles)
    cosine = jnp.concatenate([cosine, cosine], 1)
    sine = jnp.concatenate([-sine, sine], 1)

    first = far_first()[0]
    mine[0] = pl.pallas_call(
        fetch_kernel,
        in_specs=[hbm],
        out_specs=vmem,
        out_shape=jax.ShapeDtypeStruct(own.shape, own.dtype),
        scratch_shapes=[pltpu.SemaphoreType.DMA],
        compiler_params=params,
        cost_estimate=pl.CostEstimate(flops=0, bytes_accessed=64 * 1024 * 1024, transcendentals=0),
        name="fetch_own",
    )(own)
    mine[first], mine[0], cosine, sine = lax.optimization_barrier(
        (mine[first], mine[0], cosine, sine)
    )
    blocks[0], far[0] = lax.optimization_barrier((blocks[0], far[0]))
    theirs = {s: move(blocks[0] if s == 0 else mine[s], sibling) for s in [0] + far_first()}

    part_rows = 3 * (width // LANES) * rows + 16
    partials, own_tiles = {}, []
    for shifts in ((0, first), tuple(far_first()[1:])):
        *found, tiles = pl.pallas_call(
            functools.partial(project_kernel, shifts),
            in_specs=[vmem] * (2 * len(shifts) + 4 + len(own_tiles)),
            out_specs=[vmem] * (len(shifts) + 1),
            out_shape=[jax.ShapeDtypeStruct((part_rows, LANES), jnp.bfloat16)] * len(shifts)
            + [jax.ShapeDtypeStruct((GROUPS * own_queries * lines, LANES), jnp.bfloat16)],
            scratch_shapes=[
                pltpu.VMEM((len(shifts) * rows + 16, PAIR * features // n_ctx), jnp.bfloat16)
            ],
            compiler_params=params,
            cost_estimate=pl.CostEstimate(
                flops=2 * len(shifts) * rows * 2 * width * features // GROUPS,
                bytes_accessed=6 * 1024 * 1024,
                transcendentals=0,
            ),
            name="project",
        )(
            *[part[s] for s in shifts for part in (mine, theirs)],
            key_matrix,
            value_matrix,
            *far,
            *own_tiles,
        )
        partials.update(zip(shifts, found))
        own_tiles = [tiles]
    (own_tiles,) = own_tiles
    received = [move(partials[s], along(s)) for s in far_first()]
    early = pl.pallas_call(
        sum_kernel,
        in_specs=[vmem] * 2,
        out_specs=vmem,
        out_shape=jax.ShapeDtypeStruct((part_rows, LANES), jnp.float32),
        compiler_params=params,
        cost_estimate=pl.CostEstimate(flops=0, bytes_accessed=16 * 1024 * 1024, transcendentals=0),
        name="sum_early",
    )(partials[0], received[0])
    beside_tiles = move(own_tiles, beside)

    states = n_ctx * own_queries * query_width // HEAD_SIZE
    state = jax.ShapeDtypeStruct((states, LANES), jnp.float32)
    top, total, numer, queries = pl.pallas_call(
        loaded_kernel,
        in_specs=[smem, smem] + [vmem] * (PAIR + 2),
        out_specs=[vmem] * 4,
        out_shape=[state] * 3 + [jax.ShapeDtypeStruct((states, LANES), jnp.bfloat16)],
        compiler_params=params,
        cost_estimate=pl.CostEstimate(
            flops=4 * states * slot_keys.shape[0] * slot_keys.shape[1] * HEAD_SIZE,
            bytes_accessed=4 * slot_keys.size,
            transcendentals=states * slot_keys.shape[0] * slot_keys.shape[1],
        ),
        name="loaded_attention",
    )(page_slot_table, split_page, own_tiles, beside_tiles, slot_keys, slot_values)


    def payload(kind, slots):
        return jax.ShapeDtypeStruct((2 * slots * states // n_ctx, LANES), kind)

    row_shape = jax.ShapeDtypeStruct((rows, width), jnp.bfloat16)
    front_key, front_value, kept, *sent = pl.pallas_call(
        front_kernel,
        in_specs=[smem] + [vmem] * (GROUPS + 7),
        out_specs=[hbm] * 2 + [vmem] * GROUPS,
        scratch_shapes=[pltpu.VMEM((rows, width), jnp.bfloat16)] * 2 + [pltpu.SemaphoreType.DMA((2,))],
        out_shape=[row_shape] * 2 + [payload(jnp.float32, PAIR)] + [payload(jnp.bfloat16, PAIR)] * (GROUPS - 1),
        compiler_params=params,
        cost_estimate=pl.CostEstimate(flops=4 * states * rows * HEAD_SIZE, bytes_accessed=2 * 1024 * 1024, transcendentals=states * rows),
        name="front_attention",
    )(
        split_page,
        early,
        *received[1:],
        key_offset_bias.reshape(1, width),
        value_offset_bias.reshape(1, width),
        cosine,
        sine,
        queries,
        top,
        total,
        numer,
    )
    kept, sent = pl.pallas_call(
        merge_kernel,
        in_specs=[vmem] * GROUPS,
        out_specs=[vmem] * 2,
        out_shape=[payload(jnp.float32, 1), payload(jnp.bfloat16, 1)],
        compiler_params=params,
        name="merge",
    )(kept, *[move(sent[s - 1], along(s)) for s in range(GROUPS - 1, 0, -1)])
    attended = pl.pallas_call(
        last_kernel,
        in_specs=[vmem] * 2,
        out_specs=vmem,
        out_shape=jax.ShapeDtypeStruct((own_queries, query_width), jnp.bfloat16),
        compiler_params=params,
        name="finish",
    )(kept, move(sent, beside))
    return (front_key, front_value, attended)


def solution(mesh):
    per_device = exchange_plan if mesh.shape["ctx"] == GROUPS * PAIR else gathered_plan
    return jax.shard_map(
        per_device,
        mesh=mesh,
        in_specs=(
            P(("req", "ctx"), None),
            P(("req", "ctx"), None),
            P(),
            P("ctx", "tp"),
            P("ctx", "tp"),
            P("tp"),
            P("tp"),
            P(("req", "ctx"), "tp"),
            P(("req", "ctx"), None, "tp"),
            P(("req", "ctx"), None, "tp"),
            P("req"),
            P("req"),
        ),
        out_specs=(P(("req", "ctx"), "tp"), P(("req", "ctx"), "tp"), P(("req", "ctx"), "tp")),
        check_vma=False,
    )
```

```python
import functools
import math

import jax
import jax.numpy as jnp
from jax import lax
from jax.experimental import pallas as pl
from jax.experimental.pallas import tpu as pltpu
from jax.sharding import PartitionSpec as P

QUERY_HEADS = 32
KEY_VALUE_HEADS = 4
HEAD_SIZE = 128


epsilon = 1e-06
rope_base = 1000000.0
masked_score = -1e30


def rms_rows(matrix, norm_gain):
    widened = matrix.astype(jnp.float32)
    inverse = lax.rsqrt(jnp.mean(widened * widened, axis=-1, keepdims=True) + epsilon)
    return (widened * inverse * norm_gain).astype(jnp.bfloat16)


def rotate(key_rows, positions, head_dim):
    row_count = key_rows.shape[0]
    split_heads = key_rows.reshape(row_count, -1, head_dim)
    half_dim = head_dim // 2
    inverse_freq = rope_base ** (-(jnp.arange(half_dim, dtype=jnp.float32) * (2.0 / head_dim)))
    angles = positions.astype(jnp.float32)[:, None] * inverse_freq[None, :]
    cosine = jnp.concatenate([jnp.cos(angles), jnp.cos(angles)], -1)[:, None, :]
    sine = jnp.concatenate([jnp.sin(angles), jnp.sin(angles)], -1)[:, None, :]
    turned = jnp.concatenate([-split_heads[..., half_dim:], split_heads[..., :half_dim]], -1)
    return (split_heads * cosine + turned * sine).reshape(row_count, -1)


def gathered_plan(
    hidden,
    suffix_hidden,
    norm_gain,
    key_matrix,
    value_matrix,
    key_offset_bias,
    value_offset_bias,
    suffix_query_rows,
    slot_keys,
    slot_values,
    page_slot_table,
    split_page,
):
    ctx_index = lax.axis_index("ctx")
    queries = lax.all_gather(suffix_query_rows, "ctx", axis=0, tiled=True)
    front_rows = hidden.shape[0]
    suffix_rows = suffix_hidden.shape[0]
    page_size = slot_keys.shape[1]
    slot_count = slot_keys.shape[0]
    total_pages = page_slot_table.shape[0]
    prefix_len = total_pages * page_size
    normed = rms_rows(jnp.concatenate([hidden, suffix_hidden], 0), norm_gain)
    col_width = key_matrix.shape[1]

    def accumulate(block_rows):
        return jnp.dot(normed, block_rows, preferred_element_type=jnp.float32)

    key_acc = accumulate(lax.all_gather(key_matrix, "ctx", axis=0, tiled=True))
    value_acc = accumulate(lax.all_gather(value_matrix, "ctx", axis=0, tiled=True))
    front_pos = ctx_index * front_rows + jnp.arange(front_rows, dtype=jnp.int32)
    suffix_pos = prefix_len + ctx_index * suffix_rows + jnp.arange(suffix_rows, dtype=jnp.int32)
    new_keys = rotate(
        key_acc + key_offset_bias, jnp.concatenate([front_pos, suffix_pos], 0), HEAD_SIZE
    ).astype(jnp.bfloat16)
    new_values = (value_acc + value_offset_bias).astype(jnp.bfloat16)
    cut_pos = split_page[0] * page_size
    global_slot = ctx_index * slot_count + jnp.arange(slot_count, dtype=jnp.int32)
    page_index = jnp.arange(total_pages, dtype=jnp.int32)
    slot_hits = (page_slot_table[None, :] == global_slot[:, None]) & (
        page_index[None, :] >= split_page[0]
    )
    slot_live = jnp.max(slot_hits.astype(jnp.int32), axis=1) > 0
    every_key = jnp.concatenate(
        [new_keys[:front_rows], slot_keys.reshape(-1, col_width), new_keys[front_rows:]], 0
    )
    every_value = jnp.concatenate(
        [new_values[:front_rows], slot_values.reshape(-1, col_width), new_values[front_rows:]], 0
    )
    query_count = queries.shape[0]
    query_pos = prefix_len + jnp.arange(query_count, dtype=jnp.int32)
    prefix_seen = jnp.concatenate([front_pos < cut_pos, jnp.repeat(slot_live, page_size)], 0)
    suffix_seen = suffix_pos[None, :] <= query_pos[:, None]
    visible = jnp.concatenate(
        [jnp.broadcast_to(prefix_seen[None, :], (query_count, prefix_seen.shape[0])), suffix_seen],
        1,
    )
    visible_wide = visible[:, None, :]
    sharing_count = QUERY_HEADS // KEY_VALUE_HEADS
    local_heads = col_width // HEAD_SIZE
    grouped_heads = queries.reshape(query_count, local_heads, sharing_count, HEAD_SIZE)
    top_list = []
    total_list = []
    numer_list = []
    for current_head in range(local_heads):
        head_keys = every_key[:, current_head * HEAD_SIZE : (current_head + 1) * HEAD_SIZE]
        head_values = every_value[:, current_head * HEAD_SIZE : (current_head + 1) * HEAD_SIZE]
        scores = jnp.einsum(
            "qgd,ld->qgl",
            grouped_heads[:, current_head],
            head_keys,
            preferred_element_type=jnp.float32,
        ) * (1.0 / math.sqrt(HEAD_SIZE))
        scores = jnp.where(visible_wide, scores, masked_score)
        row_top = jnp.max(scores, axis=-1)
        expos = jnp.where(visible_wide, jnp.exp(scores - row_top[..., None]), 0.0)
        total_list.append(jnp.sum(expos, axis=-1))
        top_list.append(row_top)
        numer_list.append(
            jnp.einsum(
                "qgl,ld->qgd",
                expos.astype(jnp.bfloat16),
                head_values,
                preferred_element_type=jnp.float32,
            )
        )
    row_top = jnp.stack(top_list, 1)
    weight_total = jnp.stack(total_list, 1)
    numer = jnp.stack(numer_list, 1)
    global_top = lax.pmax(row_top, "ctx")
    factor = jnp.exp(row_top - global_top)
    own_total, own_numer = (
        lax.psum_scatter(
            (weight_total * factor).reshape(query_count, -1), "ctx", scatter_dimension=0, tiled=True
        ),
        lax.psum_scatter(
            (numer * factor[..., None]).reshape(query_count, -1),
            "ctx",
            scatter_dimension=0,
            tiled=True,
        ),
    )
    own_total = own_total.reshape(suffix_rows, local_heads, sharing_count)
    own_numer = own_numer.reshape(suffix_rows, local_heads, sharing_count, HEAD_SIZE)
    attended = (own_numer / own_total[..., None]).reshape(suffix_rows, -1).astype(jnp.bfloat16)
    return (new_keys[:front_rows], new_values[:front_rows], attended)

GROUPS = 4
PAIR = 2
LANES = 128
SCALE = 1.0 / math.sqrt(HEAD_SIZE)


def row_scale(values):
    mean = jnp.sum(values * values, axis=-1, keepdims=True) * (1.0 / values.shape[-1])
    return lax.rsqrt(mean + epsilon)


CHUNKS = 4


def far_first():
    return sorted(range(1, GROUPS), key=lambda s: s < GROUPS // 2)


def norm_kernel(shifts, query_any, hidden_any, suffix_any, gain_any, *rest):
    count = len(shifts)
    blocks_any, rest = rest[:count], rest[count:]
    (hidden_ref, suffix_ref, gain_ref, query_ref, tail_ref), rest = rest[:5], rest[5:]
    outs, (sems, out_sems) = rest[:count], rest[count:]
    core, ctx = lax.axis_index("tp"), lax.axis_index("ctx")
    z, x = ctx // PAIR, ctx % PAIR
    half_rows, features = hidden_ref.shape
    rows = half_rows // CHUNKS
    block = features // (GROUPS * PAIR)
    per_block = block // LANES
    pieces = PAIR * per_block
    copies = [
        pltpu.make_async_copy(gain_any, gain_ref, sems.at[CHUNKS]),
        pltpu.make_async_copy(suffix_any, suffix_ref, sems.at[CHUNKS + 1]),
        pltpu.make_async_copy(query_any, query_ref, sems.at[CHUNKS + 2]),
    ]
    for i in range(CHUNKS):
        start = pl.multiple_of(core * half_rows + i * rows, rows)
        copies.append(
            pltpu.make_async_copy(
                hidden_any.at[pl.ds(start, rows)], hidden_ref.at[i * rows : (i + 1) * rows], sems.at[i]
            )
        )
    for copy in copies:
        copy.start()

    def offset(shift, side, j):
        owner = (z ^ shift) * PAIR + (x ^ side)
        return pl.multiple_of(owner * block + j * LANES, LANES)

    copies[0].wait()
    copies[1].wait()
    copies[2].wait()
    query_rows = query_ref[...].astype(jnp.float32)
    lines = query_rows.shape[1] // LANES
    for r in range(query_rows.shape[0]):
        tile = [query_rows[r : r + 1, j * LANES : (j + 1) * LANES] for j in range(lines)]
        tile = jnp.concatenate(tile, 0).astype(jnp.bfloat16)
        start = pieces * half_rows + pieces + r * lines
        for out in outs:
            out[start : start + lines, :] = tile

    both = suffix_ref[...].astype(jnp.float32)
    normed = both * row_scale(both) * gain_ref[...]
    tail_ref[...] = jnp.where(core == 0, normed[0:1], normed[1:2])
    for shift, out in zip(shifts, outs):
        ends = [
            tail_ref[:, pl.ds(offset(shift, side, j), LANES)]
            for side in range(PAIR)
            for j in range(per_block)
        ]
        start = pieces * half_rows
        out[start : start + pieces, :] = jnp.concatenate(ends, 0).astype(jnp.bfloat16)
    inverses = []
    for i in range(CHUNKS):
        copies[3 + i].wait()
        inverses.append(row_scale(hidden_ref[i * rows : (i + 1) * rows, :].astype(jnp.float32)))
    leaving = []
    for place, (shift, out) in enumerate(zip(shifts, outs)):
        for side in range(PAIR):
            for j in range(per_block):
                columns = pl.ds(offset(shift, side, j), LANES)
                for i in range(CHUNKS):
                    piece = hidden_ref[i * rows : (i + 1) * rows, columns].astype(jnp.float32)
                    piece = piece * inverses[i] * gain_ref[:, columns]
                    start = (side * per_block + j) * half_rows + i * rows
                    out[start : start + rows, :] = piece.astype(jnp.bfloat16)
        leaving.append(pltpu.make_async_copy(out, blocks_any[place], out_sems.at[place]))
        leaving[-1].start()
    for copy in leaving:
        copy.wait()


def fetch_kernel(from_any, to_ref, sem):
    copy = pltpu.make_async_copy(from_any, to_ref, sem)
    copy.start()
    copy.wait()


def project_kernel(shifts, *refs):
    count = len(shifts)
    blocks, rest = refs[: 2 * count], refs[2 * count :]
    near_key, near_value, far_key, far_value = rest[:4]
    earlier, outs, (query_ref, lhs_ref) = rest[4 : -2 - count], rest[-2 - count : -2], rest[-2:]
    depth = near_key.shape[0]
    pieces = 2 * depth // LANES
    half_rows = (lhs_ref.shape[0] - 16) // (2 * count)
    rows = 2 * half_rows
    tails = []
    for i, block in enumerate(blocks):
        for j in range(pieces):
            lhs_ref[i * half_rows : (i + 1) * half_rows, j * LANES : (j + 1) * LANES] = block[
                j * half_rows : (j + 1) * half_rows, :
            ]
        tail = block[pieces * half_rows : pieces * half_rows + pieces, :].astype(jnp.float32)
        tails.append(jnp.concatenate([tail[j : j + 1] for j in range(pieces)], 1))
    tails.append(jnp.zeros((16 - len(tails), 2 * depth), jnp.float32))
    lines = query_ref.shape[0] // GROUPS
    if earlier:
        query_ref[...] = earlier[0][...]
    for i, shift in enumerate(shifts):
        block = blocks[2 * i]
        query_ref[shift * lines : (shift + 1) * lines, :] = block[block.shape[0] - lines :, :]
    total = count * rows
    lhs_ref[total : total + 16, :] = jnp.concatenate(tails, 0).astype(jnp.bfloat16)

    def product(near, far):
        return jnp.dot(
            lhs_ref[:, :depth], near[...], preferred_element_type=jnp.float32
        ) + jnp.dot(lhs_ref[:, depth:], far[...], preferred_element_type=jnp.float32)

    keys = product(near_key, far_key)
    values = product(near_value, far_value)
    high = keys.astype(jnp.bfloat16).astype(jnp.float32)
    low = keys - high
    columns = []
    for array in (high, low, values):
        for j in range(array.shape[1] // LANES):
            columns.append(array[:, j * LANES : (j + 1) * LANES])
    for i, out in enumerate(outs):
        for k, column in enumerate(columns):
            out[k * rows : (k + 1) * rows, :] = column[i * rows : (i + 1) * rows].astype(jnp.bfloat16)
        ends = [c[total + 2 * i : total + 2 * i + 2] for c in columns]
        ends.append(jnp.zeros((16 - 2 * len(columns), LANES), jnp.float32))
        out[len(columns) * rows :, :] = jnp.concatenate(ends, 0).astype(jnp.bfloat16)


def head_queries(parts, head, width):
    sharing = QUERY_HEADS // KEY_VALUE_HEADS
    lines = sharing * width // HEAD_SIZE
    each = parts[0].shape[0] // GROUPS
    found = []
    for group in range(GROUPS):
        for part in parts:
            tiles = part[group * each : (group + 1) * each, :].astype(jnp.float32)
            for line in range(head * sharing, (head + 1) * sharing):
                found += [tiles[start : start + 1] for start in range(line, each, lines)]
    return jnp.concatenate(found, 0).astype(jnp.bfloat16)


def times_transposed(a, b):
    return lax.dot_general(a, b, (((1,), (1,)), ((), ())), preferred_element_type=jnp.float32)


def loaded_kernel(table_ref, split_ref, *refs):
    parts = refs[:PAIR]
    key_ref, value_ref, top_ref, total_ref, numer_ref, query_ref = refs[PAIR:]
    ctx = lax.axis_index("ctx")
    slots, page, width = key_ref.shape
    heads = width // HEAD_SIZE
    split = split_ref[0]
    live = []
    for s in range(slots):
        hit = jnp.int32(0)
        for p in range(table_ref.shape[0]):
            hit = hit | ((table_ref[p] == ctx * slots + s) & (p >= split)).astype(jnp.int32)
        live.append(hit)
    for head in range(heads):
        columns = slice(head * HEAD_SIZE, (head + 1) * HEAD_SIZE)
        queries = head_queries(parts, head, width)
        count = queries.shape[0]
        query_ref[head * count : (head + 1) * count, :] = queries
        scores = [
            jnp.where(live[s] > 0, times_transposed(queries, key_ref[s, :, columns]) * SCALE, masked_score)
            for s in range(slots)
        ]
        top = scores[0].max(-1, keepdims=True)
        for s in range(1, slots):
            top = jnp.maximum(top, scores[s].max(-1, keepdims=True))
        total = jnp.zeros((count, 1), jnp.float32)
        numer = jnp.zeros((count, HEAD_SIZE), jnp.float32)
        for s in range(slots):
            expos = jnp.where(live[s] > 0, jnp.exp(scores[s] - top), 0.0)
            total += expos.sum(-1, keepdims=True)
            numer += jnp.dot(
                expos.astype(jnp.bfloat16), value_ref[s, :, columns], preferred_element_type=jnp.float32
            )
        rows = slice(head * count, (head + 1) * count)
        top_ref[rows, :] = jnp.broadcast_to(top, (count, LANES))
        total_ref[rows, :] = jnp.broadcast_to(total, (count, LANES))
        numer_ref[rows, :] = numer


def sum_kernel(one, other, key_bias, value_bias, out):
    heads = key_bias.shape[1] // HEAD_SIZE
    rows = (one.shape[0] - 16) // (3 * heads)

    def summed(start, size):
        at = slice(start, start + size)
        return one[at, :].astype(jnp.float32) + other[at, :].astype(jnp.float32)

    for head in range(heads):
        columns = slice(head * HEAD_SIZE, (head + 1) * HEAD_SIZE)
        keys = summed(head * rows, rows) + summed((heads + head) * rows, rows)
        out[head * rows : (head + 1) * rows, :] = keys + key_bias[:, columns]
        out[(heads + head) * rows : (heads + head + 1) * rows, :] = (
            summed((2 * heads + head) * rows, rows) + value_bias[:, columns]
        )
    out[2 * heads * rows :, :] = summed(3 * heads * rows, 16)


def front_kernel(split_ref, early, *refs):
    received = refs[: GROUPS - 2]
    (key_bias, value_bias, cosine_ref, sine_ref, query_ref, top_ref, total_ref, numer_ref) = refs[
        GROUPS - 2 : GROUPS + 6
    ]
    key_any, value_any, *outs = refs[GROUPS + 6 : -3]
    front_key, front_value, sems = refs[-3:]
    core, ctx = lax.axis_index("tp"), lax.axis_index("ctx")
    rows, width = front_key.shape
    half_rows = rows // 2
    heads = width // HEAD_SIZE
    sharing = QUERY_HEADS // KEY_VALUE_HEADS
    count = query_ref.shape[0] // heads
    own_queries = count // sharing // (GROUPS * PAIR)
    visible = ctx < split_ref[0]

    def summed(start, *places):
        size = rows if start < 2 * heads * rows else 16
        value = early[start : start + size, :]
        for ref in received:
            for place in places:
                value += ref[place : place + size, :].astype(jnp.float32)
        return value

    ends = summed(2 * heads * rows, 3 * heads * rows)
    row = lax.broadcasted_iota(jnp.int32, (count, 16), 0)
    query_position = (ctx ^ (row // (own_queries * sharing))) * own_queries + row % own_queries
    end_column = lax.broadcasted_iota(jnp.int32, (count, 16), 1)
    end_position = ctx * 2 + jnp.where(end_column == 0, core, 1 - core)
    end_seen = (end_column < 2) & (end_position <= query_position)
    pad = jnp.zeros((14, HEAD_SIZE), jnp.float32)
    end_pairs = []
    for head in range(heads):
        columns = slice(head * HEAD_SIZE, (head + 1) * HEAD_SIZE)
        raw = summed(head * rows, head * rows, (heads + head) * rows)
        value = summed((heads + head) * rows, (2 * heads + head) * rows).astype(jnp.bfloat16)
        end_raw = ends[2 * head : 2 * head + 2] + ends[2 * (heads + head) : 2 * (heads + head) + 2]
        end_value = ends[2 * (2 * heads + head) : 2 * (2 * heads + head) + 2] + value_bias[:, columns]
        end_raw = jnp.concatenate([end_raw + key_bias[:, columns], pad], 0)
        end_value = jnp.concatenate([end_value, pad], 0).astype(jnp.bfloat16)

        def rotated(k, part):
            turned = pltpu.roll(k, HEAD_SIZE // 2, 1)
            return (k * cosine_ref[part, :] + turned * sine_ref[part, :]).astype(jnp.bfloat16)

        key = rotated(raw, slice(0, rows))
        end_key = rotated(end_raw, slice(rows, rows + 16))
        for half in range(2):
            to = pl.ds(pl.multiple_of(lax.rem(core + half, 2) * half_rows, half_rows), half_rows)
            front_key[to, columns] = key[half * half_rows : (half + 1) * half_rows]
            front_value[to, columns] = value[half * half_rows : (half + 1) * half_rows]
        end_pairs.append((key, value, end_key, end_value))
    leaving = [
        pltpu.make_async_copy(front_key, key_any, sems.at[0]),
        pltpu.make_async_copy(front_value, value_any, sems.at[1]),
    ]
    for copy in leaving:
        copy.start()
    for head, (key, value, end_key, end_value) in enumerate(end_pairs):
        part = slice(head * count, (head + 1) * count)
        queries = query_ref[part, :]
        scores = jnp.where(visible, times_transposed(queries, key) * SCALE, masked_score)
        end_scores = jnp.where(end_seen, times_transposed(queries, end_key) * SCALE, masked_score)
        old_top = top_ref[part, :]
        top = jnp.maximum(scores.max(-1, keepdims=True), end_scores.max(-1, keepdims=True))
        top = jnp.maximum(old_top, top)
        factor = jnp.exp(old_top - top)
        expos = jnp.where(visible, jnp.exp(scores - top), 0.0)
        end_expos = jnp.where(end_seen, jnp.exp(end_scores - top[:, :16]), 0.0)
        total = total_ref[part, :] * factor + (
            expos.sum(-1, keepdims=True) + end_expos.sum(-1, keepdims=True)
        )
        numer = (
            numer_ref[part, :] * factor
            + jnp.dot(expos.astype(jnp.bfloat16), value, preferred_element_type=jnp.float32)
            + jnp.dot(end_expos.astype(jnp.bfloat16), end_value, preferred_element_type=jnp.float32)
        )
        each = own_queries * sharing
        split = PAIR * each
        stats = jnp.concatenate(
            [
                kept_stats(top[:split, 0:1], total[:split, 0:1]),
                sent_stats(top[split:, 0:1], total[split:, 0:1]).astype(jnp.float32),
            ],
            0,
        )
        for slot in range(GROUPS * PAIR):
            start = (slot % PAIR * 2 * heads + head) * each
            at = slice(slot * each, (slot + 1) * each)
            out = outs[slot // PAIR]
            out[start : start + each, :] = numer[at].astype(out.dtype)
            out[start + heads * each : start + (heads + 1) * each, :] = stats[at].astype(out.dtype)
    for copy in leaving:
        copy.wait()


def kept_stats(top, total):
    lane = lax.broadcasted_iota(jnp.int32, (top.shape[0], LANES), 1)
    return jnp.where(lane < LANES // 2, top, total)


def sent_stats(top, total):
    terms = []
    for rest, count in ((top, 3), (total, 2)):
        for _ in range(count):
            term = rest.astype(jnp.bfloat16).astype(jnp.float32)
            terms.append(term)
            rest = rest - term
    part = lax.broadcasted_iota(jnp.int32, (top.shape[0], LANES), 1) // 16
    stats = jnp.broadcast_to(terms[-1], part.shape)
    for i, term in enumerate(terms[:-1]):
        stats = jnp.where(part == i, term, stats)
    return stats.astype(jnp.bfloat16)


def merged(kept, others, start, rows):
    half = LANES // 2
    stats = kept[start + rows : start + 2 * rows, :]
    tops, totals = [stats[:, 0:1]], [stats[:, half : half + 1]]
    numers = [kept[start : start + rows, :]]
    for other in others:
        terms = other[start + rows : start + 2 * rows, :].astype(jnp.float32)
        tops.append((terms[:, 0:1] + terms[:, 16:17]) + terms[:, 32:33])
        totals.append(terms[:, 48:49] + terms[:, 64:65])
        numers.append(other[start : start + rows, :].astype(jnp.float32))
    top = functools.reduce(jnp.maximum, tops)
    factors = [jnp.exp(t - top) for t in tops]
    total = sum(f * t for f, t in zip(factors, totals))
    numer = sum(f * n for f, n in zip(factors, numers))
    return numer, top, total


def merge_kernel(kept, *refs):
    others, (keep_ref, send_ref) = refs[:-2], refs[-2:]
    each = keep_ref.shape[0]
    rows = each // 2
    numer, top, total = merged(kept, others, 0, rows)
    keep_ref[:rows, :] = numer
    keep_ref[rows:, :] = kept_stats(top, total)
    numer, top, total = merged(kept, others, each, rows)
    send_ref[:rows, :] = numer.astype(jnp.bfloat16)
    send_ref[rows:, :] = sent_stats(top, total)


def last_kernel(kept, *refs):
    others, out_ref = refs[:-1], refs[-1]
    numer, _, total = merged(kept, others, 0, kept.shape[0] // 2)
    result = numer / total
    queries = out_ref.shape[0]
    pieces = [result[s : s + queries] for s in range(0, result.shape[0], queries)]
    out_ref[...] = jnp.concatenate(pieces, 1).astype(jnp.bfloat16)


def exchange_plan(
    hidden,
    suffix_hidden,
    norm_gain,
    key_matrix,
    value_matrix,
    key_offset_bias,
    value_offset_bias,
    suffix_query_rows,
    slot_keys,
    slot_values,
    page_slot_table,
    split_page,
):
    n_ctx = GROUPS * PAIR
    ctx = lax.axis_index("ctx").astype(jnp.int32)
    core = lax.axis_index("tp").astype(jnp.int32)
    rows, features = hidden.shape
    half_rows = rows // 2
    width = key_matrix.shape[1]
    query_width = suffix_query_rows.shape[1]
    prefix_len = page_slot_table.shape[0] * slot_keys.shape[1]
    smem = pl.BlockSpec(memory_space=pltpu.SMEM)
    vmem = pl.BlockSpec(memory_space=pltpu.VMEM)
    params = pltpu.CompilerParams(vmem_limit_bytes=48 * 1024 * 1024)

    def move(array, target):
        pairs = []
        for c in range(n_ctx):
            for t in range(2):
                to_c, to_t = target(c, t)
                pairs.append((c * 2 + t, to_c * 2 + to_t))
        return lax.ppermute(array, ("ctx", "tp"), pairs)

    def partner(away):
        return lambda c, t: (c ^ away, t)

    def along(shift):
        return partner(shift * PAIR)

    def beside(c, t):
        return (c ^ 1, t)

    def sibling(c, t):
        return (c, 1 - t)

    hbm = pl.BlockSpec(memory_space=pltpu.HBM)
    pieces = features // GROUPS // LANES
    own_queries = suffix_query_rows.shape[0]
    lines = query_width // LANES
    block_rows = pieces * half_rows + pieces + own_queries * lines
    blocks = {}
    for shifts in (tuple(far_first()[:1]), tuple(far_first()[1:]) + (0,)):
        found = pl.pallas_call(
            functools.partial(norm_kernel, shifts),
            in_specs=[hbm] * 4,
            out_specs=[hbm] * len(shifts),
            out_shape=[jax.ShapeDtypeStruct((block_rows, LANES), jnp.bfloat16)] * len(shifts),
            scratch_shapes=[
                pltpu.VMEM((half_rows, features), jnp.bfloat16),
                pltpu.VMEM(suffix_hidden.shape, jnp.bfloat16),
                pltpu.VMEM((1, features), jnp.float32),
                pltpu.VMEM(suffix_query_rows.shape, jnp.bfloat16),
                pltpu.VMEM((1, features), jnp.float32),
            ]
            + [pltpu.VMEM((block_rows, LANES), jnp.bfloat16)] * len(shifts)
            + [pltpu.SemaphoreType.DMA((CHUNKS + 3,)), pltpu.SemaphoreType.DMA((len(shifts),))],
            compiler_params=pltpu.CompilerParams(vmem_limit_bytes=60 * 1024 * 1024),
            cost_estimate=pl.CostEstimate(
                flops=4 * half_rows * features,
                bytes_accessed=4 * half_rows * features,
                transcendentals=0,
            ),
            name="norm_rows",
        )(suffix_query_rows, hidden, suffix_hidden, norm_gain.reshape(1, features))
        blocks.update(zip(shifts, found))
    own = blocks[0]
    *weights, blocks[2] = lax.optimization_barrier((key_matrix, value_matrix, blocks[2]))
    far = [move(matrix, beside) for matrix in weights]

    mine = {s: move(blocks[s], along(s)) for s in far_first()}
    inverse_freq = rope_base ** (
        -(jnp.arange(HEAD_SIZE // 2, dtype=jnp.float32) * (2.0 / HEAD_SIZE))
    )
    row = jnp.arange(rows + 16, dtype=jnp.int32)
    front_position = ctx * rows + (row + core * half_rows) % rows
    end_position = prefix_len + ctx * 2 + jnp.where(row == rows, core, 1 - core)
    position = jnp.where(row < rows, front_position, end_position)
    angles = position.astype(jnp.float32)[:, None] * inverse_freq[None, :]
    cosine, sine = jnp.cos(angles), jnp.sin(angles)
    cosine = jnp.concatenate([cosine, cosine], 1)
    sine = jnp.concatenate([-sine, sine], 1)

    first = far_first()[0]
    mine[0] = pl.pallas_call(
        fetch_kernel,
        in_specs=[hbm],
        out_specs=vmem,
        out_shape=jax.ShapeDtypeStruct(own.shape, own.dtype),
        scratch_shapes=[pltpu.SemaphoreType.DMA],
        compiler_params=params,
        cost_estimate=pl.CostEstimate(flops=0, bytes_accessed=64 * 1024 * 1024, transcendentals=0),
        name="fetch_own",
    )(own)
    mine[first], mine[0], cosine, sine = lax.optimization_barrier(
        (mine[first], mine[0], cosine, sine)
    )
    blocks[0], far[0] = lax.optimization_barrier((blocks[0], far[0]))
    theirs = {s: move(blocks[0] if s == 0 else mine[s], sibling) for s in [0] + far_first()}

    part_rows = 3 * (width // LANES) * rows + 16
    partials, own_tiles = {}, []
    for shifts in ((0, first), tuple(far_first()[1:])):
        *found, tiles = pl.pallas_call(
            functools.partial(project_kernel, shifts),
            in_specs=[vmem] * (2 * len(shifts) + 4 + len(own_tiles)),
            out_specs=[vmem] * (len(shifts) + 1),
            out_shape=[jax.ShapeDtypeStruct((part_rows, LANES), jnp.bfloat16)] * len(shifts)
            + [jax.ShapeDtypeStruct((GROUPS * own_queries * lines, LANES), jnp.bfloat16)],
            scratch_shapes=[
                pltpu.VMEM((len(shifts) * rows + 16, PAIR * features // n_ctx), jnp.bfloat16)
            ],
            compiler_params=params,
            cost_estimate=pl.CostEstimate(
                flops=2 * len(shifts) * rows * 2 * width * features // GROUPS,
                bytes_accessed=6 * 1024 * 1024,
                transcendentals=0,
            ),
            name="project",
        )(
            *[part[s] for s in shifts for part in (mine, theirs)],
            key_matrix,
            value_matrix,
            *far,
            *own_tiles,
        )
        partials.update(zip(shifts, found))
        own_tiles = [tiles]
    (own_tiles,) = own_tiles
    received = [move(partials[s], along(s)) for s in far_first()]
    biases = [bias.reshape(1, width) for bias in (key_offset_bias, value_offset_bias)]
    early = pl.pallas_call(
        sum_kernel,
        in_specs=[vmem] * 4,
        out_specs=vmem,
        out_shape=jax.ShapeDtypeStruct((2 * (width // LANES) * rows + 16, LANES), jnp.float32),
        compiler_params=params,
        cost_estimate=pl.CostEstimate(flops=0, bytes_accessed=16 * 1024 * 1024, transcendentals=0),
        name="sum_early",
    )(partials[0], received[0], *biases)
    beside_tiles = move(own_tiles, beside)

    states = n_ctx * own_queries * query_width // HEAD_SIZE
    state = jax.ShapeDtypeStruct((states, LANES), jnp.float32)
    top, total, numer, queries = pl.pallas_call(
        loaded_kernel,
        in_specs=[smem, smem] + [vmem] * (PAIR + 2),
        out_specs=[vmem] * 4,
        out_shape=[state] * 3 + [jax.ShapeDtypeStruct((states, LANES), jnp.bfloat16)],
        compiler_params=params,
        cost_estimate=pl.CostEstimate(
            flops=4 * states * slot_keys.shape[0] * slot_keys.shape[1] * HEAD_SIZE,
            bytes_accessed=4 * slot_keys.size,
            transcendentals=states * slot_keys.shape[0] * slot_keys.shape[1],
        ),
        name="loaded_attention",
    )(page_slot_table, split_page, own_tiles, beside_tiles, slot_keys, slot_values)


    def payload(kind, slots):
        return jax.ShapeDtypeStruct((2 * slots * states // n_ctx, LANES), kind)

    row_shape = jax.ShapeDtypeStruct((rows, width), jnp.bfloat16)
    front_key, front_value, kept, *sent = pl.pallas_call(
        front_kernel,
        in_specs=[smem] + [vmem] * (GROUPS + 7),
        out_specs=[hbm] * 2 + [vmem] * GROUPS,
        scratch_shapes=[pltpu.VMEM((rows, width), jnp.bfloat16)] * 2 + [pltpu.SemaphoreType.DMA((2,))],
        out_shape=[row_shape] * 2 + [payload(jnp.float32, PAIR)] + [payload(jnp.bfloat16, PAIR)] * (GROUPS - 1),
        compiler_params=params,
        cost_estimate=pl.CostEstimate(flops=4 * states * rows * HEAD_SIZE, bytes_accessed=2 * 1024 * 1024, transcendentals=states * rows),
        name="front_attention",
    )(
        split_page,
        early,
        *received[1:],
        *biases,
        cosine,
        sine,
        queries,
        top,
        total,
        numer,
    )
    kept, sent = pl.pallas_call(
        merge_kernel,
        in_specs=[vmem] * GROUPS,
        out_specs=[vmem] * 2,
        out_shape=[payload(jnp.float32, 1), payload(jnp.bfloat16, 1)],
        compiler_params=params,
        name="merge",
    )(kept, *[move(sent[s - 1], along(s)) for s in range(GROUPS - 1, 0, -1)])
    attended = pl.pallas_call(
        last_kernel,
        in_specs=[vmem] * 2,
        out_specs=vmem,
        out_shape=jax.ShapeDtypeStruct((own_queries, query_width), jnp.bfloat16),
        compiler_params=params,
        name="finish",
    )(kept, move(sent, beside))
    return (front_key, front_value, attended)


def solution(mesh):
    per_device = exchange_plan if mesh.shape["ctx"] == GROUPS * PAIR else gathered_plan
    return jax.shard_map(
        per_device,
        mesh=mesh,
        in_specs=(
            P(("req", "ctx"), None),
            P(("req", "ctx"), None),
            P(),
            P("ctx", "tp"),
            P("ctx", "tp"),
            P("tp"),
            P("tp"),
            P(("req", "ctx"), "tp"),
            P(("req", "ctx"), None, "tp"),
            P(("req", "ctx"), None, "tp"),
            P("req"),
            P("req"),
        ),
        out_specs=(P(("req", "ctx"), "tp"), P(("req", "ctx"), "tp"), P(("req", "ctx"), "tp")),
        check_vma=False,
    )
```

```python
import functools
import math

import jax
import jax.numpy as jnp
from jax import lax
from jax.experimental import pallas as pl
from jax.experimental.pallas import tpu as pltpu
from jax.sharding import PartitionSpec as P

QUERY_HEADS = 32
KEY_VALUE_HEADS = 4
HEAD_SIZE = 128


epsilon = 1e-06
rope_base = 1000000.0
masked_score = -1e30


def rms_rows(matrix, norm_gain):
    widened = matrix.astype(jnp.float32)
    inverse = lax.rsqrt(jnp.mean(widened * widened, axis=-1, keepdims=True) + epsilon)
    return (widened * inverse * norm_gain).astype(jnp.bfloat16)


def rotate(key_rows, positions, head_dim):
    row_count = key_rows.shape[0]
    split_heads = key_rows.reshape(row_count, -1, head_dim)
    half_dim = head_dim // 2
    inverse_freq = rope_base ** (-(jnp.arange(half_dim, dtype=jnp.float32) * (2.0 / head_dim)))
    angles = positions.astype(jnp.float32)[:, None] * inverse_freq[None, :]
    cosine = jnp.concatenate([jnp.cos(angles), jnp.cos(angles)], -1)[:, None, :]
    sine = jnp.concatenate([jnp.sin(angles), jnp.sin(angles)], -1)[:, None, :]
    turned = jnp.concatenate([-split_heads[..., half_dim:], split_heads[..., :half_dim]], -1)
    return (split_heads * cosine + turned * sine).reshape(row_count, -1)


def gathered_plan(
    hidden,
    suffix_hidden,
    norm_gain,
    key_matrix,
    value_matrix,
    key_offset_bias,
    value_offset_bias,
    suffix_query_rows,
    slot_keys,
    slot_values,
    page_slot_table,
    split_page,
):
    ctx_index = lax.axis_index("ctx")
    queries = lax.all_gather(suffix_query_rows, "ctx", axis=0, tiled=True)
    front_rows = hidden.shape[0]
    suffix_rows = suffix_hidden.shape[0]
    page_size = slot_keys.shape[1]
    slot_count = slot_keys.shape[0]
    total_pages = page_slot_table.shape[0]
    prefix_len = total_pages * page_size
    normed = rms_rows(jnp.concatenate([hidden, suffix_hidden], 0), norm_gain)
    col_width = key_matrix.shape[1]

    def accumulate(block_rows):
        return jnp.dot(normed, block_rows, preferred_element_type=jnp.float32)

    key_acc = accumulate(lax.all_gather(key_matrix, "ctx", axis=0, tiled=True))
    value_acc = accumulate(lax.all_gather(value_matrix, "ctx", axis=0, tiled=True))
    front_pos = ctx_index * front_rows + jnp.arange(front_rows, dtype=jnp.int32)
    suffix_pos = prefix_len + ctx_index * suffix_rows + jnp.arange(suffix_rows, dtype=jnp.int32)
    new_keys = rotate(
        key_acc + key_offset_bias, jnp.concatenate([front_pos, suffix_pos], 0), HEAD_SIZE
    ).astype(jnp.bfloat16)
    new_values = (value_acc + value_offset_bias).astype(jnp.bfloat16)
    cut_pos = split_page[0] * page_size
    global_slot = ctx_index * slot_count + jnp.arange(slot_count, dtype=jnp.int32)
    page_index = jnp.arange(total_pages, dtype=jnp.int32)
    slot_hits = (page_slot_table[None, :] == global_slot[:, None]) & (
        page_index[None, :] >= split_page[0]
    )
    slot_live = jnp.max(slot_hits.astype(jnp.int32), axis=1) > 0
    every_key = jnp.concatenate(
        [new_keys[:front_rows], slot_keys.reshape(-1, col_width), new_keys[front_rows:]], 0
    )
    every_value = jnp.concatenate(
        [new_values[:front_rows], slot_values.reshape(-1, col_width), new_values[front_rows:]], 0
    )
    query_count = queries.shape[0]
    query_pos = prefix_len + jnp.arange(query_count, dtype=jnp.int32)
    prefix_seen = jnp.concatenate([front_pos < cut_pos, jnp.repeat(slot_live, page_size)], 0)
    suffix_seen = suffix_pos[None, :] <= query_pos[:, None]
    visible = jnp.concatenate(
        [jnp.broadcast_to(prefix_seen[None, :], (query_count, prefix_seen.shape[0])), suffix_seen],
        1,
    )
    visible_wide = visible[:, None, :]
    sharing_count = QUERY_HEADS // KEY_VALUE_HEADS
    local_heads = col_width // HEAD_SIZE
    grouped_heads = queries.reshape(query_count, local_heads, sharing_count, HEAD_SIZE)
    top_list = []
    total_list = []
    numer_list = []
    for current_head in range(local_heads):
        head_keys = every_key[:, current_head * HEAD_SIZE : (current_head + 1) * HEAD_SIZE]
        head_values = every_value[:, current_head * HEAD_SIZE : (current_head + 1) * HEAD_SIZE]
        scores = jnp.einsum(
            "qgd,ld->qgl",
            grouped_heads[:, current_head],
            head_keys,
            preferred_element_type=jnp.float32,
        ) * (1.0 / math.sqrt(HEAD_SIZE))
        scores = jnp.where(visible_wide, scores, masked_score)
        row_top = jnp.max(scores, axis=-1)
        expos = jnp.where(visible_wide, jnp.exp(scores - row_top[..., None]), 0.0)
        total_list.append(jnp.sum(expos, axis=-1))
        top_list.append(row_top)
        numer_list.append(
            jnp.einsum(
                "qgl,ld->qgd",
                expos.astype(jnp.bfloat16),
                head_values,
                preferred_element_type=jnp.float32,
            )
        )
    row_top = jnp.stack(top_list, 1)
    weight_total = jnp.stack(total_list, 1)
    numer = jnp.stack(numer_list, 1)
    global_top = lax.pmax(row_top, "ctx")
    factor = jnp.exp(row_top - global_top)
    own_total, own_numer = (
        lax.psum_scatter(
            (weight_total * factor).reshape(query_count, -1), "ctx", scatter_dimension=0, tiled=True
        ),
        lax.psum_scatter(
            (numer * factor[..., None]).reshape(query_count, -1),
            "ctx",
            scatter_dimension=0,
            tiled=True,
        ),
    )
    own_total = own_total.reshape(suffix_rows, local_heads, sharing_count)
    own_numer = own_numer.reshape(suffix_rows, local_heads, sharing_count, HEAD_SIZE)
    attended = (own_numer / own_total[..., None]).reshape(suffix_rows, -1).astype(jnp.bfloat16)
    return (new_keys[:front_rows], new_values[:front_rows], attended)

GROUPS = 4
PAIR = 2
LANES = 128
SCALE = 1.0 / math.sqrt(HEAD_SIZE)


def row_scale(values):
    mean = jnp.sum(values * values, axis=-1, keepdims=True) * (1.0 / values.shape[-1])
    return lax.rsqrt(mean + epsilon)


CHUNKS = 4


def far_first():
    return sorted(range(1, GROUPS), key=lambda s: s < GROUPS // 2)


def norm_kernel(shifts, query_any, hidden_any, suffix_any, gain_any, *rest):
    count = len(shifts)
    blocks_any, rest = rest[:count], rest[count:]
    (hidden_ref, suffix_ref, gain_ref, query_ref, tail_ref), rest = rest[:5], rest[5:]
    outs, (sems, out_sems) = rest[:count], rest[count:]
    core, ctx = lax.axis_index("tp"), lax.axis_index("ctx")
    z, x = ctx // PAIR, ctx % PAIR
    half_rows, features = hidden_ref.shape
    rows = half_rows // CHUNKS
    block = features // (GROUPS * PAIR)
    per_block = block // LANES
    pieces = PAIR * per_block
    copies = [
        pltpu.make_async_copy(gain_any, gain_ref, sems.at[CHUNKS]),
        pltpu.make_async_copy(suffix_any, suffix_ref, sems.at[CHUNKS + 1]),
        pltpu.make_async_copy(query_any, query_ref, sems.at[CHUNKS + 2]),
    ]
    for i in range(CHUNKS):
        start = pl.multiple_of(core * half_rows + i * rows, rows)
        copies.append(
            pltpu.make_async_copy(
                hidden_any.at[pl.ds(start, rows)], hidden_ref.at[i * rows : (i + 1) * rows], sems.at[i]
            )
        )
    for copy in copies:
        copy.start()

    def offset(shift, side, j):
        owner = (z ^ shift) * PAIR + (x ^ side)
        return pl.multiple_of(owner * block + j * LANES, LANES)

    copies[0].wait()
    copies[1].wait()
    copies[2].wait()
    query_rows = query_ref[...].astype(jnp.float32)
    lines = query_rows.shape[1] // LANES
    for r in range(query_rows.shape[0]):
        tile = [query_rows[r : r + 1, j * LANES : (j + 1) * LANES] for j in range(lines)]
        tile = jnp.concatenate(tile, 0).astype(jnp.bfloat16)
        start = pieces * half_rows + pieces + r * lines
        for out in outs:
            out[start : start + lines, :] = tile

    both = suffix_ref[...].astype(jnp.float32)
    normed = both * row_scale(both) * gain_ref[...]
    tail_ref[...] = jnp.where(core == 0, normed[0:1], normed[1:2])
    for shift, out in zip(shifts, outs):
        ends = [
            tail_ref[:, pl.ds(offset(shift, side, j), LANES)]
            for side in range(PAIR)
            for j in range(per_block)
        ]
        start = pieces * half_rows
        out[start : start + pieces, :] = jnp.concatenate(ends, 0).astype(jnp.bfloat16)
    inverses = []
    for i in range(CHUNKS):
        copies[3 + i].wait()
        inverses.append(row_scale(hidden_ref[i * rows : (i + 1) * rows, :].astype(jnp.float32)))
    leaving = []
    for place, (shift, out) in enumerate(zip(shifts, outs)):
        for side in range(PAIR):
            for j in range(per_block):
                columns = pl.ds(offset(shift, side, j), LANES)
                for i in range(CHUNKS):
                    piece = hidden_ref[i * rows : (i + 1) * rows, columns].astype(jnp.float32)
                    piece = piece * inverses[i] * gain_ref[:, columns]
                    start = (side * per_block + j) * half_rows + i * rows
                    out[start : start + rows, :] = piece.astype(jnp.bfloat16)
        leaving.append(pltpu.make_async_copy(out, blocks_any[place], out_sems.at[place]))
        leaving[-1].start()
    for copy in leaving:
        copy.wait()


def fetch_kernel(from_any, to_ref, sem):
    copy = pltpu.make_async_copy(from_any, to_ref, sem)
    copy.start()
    copy.wait()


def project_kernel(shifts, *refs):
    count = len(shifts)
    blocks, rest = refs[: 2 * count], refs[2 * count :]
    near_key, near_value, far_key, far_value = rest[:4]
    earlier, outs, (query_ref, lhs_ref) = rest[4 : -2 - count], rest[-2 - count : -2], rest[-2:]
    depth = near_key.shape[0]
    pieces = 2 * depth // LANES
    half_rows = (lhs_ref.shape[0] - 16) // (2 * count)
    rows = 2 * half_rows
    tails = []
    for i, block in enumerate(blocks):
        for j in range(pieces):
            lhs_ref[i * half_rows : (i + 1) * half_rows, j * LANES : (j + 1) * LANES] = block[
                j * half_rows : (j + 1) * half_rows, :
            ]
        tail = block[pieces * half_rows : pieces * half_rows + pieces, :].astype(jnp.float32)
        tails.append(jnp.concatenate([tail[j : j + 1] for j in range(pieces)], 1))
    tails.append(jnp.zeros((16 - len(tails), 2 * depth), jnp.float32))
    lines = query_ref.shape[0] // GROUPS
    if earlier:
        query_ref[...] = earlier[0][...]
    for i, shift in enumerate(shifts):
        block = blocks[2 * i]
        query_ref[shift * lines : (shift + 1) * lines, :] = block[block.shape[0] - lines :, :]
    total = count * rows
    lhs_ref[total : total + 16, :] = jnp.concatenate(tails, 0).astype(jnp.bfloat16)

    def product(near, far):
        return jnp.dot(
            lhs_ref[:, :depth], near[...], preferred_element_type=jnp.float32
        ) + jnp.dot(lhs_ref[:, depth:], far[...], preferred_element_type=jnp.float32)

    keys = product(near_key, far_key)
    values = product(near_value, far_value)
    high = keys.astype(jnp.bfloat16).astype(jnp.float32)
    low = keys - high
    columns = []
    for array in (high, low, values):
        for j in range(array.shape[1] // LANES):
            columns.append(array[:, j * LANES : (j + 1) * LANES])
    for i, out in enumerate(outs):
        for k, column in enumerate(columns):
            out[k * rows : (k + 1) * rows, :] = column[i * rows : (i + 1) * rows].astype(jnp.bfloat16)
        ends = [c[total + 2 * i : total + 2 * i + 2] for c in columns]
        ends.append(jnp.zeros((16 - 2 * len(columns), LANES), jnp.float32))
        out[len(columns) * rows :, :] = jnp.concatenate(ends, 0).astype(jnp.bfloat16)


def head_queries(parts, head, width):
    sharing = QUERY_HEADS // KEY_VALUE_HEADS
    lines = sharing * width // HEAD_SIZE
    each = parts[0].shape[0] // GROUPS
    found = []
    for group in range(GROUPS):
        for part in parts:
            tiles = part[group * each : (group + 1) * each, :].astype(jnp.float32)
            for line in range(head * sharing, (head + 1) * sharing):
                found += [tiles[start : start + 1] for start in range(line, each, lines)]
    return jnp.concatenate(found, 0).astype(jnp.bfloat16)


def times_transposed(a, b):
    return lax.dot_general(a, b, (((1,), (1,)), ((), ())), preferred_element_type=jnp.float32)


def loaded_kernel(table_ref, split_ref, *refs):
    parts = refs[:PAIR]
    key_ref, value_ref, top_ref, total_ref, numer_ref, query_ref = refs[PAIR:]
    ctx = lax.axis_index("ctx")
    slots, page, width = key_ref.shape
    heads = width // HEAD_SIZE
    split = split_ref[0]
    live = []
    for s in range(slots):
        hit = jnp.int32(0)
        for p in range(table_ref.shape[0]):
            hit = hit | ((table_ref[p] == ctx * slots + s) & (p >= split)).astype(jnp.int32)
        live.append(hit)
    for head in range(heads):
        columns = slice(head * HEAD_SIZE, (head + 1) * HEAD_SIZE)
        queries = head_queries(parts, head, width)
        count = queries.shape[0]
        query_ref[head * count : (head + 1) * count, :] = queries
        scores = [
            jnp.where(live[s] > 0, times_transposed(queries, key_ref[s, :, columns]) * SCALE, masked_score)
            for s in range(slots)
        ]
        top = scores[0].max(-1, keepdims=True)
        for s in range(1, slots):
            top = jnp.maximum(top, scores[s].max(-1, keepdims=True))
        total = jnp.zeros((count, 1), jnp.float32)
        numer = jnp.zeros((count, HEAD_SIZE), jnp.float32)
        for s in range(slots):
            expos = jnp.where(live[s] > 0, jnp.exp(scores[s] - top), 0.0)
            total += expos.sum(-1, keepdims=True)
            numer += jnp.dot(
                expos.astype(jnp.bfloat16), value_ref[s, :, columns], preferred_element_type=jnp.float32
            )
        rows = slice(head * count, (head + 1) * count)
        top_ref[rows, :] = jnp.broadcast_to(top, (count, LANES))
        total_ref[rows, :] = jnp.broadcast_to(total, (count, LANES))
        numer_ref[rows, :] = numer


def sum_kernel(one, other, out):
    out[...] = one[...].astype(jnp.float32) + other[...].astype(jnp.float32)


def front_kernel(split_ref, early, *refs):
    received = refs[: GROUPS - 2]
    (key_bias, value_bias, cosine_ref, sine_ref, query_ref, top_ref, total_ref, numer_ref) = refs[
        GROUPS - 2 : GROUPS + 6
    ]
    key_any, value_any, *outs = refs[GROUPS + 6 : -3]
    front_key, front_value, sems = refs[-3:]
    core, ctx = lax.axis_index("tp"), lax.axis_index("ctx")
    rows, width = front_key.shape
    half_rows = rows // 2
    heads = width // HEAD_SIZE
    sharing = QUERY_HEADS // KEY_VALUE_HEADS
    count = query_ref.shape[0] // heads
    own_queries = count // sharing // (GROUPS * PAIR)
    visible = ctx < split_ref[0]

    def summed(start, size):
        value = early[start : start + size, :]
        for ref in received:
            value += ref[start : start + size, :].astype(jnp.float32)
        return value

    ends = summed(3 * heads * rows, 16)
    row = lax.broadcasted_iota(jnp.int32, (count, 16), 0)
    query_position = (ctx ^ (row // (own_queries * sharing))) * own_queries + row % own_queries
    end_column = lax.broadcasted_iota(jnp.int32, (count, 16), 1)
    end_position = ctx * 2 + jnp.where(end_column == 0, core, 1 - core)
    end_seen = (end_column < 2) & (end_position <= query_position)
    pad = jnp.zeros((14, HEAD_SIZE), jnp.float32)
    end_pairs = []
    for head in range(heads):
        columns = slice(head * HEAD_SIZE, (head + 1) * HEAD_SIZE)
        raw = summed(head * rows, rows) + summed((heads + head) * rows, rows)
        value = (summed((2 * heads + head) * rows, rows) + value_bias[:, columns]).astype(jnp.bfloat16)
        end_raw = ends[2 * head : 2 * head + 2] + ends[2 * (heads + head) : 2 * (heads + head) + 2]
        end_value = ends[2 * (2 * heads + head) : 2 * (2 * heads + head) + 2] + value_bias[:, columns]
        end_raw = jnp.concatenate([end_raw + key_bias[:, columns], pad], 0)
        end_value = jnp.concatenate([end_value, pad], 0).astype(jnp.bfloat16)
        raw = raw + key_bias[:, columns]

        def rotated(k, part):
            turned = pltpu.roll(k, HEAD_SIZE // 2, 1)
            return (k * cosine_ref[part, :] + turned * sine_ref[part, :]).astype(jnp.bfloat16)

        key = rotated(raw, slice(0, rows))
        end_key = rotated(end_raw, slice(rows, rows + 16))
        for half in range(2):
            to = pl.ds(pl.multiple_of(lax.rem(core + half, 2) * half_rows, half_rows), half_rows)
            front_key[to, columns] = key[half * half_rows : (half + 1) * half_rows]
            front_value[to, columns] = value[half * half_rows : (half + 1) * half_rows]
        end_pairs.append((key, value, end_key, end_value))
    leaving = [
        pltpu.make_async_copy(front_key, key_any, sems.at[0]),
        pltpu.make_async_copy(front_value, value_any, sems.at[1]),
    ]
    for copy in leaving:
        copy.start()
    for head, (key, value, end_key, end_value) in enumerate(end_pairs):
        part = slice(head * count, (head + 1) * count)
        queries = query_ref[part, :]
        scores = jnp.where(visible, times_transposed(queries, key) * SCALE, masked_score)
        end_scores = jnp.where(end_seen, times_transposed(queries, end_key) * SCALE, masked_score)
        old_top = top_ref[part, :]
        top = jnp.maximum(scores.max(-1, keepdims=True), end_scores.max(-1, keepdims=True))
        top = jnp.maximum(old_top, top)
        factor = jnp.exp(old_top - top)
        expos = jnp.where(visible, jnp.exp(scores - top), 0.0)
        end_expos = jnp.where(end_seen, jnp.exp(end_scores - top[:, :16]), 0.0)
        total = total_ref[part, :] * factor + (
            expos.sum(-1, keepdims=True) + end_expos.sum(-1, keepdims=True)
        )
        numer = (
            numer_ref[part, :] * factor
            + jnp.dot(expos.astype(jnp.bfloat16), value, preferred_element_type=jnp.float32)
            + jnp.dot(end_expos.astype(jnp.bfloat16), end_value, preferred_element_type=jnp.float32)
        )
        each = own_queries * sharing
        split = PAIR * each
        stats = jnp.concatenate(
            [
                kept_stats(top[:split, 0:1], total[:split, 0:1]),
                sent_stats(top[split:, 0:1], total[split:, 0:1]).astype(jnp.float32),
            ],
            0,
        )
        for slot in range(GROUPS * PAIR):
            start = (slot % PAIR * 2 * heads + head) * each
            at = slice(slot * each, (slot + 1) * each)
            out = outs[slot // PAIR]
            out[start : start + each, :] = numer[at].astype(out.dtype)
            out[start + heads * each : start + (heads + 1) * each, :] = stats[at].astype(out.dtype)
    for copy in leaving:
        copy.wait()


def kept_stats(top, total):
    lane = lax.broadcasted_iota(jnp.int32, (top.shape[0], LANES), 1)
    return jnp.where(lane < LANES // 2, top, total)


def sent_stats(top, total):
    terms = []
    for rest, count in ((top, 3), (total, 2)):
        for _ in range(count):
            term = rest.astype(jnp.bfloat16).astype(jnp.float32)
            terms.append(term)
            rest = rest - term
    part = lax.broadcasted_iota(jnp.int32, (top.shape[0], LANES), 1) // 16
    stats = jnp.broadcast_to(terms[-1], part.shape)
    for i, term in enumerate(terms[:-1]):
        stats = jnp.where(part == i, term, stats)
    return stats.astype(jnp.bfloat16)


def merged(kept, others, start, rows):
    half = LANES // 2
    stats = kept[start + rows : start + 2 * rows, :]
    tops, totals = [stats[:, 0:1]], [stats[:, half : half + 1]]
    numers = [kept[start : start + rows, :]]
    for other in others:
        terms = other[start + rows : start + 2 * rows, :].astype(jnp.float32)
        tops.append((terms[:, 0:1] + terms[:, 16:17]) + terms[:, 32:33])
        totals.append(terms[:, 48:49] + terms[:, 64:65])
        numers.append(other[start : start + rows, :].astype(jnp.float32))
    top = functools.reduce(jnp.maximum, tops)
    factors = [jnp.exp(t - top) for t in tops]
    total = sum(f * t for f, t in zip(factors, totals))
    numer = sum(f * n for f, n in zip(factors, numers))
    return numer, top, total


def merge_kernel(kept, *refs):
    others, (keep_ref, send_ref) = refs[:-2], refs[-2:]
    each = keep_ref.shape[0]
    rows = each // 2
    numer, top, total = merged(kept, others, 0, rows)
    keep_ref[:rows, :] = numer
    keep_ref[rows:, :] = kept_stats(top, total)
    numer, top, total = merged(kept, others, each, rows)
    send_ref[:rows, :] = numer.astype(jnp.bfloat16)
    send_ref[rows:, :] = sent_stats(top, total)


def last_kernel(kept, *refs):
    others, out_ref = refs[:-1], refs[-1]
    numer, _, total = merged(kept, others, 0, kept.shape[0] // 2)
    result = numer / total
    queries = out_ref.shape[0]
    pieces = [result[s : s + queries] for s in range(0, result.shape[0], queries)]
    out_ref[...] = jnp.concatenate(pieces, 1).astype(jnp.bfloat16)


def exchange_plan(
    hidden,
    suffix_hidden,
    norm_gain,
    key_matrix,
    value_matrix,
    key_offset_bias,
    value_offset_bias,
    suffix_query_rows,
    slot_keys,
    slot_values,
    page_slot_table,
    split_page,
):
    n_ctx = GROUPS * PAIR
    ctx = lax.axis_index("ctx").astype(jnp.int32)
    core = lax.axis_index("tp").astype(jnp.int32)
    rows, features = hidden.shape
    half_rows = rows // 2
    width = key_matrix.shape[1]
    query_width = suffix_query_rows.shape[1]
    prefix_len = page_slot_table.shape[0] * slot_keys.shape[1]
    smem = pl.BlockSpec(memory_space=pltpu.SMEM)
    vmem = pl.BlockSpec(memory_space=pltpu.VMEM)
    params = pltpu.CompilerParams(vmem_limit_bytes=48 * 1024 * 1024)

    def move(array, target):
        pairs = []
        for c in range(n_ctx):
            for t in range(2):
                to_c, to_t = target(c, t)
                pairs.append((c * 2 + t, to_c * 2 + to_t))
        return lax.ppermute(array, ("ctx", "tp"), pairs)

    def partner(away):
        return lambda c, t: (c ^ away, t)

    def along(shift):
        return partner(shift * PAIR)

    def beside(c, t):
        return (c ^ 1, t)

    def sibling(c, t):
        return (c, 1 - t)

    hbm = pl.BlockSpec(memory_space=pltpu.HBM)
    pieces = features // GROUPS // LANES
    own_queries = suffix_query_rows.shape[0]
    lines = query_width // LANES
    block_rows = pieces * half_rows + pieces + own_queries * lines
    blocks = {}
    for shifts in (tuple(far_first()[:1]), tuple(far_first()[1:]) + (0,)):
        found = pl.pallas_call(
            functools.partial(norm_kernel, shifts),
            in_specs=[hbm] * 4,
            out_specs=[hbm] * len(shifts),
            out_shape=[jax.ShapeDtypeStruct((block_rows, LANES), jnp.bfloat16)] * len(shifts),
            scratch_shapes=[
                pltpu.VMEM((half_rows, features), jnp.bfloat16),
                pltpu.VMEM(suffix_hidden.shape, jnp.bfloat16),
                pltpu.VMEM((1, features), jnp.float32),
                pltpu.VMEM(suffix_query_rows.shape, jnp.bfloat16),
                pltpu.VMEM((1, features), jnp.float32),
            ]
            + [pltpu.VMEM((block_rows, LANES), jnp.bfloat16)] * len(shifts)
            + [pltpu.SemaphoreType.DMA((CHUNKS + 3,)), pltpu.SemaphoreType.DMA((len(shifts),))],
            compiler_params=pltpu.CompilerParams(vmem_limit_bytes=60 * 1024 * 1024),
            cost_estimate=pl.CostEstimate(
                flops=4 * half_rows * features,
                bytes_accessed=4 * half_rows * features,
                transcendentals=0,
            ),
            name="norm_rows",
        )(suffix_query_rows, hidden, suffix_hidden, norm_gain.reshape(1, features))
        blocks.update(zip(shifts, found))
    own = blocks[0]
    late, blocks[2] = lax.optimization_barrier((value_matrix, blocks[2]))
    weights = (key_matrix, late)
    far = [move(matrix, beside) for matrix in weights]

    mine = {s: move(blocks[s], along(s)) for s in far_first()}
    inverse_freq = rope_base ** (
        -(jnp.arange(HEAD_SIZE // 2, dtype=jnp.float32) * (2.0 / HEAD_SIZE))
    )
    row = jnp.arange(rows + 16, dtype=jnp.int32)
    front_position = ctx * rows + (row + core * half_rows) % rows
    end_position = prefix_len + ctx * 2 + jnp.where(row == rows, core, 1 - core)
    position = jnp.where(row < rows, front_position, end_position)
    angles = position.astype(jnp.float32)[:, None] * inverse_freq[None, :]
    cosine, sine = jnp.cos(angles), jnp.sin(angles)
    cosine = jnp.concatenate([cosine, cosine], 1)
    sine = jnp.concatenate([-sine, sine], 1)

    first = far_first()[0]
    mine[0] = pl.pallas_call(
        fetch_kernel,
        in_specs=[hbm],
        out_specs=vmem,
        out_shape=jax.ShapeDtypeStruct(own.shape, own.dtype),
        scratch_shapes=[pltpu.SemaphoreType.DMA],
        compiler_params=params,
        cost_estimate=pl.CostEstimate(flops=0, bytes_accessed=64 * 1024 * 1024, transcendentals=0),
        name="fetch_own",
    )(own)
    mine[first], mine[0], cosine, sine = lax.optimization_barrier(
        (mine[first], mine[0], cosine, sine)
    )
    blocks[0], far[0] = lax.optimization_barrier((blocks[0], far[0]))
    theirs = {s: move(blocks[0] if s == 0 else mine[s], sibling) for s in [0] + far_first()}

    part_rows = 3 * (width // LANES) * rows + 16
    partials, own_tiles = {}, []
    for shifts in ((0, first), tuple(far_first()[1:])):
        *found, tiles = pl.pallas_call(
            functools.partial(project_kernel, shifts),
            in_specs=[vmem] * (2 * len(shifts) + 4 + len(own_tiles)),
            out_specs=[vmem] * (len(shifts) + 1),
            out_shape=[jax.ShapeDtypeStruct((part_rows, LANES), jnp.bfloat16)] * len(shifts)
            + [jax.ShapeDtypeStruct((GROUPS * own_queries * lines, LANES), jnp.bfloat16)],
            scratch_shapes=[
                pltpu.VMEM((len(shifts) * rows + 16, PAIR * features // n_ctx), jnp.bfloat16)
            ],
            compiler_params=params,
            cost_estimate=pl.CostEstimate(
                flops=2 * len(shifts) * rows * 2 * width * features // GROUPS,
                bytes_accessed=6 * 1024 * 1024,
                transcendentals=0,
            ),
            name="project",
        )(
            *[part[s] for s in shifts for part in (mine, theirs)],
            key_matrix,
            value_matrix,
            *far,
            *own_tiles,
        )
        partials.update(zip(shifts, found))
        own_tiles = [tiles]
    (own_tiles,) = own_tiles
    received = [move(partials[s], along(s)) for s in far_first()]
    early = pl.pallas_call(
        sum_kernel,
        in_specs=[vmem] * 2,
        out_specs=vmem,
        out_shape=jax.ShapeDtypeStruct((part_rows, LANES), jnp.float32),
        compiler_params=params,
        cost_estimate=pl.CostEstimate(flops=0, bytes_accessed=16 * 1024 * 1024, transcendentals=0),
        name="sum_early",
    )(partials[0], received[0])
    beside_tiles = move(own_tiles, beside)

    states = n_ctx * own_queries * query_width // HEAD_SIZE
    state = jax.ShapeDtypeStruct((states, LANES), jnp.float32)
    top, total, numer, queries = pl.pallas_call(
        loaded_kernel,
        in_specs=[smem, smem] + [vmem] * (PAIR + 2),
        out_specs=[vmem] * 4,
        out_shape=[state] * 3 + [jax.ShapeDtypeStruct((states, LANES), jnp.bfloat16)],
        compiler_params=params,
        cost_estimate=pl.CostEstimate(
            flops=4 * states * slot_keys.shape[0] * slot_keys.shape[1] * HEAD_SIZE,
            bytes_accessed=4 * slot_keys.size,
            transcendentals=states * slot_keys.shape[0] * slot_keys.shape[1],
        ),
        name="loaded_attention",
    )(page_slot_table, split_page, own_tiles, beside_tiles, slot_keys, slot_values)


    def payload(kind, slots):
        return jax.ShapeDtypeStruct((2 * slots * states // n_ctx, LANES), kind)

    row_shape = jax.ShapeDtypeStruct((rows, width), jnp.bfloat16)
    front_key, front_value, kept, *sent = pl.pallas_call(
        front_kernel,
        in_specs=[smem] + [vmem] * (GROUPS + 7),
        out_specs=[hbm] * 2 + [vmem] * GROUPS,
        scratch_shapes=[pltpu.VMEM((rows, width), jnp.bfloat16)] * 2 + [pltpu.SemaphoreType.DMA((2,))],
        out_shape=[row_shape] * 2 + [payload(jnp.float32, PAIR)] + [payload(jnp.bfloat16, PAIR)] * (GROUPS - 1),
        compiler_params=params,
        cost_estimate=pl.CostEstimate(flops=4 * states * rows * HEAD_SIZE, bytes_accessed=2 * 1024 * 1024, transcendentals=states * rows),
        name="front_attention",
    )(
        split_page,
        early,
        *received[1:],
        key_offset_bias.reshape(1, width),
        value_offset_bias.reshape(1, width),
        cosine,
        sine,
        queries,
        top,
        total,
        numer,
    )
    kept, sent = pl.pallas_call(
        merge_kernel,
        in_specs=[vmem] * GROUPS,
        out_specs=[vmem] * 2,
        out_shape=[payload(jnp.float32, 1), payload(jnp.bfloat16, 1)],
        compiler_params=params,
        name="merge",
    )(kept, *[move(sent[s - 1], along(s)) for s in range(GROUPS - 1, 0, -1)])
    attended = pl.pallas_call(
        last_kernel,
        in_specs=[vmem] * 2,
        out_specs=vmem,
        out_shape=jax.ShapeDtypeStruct((own_queries, query_width), jnp.bfloat16),
        compiler_params=params,
        name="finish",
    )(kept, move(sent, beside))
    return (front_key, front_value, attended)


def solution(mesh):
    per_device = exchange_plan if mesh.shape["ctx"] == GROUPS * PAIR else gathered_plan
    return jax.shard_map(
        per_device,
        mesh=mesh,
        in_specs=(
            P(("req", "ctx"), None),
            P(("req", "ctx"), None),
            P(),
            P("ctx", "tp"),
            P("ctx", "tp"),
            P("tp"),
            P("tp"),
            P(("req", "ctx"), "tp"),
            P(("req", "ctx"), None, "tp"),
            P(("req", "ctx"), None, "tp"),
            P("req"),
            P("req"),
        ),
        out_specs=(P(("req", "ctx"), "tp"), P(("req", "ctx"), "tp"), P(("req", "ctx"), "tp")),
        check_vma=False,
    )
```
